32 devices in a mesh: group: 2 (over y), expert: 4 (over z), segment: 2 (over core), attn: 2 (over x).
Axes of the slice: x: 2, y: 2, z: 4, core: 2. Of those that a mesh axis runs over, the one named last changes fastest.
Arguments:
- res_cache: bfloat16 [128, 256, 576], P(('group', 'expert', 'segment', 'attn')), parts along dimension 0, may hold values from -8 to 8
- res_scales: bfloat16 [128, 4, 256], P(('group', 'expert', 'segment', 'attn')), parts along dimension 0, may hold values from 0.125 to 1
- res_lengths: int32 [128], P(('group', 'expert', 'segment', 'attn')), parts along dimension 0, may hold values from 2 to 256, as said below
- res_query: bfloat16 [128, 128, 576], P(('group', 'expert', 'segment', 'attn')), parts along dimension 0, may hold values from -256 to 256
- new_cache: bfloat16 [512, 128, 576], P(('group', 'expert', 'segment', 'attn')), parts along dimension 0, may hold values from -8 to 8
- new_scales: bfloat16 [512, 4, 128], P(('group', 'expert', 'segment', 'attn')), parts along dimension 0, may hold values from 0.125 to 1
- new_lengths: int32 [512], P(('group', 'expert', 'segment', 'attn')), parts along dimension 0, may hold values from 2 to 128, as said below
- new_query: bfloat16 [512, 128, 576], P(('group', 'expert', 'segment', 'attn')), parts along dimension 0, may hold values from -256 to 256
- owner: int32 [512], P(('group', 'expert', 'segment', 'attn')), parts along dimension 0, may hold values from 0 to 3, as said below
Outputs:
- res_context: bfloat16 [128, 128, 512], P(('group', 'expert', 'segment', 'attn')), parts along dimension 0
- new_context: bfloat16 [512, 128, 512], P(('group', 'expert', 'segment', 'attn')), parts along dimension 0
- owned_cache: bfloat16 [1024, 128, 576], P(('group', 'expert', 'segment', 'attn')), parts along dimension 0
- owned_scales: bfloat16 [1024, 4, 128], P(('group', 'expert', 'segment', 'attn')), parts along dimension 0
The draws below stay inside these ranges and needn't reach their ends.
There are 2 independent parts, one for each index of `group`. The reference program is written for one: setup_inputs(seed, part) draws one part's arguments, and reference() takes and returns one part's arrays. A program takes and returns all parts, laid end to end along the dimension named above; each array names one. Nothing has to cross between parts.
Inputs may be any that keep to these rules, and one draw needn't show every extreme that they name: `res_lengths`: every device holds a resident request of length 256. `new_lengths`: every device holds a new request of length 128. Of the 16 requests of one device at most 8 name the same owner; in every draw one owner index is named by exactly 8 requests of every device.
All inputs are finite; a program needn't handle non-finite values.
Results may differ from the reference program's by a relative error of at most 0.0039.
Values may be sent and summed in bfloat16 or wider, within the bound.
No kernel may reach another device: no remote copies, remote signals or barrier semaphores. Data moves between devices by JAX's collectives and lax.ppermute only.
A program may use at most 64 MiB of HBM per device.

```python
import math
import jax
import jax.numpy as jnp
from jax import lax

HEADS = 128
LATENT = 512
ROPE = 64
BLOCK = 128
RES = 4
CTX = 256
NEW = 16
PLEN = 128
CAP = 8
RES_ALL = 64
NEW_ALL = 256
SLOTS_ALL = 512
N_EXPERT = 4
N_SEGMENT = 2
N_ATTN = 2


def rope_columns(key, salt, requests, positions):
    key = jax.random.fold_in(key, salt)
    return jnp.clip(jax.random.normal(key, (requests, positions, ROPE), jnp.float32), -4.0, 4.0)


def latent_columns(key, requests, positions):
    key_centre, key_noise = jax.random.split(key)
    centre = jnp.clip(jax.random.normal(key_centre, (requests, 1, LATENT), jnp.float32), -4.0, 4.0)
    noise = jnp.clip(jax.random.normal(key_noise, (requests, positions, LATENT), jnp.float32), -4.0, 4.0)
    return centre + noise


def drawn_query(key, requests):
    return jnp.clip(jax.random.normal(key, (requests, HEADS, LATENT + ROPE), jnp.float32), -4.0, 4.0)


def ragged_lengths(key, per_device, longest):
    device_count = N_EXPERT * N_SEGMENT * N_ATTN
    key_lengths, key_longest = jax.random.split(key)
    lengths = jax.random.randint(key_lengths, (device_count, per_device), 2, longest + 1)
    chosen = jax.random.randint(key_longest, (device_count, 1), 0, per_device)
    lengths = jnp.where(jnp.arange(per_device)[None, :] == chosen, longest, lengths)
    return lengths.reshape(-1).astype(jnp.int32)


def draw_res_cache(key, part):
    rope = rope_columns(key, 1, RES_ALL, CTX)
    key = jax.random.fold_in(key, 31)
    latent = latent_columns(key, RES_ALL, CTX)
    return jnp.concatenate([latent, rope], axis=-1).astype(jnp.bfloat16)


def draw_res_query(key, part):
    key = jax.random.fold_in(key, 32)
    query = drawn_query(key, RES_ALL)
    return query.astype(jnp.bfloat16)


def draw_new_cache(key, part):
    rope = rope_columns(key, 2, NEW_ALL, PLEN)
    key = jax.random.fold_in(key, 33)
    latent = latent_columns(key, NEW_ALL, PLEN)
    return jnp.concatenate([latent, rope], axis=-1).astype(jnp.bfloat16)


def draw_new_query(key, part):
    key = jax.random.fold_in(key, 34)
    query = drawn_query(key, NEW_ALL)
    return query.astype(jnp.bfloat16)


def draw_res_lengths(key, part):
    key = jax.random.fold_in(key, 41)
    return ragged_lengths(key, RES, CTX)


def draw_new_lengths(key, part):
    key = jax.random.fold_in(key, 42)
    return ragged_lengths(key, NEW, PLEN)


def draw_owner(key, part):
    key = jax.random.fold_in(key, 51)
    device_count = N_EXPERT * N_SEGMENT * N_ATTN
    key_hot, key_rows = jax.random.split(key)
    hot_owner = jax.random.randint(key_hot, (), 0, N_EXPERT)
    others = (hot_owner + 1 + jnp.arange((N_EXPERT - 1) * CAP) // CAP) % N_EXPERT

    def one_device(device_key):
        key_pool, key_order = jax.random.split(device_key)
        pool = jax.random.permutation(key_pool, others)[:NEW - CAP]
        row = jnp.concatenate([jnp.full((CAP,), hot_owner), pool])
        return jax.random.permutation(key_order, row)
    table = jax.vmap(one_device)(jax.random.split(key_rows, device_count))
    return table.reshape(-1).astype(jnp.int32)


def block_scale(key, shape, cuts, smallest, high):
    level, own = 1.0, jax.random.fold_in(key, 6)
    for position, shards_of in cuts:
        steps = jnp.exp(jax.random.uniform(jax.random.fold_in(own, position), (shards_of,), jnp.float32, smallest / len(cuts), high / len(cuts)))
        level = level * jnp.repeat(steps, shape[position] // shards_of).reshape([-1 if axis == position else 1 for axis in range(len(shape))])
    return level


def setup_inputs(seed: int = 0, part: int = 0) -> dict:
    seeds = jax.random.split(jax.random.key(seed), 10)
    part_splits = jax.random.split(jax.random.fold_in(seeds[9], part), 10)
    res_cache = draw_res_cache(jax.random.fold_in(jax.random.fold_in(seeds[9], part), 71), part)
    res_scales = jnp.clip(jnp.exp(math.log(1.0) - 2.0794415 * jax.random.uniform(part_splits[1], (RES_ALL, LATENT // BLOCK, CTX), jnp.float32) ** block_scale(part_splits[1], (RES_ALL, LATENT // BLOCK, CTX), ((0, 16),), -0.2, 0.2)), 0.125, 1.0).astype(jnp.bfloat16)
    res_lengths = draw_res_lengths(jax.random.fold_in(jax.random.fold_in(seeds[9], part), 71), part)
    res_query = draw_res_query(jax.random.fold_in(jax.random.fold_in(seeds[9], part), 71), part)
    new_cache = draw_new_cache(jax.random.fold_in(jax.random.fold_in(seeds[9], part), 71), part)
    new_scales = jnp.clip(jnp.exp(math.log(1.0) - 2.0794415 * jax.random.uniform(part_splits[5], (NEW_ALL, LATENT // BLOCK, PLEN), jnp.float32) ** block_scale(part_splits[5], (NEW_ALL, LATENT // BLOCK, PLEN), ((0, 16),), -0.2, 0.2)), 0.125, 1.0).astype(jnp.bfloat16)
    new_lengths = draw_new_lengths(jax.random.fold_in(jax.random.fold_in(seeds[9], part), 71), part)
    new_query = draw_new_query(jax.random.fold_in(jax.random.fold_in(seeds[9], part), 71), part)
    owner = draw_owner(jax.random.fold_in(jax.random.fold_in(seeds[9], part), 71), part)
    return dict(res_cache=res_cache, res_scales=res_scales, res_lengths=res_lengths, res_query=res_query, new_cache=new_cache, new_scales=new_scales, new_lengths=new_lengths, new_query=new_query, owner=owner)


softmax_scale = 192.0 ** -0.5


def attend(query, cache, scales, lengths):
    batch_rows = query.shape[0]
    head_count = query.shape[1]
    positions = cache.shape[1]
    blocks = LATENT // BLOCK
    query_latent = query[:, :, :LATENT].astype(jnp.float32).reshape(batch_rows, head_count, blocks, BLOCK)
    cache_latent = cache[:, :, :LATENT].astype(jnp.float32).reshape(batch_rows, positions, blocks, BLOCK)
    partial_value = jnp.einsum("rhbc,rpbc->rbhp", query_latent, cache_latent)
    rope_term = jnp.einsum("rhc,rpc->rhp", query[:, :, LATENT:].astype(jnp.float32), cache[:, :, LATENT:].astype(jnp.float32))
    factors = scales.astype(jnp.float32)
    scores = (jnp.sum(partial_value * factors[:, :, None, :], axis=1) + rope_term) * softmax_scale
    valid_rows = jnp.arange(positions)[None, :] < lengths[:, None]
    scores = jnp.where(valid_rows[:, None, :], scores, -jnp.inf)
    row_max = jnp.max(scores, axis=-1, keepdims=True)
    exponent = jnp.exp(scores - row_max)
    probabilities = exponent / jnp.sum(exponent, axis=-1, keepdims=True)
    weights = (probabilities[:, None, :, :] * factors[:, :, None, :]).astype(jnp.bfloat16)
    context = jnp.einsum("rbhp,rpbc->rhbc", weights.astype(jnp.float32), cache_latent)
    return context.reshape(batch_rows, head_count, LATENT).astype(jnp.bfloat16)


def blockwise(query, cache, scales, lengths, per_device):
    device_count = N_EXPERT * N_SEGMENT * N_ATTN

    def one_device(pieces):
        return attend(pieces[0], pieces[1], pieces[2], pieces[3])

    stacked = (query.reshape((device_count, per_device) + query.shape[1:]),
               cache.reshape((device_count, per_device) + cache.shape[1:]),
               scales.reshape((device_count, per_device) + scales.shape[1:]),
               lengths.reshape(device_count, per_device))
    result = lax.map(one_device, stacked)
    return result.reshape((device_count * per_device,) + result.shape[2:])


def reference(res_cache, res_scales, res_lengths, res_query, new_cache, new_scales, new_lengths, new_query, owner):
    device_count = N_EXPERT * N_SEGMENT * N_ATTN
    res_context = blockwise(res_query, res_cache, res_scales, res_lengths, RES)
    new_context = blockwise(new_query, new_cache, new_scales, new_lengths, NEW)
    owner_table = owner.reshape(device_count, NEW)
    indices = jnp.arange(NEW, dtype=jnp.int32)
    earlier = indices[None, :] < indices[:, None]
    same_owner = owner_table[:, :, None] == owner_table[:, None, :]
    arrival_rank = jnp.sum(jnp.logical_and(same_owner, earlier[None, :, :]), axis=2).astype(jnp.int32)
    device_ids = jnp.arange(device_count, dtype=jnp.int32)
    expert_ids = device_ids // (N_SEGMENT * N_ATTN)
    segment_ids = (device_ids // N_ATTN) % N_SEGMENT
    attn_ids = device_ids % N_ATTN
    target_device = (owner_table * N_SEGMENT + (1 - segment_ids)[:, None]) * N_ATTN + attn_ids[:, None]
    slots = (target_device * (N_EXPERT * CAP) + expert_ids[:, None] * CAP + arrival_rank).reshape(-1).astype(jnp.int32)
    live_rows = jnp.arange(PLEN)[None, :] < new_lengths[:, None]
    masked_cache = jnp.where(live_rows[:, :, None], new_cache, jnp.zeros((), new_cache.dtype))
    masked_scales = jnp.where(live_rows[:, None, :], new_scales, jnp.zeros((), new_scales.dtype))
    owned_cache = jnp.zeros((SLOTS_ALL, PLEN, LATENT + ROPE), new_cache.dtype).at[slots].set(masked_cache)
    owned_scales = jnp.zeros((SLOTS_ALL, LATENT // BLOCK, PLEN), new_scales.dtype).at[slots].set(masked_scales)
    return (res_context, new_context, owned_cache, owned_scales)
```

```python
import functools
import jax
import jax.numpy as jnp
from jax import lax
from jax.experimental import pallas as pl
from jax.experimental.pallas import tpu as pltpu
from jax.sharding import PartitionSpec as P

LATENT = 512
BLOCK = 128
UNIT = 64
FIRST = 2
PLANS = ((11, 7), (12, 7), (13, 8), (14, 10), (16, 16))

softmax_scale = 192.0 ** (-0.5)
MIB = 1 << 20


def attend_kernel(lengths_ref, query_ref, cache_ref, scales_ref, out_ref):
    per_step, _, positions = cache_ref.shape
    blocks = LATENT // BLOCK
    contract_rows = (((0,), (0,)), ((), ()))
    contract_positions = (((1,), (1,)), ((), ()))
    for r in range(per_step):
        length = lengths_ref[pl.program_id(0) * per_step + r]
        factors = scales_ref[r].astype(jnp.float32)
        scores = lax.dot_general(
            query_ref[r, LATENT:, :], cache_ref[r, LATENT:, :], contract_rows, preferred_element_type=jnp.float32
        )
        for b in range(blocks):
            part = lax.dot_general(
                query_ref[r, b * BLOCK : (b + 1) * BLOCK, :],
                cache_ref[r, b * BLOCK : (b + 1) * BLOCK, :],
                contract_rows,
                preferred_element_type=jnp.float32,
            )
            scores = scores + part * factors[b : b + 1, :]
        live = lax.broadcasted_iota(jnp.int32, (1, positions), 1) < length
        scores = jnp.where(live, scores * softmax_scale, -jnp.inf)
        exponent = jnp.exp(scores - jnp.max(scores, axis=-1, keepdims=True))
        probabilities = exponent / jnp.sum(exponent, axis=-1, keepdims=True)
        for b in range(blocks):
            weights = (probabilities * factors[b : b + 1, :]).astype(jnp.bfloat16)
            out_ref[r, :, b * BLOCK : (b + 1) * BLOCK] = lax.dot_general(
                weights,
                cache_ref[r, b * BLOCK : (b + 1) * BLOCK, :],
                contract_positions,
                preferred_element_type=jnp.float32,
            ).astype(jnp.bfloat16)


def attend(query, cache, scales, lengths, per_step):
    requests, columns, heads = query.shape
    positions = cache.shape[2]
    return pl.pallas_call(
        attend_kernel,
        grid=(requests // per_step,),
        in_specs=[
            pl.BlockSpec(memory_space=pltpu.SMEM),
            pl.BlockSpec((per_step, columns, heads), lambda i: (i, 0, 0)),
            pl.BlockSpec((per_step, columns, positions), lambda i: (i, 0, 0)),
            pl.BlockSpec((per_step, scales.shape[1], positions), lambda i: (i, 0, 0)),
        ],
        out_specs=pl.BlockSpec((per_step, heads, LATENT), lambda i: (i, 0, 0)),
        out_shape=jax.ShapeDtypeStruct((requests, heads, LATENT), jnp.bfloat16),
        compiler_params=pltpu.CompilerParams(vmem_limit_bytes=24 * MIB),
        cost_estimate=pl.CostEstimate(
            flops=4 * requests * heads * positions * columns,
            bytes_accessed=2 * requests * (heads * (columns + LATENT) + positions * columns),
            transcendentals=requests * heads * positions,
        ),
    )(lengths, query, cache, scales)


def stream_gap(rows, columns, positions, window):
    shape = (window, 2 * positions) if rows == "window" else (2 * positions, window)
    first, second = lax.broadcasted_iota(jnp.int32, shape, 0), lax.broadcasted_iota(jnp.int32, shape, 1)
    lane, own = (first, second) if rows == "window" else (second, first)
    within = lane % (2 * UNIT)
    place = lane // (2 * UNIT) * UNIT + within % UNIT
    position = own % positions
    meet = within // UNIT == own // positions
    return jnp.where(meet, place - position, -4096), position


def pack_kernel(owner_ref, lengths_ref, me_ref, cache_ref, *refs):
    experts = 4
    out_refs, (acc, ends) = refs[:-2], refs[-2:]
    requests, columns, positions = cache_ref.shape
    half = columns // 2
    window = (positions // UNIT + 1) * 2 * UNIT
    gap, position = stream_gap("request", columns, positions, window)
    for k in range(experts):
        ends[k] = 0
        acc[k, 0] = jnp.zeros((half, 2 * UNIT), jnp.bfloat16)

    def place(i, _):
        k = (owner_ref[i] - me_ref[0]) & (experts - 1)
        length = lengths_ref[i]
        start = ends[k]
        ends[k] = start + length
        unit, shift = start // UNIT, start % UNIT
        move = jnp.logical_and(gap == shift, position < length).astype(jnp.bfloat16)
        both = jnp.concatenate([cache_ref[i, :half, :], cache_ref[i, half:, :]], axis=1)
        moved = jnp.dot(both, move, preferred_element_type=jnp.float32).astype(jnp.bfloat16)
        acc[k, unit] += moved[:, : 2 * UNIT]
        for j in range(1, window // (2 * UNIT)):
            acc[k, unit + j] = moved[:, 2 * UNIT * j : 2 * UNIT * (j + 1)]
        return 0

    lax.fori_loop(0, requests, place, 0, unroll=4)
    for k in range(1, experts):
        out_refs[k][...] = acc[k, :FIRST]
    for k in range(experts):
        out_refs[experts][k] = acc[k, : out_refs[experts].shape[1]]
    out_refs[0][...] = acc[0, : out_refs[0].shape[0]]


def pack(owner, lengths, me, cache, units):
    requests, columns, positions = cache.shape
    half = columns // 2
    window = positions // UNIT + 1
    smem = pl.BlockSpec(memory_space=pltpu.SMEM)
    vmem = pl.BlockSpec(memory_space=pltpu.VMEM)
    unit = (half, 2 * UNIT)
    outs = [jax.ShapeDtypeStruct((units,) + unit, jnp.bfloat16)]
    outs += [jax.ShapeDtypeStruct((FIRST,) + unit, jnp.bfloat16)] * 3
    outs += [jax.ShapeDtypeStruct((4, units) + unit, jnp.bfloat16)]
    return pl.pallas_call(
        pack_kernel,
        in_specs=[smem, smem, smem, vmem],
        out_specs=[vmem] * len(outs),
        out_shape=outs,
        scratch_shapes=[pltpu.VMEM((4, units + window - 1) + unit, jnp.bfloat16), pltpu.SMEM((4,), jnp.int32)],
        compiler_params=pltpu.CompilerParams(vmem_limit_bytes=40 * MIB),
        cost_estimate=pl.CostEstimate(flops=2 * requests * half * 256 * 384, bytes_accessed=10 * MIB, transcendentals=0),
    )(owner, lengths, me, cache)


def unpack_kernel(meta_ref, place_ref, own_ref, f1, f2, f3, rest, out_ref, held, stage, starts, counts, sems, out_sem):
    experts = 4
    requests = meta_ref.shape[1] // 2
    slots = out_ref.shape[0] // experts
    columns, positions = out_ref.shape[1], out_ref.shape[2]
    half = columns // 2
    window = positions // UNIT + 1
    lanes = window * 2 * UNIT
    me = place_ref[0]
    firsts = (None, f1, f2, f3)

    def source_of(k):
        return (me - k) & (experts - 1)

    for k in range(experts):
        source = source_of(k)

        def note(i, carry):
            rank, end = carry
            mine = meta_ref[source, i] == me
            length = meta_ref[source, requests + i]

            @pl.when(mine)
            def _():
                starts[k, rank] = end
                counts[k, rank] = length

            return (jnp.where(mine, rank + 1, rank), jnp.where(mine, end + length, end))

        rank, end = lax.fori_loop(0, requests, note, (0, 0))
        starts[k, slots] = rank
        counts[k, slots] = end

    def fetches(k, go):
        used = (counts[k, slots] + UNIT - 1) // UNIT
        if k == 0:

            def fetch(u, _):
                go(pltpu.make_async_copy(own_ref.at[u], held.at[k, u], sems.at[k]))
                return 0

            lax.fori_loop(0, used, fetch, 0)
        else:
            go(pltpu.make_async_copy(firsts[k], held.at[k, pl.ds(0, FIRST)], sems.at[k]))
            stream = place_ref[1 + source_of(k)]

            def fetch(u, _):
                go(pltpu.make_async_copy(rest.at[stream, u], held.at[k, u + FIRST], sems.at[k]))
                return 0

            lax.fori_loop(0, jnp.maximum(used - FIRST, 0), fetch, 0)

    for k in range(experts):
        fetches(k, lambda copy: copy.start())
    gap, position = stream_gap("window", columns, positions, lanes)
    for k in range(experts):
        fetches(k, lambda copy: copy.wait())
        used = (counts[k, slots] + UNIT - 1) // UNIT
        for j in range(window - 1):
            held[k, used + j] = jnp.zeros((half, 2 * UNIT), jnp.bfloat16)
        ranks = starts[k, slots]

        def put(rank, _):
            @pl.when(rank < ranks)
            def _():
                start, length = starts[k, rank], counts[k, rank]
                unit, shift = start // UNIT, start % UNIT
                move = jnp.logical_and(gap == shift, position < length).astype(jnp.bfloat16)
                seen = jnp.concatenate([held[k, unit + j] for j in range(window)], axis=1)
                moved = jnp.dot(seen, move, preferred_element_type=jnp.float32).astype(jnp.bfloat16)
                stage[k, rank, :half, :] = moved[:, :positions]
                stage[k, rank, half:, :] = moved[:, positions:]

            @pl.when(rank >= ranks)
            def _():
                stage[k, rank] = jnp.zeros((columns, positions), jnp.bfloat16)

            return 0

        lax.fori_loop(0, slots, put, 0)
        pltpu.make_async_copy(stage.at[k], out_ref.at[pl.ds(source_of(k) * slots, slots)], out_sem.at[k]).start()
    for k in range(experts):
        pltpu.make_async_copy(stage.at[k], out_ref.at[pl.ds(source_of(k) * slots, slots)], out_sem.at[k]).wait()


def unpack(meta, place, own, firsts, rest, slots, columns, positions):
    half = columns // 2
    units = own.shape[0]
    window = positions // UNIT + 1
    smem = pl.BlockSpec(memory_space=pltpu.SMEM)
    hbm = pl.BlockSpec(memory_space=pl.ANY)
    return pl.pallas_call(
        unpack_kernel,
        in_specs=[smem, smem] + [hbm] * 5,
        out_specs=hbm,
        out_shape=jax.ShapeDtypeStruct((4 * slots, columns, positions), jnp.bfloat16),
        scratch_shapes=[
            pltpu.VMEM((4, units + window - 1, half, 2 * UNIT), jnp.bfloat16),
            pltpu.VMEM((4, slots, columns, positions), jnp.bfloat16),
            pltpu.SMEM((4, slots + 1), jnp.int32),
            pltpu.SMEM((4, slots + 1), jnp.int32),
            pltpu.SemaphoreType.DMA((4,)),
            pltpu.SemaphoreType.DMA((4,)),
        ],
        compiler_params=pltpu.CompilerParams(vmem_limit_bytes=40 * MIB),
        cost_estimate=pl.CostEstimate(flops=2 * 32 * half * 256 * 384, bytes_accessed=10 * MIB, transcendentals=0),
    )(meta, place, own, *firsts, rest)


def choose_kernel(owner_ref, lengths_ref, out_ref, loads, worst):
    experts = 4
    rows, requests = owner_ref.shape
    for o in range(experts):
        worst[o] = 0
    for row in range(rows):
        for o in range(experts):
            loads[o] = 0

        def add(i, _):
            o = owner_ref[row, i]
            loads[o] += lengths_ref[row, i]
            return 0

        lax.fori_loop(0, requests, add, 0)
        for o in range(experts):
            if o != row // 2:
                worst[o] = jnp.maximum(worst[o], (loads[o] + UNIT - 1) // UNIT)
    hot, most, second = jnp.int32(0), worst[0], jnp.int32(0)
    for o in range(1, experts):
        second = jnp.maximum(second, jnp.minimum(most, worst[o]))
        hot = jnp.where(worst[o] > most, o, hot)
        most = jnp.maximum(most, worst[o])
    plan = jnp.int32(len(PLANS) - 1)
    for p in range(len(PLANS) - 2, -1, -1):
        plan = jnp.where(jnp.logical_and(most <= PLANS[p][0], second <= PLANS[p][1]), p, plan)
    out_ref[0] = hot * len(PLANS) + plan
    out_ref[1] = hot


def choose(owner, lengths):
    smem = pl.BlockSpec(memory_space=pltpu.SMEM)
    return pl.pallas_call(
        choose_kernel,
        in_specs=[smem, smem],
        out_specs=smem,
        out_shape=jax.ShapeDtypeStruct((2,), jnp.int32),
        scratch_shapes=[pltpu.SMEM((4,), jnp.int32), pltpu.SMEM((4,), jnp.int32)],
    )(owner, lengths)


def other_pairs(hot):
    others = [i for i in range(4) if i != hot]
    permutes = []
    for k in range(3):
        permutes.append([(hot if i == (k - i) % 3 else others[i], others[(k - i) % 3]) for i in range(3)])
    return permutes


def crossed(pairs):
    return [(source * 2 + s, target * 2 + 1 - s) for source, target in pairs for s in range(2)]


def exchange_rest(streams, me, branch):
    units = streams.shape[1]
    axes = ("expert", "segment")

    def send(hot, plan):
        most, second = PLANS[plan]

        def run(streams, me):
            def stream_to(target, size):
                part = lax.dynamic_slice_in_dim(streams, (target - me) & 3, 1, 0)
                return part[0, FIRST:size]

            to_hot = stream_to(jnp.int32(hot), most)
            from_each = [
                lax.ppermute(to_hot, axes, crossed([(source, hot)])) for source in range(4) if source != hot
            ]
            to_others = []
            for pairs in other_pairs(hot):
                target = jnp.int32(0)
                for source, owner in pairs:
                    target = jnp.where(me == source, owner, target)
                to_others.append(lax.ppermute(stream_to(target, second), axes, crossed(pairs)))
            got = []
            for a, b in zip(from_each, to_others):
                a = jnp.pad(a, ((0, units - most), (0, 0), (0, 0)))
                b = jnp.pad(b, ((0, units - second), (0, 0), (0, 0)))
                got.append(jnp.where(me == hot, a, b))
            return jnp.stack(got)

        return run

    branches = [send(hot, plan) for hot in range(4) for plan in range(len(PLANS))]
    return lax.switch(branch, branches, streams, me)


def stream_places(hot, me):
    table = []
    for h in range(4):
        rows = []
        for target in range(4):
            row = [0] * 4
            if target == h:
                for place, source in enumerate(s for s in range(4) if s != h):
                    row[source] = place
            else:
                for place, pairs in enumerate(other_pairs(h)):
                    for source, owner in pairs:
                        if owner == target:
                            row[source] = place
            rows.append(row)
        table.append(rows)
    return jnp.array(table, jnp.int32)[hot, me]


def slot_layout(owner, experts, capacity):
    requests = owner.shape[0]
    indices = jnp.arange(requests, dtype=jnp.int32)
    earlier = indices[None, :] < indices[:, None]
    same_owner = owner[:, None] == owner[None, :]
    arrival_rank = jnp.sum(jnp.logical_and(same_owner, earlier), axis=1)
    target = owner * capacity + arrival_rank
    routing = target[None, :] == jnp.arange(experts * capacity, dtype=jnp.int32)[:, None]
    filled = jnp.any(routing, axis=1)
    source = jnp.sum(jnp.where(routing, indices[None, :], 0), axis=1)
    return (filled, source)


def pick_slots(values, filled, source):
    zero_value = jnp.zeros((), values.dtype)
    return jnp.where(filled[:, None, None], jnp.take(values, source, axis=0), zero_value)


def on_device(
    res_cache,
    res_scales,
    res_lengths,
    res_query,
    new_cache,
    new_scales,
    new_lengths,
    new_query,
    owner,
):
    experts = lax.axis_size("expert")
    sections = lax.axis_size("segment")
    requests, positions, columns = new_cache.shape
    capacity = max(2, 2 * requests // experts)
    live_rows = jnp.arange(positions)[None, :] < new_lengths[:, None]
    zero_value = jnp.zeros((), jnp.bfloat16)
    masked_scales = jnp.where(live_rows[:, None, :], new_scales, zero_value)
    filled, source = slot_layout(owner, experts, capacity)
    send_scales = pick_slots(masked_scales, filled, source)
    swap = [(0, 1), (1, 0)]
    cache_t = jnp.transpose(new_cache, (0, 2, 1))

    def attention():
        res_context = attend(
            jnp.transpose(res_query, (0, 2, 1)), jnp.transpose(res_cache, (0, 2, 1)), res_scales, res_lengths, 1
        )
        new_context = attend(jnp.transpose(new_query, (0, 2, 1)), cache_t, new_scales, new_lengths, 2)
        return res_context, new_context

    if experts != 4 or sections != 2 or positions % UNIT or columns % 32:
        send_cache = pick_slots(jnp.where(live_rows[:, :, None], new_cache, zero_value), filled, source)
        got_cache = lax.all_to_all(send_cache, "expert", split_axis=0, concat_axis=0, tiled=True)
        got_scales = lax.all_to_all(send_scales, "expert", split_axis=0, concat_axis=0, tiled=True)
        owned_cache, owned_scales = lax.ppermute((got_cache, got_scales), "segment", swap)
        return (*attention(), owned_cache, owned_scales)

    me = lax.axis_index("expert")
    section = lax.axis_index("segment")
    units = capacity * positions // UNIT
    own, f1, f2, f3, streams = pack(owner, new_lengths, me[None], cache_t, units)
    firsts = []
    for k, part in ((1, f1), (2, f2), (3, f3)):
        firsts.append(lax.ppermute(part, ("expert", "segment"), crossed([(e, (e + k) % 4) for e in range(4)])))
    own = lax.ppermute(own, "segment", swap)

    facts = jnp.concatenate([owner, new_lengths])[None]
    facts = jnp.broadcast_to(facts, (experts * sections, 2 * requests))
    facts = lax.all_to_all(facts, ("expert", "segment"), split_axis=0, concat_axis=0, tiled=True)
    got_scales = lax.all_to_all(send_scales, "expert", split_axis=0, concat_axis=0, tiled=True)
    owned_scales = lax.ppermute(got_scales, "segment", swap)

    chosen = choose(facts[:, :requests], facts[:, requests:])
    branch, hot = chosen[0], chosen[1]
    res_context, new_context = attention()
    rest = exchange_rest(streams, me, branch)
    from_other = facts.reshape(experts, sections, 2 * requests)[:, 1 - section]
    place = jnp.concatenate([me[None], stream_places(hot, me)])
    owned = unpack(from_other, place, own, firsts, rest, capacity, columns, positions)
    return (res_context, new_context, jnp.transpose(owned, (0, 2, 1)), owned_scales)


def solution(mesh):
    placed = (
        P(("group", "expert", "segment", "attn"), None, None),
        P(("group", "expert", "segment", "attn"), None, None),
        P(("group", "expert", "segment", "attn")),
        P(("group", "expert", "segment", "attn"), None, None),
        P(("group", "expert", "segment", "attn"), None, None),
        P(("group", "expert", "segment", "attn"), None, None),
        P(("group", "expert", "segment", "attn")),
        P(("group", "expert", "segment", "attn"), None, None),
        P(("group", "expert", "segment", "attn")),
    )
    return jax.shard_map(
        on_device,
        mesh=mesh,
        in_specs=placed,
        out_specs=(
            P(("group", "expert", "segment", "attn"), None, None),
            P(("group", "expert", "segment", "attn"), None, None),
            P(("group", "expert", "segment", "attn"), None, None),
            P(("group", "expert", "segment", "attn"), None, None),
        ),
        check_vma=False,
    )
```

```python
import functools
import jax
import jax.numpy as jnp
from jax import lax
from jax.experimental import pallas as pl
from jax.experimental.pallas import tpu as pltpu
from jax.sharding import PartitionSpec as P

LATENT = 512
BLOCK = 128
UNIT = 64
FIRST = 4
PLANS = (
    (11, 7), (11, 8), (12, 7), (12, 8), (13, 7), (13, 9), (15, 10), (16, 16),
)

softmax_scale = 192.0 ** (-0.5)
MIB = 1 << 20
VMEM_LIMIT = 56 * MIB


def attend_kernel(lengths_ref, query_ref, cache_ref, scales_ref, out_ref):
    per_step, _, positions = cache_ref.shape
    blocks = LATENT // BLOCK
    contract_rows = (((0,), (0,)), ((), ()))
    contract_positions = (((1,), (1,)), ((), ()))
    for r in range(per_step):
        length = lengths_ref[pl.program_id(0) * per_step + r]
        factors = scales_ref[r].astype(jnp.float32)
        scores = lax.dot_general(
            query_ref[r, LATENT:, :], cache_ref[r, LATENT:, :], contract_rows, preferred_element_type=jnp.float32
        )
        for b in range(blocks):
            part = lax.dot_general(
                query_ref[r, b * BLOCK : (b + 1) * BLOCK, :],
                cache_ref[r, b * BLOCK : (b + 1) * BLOCK, :],
                contract_rows,
                preferred_element_type=jnp.float32,
            )
            scores = scores + part * factors[b : b + 1, :]
        live = lax.broadcasted_iota(jnp.int32, (1, positions), 1) < length
        scores = jnp.where(live, scores * softmax_scale, -jnp.inf)
        exponent = jnp.exp(scores - jnp.max(scores, axis=-1, keepdims=True))
        probabilities = exponent / jnp.sum(exponent, axis=-1, keepdims=True)
        for b in range(blocks):
            weights = (probabilities * factors[b : b + 1, :]).astype(jnp.bfloat16)
            out_ref[r, :, b * BLOCK : (b + 1) * BLOCK] = lax.dot_general(
                weights,
                cache_ref[r, b * BLOCK : (b + 1) * BLOCK, :],
                contract_positions,
                preferred_element_type=jnp.float32,
            ).astype(jnp.bfloat16)


def attend(query, cache, scales, lengths, per_step):
    requests, columns, heads = query.shape
    positions = cache.shape[2]
    return pl.pallas_call(
        attend_kernel,
        grid=(requests // per_step,),
        in_specs=[
            pl.BlockSpec(memory_space=pltpu.SMEM),
            pl.BlockSpec((per_step, columns, heads), lambda i: (i, 0, 0)),
            pl.BlockSpec((per_step, columns, positions), lambda i: (i, 0, 0)),
            pl.BlockSpec((per_step, scales.shape[1], positions), lambda i: (i, 0, 0)),
        ],
        out_specs=pl.BlockSpec((per_step, heads, LATENT), lambda i: (i, 0, 0)),
        out_shape=jax.ShapeDtypeStruct((requests, heads, LATENT), jnp.bfloat16),
        compiler_params=pltpu.CompilerParams(vmem_limit_bytes=VMEM_LIMIT),
        cost_estimate=pl.CostEstimate(
            flops=4 * requests * heads * positions * columns,
            bytes_accessed=2 * requests * (heads * (columns + LATENT) + positions * columns),
            transcendentals=requests * heads * positions,
        ),
    )(lengths, query, cache, scales)


def stream_gap(rows, columns, positions, window):
    shape = (window, 2 * positions) if rows == "window" else (2 * positions, window)
    first, second = lax.broadcasted_iota(jnp.int32, shape, 0), lax.broadcasted_iota(jnp.int32, shape, 1)
    lane, own = (first, second) if rows == "window" else (second, first)
    within = lane % (2 * UNIT)
    place = lane // (2 * UNIT) * UNIT + within % UNIT
    position = own % positions
    meet = within // UNIT == own // positions
    return jnp.where(meet, place - position, -4096), position


def pack_kernel(owner_ref, lengths_ref, scales_ref, cache_ref, *refs):
    experts = 4
    (own_ref, f1, f2, f3, rest_ref, slots_ref, facts_ref), (held, acc, ends, ranks, in_sem, out_sem) = refs[:7], refs[7:]
    requests, columns, positions = cache_ref.shape
    units = own_ref.shape[0]
    capacity = slots_ref.shape[0] // experts
    half = columns // 2
    window = (positions // UNIT + 1) * 2 * UNIT
    me = lax.axis_index("expert")
    parts = in_sem.shape[0]
    share = requests // parts

    def fetch(part):
        here = pl.ds(part * share, share)
        return pltpu.make_async_copy(cache_ref.at[here], held.at[here], in_sem.at[part])

    for part in range(parts):
        fetch(part).start()
    gap, position = stream_gap("request", columns, positions, window)
    for k in range(experts):
        ends[k] = 0
        ranks[k] = 0
        acc[k, 0] = jnp.zeros((half, 2 * UNIT), jnp.bfloat16)
    slots_ref[...] = jnp.zeros(slots_ref.shape, jnp.bfloat16)
    live = lax.broadcasted_iota(jnp.int32, scales_ref.shape[1:], 1)

    def place(i, _):
        owner = owner_ref[i]
        k = (owner - me) & (experts - 1)
        length = lengths_ref[i]
        start = ends[k]
        ends[k] = start + length
        slot = owner * capacity + ranks[k]
        ranks[k] += 1
        slots_ref[slot] = jnp.where(live < length, scales_ref[i], jnp.zeros((), jnp.bfloat16))
        unit, shift = start // UNIT, start % UNIT
        move = jnp.logical_and(gap == shift, position < length).astype(jnp.bfloat16)
        both = jnp.concatenate([held[i, :half, :], held[i, half:, :]], axis=1)
        moved = jnp.dot(both, move, preferred_element_type=jnp.float32).astype(jnp.bfloat16)
        acc[k, unit] += moved[:, : 2 * UNIT]
        for j in range(1, window // (2 * UNIT)):
            acc[k, unit + j] = moved[:, 2 * UNIT * j : 2 * UNIT * (j + 1)]
        return 0

    for part in range(parts):
        fetch(part).wait()
        lax.fori_loop(part * share, (part + 1) * share, place, 0, unroll=True)
    copies = []
    for k, ref in ((1, f1), (2, f2), (3, f3)):
        copies.append(pltpu.make_async_copy(acc.at[k, pl.ds(0, FIRST)], ref, out_sem.at[len(copies)]))
    for k in range(1, experts):
        later = pl.ds(FIRST, units - FIRST)
        copies.append(pltpu.make_async_copy(acc.at[k, later], rest_ref.at[k - 1], out_sem.at[len(copies)]))
    copies.append(pltpu.make_async_copy(acc.at[0, pl.ds(0, units)], own_ref, out_sem.at[len(copies)]))
    for copy in copies:
        copy.start()
    for row in range(facts_ref.shape[0]):
        for i in range(requests):
            facts_ref[row, i] = owner_ref[i]
            facts_ref[row, requests + i] = lengths_ref[i]
    for copy in copies:
        copy.wait()


def pack(owner, lengths, scales, cache, units, capacity):
    requests, columns, positions = cache.shape
    half = columns // 2
    window = positions // UNIT + 1
    smem = pl.BlockSpec(memory_space=pltpu.SMEM)
    vmem = pl.BlockSpec(memory_space=pltpu.VMEM)
    hbm = pl.BlockSpec(memory_space=pl.ANY)
    unit = (half, 2 * UNIT)
    outs = [jax.ShapeDtypeStruct((units,) + unit, jnp.bfloat16)]
    outs += [jax.ShapeDtypeStruct((FIRST,) + unit, jnp.bfloat16)] * 3
    outs += [jax.ShapeDtypeStruct((3, units - FIRST) + unit, jnp.bfloat16)]
    outs += [jax.ShapeDtypeStruct((4 * capacity,) + scales.shape[1:], jnp.bfloat16)]
    outs += [jax.ShapeDtypeStruct((8, 2 * requests), jnp.int32)]
    return pl.pallas_call(
        pack_kernel,
        in_specs=[smem, smem, vmem, hbm],
        out_specs=[hbm] * 5 + [vmem, smem],
        out_shape=outs,
        scratch_shapes=[
            pltpu.VMEM(cache.shape, jnp.bfloat16),
            pltpu.VMEM((4, units + window - 1) + unit, jnp.bfloat16),
            pltpu.SMEM((4,), jnp.int32),
            pltpu.SMEM((4,), jnp.int32),
            pltpu.SemaphoreType.DMA((4,)),
            pltpu.SemaphoreType.DMA((7,)),
        ],
        compiler_params=pltpu.CompilerParams(vmem_limit_bytes=VMEM_LIMIT),
        cost_estimate=pl.CostEstimate(flops=2 * requests * half * 256 * 384, bytes_accessed=8 * MIB, transcendentals=0),
    )(owner, lengths, scales, cache)


def unpack_kernel(facts_ref, chosen_ref, own_ref, f1, f2, f3, rest, out_ref, held, stage, starts, counts, sems, out_sem):
    experts = 4
    requests = facts_ref.shape[1] // 2
    slots = out_ref.shape[0] // experts
    columns, positions = out_ref.shape[1], out_ref.shape[2]
    half = columns // 2
    window = positions // UNIT + 1
    lanes = window * 2 * UNIT
    me = lax.axis_index("expert")
    other = 1 - lax.axis_index("segment")
    firsts = (None, f1, f2, f3)

    def source_of(k):
        return (me - k) & (experts - 1)

    for k in range(experts):
        row = source_of(k) * 2 + other

        def note(i, carry):
            rank, end = carry
            mine = facts_ref[row, i] == me
            length = facts_ref[row, requests + i]

            @pl.when(mine)
            def _():
                starts[k, rank] = end
                counts[k, rank] = length

            return (jnp.where(mine, rank + 1, rank), jnp.where(mine, end + length, end))

        rank, end = lax.fori_loop(0, requests, note, (0, 0))
        starts[k, slots] = rank
        counts[k, slots] = end

    def fetches(k, go):
        used = (counts[k, slots] + UNIT - 1) // UNIT
        if k == 0:

            def fetch(u, _):
                go(pltpu.make_async_copy(own_ref.at[u], held.at[k, u], sems.at[k]))
                return 0

            lax.fori_loop(0, used, fetch, 0)
        else:
            go(pltpu.make_async_copy(firsts[k], held.at[k, pl.ds(0, FIRST)], sems.at[k]))
            stream = chosen_ref[1 + source_of(k)]

            def fetch(u, _):
                go(pltpu.make_async_copy(rest.at[stream, u], held.at[k, u + FIRST], sems.at[k]))
                return 0

            lax.fori_loop(0, jnp.maximum(used - FIRST, 0), fetch, 0)

    for k in range(experts):
        fetches(k, lambda copy: copy.start())
    gap, position = stream_gap("window", columns, positions, lanes)
    for k in range(experts):
        fetches(k, lambda copy: copy.wait())
        used = (counts[k, slots] + UNIT - 1) // UNIT
        for j in range(window - 1):
            held[k, used + j] = jnp.zeros((half, 2 * UNIT), jnp.bfloat16)
        ranks = starts[k, slots]

        def put(rank, _):
            @pl.when(rank < ranks)
            def _():
                start, length = starts[k, rank], counts[k, rank]
                unit, shift = start // UNIT, start % UNIT
                move = jnp.logical_and(gap == shift, position < length).astype(jnp.bfloat16)
                seen = jnp.concatenate([held[k, unit + j] for j in range(window)], axis=1)
                moved = jnp.dot(seen, move, preferred_element_type=jnp.float32).astype(jnp.bfloat16)
                stage[k, rank, :half, :] = moved[:, :positions]
                stage[k, rank, half:, :] = moved[:, positions:]

            @pl.when(rank >= ranks)
            def _():
                stage[k, rank] = jnp.zeros((columns, positions), jnp.bfloat16)

            return 0

        lax.fori_loop(0, slots, put, 0)
        pltpu.make_async_copy(stage.at[k], out_ref.at[pl.ds(source_of(k) * slots, slots)], out_sem.at[k]).start()
    for k in range(experts):
        pltpu.make_async_copy(stage.at[k], out_ref.at[pl.ds(source_of(k) * slots, slots)], out_sem.at[k]).wait()


def unpack(facts, chosen, own, firsts, rest, slots, columns, positions):
    half = columns // 2
    units = own.shape[0]
    window = positions // UNIT + 1
    smem = pl.BlockSpec(memory_space=pltpu.SMEM)
    hbm = pl.BlockSpec(memory_space=pl.ANY)
    return pl.pallas_call(
        unpack_kernel,
        in_specs=[smem, smem] + [hbm] * 5,
        out_specs=hbm,
        out_shape=jax.ShapeDtypeStruct((4 * slots, columns, positions), jnp.bfloat16),
        scratch_shapes=[
            pltpu.VMEM((4, units + window - 1, half, 2 * UNIT), jnp.bfloat16),
            pltpu.VMEM((4, slots, columns, positions), jnp.bfloat16),
            pltpu.SMEM((4, slots + 1), jnp.int32),
            pltpu.SMEM((4, slots + 1), jnp.int32),
            pltpu.SemaphoreType.DMA((4,)),
            pltpu.SemaphoreType.DMA((4,)),
        ],
        compiler_params=pltpu.CompilerParams(vmem_limit_bytes=VMEM_LIMIT),
        cost_estimate=pl.CostEstimate(flops=2 * 32 * half * 256 * 384, bytes_accessed=10 * MIB, transcendentals=0),
    )(facts, chosen, own, *firsts, rest)


def routes(hot):
    if hot >= 2:
        return [[(3 - source, 3 - target) for source, target in pairs] for pairs in routes(3 - hot)]
    if hot == 0:
        return [
            [(1, 0), (2, 3)],
            [(2, 0), (0, 1)],
            [(3, 0), (1, 2)],
            [(0, 2), (1, 3), (3, 1)],
            [(0, 3), (2, 1), (3, 2)],
        ]
    return [
        [(0, 1), (2, 3)],
        [(2, 1), (1, 0)],
        [(3, 1), (1, 2)],
        [(2, 0), (0, 3), (3, 2)],
        [(3, 0), (0, 2), (1, 3)],
    ]


def places(hot, target):
    by = [any(owner == target for _, owner in pairs) for pairs in routes(hot)]
    kept = [place if by[place] else None for place in range(3)] + [None, None]
    free = [place for place in range(3) if not by[place]]
    for permute in (3, 4):
        if by[permute]:
            kept[permute] = free.pop(0)
    return kept


def choose_kernel(facts_ref, out_ref):
    experts = 4
    rows, requests = facts_ref.shape[0], facts_ref.shape[1] // 2
    me = lax.axis_index("expert")
    worst = [jnp.int32(0)] * experts
    for row in range(rows):

        def add(i, loads):
            owner, length = facts_ref[row, i], facts_ref[row, requests + i]
            return tuple(load + jnp.where(owner == o, length, 0) for o, load in enumerate(loads))

        loads = lax.fori_loop(0, requests, add, (jnp.int32(0),) * experts, unroll=4)
        for o in range(experts):
            if o != row // 2:
                worst[o] = jnp.maximum(worst[o], (loads[o] + UNIT - 1) // UNIT)
    hot, most, second = jnp.int32(0), worst[0], jnp.int32(0)
    for o in range(1, experts):
        second = jnp.maximum(second, jnp.minimum(most, worst[o]))
        hot = jnp.where(worst[o] > most, o, hot)
        most = jnp.maximum(most, worst[o])
    plan = jnp.int32(len(PLANS) - 1)
    for p in range(len(PLANS) - 2, -1, -1):
        plan = jnp.where(jnp.logical_and(most <= PLANS[p][0], second <= PLANS[p][1]), p, plan)
    out_ref[0] = hot * len(PLANS) + plan
    for source in range(experts):
        kept = jnp.int32(0)
        for h in range(experts):
            for target in range(experts):
                for permute, pairs in enumerate(routes(h)):
                    if (source, target) in pairs:
                        here = jnp.logical_and(hot == h, me == target)
                        kept = jnp.where(here, places(h, target)[permute], kept)
        out_ref[1 + source] = kept


def choose(facts):
    smem = pl.BlockSpec(memory_space=pltpu.SMEM)
    return pl.pallas_call(
        choose_kernel,
        in_specs=[smem],
        out_specs=smem,
        out_shape=jax.ShapeDtypeStruct((5,), jnp.int32),
    )(facts)


def crossed(pairs):
    return [(source * 2 + s, target * 2 + 1 - s) for source, target in pairs for s in range(2)]


def by_halves(branches, index, *operands):
    def run(low, high, *operands):
        if high - low == 1:
            return branches[low](*operands)
        middle = (low + high) // 2
        return lax.cond(
            index < middle, functools.partial(run, low, middle), functools.partial(run, middle, high), *operands
        )

    return run(0, len(branches), *operands)


def exchange_rest(streams, me, branch):
    units = streams.shape[1]
    axes = ("expert", "segment")

    def send(hot, plan):
        most, second = (size - FIRST for size in PLANS[plan])

        def run(streams, me):
            def stream_by(pairs, size):
                apart = jnp.int32(0)
                for source, target in pairs:
                    apart = jnp.where(me == source, (target - source) % 4 - 1, apart)
                return lax.dynamic_slice_in_dim(streams, apart, 1, 0)[0, :size]

            got = []
            for permute, pairs in enumerate(routes(hot)):
                size = most if permute < 3 else second
                part = lax.ppermute(stream_by(pairs, size), axes, crossed(pairs))
                got.append(jnp.pad(part, ((0, units - size), (0, 0), (0, 0))))
            kept = []
            for place in range(3):
                value = got[place]
                for target in range(4):
                    for permute in (3, 4):
                        if places(hot, target)[permute] == place:
                            value = jnp.where(me == target, got[permute], value)
                kept.append(value)
            return jnp.stack(kept)

        return run

    branches = [send(hot, plan) for hot in range(4) for plan in range(len(PLANS))]
    return by_halves(branches, branch, streams, me)


def slot_layout(owner, experts, capacity):
    requests = owner.shape[0]
    indices = jnp.arange(requests, dtype=jnp.int32)
    earlier = indices[None, :] < indices[:, None]
    same_owner = owner[:, None] == owner[None, :]
    arrival_rank = jnp.sum(jnp.logical_and(same_owner, earlier), axis=1)
    target = owner * capacity + arrival_rank
    routing = target[None, :] == jnp.arange(experts * capacity, dtype=jnp.int32)[:, None]
    filled = jnp.any(routing, axis=1)
    source = jnp.sum(jnp.where(routing, indices[None, :], 0), axis=1)
    return (filled, source)


def pick_slots(values, filled, source):
    zero_value = jnp.zeros((), values.dtype)
    return jnp.where(filled[:, None, None], jnp.take(values, source, axis=0), zero_value)


def on_device(
    res_cache,
    res_scales,
    res_lengths,
    res_query,
    new_cache,
    new_scales,
    new_lengths,
    new_query,
    owner,
):
    experts = lax.axis_size("expert")
    sections = lax.axis_size("segment")
    requests, positions, columns = new_cache.shape
    capacity = max(2, 2 * requests // experts)
    swap = [(0, 1), (1, 0)]
    cache_t = jnp.transpose(new_cache, (0, 2, 1))

    def attention():
        res_context = attend(
            jnp.transpose(res_query, (0, 2, 1)), jnp.transpose(res_cache, (0, 2, 1)), res_scales, res_lengths, 1
        )
        new_context = attend(jnp.transpose(new_query, (0, 2, 1)), cache_t, new_scales, new_lengths, 2)
        return res_context, new_context

    if experts != 4 or sections != 2 or positions % UNIT or columns % 32:
        live_rows = jnp.arange(positions)[None, :] < new_lengths[:, None]
        zero_value = jnp.zeros((), jnp.bfloat16)
        filled, source = slot_layout(owner, experts, capacity)
        send_cache = pick_slots(jnp.where(live_rows[:, :, None], new_cache, zero_value), filled, source)
        send_scales = pick_slots(jnp.where(live_rows[:, None, :], new_scales, zero_value), filled, source)
        got_cache = lax.all_to_all(send_cache, "expert", split_axis=0, concat_axis=0, tiled=True)
        got_scales = lax.all_to_all(send_scales, "expert", split_axis=0, concat_axis=0, tiled=True)
        owned_cache, owned_scales = lax.ppermute((got_cache, got_scales), "segment", swap)
        return (*attention(), owned_cache, owned_scales)

    me = lax.axis_index("expert")
    units = capacity * positions // UNIT
    own, f1, f2, f3, streams, send_scales, facts = pack(owner, new_lengths, new_scales, cache_t, units, capacity)
    firsts = []
    for k, part in ((1, f1), (2, f2), (3, f3)):
        firsts.append(lax.ppermute(part, ("expert", "segment"), crossed([(e, (e + k) % 4) for e in range(4)])))
    own = lax.ppermute(own, "segment", swap)
    facts = lax.all_to_all(facts, ("expert", "segment"), split_axis=0, concat_axis=0, tiled=True)
    chosen = choose(facts)
    got_scales = lax.all_to_all(send_scales, "expert", split_axis=0, concat_axis=0, tiled=True)
    owned_scales = lax.ppermute(got_scales, "segment", swap)
    res_context, new_context = attention()
    streams, chosen, own, firsts, owned_scales, res_context, new_context = lax.optimization_barrier(
        (streams, chosen, own, firsts, owned_scales, res_context, new_context)
    )
    rest = exchange_rest(streams, me, chosen[0])
    owned = unpack(facts, chosen, own, firsts, rest, capacity, columns, positions)
    return (res_context, new_context, jnp.transpose(owned, (0, 2, 1)), owned_scales)


def solution(mesh):
    placed = (
        P(("group", "expert", "segment", "attn"), None, None),
        P(("group", "expert", "segment", "attn"), None, None),
        P(("group", "expert", "segment", "attn")),
        P(("group", "expert", "segment", "attn"), None, None),
        P(("group", "expert", "segment", "attn"), None, None),
        P(("group", "expert", "segment", "attn"), None, None),
        P(("group", "expert", "segment", "attn")),
        P(("group", "expert", "segment", "attn"), None, None),
        P(("group", "expert", "segment", "attn")),
    )
    return jax.shard_map(
        on_device,
        mesh=mesh,
        in_specs=placed,
        out_specs=(
            P(("group", "expert", "segment", "attn"), None, None),
            P(("group", "expert", "segment", "attn"), None, None),
            P(("group", "expert", "segment", "attn"), None, None),
            P(("group", "expert", "segment", "attn"), None, None),
        ),
        check_vma=False,
    )
```

```python
import functools
import jax
import jax.numpy as jnp
from jax import lax
from jax.experimental import pallas as pl
from jax.experimental.pallas import tpu as pltpu
from jax.sharding import PartitionSpec as P

LATENT = 512
BLOCK = 128
UNIT = 64
FIRST = 2
PLANS = ((12, 7), (13, 8), (14, 10), (16, 16))
FACT = 256

softmax_scale = 192.0 ** (-0.5)
MIB = 1 << 20
VMEM_LIMIT = 56 * MIB


def attend_kernel(lengths_ref, query_ref, cache_ref, scales_ref, *refs):
    out_ref = refs[-1]
    per_step, _, positions = cache_ref.shape
    blocks = LATENT // BLOCK
    contract_rows = (((0,), (0,)), ((), ()))
    contract_positions = (((1,), (1,)), ((), ()))
    for r in range(per_step):
        length = lengths_ref[pl.program_id(0) * per_step + r]
        factors = scales_ref[r].astype(jnp.float32)
        scores = lax.dot_general(
            query_ref[r, LATENT:, :], cache_ref[r, LATENT:, :], contract_rows, preferred_element_type=jnp.float32
        )
        for b in range(blocks):
            part = lax.dot_general(
                query_ref[r, b * BLOCK : (b + 1) * BLOCK, :],
                cache_ref[r, b * BLOCK : (b + 1) * BLOCK, :],
                contract_rows,
                preferred_element_type=jnp.float32,
            )
            scores = scores + part * factors[b : b + 1, :]
        live = lax.broadcasted_iota(jnp.int32, (1, positions), 1) < length
        scores = jnp.where(live, scores * softmax_scale, -jnp.inf)
        exponent = jnp.exp(scores - jnp.max(scores, axis=-1, keepdims=True))
        probabilities = exponent / jnp.sum(exponent, axis=-1, keepdims=True)
        for b in range(blocks):
            weights = (probabilities * factors[b : b + 1, :]).astype(jnp.bfloat16)
            out_ref[r, :, b * BLOCK : (b + 1) * BLOCK] = lax.dot_general(
                weights,
                cache_ref[r, b * BLOCK : (b + 1) * BLOCK, :],
                contract_positions,
                preferred_element_type=jnp.float32,
            ).astype(jnp.bfloat16)


def attend(query, cache, scales, lengths, per_step, after=()):
    requests, columns, heads = query.shape
    positions = cache.shape[2]
    return pl.pallas_call(
        attend_kernel,
        grid=(requests // per_step,),
        in_specs=[
            pl.BlockSpec(memory_space=pltpu.SMEM),
            pl.BlockSpec((per_step, columns, heads), lambda i: (i, 0, 0)),
            pl.BlockSpec((per_step, columns, positions), lambda i: (i, 0, 0)),
            pl.BlockSpec((per_step, scales.shape[1], positions), lambda i: (i, 0, 0)),
        ]
        + [pl.BlockSpec(memory_space=pl.ANY)] * len(after),
        out_specs=pl.BlockSpec((per_step, heads, LATENT), lambda i: (i, 0, 0)),
        out_shape=jax.ShapeDtypeStruct((requests, heads, LATENT), jnp.bfloat16),
        compiler_params=pltpu.CompilerParams(vmem_limit_bytes=VMEM_LIMIT),
        cost_estimate=pl.CostEstimate(
            flops=4 * requests * heads * positions * columns,
            bytes_accessed=2 * requests * (heads * (columns + LATENT) + positions * columns),
            transcendentals=requests * heads * positions,
        ),
    )(lengths, query, cache, scales, *after)


def stream_gap(rows, positions, units):
    window = units * 2 * UNIT
    shape = (window, 2 * positions) if rows == "window" else (2 * positions, window)
    first, second = lax.broadcasted_iota(jnp.int32, shape, 0), lax.broadcasted_iota(jnp.int32, shape, 1)
    lane, own = (first, second) if rows == "window" else (second, first)
    within = lane % (2 * UNIT)
    place = lane // (2 * UNIT) * UNIT + within % UNIT
    position = own % positions
    meet = within // UNIT == own // positions
    return jnp.where(meet, place - position, -4096), position


def pack_kernel(owner_ref, lengths_ref, scales_ref, cache_ref, *refs):
    experts = 4
    outs, (held, acc, slots, tails, ends, ranks, in_sem, out_sem) = refs[:5], refs[5:]
    requests, columns, positions = cache_ref.shape
    blocks = scales_ref.shape[1]
    half = columns // 2
    units = outs[4].shape[1] // half + FIRST
    window = positions // UNIT + 1
    me = lax.axis_index("expert")
    parts = in_sem.shape[0]
    share = requests // parts

    def rows_of(unit):
        return pl.ds(pl.multiple_of(unit * half, half), half)

    def fetch(part):
        here = pl.ds(part * share, share)
        return pltpu.make_async_copy(cache_ref.at[here], held.at[here], in_sem.at[part])

    for part in range(parts):
        fetch(part).start()
    gap, position = stream_gap("request", positions, window)
    for k in range(experts):
        ends[k] = 0
        ranks[k] = 0
        acc[k, :half] = jnp.zeros((half, 2 * UNIT), jnp.bfloat16)
    slots[...] = jnp.zeros(slots.shape, jnp.float32)
    live = lax.broadcasted_iota(jnp.int32, (blocks, positions), 1)

    def place(i, _):
        k = (owner_ref[i] - me) & (experts - 1)
        length = lengths_ref[i]
        start, rank = ends[k], ranks[k]
        ends[k] = start + length
        ranks[k] = rank + 1
        slots[k, pl.ds(rank * blocks, blocks), :] = jnp.where(live < length, scales_ref[i].astype(jnp.float32), 0.0)
        unit, shift = start // UNIT, start % UNIT
        move = jnp.logical_and(gap == shift, position < length).astype(jnp.bfloat16)
        both = jnp.concatenate([held[i, :half, :], held[i, half:, :]], axis=1)
        moved = jnp.dot(both, move, preferred_element_type=jnp.float32).astype(jnp.bfloat16)
        acc[k, rows_of(unit), :] += moved[:, : 2 * UNIT]
        for j in range(1, window):
            acc[k, rows_of(unit + j), :] = moved[:, 2 * UNIT * j : 2 * UNIT * (j + 1)]
        return 0

    for part in range(parts):
        fetch(part).wait()
        lax.fori_loop(part * share, (part + 1) * share, place, 0, unroll=2)
    tails[...] = slots[...].astype(jnp.bfloat16)
    copies = []

    def copy(source, target):
        copies.append(pltpu.make_async_copy(source, target, out_sem.at[len(copies)]))

    for k in range(experts):
        size = FIRST if k else units
        copy(acc.at[k, pl.ds(0, size * half)], outs[k].at[pl.ds(0, size * half)])
        copy(tails.at[k], outs[k].at[pl.ds(size * half, tails.shape[1])])
        if k:
            copy(acc.at[k, pl.ds(FIRST * half, (units - FIRST) * half)], outs[4].at[k - 1])
    for each in copies:
        each.start()
    for each in copies:
        each.wait()


def pack(owner, lengths, scales, cache, units, capacity):
    requests, columns, positions = cache.shape
    half = columns // 2
    window = positions // UNIT + 1
    tail = capacity * scales.shape[1]
    smem = pl.BlockSpec(memory_space=pltpu.SMEM)
    vmem = pl.BlockSpec(memory_space=pltpu.VMEM)
    hbm = pl.BlockSpec(memory_space=pl.ANY)
    lanes = 2 * UNIT
    shapes = [(units * half + tail, lanes)] + [(FIRST * half + tail, lanes)] * 3 + [(3, (units - FIRST) * half, lanes)]
    return pl.pallas_call(
        pack_kernel,
        in_specs=[smem, smem, vmem, hbm],
        out_specs=[hbm] * 5,
        out_shape=[jax.ShapeDtypeStruct(shape, jnp.bfloat16) for shape in shapes],
        scratch_shapes=[
            pltpu.VMEM(cache.shape, jnp.bfloat16),
            pltpu.VMEM((4, (units + window - 1) * half, lanes), jnp.bfloat16),
            pltpu.VMEM((4, tail, positions), jnp.float32),
            pltpu.VMEM((4, tail, positions), jnp.bfloat16),
            pltpu.SMEM((4,), jnp.int32),
            pltpu.SMEM((4,), jnp.int32),
            pltpu.SemaphoreType.DMA((4,)),
            pltpu.SemaphoreType.DMA((11,)),
        ],
        compiler_params=pltpu.CompilerParams(vmem_limit_bytes=VMEM_LIMIT),
        cost_estimate=pl.CostEstimate(flops=2 * requests * half * 256 * 384, bytes_accessed=8 * MIB, transcendentals=0),
    )(owner, lengths, scales, cache)


def unpack_kernel(facts_ref, chosen_ref, own, f1, f2, f3, rest, out_ref, scales_ref, *scratch):
    held, stage, tails, slots, starts, counts, sems, out_sem = scratch
    experts = 4
    requests = facts_ref.shape[1]
    capacity = out_ref.shape[0] // experts
    columns, positions = out_ref.shape[1], out_ref.shape[2]
    blocks = scales_ref.shape[1]
    half = columns // 2
    units = rest.shape[1] // half + FIRST
    window = positions // UNIT + 1
    me = lax.axis_index("expert")

    def rows_of(unit):
        return pl.ds(pl.multiple_of(unit * half, half), half)

    def source_of(k):
        return (me - k) & (experts - 1)

    def scan(k, _):
        def note(i, carry):
            rank, end = carry
            mine = facts_ref[k, i] // FACT == me
            length = facts_ref[k, i] % FACT

            @pl.when(mine)
            def _():
                starts[k, rank] = end
                counts[k, rank] = length

            return (jnp.where(mine, rank + 1, rank), jnp.where(mine, end + length, end))

        rank, end = lax.fori_loop(0, requests, note, (0, 0))
        starts[k, capacity] = rank
        counts[k, capacity] = (end + UNIT - 1) // UNIT
        return 0

    lax.fori_loop(0, experts, scan, 0)
    for k, stream in enumerate((own, f1, f2, f3)):
        used = counts[k, capacity]
        size = FIRST if k else units

        def fetch(u, _):
            pltpu.make_async_copy(stream.at[rows_of(u)], held.at[k, rows_of(u)], sems.at[k]).start()
            return 0

        lax.fori_loop(0, jnp.minimum(used, size), fetch, 0)
        tail = pl.ds(size * half, capacity * blocks)
        pltpu.make_async_copy(stream.at[tail], tails.at[k], sems.at[experts]).start()
        if k:
            place = chosen_ref[1 + source_of(k)]

            def fetch_rest(u, _):
                pltpu.make_async_copy(
                    rest.at[place, rows_of(u - FIRST)], held.at[k, rows_of(u)], sems.at[k]
                ).start()
                return 0

            lax.fori_loop(FIRST, used, fetch_rest, 0)
    gap, position = stream_gap("window", positions, window)

    def write(k):
        there = out_ref.at[pl.ds(source_of(k) * capacity, capacity)]
        return pltpu.make_async_copy(stage.at[k], there, out_sem.at[k])

    def put_stream(k, _):
        used, ranks = counts[k, capacity], starts[k, capacity]

        def arrive(u, _):
            pltpu.make_async_copy(own.at[rows_of(0)], held.at[k, rows_of(0)], sems.at[k]).wait()
            return 0

        lax.fori_loop(0, used, arrive, 0)
        for j in range(window - 1):
            held[k, rows_of(used + j), :] = jnp.zeros((half, 2 * UNIT), jnp.bfloat16)

        def put(rank, _):
            start, length = starts[k, rank], counts[k, rank]
            unit, shift = start // UNIT, start % UNIT
            move = jnp.logical_and(gap == shift, position < length).astype(jnp.bfloat16)
            seen = jnp.concatenate([held[k, rows_of(unit + j), :] for j in range(window)], axis=1)
            moved = jnp.dot(seen, move, preferred_element_type=jnp.float32).astype(jnp.bfloat16)
            stage[k, rank, :half, :] = moved[:, :positions]
            stage[k, rank, half:, :] = moved[:, positions:]
            return 0

        def clear(rank, _):
            stage[k, rank] = jnp.zeros((columns, positions), jnp.bfloat16)
            return 0

        lax.fori_loop(0, ranks, put, 0)
        lax.fori_loop(ranks, capacity, clear, 0)
        write(k).start()
        return 0

    lax.fori_loop(0, experts, put_stream, 0)
    for k in range(experts):
        pltpu.make_async_copy(own.at[pl.ds(0, capacity * blocks)], tails.at[k], sems.at[experts]).wait()
    slots[...] = tails[...].astype(jnp.float32)
    for k in range(experts):
        for rank in range(capacity):
            scales_ref[source_of(k) * capacity + rank] = slots[k, rank * blocks : (rank + 1) * blocks, :].astype(
                jnp.bfloat16
            )
    for k in range(experts):
        write(k).wait()


def unpack(facts, chosen, own, firsts, rest, capacity, columns, positions, blocks):
    half = columns // 2
    units = rest.shape[1] // half + FIRST
    window = positions // UNIT + 1
    smem = pl.BlockSpec(memory_space=pltpu.SMEM)
    vmem = pl.BlockSpec(memory_space=pltpu.VMEM)
    hbm = pl.BlockSpec(memory_space=pl.ANY)
    return pl.pallas_call(
        unpack_kernel,
        in_specs=[smem, smem] + [hbm] * 5,
        out_specs=[hbm, vmem],
        out_shape=[
            jax.ShapeDtypeStruct((4 * capacity, columns, positions), jnp.bfloat16),
            jax.ShapeDtypeStruct((4 * capacity, blocks, positions), jnp.bfloat16),
        ],
        scratch_shapes=[
            pltpu.VMEM((4, (units + window - 1) * half, 2 * UNIT), jnp.bfloat16),
            pltpu.VMEM((4, capacity, columns, positions), jnp.bfloat16),
            pltpu.VMEM((4, capacity * blocks, positions), jnp.bfloat16),
            pltpu.VMEM((4, capacity * blocks, positions), jnp.float32),
            pltpu.SMEM((4, capacity + 1), jnp.int32),
            pltpu.SMEM((4, capacity + 1), jnp.int32),
            pltpu.SemaphoreType.DMA((5,)),
            pltpu.SemaphoreType.DMA((4,)),
        ],
        compiler_params=pltpu.CompilerParams(vmem_limit_bytes=VMEM_LIMIT),
        cost_estimate=pl.CostEstimate(flops=2 * 32 * half * 256 * 384, bytes_accessed=10 * MIB, transcendentals=0),
    )(facts, chosen, own, *firsts, rest)


def routes(hot):
    if hot >= 2:
        return [[(3 - source, 3 - target) for source, target in pairs] for pairs in routes(3 - hot)]
    if hot == 0:
        return [
            [(1, 0), (0, 1), (2, 3), (3, 2)],
            [(2, 0), (1, 2)],
            [(3, 0), (1, 3)],
            [(2, 1), (0, 2)],
            [(3, 1), (0, 3)],
        ]
    return [
        [(0, 1), (1, 2), (2, 3)],
        [(2, 1), (1, 0), (3, 2)],
        [(3, 1), (1, 3)],
        [(2, 0), (0, 2)],
        [(3, 0), (0, 3)],
    ]


def places(hot, target):
    by = [any(owner == target for _, owner in pairs) for pairs in routes(hot)]
    kept = [place if by[place] else None for place in range(3)] + [None, None]
    free = [place for place in range(3) if not by[place]]
    for permute in (3, 4):
        if by[permute]:
            kept[permute] = free.pop(0)
    return kept


def choose_kernel(there_ref, here_ref, out_ref, loads_ref):
    experts = 4
    requests = here_ref.shape[1]
    me = lax.axis_index("expert")
    for k in range(experts):
        most = [jnp.int32(0)] * experts
        for ref in (there_ref, here_ref):

            def add(i, loads):
                owner, length = ref[k, i] // FACT, ref[k, i] % FACT
                return tuple(load + jnp.where(owner == o, length, 0) for o, load in enumerate(loads))

            loads = lax.fori_loop(0, requests, add, (jnp.int32(0),) * experts, unroll=4)
            most = [jnp.maximum(m, (load + UNIT - 1) // UNIT) for m, load in zip(most, loads)]
        source = (me - k) & (experts - 1)
        for o in range(experts):
            loads_ref[source * experts + o] = most[o]
    load = [[loads_ref[source * experts + o] for o in range(experts)] for source in range(experts)]
    hot, highest = jnp.int32(0), jnp.int32(-1)
    for o in range(experts):
        worst = functools.reduce(jnp.maximum, [load[source][o] for source in range(experts) if source != o])
        hot = jnp.where(worst > highest, o, hot)
        highest = jnp.maximum(worst, highest)
    most, second = jnp.int32(0), jnp.int32(0)
    for h in range(experts):
        for permute, pairs in enumerate(routes(h)):
            for source, target in pairs:
                here = jnp.where(hot == h, load[source][target], 0)
                if permute < 3:
                    most = jnp.maximum(most, here)
                else:
                    second = jnp.maximum(second, here)
    plan = jnp.int32(len(PLANS) - 1)
    for p in range(len(PLANS) - 2, -1, -1):
        plan = jnp.where(jnp.logical_and(most <= PLANS[p][0], second <= PLANS[p][1]), p, plan)
    out_ref[0] = hot * len(PLANS) + plan
    for source in range(experts):
        kept = jnp.int32(0)
        for h in range(experts):
            for target in range(experts):
                for permute, pairs in enumerate(routes(h)):
                    if (source, target) in pairs:
                        here = jnp.logical_and(hot == h, me == target)
                        kept = jnp.where(here, places(h, target)[permute], kept)
        out_ref[1 + source] = kept


def choose(there, here):
    smem = pl.BlockSpec(memory_space=pltpu.SMEM)
    return pl.pallas_call(
        choose_kernel,
        in_specs=[smem, smem],
        out_specs=smem,
        out_shape=jax.ShapeDtypeStruct((5,), jnp.int32),
        scratch_shapes=[pltpu.SMEM((16,), jnp.int32)],
    )(there, here)


def crossed(pairs):
    return [(source * 2 + s, target * 2 + 1 - s) for source, target in pairs for s in range(2)]


def by_halves(branches, index, *operands):
    def run(low, high, *operands):
        if high - low == 1:
            return branches[low](*operands)
        middle = (low + high) // 2
        return lax.cond(
            index < middle, functools.partial(run, low, middle), functools.partial(run, middle, high), *operands
        )

    return run(0, len(branches), *operands)


def keep_kernel(hot, *refs):
    got, kept, sem = refs[:5], refs[5], refs[6]
    me = lax.axis_index("expert")
    for target in range(4):

        @pl.when(me == target)
        def _():
            copies = []
            for permute, place in enumerate(places(hot, target)):
                if place is not None:
                    size = got[permute].shape[0]
                    there = kept.at[place, pl.ds(0, size)]
                    copies.append(pltpu.make_async_copy(got[permute], there, sem.at[place]))
            for copy in copies:
                copy.start()
            for copy in copies:
                copy.wait()


def keep(hot, got, shape):
    hbm = pl.BlockSpec(memory_space=pl.ANY)
    return pl.pallas_call(
        functools.partial(keep_kernel, hot),
        in_specs=[hbm] * 5,
        out_specs=hbm,
        out_shape=jax.ShapeDtypeStruct(shape, jnp.bfloat16),
        scratch_shapes=[pltpu.SemaphoreType.DMA((3,))],
    )(*got)


def exchange_rest(streams, half, me, branch):
    axes = ("expert", "segment")

    def send(hot, plan):
        most, second = (size - FIRST for size in PLANS[plan])

        def run(streams, me):
            def stream_by(pairs, size):
                apart = jnp.int32(0)
                for source, target in pairs:
                    apart = jnp.where(me == source, (target - source) % 4 - 1, apart)
                return lax.dynamic_slice_in_dim(streams, apart, 1, 0)[0, : size * half]

            got = []
            for permute, pairs in enumerate(routes(hot)):
                size = most if permute < 3 else second
                got.append(lax.ppermute(stream_by(pairs, size), axes, crossed(pairs)))
            return keep(hot, got, streams.shape)

        return run

    branches = [send(hot, plan) for hot in range(4) for plan in range(len(PLANS))]
    return by_halves(branches, branch, streams, me)


def slot_layout(owner, experts, capacity):
    requests = owner.shape[0]
    indices = jnp.arange(requests, dtype=jnp.int32)
    earlier = indices[None, :] < indices[:, None]
    same_owner = owner[:, None] == owner[None, :]
    arrival_rank = jnp.sum(jnp.logical_and(same_owner, earlier), axis=1)
    target = owner * capacity + arrival_rank
    routing = target[None, :] == jnp.arange(experts * capacity, dtype=jnp.int32)[:, None]
    filled = jnp.any(routing, axis=1)
    source = jnp.sum(jnp.where(routing, indices[None, :], 0), axis=1)
    return (filled, source)


def pick_slots(values, filled, source):
    zero_value = jnp.zeros((), values.dtype)
    return jnp.where(filled[:, None, None], jnp.take(values, source, axis=0), zero_value)


def on_device(
    res_cache,
    res_scales,
    res_lengths,
    res_query,
    new_cache,
    new_scales,
    new_lengths,
    new_query,
    owner,
):
    experts = lax.axis_size("expert")
    sections = lax.axis_size("segment")
    requests, positions, columns = new_cache.shape
    capacity = max(2, 2 * requests // experts)
    swap = [(0, 1), (1, 0)]
    cache_t = jnp.transpose(new_cache, (0, 2, 1))

    def attention(*after):
        res_context = attend(
            jnp.transpose(res_query, (0, 2, 1)), jnp.transpose(res_cache, (0, 2, 1)), res_scales, res_lengths, 1
        )
        new_context = attend(jnp.transpose(new_query, (0, 2, 1)), cache_t, new_scales, new_lengths, 2, after)
        return res_context, new_context

    if experts != 4 or sections != 2 or positions % UNIT or columns % 32:
        live_rows = jnp.arange(positions)[None, :] < new_lengths[:, None]
        zero_value = jnp.zeros((), jnp.bfloat16)
        filled, source = slot_layout(owner, experts, capacity)
        send_cache = pick_slots(jnp.where(live_rows[:, :, None], new_cache, zero_value), filled, source)
        send_scales = pick_slots(jnp.where(live_rows[:, None, :], new_scales, zero_value), filled, source)
        got_cache = lax.all_to_all(send_cache, "expert", split_axis=0, concat_axis=0, tiled=True)
        got_scales = lax.all_to_all(send_scales, "expert", split_axis=0, concat_axis=0, tiled=True)
        owned_cache, owned_scales = lax.ppermute((got_cache, got_scales), "segment", swap)
        return (*attention(), owned_cache, owned_scales)

    me = lax.axis_index("expert")
    units = capacity * positions // UNIT
    axes = ("expert", "segment")

    def shifted(value, k):
        return lax.ppermute(value, axes, crossed([(e, (e + k) % 4) for e in range(4)]))

    facts = owner * FACT + new_lengths
    there = jnp.stack([shifted(facts, k) for k in range(4)])
    own, f1, f2, f3, streams = pack(owner, new_lengths, new_scales, cache_t, units, capacity)
    here = lax.ppermute(there, "segment", swap)
    firsts = [shifted(part, k) for k, part in ((1, f1), (2, f2), (3, f3))]
    own = lax.ppermute(own, "segment", swap)
    chosen = choose(there, here)
    res_context, new_context = attention(chosen)
    streams, chosen, own, firsts, res_context, new_context = lax.optimization_barrier(
        (streams, chosen, own, firsts, res_context, new_context)
    )
    rest = exchange_rest(streams, columns // 2, me, chosen[0])
    owned, owned_scales = unpack(there, chosen, own, firsts, rest, capacity, columns, positions, new_scales.shape[1])
    return (res_context, new_context, jnp.transpose(owned, (0, 2, 1)), owned_scales)


def solution(mesh):
    placed = (
        P(("group", "expert", "segment", "attn"), None, None),
        P(("group", "expert", "segment", "attn"), None, None),
        P(("group", "expert", "segment", "attn")),
        P(("group", "expert", "segment", "attn"), None, None),
        P(("group", "expert", "segment", "attn"), None, None),
        P(("group", "expert", "segment", "attn"), None, None),
        P(("group", "expert", "segment", "attn")),
        P(("group", "expert", "segment", "attn"), None, None),
        P(("group", "expert", "segment", "attn")),
    )
    return jax.shard_map(
        on_device,
        mesh=mesh,
        in_specs=placed,
        out_specs=(
            P(("group", "expert", "segment", "attn"), None, None),
            P(("group", "expert", "segment", "attn"), None, None),
            P(("group", "expert", "segment", "attn"), None, None),
            P(("group", "expert", "segment", "attn"), None, None),
        ),
        check_vma=False,
    )
```

```python
import functools
import jax
import jax.numpy as jnp
from jax import lax
from jax.experimental import pallas as pl
from jax.experimental.pallas import tpu as pltpu
from jax.sharding import PartitionSpec as P

LATENT = 512
BLOCK = 128
UNIT_BITS = 6
UNIT = 1 << UNIT_BITS
FIRST = 2
PLANS = ((12, 7), (13, 8), (14, 10), (16, 16))
FACT_BITS = 8
FACT = 1 << FACT_BITS

softmax_scale = 192.0 ** (-0.5)
MIB = 1 << 20
VMEM_LIMIT = 56 * MIB


def attend_kernel(lengths_ref, query_ref, cache_ref, scales_ref, *refs):
    out_ref = refs[-1]
    per_step, _, positions = cache_ref.shape
    blocks = LATENT // BLOCK
    contract_rows = (((0,), (0,)), ((), ()))
    contract_positions = (((1,), (1,)), ((), ()))
    for r in range(per_step):
        length = lengths_ref[pl.program_id(0) * per_step + r]
        factors = scales_ref[r].astype(jnp.float32)
        scores = lax.dot_general(
            query_ref[r, LATENT:, :], cache_ref[r, LATENT:, :], contract_rows, preferred_element_type=jnp.float32
        )
        for b in range(blocks):
            part = lax.dot_general(
                query_ref[r, b * BLOCK : (b + 1) * BLOCK, :],
                cache_ref[r, b * BLOCK : (b + 1) * BLOCK, :],
                contract_rows,
                preferred_element_type=jnp.float32,
            )
            scores = scores + part * factors[b : b + 1, :]
        live = lax.broadcasted_iota(jnp.int32, (1, positions), 1) < length
        scores = jnp.where(live, scores * softmax_scale, -jnp.inf)
        exponent = jnp.exp(scores - jnp.max(scores, axis=-1, keepdims=True))
        probabilities = exponent * (1.0 / jnp.sum(exponent, axis=-1, keepdims=True))
        for b in range(blocks):
            weights = (probabilities * factors[b : b + 1, :]).astype(jnp.bfloat16)
            out_ref[r, :, b * BLOCK : (b + 1) * BLOCK] = lax.dot_general(
                weights,
                cache_ref[r, b * BLOCK : (b + 1) * BLOCK, :],
                contract_positions,
                preferred_element_type=jnp.float32,
            ).astype(jnp.bfloat16)


def attend(query, cache, scales, lengths, per_step, after=()):
    requests, columns, heads = query.shape
    positions = cache.shape[2]
    return pl.pallas_call(
        attend_kernel,
        grid=(requests // per_step,),
        in_specs=[
            pl.BlockSpec(memory_space=pltpu.SMEM),
            pl.BlockSpec((per_step, columns, heads), lambda i: (i, 0, 0)),
            pl.BlockSpec((per_step, columns, positions), lambda i: (i, 0, 0)),
            pl.BlockSpec((per_step, scales.shape[1], positions), lambda i: (i, 0, 0)),
        ]
        + [pl.BlockSpec(memory_space=pl.ANY)] * len(after),
        out_specs=pl.BlockSpec((per_step, heads, LATENT), lambda i: (i, 0, 0)),
        out_shape=jax.ShapeDtypeStruct((requests, heads, LATENT), jnp.bfloat16),
        compiler_params=pltpu.CompilerParams(vmem_limit_bytes=VMEM_LIMIT),
        cost_estimate=pl.CostEstimate(
            flops=4 * requests * heads * positions * columns,
            bytes_accessed=2 * requests * (heads * (columns + LATENT) + positions * columns),
            transcendentals=requests * heads * positions,
        ),
    )(lengths, query, cache, scales, *after)


def stream_gap(rows, positions, units):
    window = units * 2 * UNIT
    shape = (window, 2 * positions) if rows == "window" else (2 * positions, window)
    first, second = lax.broadcasted_iota(jnp.int32, shape, 0), lax.broadcasted_iota(jnp.int32, shape, 1)
    lane, own = (first, second) if rows == "window" else (second, first)
    within = lane % (2 * UNIT)
    place = lane // (2 * UNIT) * UNIT + within % UNIT
    meet = within // UNIT == own // positions
    side = (1, 2 * positions) if rows == "window" else (2 * positions, 1)
    position = lax.broadcasted_iota(jnp.int32, side, 1 if rows == "window" else 0) % positions
    return jnp.where(meet, place - own % positions, -512).astype(jnp.bfloat16), position


def moving(gap, position, shift, length):
    wanted = jnp.where(position < length, shift, 512).astype(jnp.bfloat16)
    return jnp.where(gap == wanted, jnp.ones((), jnp.bfloat16), jnp.zeros((), jnp.bfloat16))


def pack_kernel(owner_ref, lengths_ref, scales_ref, cache_ref, after_ref, *refs):
    experts = 4
    outs, (held, acc, slots, tails, ends, ranks, in_sem, out_sem) = refs[:5], refs[5:]
    requests, columns, positions = cache_ref.shape
    blocks = scales_ref.shape[1]
    half = columns // 2
    units = outs[4].shape[1] // half + FIRST
    window = positions // UNIT + 1
    me = lax.axis_index("expert")
    parts = in_sem.shape[0]
    share = requests // parts

    def rows_of(unit):
        return pl.ds(pl.multiple_of(unit * half, half), half)

    def fetch(part):
        here = pl.ds(part * share, share)
        return pltpu.make_async_copy(cache_ref.at[here], held.at[here], in_sem.at[part])

    for part in range(parts):
        fetch(part).start()
    gap, position = stream_gap("request", positions, window)
    for k in range(experts):
        ends[k] = 0
        ranks[k] = 0
        acc[k, :half] = jnp.zeros((half, 2 * UNIT), jnp.bfloat16)
    slots[...] = jnp.zeros(slots.shape, jnp.float32)
    live = lax.broadcasted_iota(jnp.int32, (blocks, positions), 1)

    def place(i, _):
        k = (owner_ref[i] - me) & (experts - 1)
        length = lengths_ref[i]
        start, rank = ends[k], ranks[k]
        ends[k] = start + length
        ranks[k] = rank + 1
        slots[k, pl.ds(rank * blocks, blocks), :] = jnp.where(live < length, scales_ref[i].astype(jnp.float32), 0.0)
        unit, shift = start >> UNIT_BITS, start & (UNIT - 1)
        move = moving(gap, position, shift, length)
        both = jnp.concatenate([held[i, :half, :], held[i, half:, :]], axis=1)
        moved = jnp.dot(both, move, preferred_element_type=jnp.float32).astype(jnp.bfloat16)
        acc[k, rows_of(unit), :] += moved[:, : 2 * UNIT]
        for j in range(1, window):
            acc[k, rows_of(unit + j), :] = moved[:, 2 * UNIT * j : 2 * UNIT * (j + 1)]
        return 0

    for part in range(parts):
        fetch(part).wait()
        lax.fori_loop(part * share, (part + 1) * share, place, 0, unroll=2)
    tails[...] = slots[...].astype(jnp.bfloat16)
    copies = []

    def copy(source, target):
        copies.append(pltpu.make_async_copy(source, target, out_sem.at[len(copies)]))

    for k in range(experts):
        size = FIRST if k else units
        copy(acc.at[k, pl.ds(0, size * half)], outs[k].at[pl.ds(0, size * half)])
        copy(tails.at[k], outs[k].at[pl.ds(size * half, tails.shape[1])])
        if k:
            copy(acc.at[k, pl.ds(FIRST * half, (units - FIRST) * half)], outs[4].at[k - 1])
    for each in copies:
        each.start()
    for each in copies:
        each.wait()


def pack(owner, lengths, scales, cache, after, units, capacity):
    requests, columns, positions = cache.shape
    half = columns // 2
    window = positions // UNIT + 1
    tail = capacity * scales.shape[1]
    smem = pl.BlockSpec(memory_space=pltpu.SMEM)
    vmem = pl.BlockSpec(memory_space=pltpu.VMEM)
    hbm = pl.BlockSpec(memory_space=pl.ANY)
    lanes = 2 * UNIT
    shapes = [(units * half + tail, lanes)] + [(FIRST * half + tail, lanes)] * 3 + [(3, (units - FIRST) * half, lanes)]
    return pl.pallas_call(
        pack_kernel,
        in_specs=[smem, smem, vmem, hbm, hbm],
        out_specs=[hbm] * 5,
        out_shape=[jax.ShapeDtypeStruct(shape, jnp.bfloat16) for shape in shapes],
        scratch_shapes=[
            pltpu.VMEM(cache.shape, jnp.bfloat16),
            pltpu.VMEM((4, (units + window - 1) * half, lanes), jnp.bfloat16),
            pltpu.VMEM((4, tail, positions), jnp.float32),
            pltpu.VMEM((4, tail, positions), jnp.bfloat16),
            pltpu.SMEM((4,), jnp.int32),
            pltpu.SMEM((4,), jnp.int32),
            pltpu.SemaphoreType.DMA((4,)),
            pltpu.SemaphoreType.DMA((11,)),
        ],
        compiler_params=pltpu.CompilerParams(vmem_limit_bytes=VMEM_LIMIT),
        cost_estimate=pl.CostEstimate(flops=2 * requests * half * 256 * 384, bytes_accessed=8 * MIB, transcendentals=0),
    )(owner, lengths, scales, cache, after)


def unpack_kernel(facts_ref, chosen_ref, own, f1, f2, f3, rest, out_ref, scales_ref, *scratch):
    held, stage, tails, slots, starts, counts, sems, out_sem = scratch
    experts = 4
    requests = facts_ref.shape[1]
    capacity = out_ref.shape[0] // experts
    columns, positions = out_ref.shape[1], out_ref.shape[2]
    blocks = scales_ref.shape[1]
    half = columns // 2
    units = rest.shape[1] // half + FIRST
    window = positions // UNIT + 1
    me = lax.axis_index("expert")

    def rows_of(unit):
        return pl.ds(pl.multiple_of(unit * half, half), half)

    def source_of(k):
        return (me - k) & (experts - 1)

    def scan(k, _):
        def note(i, carry):
            rank, end = carry
            mine = facts_ref[k, i] >> FACT_BITS == me
            length = facts_ref[k, i] & (FACT - 1)

            @pl.when(mine)
            def _():
                starts[k, rank] = end
                counts[k, rank] = length

            return (jnp.where(mine, rank + 1, rank), jnp.where(mine, end + length, end))

        rank, end = lax.fori_loop(0, requests, note, (0, 0))
        starts[k, capacity] = rank
        counts[k, capacity] = (end + UNIT - 1) >> UNIT_BITS
        return 0

    lax.fori_loop(0, experts, scan, 0)
    for k, stream in enumerate((own, f1, f2, f3)):
        used = counts[k, capacity]
        size = FIRST if k else units

        def fetch(u, _):
            pltpu.make_async_copy(stream.at[rows_of(u)], held.at[k, rows_of(u)], sems.at[k]).start()
            return 0

        lax.fori_loop(0, jnp.minimum(used, size), fetch, 0)
        tail = pl.ds(size * half, capacity * blocks)
        pltpu.make_async_copy(stream.at[tail], tails.at[k], sems.at[experts]).start()
        if k:
            place = chosen_ref[1 + source_of(k)]

            def fetch_rest(u, _):
                pltpu.make_async_copy(
                    rest.at[place, rows_of(u - FIRST)], held.at[k, rows_of(u)], sems.at[k]
                ).start()
                return 0

            lax.fori_loop(FIRST, used, fetch_rest, 0)
    gap, position = stream_gap("window", positions, window)

    def write(k):
        there = out_ref.at[pl.ds(source_of(k) * capacity, capacity)]
        return pltpu.make_async_copy(stage.at[k], there, out_sem.at[k])

    def put_stream(k, _):
        used, ranks = counts[k, capacity], starts[k, capacity]

        def arrive(u, _):
            pltpu.make_async_copy(own.at[rows_of(0)], held.at[k, rows_of(0)], sems.at[k]).wait()
            return 0

        lax.fori_loop(0, used, arrive, 0)
        for j in range(window):
            held[k, rows_of(used + j), :] = jnp.zeros((half, 2 * UNIT), jnp.bfloat16)

        def put(pair, _):
            for rank in (2 * pair, 2 * pair + 1):
                filled = rank < ranks
                start, length = jnp.where(filled, starts[k, rank], 0), jnp.where(filled, counts[k, rank], 0)
                unit, shift = start >> UNIT_BITS, start & (UNIT - 1)
                move = moving(gap, position, shift, length)
                seen = jnp.concatenate([held[k, rows_of(unit + j), :] for j in range(window)], axis=1)
                moved = jnp.dot(seen, move, preferred_element_type=jnp.float32).astype(jnp.bfloat16)
                stage[k, rank, :half, :] = moved[:, :positions]
                stage[k, rank, half:, :] = moved[:, positions:]
            return 0

        def clear(pair, _):
            stage[k, pl.ds(2 * pair, 2)] = jnp.zeros((2, columns, positions), jnp.bfloat16)
            return 0

        pairs = (ranks + 1) >> 1
        lax.fori_loop(0, pairs, put, 0)
        lax.fori_loop(pairs, capacity // 2, clear, 0)
        write(k).start()
        return 0

    lax.fori_loop(0, experts, put_stream, 0)
    for k in range(experts):
        pltpu.make_async_copy(own.at[pl.ds(0, capacity * blocks)], tails.at[k], sems.at[experts]).wait()
    slots[...] = tails[...].astype(jnp.float32)
    for k in range(experts):
        for rank in range(capacity):
            scales_ref[source_of(k) * capacity + rank] = slots[k, rank * blocks : (rank + 1) * blocks, :].astype(
                jnp.bfloat16
            )
    for k in range(experts):
        write(k).wait()


def unpack(facts, chosen, own, firsts, rest, capacity, columns, positions, blocks):
    half = columns // 2
    units = rest.shape[1] // half + FIRST
    window = positions // UNIT + 1
    smem = pl.BlockSpec(memory_space=pltpu.SMEM)
    vmem = pl.BlockSpec(memory_space=pltpu.VMEM)
    hbm = pl.BlockSpec(memory_space=pl.ANY)
    return pl.pallas_call(
        unpack_kernel,
        in_specs=[smem, smem] + [hbm] * 5,
        out_specs=[hbm, vmem],
        out_shape=[
            jax.ShapeDtypeStruct((4 * capacity, columns, positions), jnp.bfloat16),
            jax.ShapeDtypeStruct((4 * capacity, blocks, positions), jnp.bfloat16),
        ],
        scratch_shapes=[
            pltpu.VMEM((4, (units + window) * half, 2 * UNIT), jnp.bfloat16),
            pltpu.VMEM((4, capacity, columns, positions), jnp.bfloat16),
            pltpu.VMEM((4, capacity * blocks, positions), jnp.bfloat16),
            pltpu.VMEM((4, capacity * blocks, positions), jnp.float32),
            pltpu.SMEM((4, capacity + 1), jnp.int32),
            pltpu.SMEM((4, capacity + 1), jnp.int32),
            pltpu.SemaphoreType.DMA((5,)),
            pltpu.SemaphoreType.DMA((4,)),
        ],
        compiler_params=pltpu.CompilerParams(vmem_limit_bytes=VMEM_LIMIT),
        cost_estimate=pl.CostEstimate(flops=2 * 32 * half * 256 * 384, bytes_accessed=10 * MIB, transcendentals=0),
    )(facts, chosen, own, *firsts, rest)


def routes(hot):
    if hot >= 2:
        return [[(3 - source, 3 - target) for source, target in pairs] for pairs in routes(3 - hot)]
    if hot == 0:
        return [
            [(1, 0), (0, 1), (2, 3), (3, 2)],
            [(2, 0), (1, 2)],
            [(3, 0), (1, 3)],
            [(2, 1), (0, 2)],
            [(3, 1), (0, 3)],
        ]
    return [
        [(0, 1), (1, 2), (2, 3)],
        [(2, 1), (1, 0), (3, 2)],
        [(3, 1), (1, 3)],
        [(2, 0), (0, 2)],
        [(3, 0), (0, 3)],
    ]


def places(hot, target):
    by = [any(owner == target for _, owner in pairs) for pairs in routes(hot)]
    kept = [place if by[place] else None for place in range(3)] + [None, None]
    free = [place for place in range(3) if not by[place]]
    for permute in (3, 4):
        if by[permute]:
            kept[permute] = free.pop(0)
    return kept


def choose_kernel(there_ref, here_ref, out_ref, loads_ref):
    experts = 4
    requests = here_ref.shape[1]
    me = lax.axis_index("expert")
    for k in range(experts):
        most = [jnp.int32(0)] * experts
        for ref in (there_ref, here_ref):

            def add(i, loads):
                owner, length = ref[k, i] >> FACT_BITS, ref[k, i] & (FACT - 1)
                return tuple(load + jnp.where(owner == o, length, 0) for o, load in enumerate(loads))

            loads = lax.fori_loop(0, requests, add, (jnp.int32(0),) * experts, unroll=4)
            most = [jnp.maximum(m, (load + UNIT - 1) >> UNIT_BITS) for m, load in zip(most, loads)]
        source = (me - k) & (experts - 1)
        for o in range(experts):
            loads_ref[source * experts + o] = most[o]
    load = [[loads_ref[source * experts + o] for o in range(experts)] for source in range(experts)]
    hot, highest = jnp.int32(0), jnp.int32(-1)
    for o in range(experts):
        worst = functools.reduce(jnp.maximum, [load[source][o] for source in range(experts) if source != o])
        hot = jnp.where(worst > highest, o, hot)
        highest = jnp.maximum(worst, highest)
    most, second = jnp.int32(0), jnp.int32(0)
    for h in range(experts):
        for permute, pairs in enumerate(routes(h)):
            for source, target in pairs:
                here = jnp.where(hot == h, load[source][target], 0)
                if permute < 3:
                    most = jnp.maximum(most, here)
                else:
                    second = jnp.maximum(second, here)
    plan = jnp.int32(len(PLANS) - 1)
    for p in range(len(PLANS) - 2, -1, -1):
        plan = jnp.where(jnp.logical_and(most <= PLANS[p][0], second <= PLANS[p][1]), p, plan)
    out_ref[0] = hot * len(PLANS) + plan
    for source in range(experts):
        kept = jnp.int32(0)
        for h in range(experts):
            for target in range(experts):
                for permute, pairs in enumerate(routes(h)):
                    if (source, target) in pairs:
                        here = jnp.logical_and(hot == h, me == target)
                        kept = jnp.where(here, places(h, target)[permute], kept)
        out_ref[1 + source] = kept


def choose(there, here):
    smem = pl.BlockSpec(memory_space=pltpu.SMEM)
    return pl.pallas_call(
        choose_kernel,
        in_specs=[smem, smem],
        out_specs=smem,
        out_shape=jax.ShapeDtypeStruct((5,), jnp.int32),
        scratch_shapes=[pltpu.SMEM((16,), jnp.int32)],
    )(there, here)


def crossed(pairs):
    return [(source * 2 + s, target * 2 + 1 - s) for source, target in pairs for s in range(2)]


def by_halves(branches, index, *operands):
    def run(low, high, *operands):
        if high - low == 1:
            return branches[low](*operands)
        middle = (low + high) // 2
        return lax.cond(
            index < middle, functools.partial(run, low, middle), functools.partial(run, middle, high), *operands
        )

    return run(0, len(branches), *operands)


def keep_kernel(hot, *refs):
    got, kept, held, arrived, left = refs[:5], *refs[5:]
    me = lax.axis_index("expert")
    for target in range(4):

        @pl.when(me == target)
        def _():
            steps = []
            for permute, place in enumerate(places(hot, target)):
                if place is not None:
                    size = pl.ds(0, got[permute].shape[0])
                    into = pltpu.make_async_copy(got[permute], held.at[place, size], arrived.at[place])
                    out = pltpu.make_async_copy(held.at[place, size], kept.at[place, size], left.at[place])
                    steps.append((into, out))
            for into, _ in steps:
                into.start()
            for into, out in steps:
                into.wait()
                out.start()
            for _, out in steps:
                out.wait()


def keep(hot, got, shape):
    hbm = pl.BlockSpec(memory_space=pl.ANY)
    return pl.pallas_call(
        functools.partial(keep_kernel, hot),
        in_specs=[hbm] * 5,
        out_specs=hbm,
        out_shape=jax.ShapeDtypeStruct(shape, jnp.bfloat16),
        scratch_shapes=[
            pltpu.VMEM(shape, jnp.bfloat16),
            pltpu.SemaphoreType.DMA((3,)),
            pltpu.SemaphoreType.DMA((3,)),
        ],
    )(*got)


def exchange_rest(streams, half, me, branch):
    axes = ("expert", "segment")

    def send(hot, plan):
        most, second = (size - FIRST for size in PLANS[plan])

        def run(streams, me):
            def stream_by(pairs, size):
                apart = jnp.int32(0)
                for source, target in pairs:
                    apart = jnp.where(me == source, (target - source) % 4 - 1, apart)
                return lax.dynamic_slice_in_dim(streams, apart, 1, 0)[0, : size * half]

            got = []
            for permute, pairs in enumerate(routes(hot)):
                size = most if permute < 3 else second
                got.append(lax.ppermute(stream_by(pairs, size), axes, crossed(pairs)))
            return keep(hot, got, streams.shape)

        return run

    branches = [send(hot, plan) for hot in range(4) for plan in range(len(PLANS))]
    return by_halves(branches, branch, streams, me)


def slot_layout(owner, experts, capacity):
    requests = owner.shape[0]
    indices = jnp.arange(requests, dtype=jnp.int32)
    earlier = indices[None, :] < indices[:, None]
    same_owner = owner[:, None] == owner[None, :]
    arrival_rank = jnp.sum(jnp.logical_and(same_owner, earlier), axis=1)
    target = owner * capacity + arrival_rank
    routing = target[None, :] == jnp.arange(experts * capacity, dtype=jnp.int32)[:, None]
    filled = jnp.any(routing, axis=1)
    source = jnp.sum(jnp.where(routing, indices[None, :], 0), axis=1)
    return (filled, source)


def pick_slots(values, filled, source):
    zero_value = jnp.zeros((), values.dtype)
    return jnp.where(filled[:, None, None], jnp.take(values, source, axis=0), zero_value)


def on_device(
    res_cache,
    res_scales,
    res_lengths,
    res_query,
    new_cache,
    new_scales,
    new_lengths,
    new_query,
    owner,
):
    experts = lax.axis_size("expert")
    sections = lax.axis_size("segment")
    requests, positions, columns = new_cache.shape
    capacity = max(2, 2 * requests // experts)
    swap = [(0, 1), (1, 0)]
    cache_t = jnp.transpose(new_cache, (0, 2, 1))

    def attention(*after):
        res_context = attend(
            jnp.transpose(res_query, (0, 2, 1)), jnp.transpose(res_cache, (0, 2, 1)), res_scales, res_lengths, 2
        )
        new_context = attend(jnp.transpose(new_query, (0, 2, 1)), cache_t, new_scales, new_lengths, 4, after)
        return res_context, new_context

    if experts != 4 or sections != 2 or positions % UNIT or columns % 32:
        live_rows = jnp.arange(positions)[None, :] < new_lengths[:, None]
        zero_value = jnp.zeros((), jnp.bfloat16)
        filled, source = slot_layout(owner, experts, capacity)
        send_cache = pick_slots(jnp.where(live_rows[:, :, None], new_cache, zero_value), filled, source)
        send_scales = pick_slots(jnp.where(live_rows[:, None, :], new_scales, zero_value), filled, source)
        got_cache = lax.all_to_all(send_cache, "expert", split_axis=0, concat_axis=0, tiled=True)
        got_scales = lax.all_to_all(send_scales, "expert", split_axis=0, concat_axis=0, tiled=True)
        owned_cache, owned_scales = lax.ppermute((got_cache, got_scales), "segment", swap)
        return (*attention(), owned_cache, owned_scales)

    me = lax.axis_index("expert")
    units = capacity * positions // UNIT
    axes = ("expert", "segment")

    def shifted(value, k):
        return lax.ppermute(value, axes, crossed([(e, (e + k) % 4) for e in range(4)]))

    facts = owner * FACT + new_lengths
    there = jnp.stack([shifted(facts, k) for k in range(4)])
    own, f1, f2, f3, streams = pack(owner, new_lengths, new_scales, cache_t, there, units, capacity)
    here = lax.ppermute(there, "segment", swap)
    firsts = [shifted(part, k) for k, part in ((1, f1), (2, f2), (3, f3))]
    own = lax.ppermute(own, "segment", swap)
    chosen = choose(there, here)
    res_context, new_context = attention(chosen)
    streams, chosen, own, firsts, res_context, new_context = lax.optimization_barrier(
        (streams, chosen, own, firsts, res_context, new_context)
    )
    rest = exchange_rest(streams, columns // 2, me, chosen[0])
    owned, owned_scales = unpack(there, chosen, own, firsts, rest, capacity, columns, positions, new_scales.shape[1])
    return (res_context, new_context, jnp.transpose(owned, (0, 2, 1)), owned_scales)


def solution(mesh):
    placed = (
        P(("group", "expert", "segment", "attn"), None, None),
        P(("group", "expert", "segment", "attn"), None, None),
        P(("group", "expert", "segment", "attn")),
        P(("group", "expert", "segment", "attn"), None, None),
        P(("group", "expert", "segment", "attn"), None, None),
        P(("group", "expert", "segment", "attn"), None, None),
        P(("group", "expert", "segment", "attn")),
        P(("group", "expert", "segment", "attn"), None, None),
        P(("group", "expert", "segment", "attn")),
    )
    return jax.shard_map(
        on_device,
        mesh=mesh,
        in_specs=placed,
        out_specs=(
            P(("group", "expert", "segment", "attn"), None, None),
            P(("group", "expert", "segment", "attn"), None, None),
            P(("group", "expert", "segment", "attn"), None, None),
            P(("group", "expert", "segment", "attn"), None, None),
        ),
        check_vma=False,
    )
```

```python
import functools
import jax
import jax.numpy as jnp
from jax import lax
from jax.experimental import pallas as pl
from jax.experimental.pallas import tpu as pltpu
from jax.sharding import PartitionSpec as P

LATENT = 512
BLOCK = 128
UNIT_BITS = 6
UNIT = 1 << UNIT_BITS
PLANS = ((12, 7), (13, 8), (14, 10), (16, 16))
FACT_BITS = 8
FACT = 1 << FACT_BITS

softmax_scale = 192.0 ** (-0.5)
MIB = 1 << 20
VMEM_LIMIT = 56 * MIB


def attend_kernel(lengths_ref, query_ref, cache_ref, scales_ref, out_ref):
    per_step, _, positions = cache_ref.shape
    blocks = LATENT // BLOCK
    contract_rows = (((0,), (0,)), ((), ()))
    contract_positions = (((1,), (1,)), ((), ()))
    for r in range(per_step):
        length = lengths_ref[pl.program_id(0) * per_step + r]
        factors = scales_ref[r].astype(jnp.float32)
        scores = lax.dot_general(
            query_ref[r, LATENT:, :], cache_ref[r, LATENT:, :], contract_rows, preferred_element_type=jnp.float32
        )
        for b in range(blocks):
            part = lax.dot_general(
                query_ref[r, b * BLOCK : (b + 1) * BLOCK, :],
                cache_ref[r, b * BLOCK : (b + 1) * BLOCK, :],
                contract_rows,
                preferred_element_type=jnp.float32,
            )
            scores = scores + part * factors[b : b + 1, :]
        live = lax.broadcasted_iota(jnp.int32, (1, positions), 1) < length
        scores = jnp.where(live, scores * softmax_scale, -jnp.inf)
        exponent = jnp.exp(scores - jnp.max(scores, axis=-1, keepdims=True))
        probabilities = exponent * (1.0 / jnp.sum(exponent, axis=-1, keepdims=True))
        for b in range(blocks):
            weights = (probabilities * factors[b : b + 1, :]).astype(jnp.bfloat16)
            out_ref[r, :, b * BLOCK : (b + 1) * BLOCK] = lax.dot_general(
                weights,
                cache_ref[r, b * BLOCK : (b + 1) * BLOCK, :],
                contract_positions,
                preferred_element_type=jnp.float32,
            ).astype(jnp.bfloat16)


def attend(query, cache, scales, lengths, per_step):
    requests, columns, heads = query.shape
    positions = cache.shape[2]
    return pl.pallas_call(
        attend_kernel,
        grid=(requests // per_step,),
        in_specs=[
            pl.BlockSpec(memory_space=pltpu.SMEM),
            pl.BlockSpec((per_step, columns, heads), lambda i: (i, 0, 0)),
            pl.BlockSpec((per_step, columns, positions), lambda i: (i, 0, 0)),
            pl.BlockSpec((per_step, scales.shape[1], positions), lambda i: (i, 0, 0)),
        ],
        out_specs=pl.BlockSpec((per_step, heads, LATENT), lambda i: (i, 0, 0)),
        out_shape=jax.ShapeDtypeStruct((requests, heads, LATENT), jnp.bfloat16),
        compiler_params=pltpu.CompilerParams(vmem_limit_bytes=VMEM_LIMIT),
        cost_estimate=pl.CostEstimate(
            flops=4 * requests * heads * positions * columns,
            bytes_accessed=2 * requests * (heads * (columns + LATENT) + positions * columns),
            transcendentals=requests * heads * positions,
        ),
    )(lengths, query, cache, scales)


def stream_gap(rows, positions, units):
    window = units * 2 * UNIT
    shape = (window, 2 * positions) if rows == "window" else (2 * positions, window)
    first, second = lax.broadcasted_iota(jnp.int32, shape, 0), lax.broadcasted_iota(jnp.int32, shape, 1)
    lane, own = (first, second) if rows == "window" else (second, first)
    within = lane % (2 * UNIT)
    place = lane // (2 * UNIT) * UNIT + within % UNIT
    meet = within // UNIT == own // positions
    side = (1, 2 * positions) if rows == "window" else (2 * positions, 1)
    position = lax.broadcasted_iota(jnp.int32, side, 1 if rows == "window" else 0) % positions
    return jnp.where(meet, place - own % positions, -512).astype(jnp.bfloat16), position


def moving(gap, position, shift, length):
    wanted = jnp.where(position < length, shift, 512).astype(jnp.bfloat16)
    return jnp.where(gap == wanted, jnp.ones((), jnp.bfloat16), jnp.zeros((), jnp.bfloat16))


def pack_kernel(owner_ref, lengths_ref, scales_ref, cache_ref, after_ref, out_ref, *scratch):
    held, acc, slots, ends, ranks, in_sem, out_sem = scratch
    experts = 4
    requests, columns, positions = cache_ref.shape
    blocks = scales_ref.shape[1]
    half = columns // 2
    tail = slots.shape[1]
    window = positions // UNIT + 1
    me = lax.axis_index("expert")
    parts = in_sem.shape[0]
    share = requests // parts

    def rows_of(unit):
        return pl.ds(pl.multiple_of(tail + unit * half, 16), half)

    def fetch(part):
        here = pl.ds(part * share, share)
        return pltpu.make_async_copy(cache_ref.at[here], held.at[here], in_sem.at[part])

    for part in range(parts):
        fetch(part).start()
    gap, position = stream_gap("request", positions, window)
    for k in range(experts):
        ends[k] = 0
        ranks[k] = 0
        acc[k, rows_of(0), :] = jnp.zeros((half, 2 * UNIT), jnp.bfloat16)
    slots[...] = jnp.zeros(slots.shape, jnp.float32)
    live = lax.broadcasted_iota(jnp.int32, (blocks, positions), 1)

    def place(i, _):
        k = (owner_ref[i] - me) & (experts - 1)
        length = lengths_ref[i]
        start, rank = ends[k], ranks[k]
        ends[k] = start + length
        ranks[k] = rank + 1
        slots[k, pl.ds(rank * blocks, blocks), :] = jnp.where(live < length, scales_ref[i].astype(jnp.float32), 0.0)
        unit, shift = start >> UNIT_BITS, start & (UNIT - 1)
        move = moving(gap, position, shift, length)
        both = jnp.concatenate([held[i, :half, :], held[i, half:, :]], axis=1)
        moved = jnp.dot(both, move, preferred_element_type=jnp.float32).astype(jnp.bfloat16)
        acc[k, rows_of(unit), :] += moved[:, : 2 * UNIT]
        for j in range(1, window):
            acc[k, rows_of(unit + j), :] = moved[:, 2 * UNIT * j : 2 * UNIT * (j + 1)]
        return 0

    for part in range(parts):
        fetch(part).wait()
        lax.fori_loop(part * share, (part + 1) * share, place, 0, unroll=2)
    acc[:, :tail, :] = slots[...].astype(jnp.bfloat16)
    rows = pl.ds(0, out_ref.shape[1])
    copies = [pltpu.make_async_copy(acc.at[k, rows], out_ref.at[k], out_sem.at[k]) for k in range(experts)]
    for each in copies:
        each.start()
    for each in copies:
        each.wait()


def pack(owner, lengths, scales, cache, after, units, capacity):
    requests, columns, positions = cache.shape
    half = columns // 2
    window = positions // UNIT + 1
    tail = capacity * scales.shape[1]
    smem = pl.BlockSpec(memory_space=pltpu.SMEM)
    vmem = pl.BlockSpec(memory_space=pltpu.VMEM)
    hbm = pl.BlockSpec(memory_space=pl.ANY)
    lanes = 2 * UNIT
    return pl.pallas_call(
        pack_kernel,
        in_specs=[smem, smem, vmem, hbm, hbm],
        out_specs=hbm,
        out_shape=jax.ShapeDtypeStruct((4, tail + units * half, lanes), jnp.bfloat16),
        scratch_shapes=[
            pltpu.VMEM(cache.shape, jnp.bfloat16),
            pltpu.VMEM((4, tail + (units + window - 1) * half, lanes), jnp.bfloat16),
            pltpu.VMEM((4, tail, positions), jnp.float32),
            pltpu.SMEM((4,), jnp.int32),
            pltpu.SMEM((4,), jnp.int32),
            pltpu.SemaphoreType.DMA((4,)),
            pltpu.SemaphoreType.DMA((4,)),
        ],
        compiler_params=pltpu.CompilerParams(vmem_limit_bytes=VMEM_LIMIT),
        cost_estimate=pl.CostEstimate(flops=2 * requests * half * 256 * 384, bytes_accessed=8 * MIB, transcendentals=0),
    )(owner, lengths, scales, cache, after)


def fours(hot):
    beside = hot ^ 1
    return (hot, beside, *(e for e in range(4) if e not in (hot, beside)))


def routes(hot):
    hot, beside, one, two = fours(hot)
    permutations = [[e ^ 1 for e in range(4)]]
    for a, b in ((hot, one), (hot, two), (beside, one), (beside, two)):
        permutations.append([b if e == a else a if e == b else e for e in range(4)])
    return permutations


def own_routes(hot):
    hot, beside, one, two = fours(hot)
    return {hot: (3, 4), beside: (1,), one: (2,), two: (1,)}


def pick(index, values):
    value = jnp.int32(values[0])
    for at in range(1, len(values)):
        value = jnp.where(index == at, values[at], value)
    return value


def unpack_kernel(hot, second, facts_ref, g0, g1, g2, g3, g4, out_ref, scales_ref, *scratch):
    held, stage, tails, slots, starts, counts, sems, out_sem = scratch
    got = (g0, g1, g2, g3, g4)
    experts = 4
    requests = facts_ref.shape[1]
    capacity = out_ref.shape[0] // experts
    columns, positions = out_ref.shape[1], out_ref.shape[2]
    blocks = scales_ref.shape[1]
    half = columns // 2
    tail = tails.shape[1]
    window = positions // UNIT + 1
    units = held.shape[1] // half - window
    me = lax.axis_index("expert")
    other = 1 - lax.axis_index("segment")

    def rows_of(unit):
        return pl.ds(pl.multiple_of(unit * half, 16), half)

    def units_of(unit):
        return pl.ds(pl.multiple_of(tail + unit * half, 16), half)

    def source_of(k):
        return (me - k) & (experts - 1)

    def scan(k, _):
        row = source_of(k) * 2 + other

        def note(i, carry):
            rank, end = carry
            mine = facts_ref[row, i] >> FACT_BITS == me
            length = facts_ref[row, i] & (FACT - 1)

            @pl.when(mine)
            def _():
                starts[k, rank] = end
                counts[k, rank] = length

            return (jnp.where(mine, rank + 1, rank), jnp.where(mine, end + length, end))

        rank, end = lax.fori_loop(0, requests, note, (0, 0))
        starts[k, capacity] = rank
        counts[k, capacity] = (end + UNIT - 1) >> UNIT_BITS
        return 0

    lax.fori_loop(0, experts, scan, 0)

    def fetch(ref, k, low, high, before):
        def one(u, _):
            pltpu.make_async_copy(ref.at[units_of(u - before)], held.at[k, rows_of(u)], sems.at[k]).start()
            return 0

        lax.fori_loop(low, high, one, 0)

    def fetch_stream(k, _):
        source = source_of(k)
        used = counts[k, capacity]
        routed = [pick(source, routes(hot)[permute]) == me for permute in range(5)]
        stays = [pick(me, [int(permute in own_routes(hot)[e]) for e in range(4)]) == 1 for permute in range(5)]
        for permute in range(5):
            held_units = (got[permute].shape[0] - tail) // half

            @pl.when(jnp.logical_and(routed[permute], jnp.logical_or(k > 0, stays[permute])))
            def _():
                if permute < 4:
                    pltpu.make_async_copy(got[permute].at[pl.ds(0, tail)], tails.at[k], sems.at[experts]).start()
                    fetch(got[permute], k, 0, jnp.minimum(used, held_units), 0)
                else:
                    split = jnp.logical_and(k == 0, me == hot)

                    @pl.when(jnp.logical_not(split))
                    def _():
                        pltpu.make_async_copy(got[permute].at[pl.ds(0, tail)], tails.at[k], sems.at[experts]).start()

                    before = jnp.where(split, min(second, units - second), 0)
                    fetch(got[permute], k, jnp.where(split, second, 0), used, before)

        return 0

    lax.fori_loop(0, experts, fetch_stream, 0)
    gap, position = stream_gap("window", positions, window)

    def write(k):
        there = out_ref.at[pl.ds(source_of(k) * capacity, capacity)]
        return pltpu.make_async_copy(stage.at[k], there, out_sem.at[k])

    def put_stream(k, _):
        used, ranks = counts[k, capacity], starts[k, capacity]

        def arrive(u, _):
            pltpu.make_async_copy(g0.at[units_of(0)], held.at[k, rows_of(0)], sems.at[k]).wait()
            return 0

        lax.fori_loop(0, used, arrive, 0)
        for j in range(window):
            held[k, rows_of(used + j), :] = jnp.zeros((half, 2 * UNIT), jnp.bfloat16)

        def put(pair, _):
            for rank in (2 * pair, 2 * pair + 1):
                filled = rank < ranks
                start, length = jnp.where(filled, starts[k, rank], 0), jnp.where(filled, counts[k, rank], 0)
                unit, shift = start >> UNIT_BITS, start & (UNIT - 1)
                move = moving(gap, position, shift, length)
                seen = jnp.concatenate([held[k, rows_of(unit + j), :] for j in range(window)], axis=1)
                moved = jnp.dot(seen, move, preferred_element_type=jnp.float32).astype(jnp.bfloat16)
                stage[k, rank, :half, :] = moved[:, :positions]
                stage[k, rank, half:, :] = moved[:, positions:]
            return 0

        def clear(pair, _):
            stage[k, pl.ds(2 * pair, 2)] = jnp.zeros((2, columns, positions), jnp.bfloat16)
            return 0

        pairs = (ranks + 1) >> 1
        lax.fori_loop(0, pairs, put, 0)
        lax.fori_loop(pairs, capacity // 2, clear, 0)
        write(k).start()
        return 0

    lax.fori_loop(0, experts, put_stream, 0)
    for k in range(experts):
        pltpu.make_async_copy(g0.at[pl.ds(0, tail)], tails.at[k], sems.at[experts]).wait()
    slots[...] = tails[...].astype(jnp.float32)

    def put_scales(k, _):
        for rank in range(capacity):
            scales_ref[source_of(k) * capacity + rank] = slots[k, rank * blocks : (rank + 1) * blocks, :].astype(
                jnp.bfloat16
            )
        return 0

    lax.fori_loop(0, experts, put_scales, 0)
    for k in range(experts):
        write(k).wait()


def unpack(hot, plan, facts, got, units, capacity, columns, positions, blocks):
    half = columns // 2
    window = positions // UNIT + 1
    smem = pl.BlockSpec(memory_space=pltpu.SMEM)
    vmem = pl.BlockSpec(memory_space=pltpu.VMEM)
    hbm = pl.BlockSpec(memory_space=pl.ANY)
    return pl.pallas_call(
        functools.partial(unpack_kernel, hot, PLANS[plan][1]),
        in_specs=[smem] + [hbm] * 5,
        out_specs=[hbm, vmem],
        out_shape=[
            jax.ShapeDtypeStruct((4 * capacity, columns, positions), jnp.bfloat16),
            jax.ShapeDtypeStruct((4 * capacity, blocks, positions), jnp.bfloat16),
        ],
        scratch_shapes=[
            pltpu.VMEM((4, (units + window) * half, 2 * UNIT), jnp.bfloat16),
            pltpu.VMEM((4, capacity, columns, positions), jnp.bfloat16),
            pltpu.VMEM((4, capacity * blocks, positions), jnp.bfloat16),
            pltpu.VMEM((4, capacity * blocks, positions), jnp.float32),
            pltpu.SMEM((4, capacity + 1), jnp.int32),
            pltpu.SMEM((4, capacity + 1), jnp.int32),
            pltpu.SemaphoreType.DMA((5,)),
            pltpu.SemaphoreType.DMA((4,)),
        ],
        compiler_params=pltpu.CompilerParams(vmem_limit_bytes=VMEM_LIMIT),
        cost_estimate=pl.CostEstimate(flops=2 * 32 * half * 256 * 384, bytes_accessed=10 * MIB, transcendentals=0),
    )(facts, *got)


def choose_kernel(facts_ref, out_ref):
    experts = 4
    rows, requests = facts_ref.shape
    load = [[jnp.int32(0)] * experts for _ in range(experts)]
    for row in range(rows):

        def add(i, sums):
            owner, length = facts_ref[row, i] >> FACT_BITS, facts_ref[row, i] & (FACT - 1)
            part = length << ((owner >> 1) << 4)
            odd = (owner & 1) == 1
            return (sums[0] + jnp.where(odd, 0, part), sums[1] + jnp.where(odd, part, 0))

        even, odd = lax.fori_loop(0, requests, add, (jnp.int32(0), jnp.int32(0)), unroll=8)
        for o, sums in enumerate((even, odd, even >> 16, odd >> 16)):
            units = ((sums & 0xFFFF) + UNIT - 1) >> UNIT_BITS
            load[row // 2][o] = jnp.maximum(load[row // 2][o], units)
    hot, highest = jnp.int32(0), jnp.int32(-1)
    for o in range(experts):
        worst = functools.reduce(jnp.maximum, [load[source][o] for source in range(experts) if source != o])
        hot = jnp.where(worst > highest, o, hot)
        highest = jnp.maximum(worst, highest)
    most, second = jnp.int32(0), jnp.int32(0)
    for h in range(experts):
        sizes = [jnp.int32(0), jnp.int32(0)]
        for permute, targets in enumerate(routes(h)):
            for source, target in enumerate(targets):
                if source != target:
                    sizes[permute // 3] = jnp.maximum(sizes[permute // 3], load[source][target])
        for e in range(experts):
            if e == h:
                sizes[1] = jnp.maximum(sizes[1], (load[e][e] + 1) >> 1)
            else:
                sizes[0] = jnp.maximum(sizes[0], load[e][e])
        most = jnp.where(hot == h, sizes[0], most)
        second = jnp.where(hot == h, sizes[1], second)
    plan = jnp.int32(len(PLANS) - 1)
    for p in range(len(PLANS) - 2, -1, -1):
        plan = jnp.where(jnp.logical_and(most <= PLANS[p][0], second <= PLANS[p][1]), p, plan)
    out_ref[0] = hot * len(PLANS) + plan


def choose(facts):
    smem = pl.BlockSpec(memory_space=pltpu.SMEM)
    return pl.pallas_call(
        choose_kernel,
        in_specs=[smem],
        out_specs=smem,
        out_shape=jax.ShapeDtypeStruct((1,), jnp.int32),
    )(facts)


def crossed(targets):
    return [(source * 2 + s, target * 2 + 1 - s) for source, target in enumerate(targets) for s in range(2)]


def by_halves(branches, index, operands):
    def run(low, high, operands):
        if high - low == 1:
            return branches[low](operands)
        middle = (low + high) // 2
        return lax.cond(
            index < middle, functools.partial(run, low, middle), functools.partial(run, middle, high), operands
        )

    return run(0, len(branches), operands)


def exchange(streams, facts, me, hot, plan, capacity, columns, positions, blocks):
    half = columns // 2
    tail = capacity * blocks
    units = (streams.shape[1] - tail) // half
    got = []
    for permute, targets in enumerate(routes(hot)):
        size = PLANS[plan][permute // 3]
        k = pick(me, [(target - source) % 4 for source, target in enumerate(targets)])
        first = jnp.int32(0)
        if permute == 4:
            first = jnp.where(me == hot, min(size, units - size) * half, 0)
        part = lax.dynamic_slice(streams, (k, first, jnp.int32(0)), (1, tail + size * half, streams.shape[2]))[0]
        got.append(lax.ppermute(part, ("expert", "segment"), crossed(targets)))
    return unpack(hot, plan, facts, got, units, capacity, columns, positions, blocks)


def slot_layout(owner, experts, capacity):
    requests = owner.shape[0]
    indices = jnp.arange(requests, dtype=jnp.int32)
    earlier = indices[None, :] < indices[:, None]
    same_owner = owner[:, None] == owner[None, :]
    arrival_rank = jnp.sum(jnp.logical_and(same_owner, earlier), axis=1)
    target = owner * capacity + arrival_rank
    routing = target[None, :] == jnp.arange(experts * capacity, dtype=jnp.int32)[:, None]
    filled = jnp.any(routing, axis=1)
    source = jnp.sum(jnp.where(routing, indices[None, :], 0), axis=1)
    return (filled, source)


def pick_slots(values, filled, source):
    zero_value = jnp.zeros((), values.dtype)
    return jnp.where(filled[:, None, None], jnp.take(values, source, axis=0), zero_value)


def on_device(
    res_cache,
    res_scales,
    res_lengths,
    res_query,
    new_cache,
    new_scales,
    new_lengths,
    new_query,
    owner,
):
    experts = lax.axis_size("expert")
    sections = lax.axis_size("segment")
    requests, positions, columns = new_cache.shape
    capacity = max(2, 2 * requests // experts)
    swap = [(0, 1), (1, 0)]
    cache_t = jnp.transpose(new_cache, (0, 2, 1))
    res_inputs = (jnp.transpose(res_query, (0, 2, 1)), jnp.transpose(res_cache, (0, 2, 1)), res_scales, res_lengths)
    inputs = (res_inputs, (jnp.transpose(new_query, (0, 2, 1)), cache_t, new_scales, new_lengths))

    def attention(res_inputs, new_inputs):
        return attend(*res_inputs, 1), attend(*new_inputs, 1)

    if experts != 4 or sections != 2 or positions % UNIT or columns % 32:
        live_rows = jnp.arange(positions)[None, :] < new_lengths[:, None]
        zero_value = jnp.zeros((), jnp.bfloat16)
        filled, source = slot_layout(owner, experts, capacity)
        send_cache = pick_slots(jnp.where(live_rows[:, :, None], new_cache, zero_value), filled, source)
        send_scales = pick_slots(jnp.where(live_rows[:, None, :], new_scales, zero_value), filled, source)
        got_cache = lax.all_to_all(send_cache, "expert", split_axis=0, concat_axis=0, tiled=True)
        got_scales = lax.all_to_all(send_scales, "expert", split_axis=0, concat_axis=0, tiled=True)
        owned_cache, owned_scales = lax.ppermute((got_cache, got_scales), "segment", swap)
        return (*attention(*inputs), owned_cache, owned_scales)

    me = lax.axis_index("expert")
    section = lax.axis_index("segment")
    units = capacity * positions // UNIT
    facts = owner * FACT + new_lengths
    sibling = lax.ppermute(facts, "segment", swap)
    chip = jnp.where(section == 0, jnp.stack([facts, sibling]), jnp.stack([sibling, facts]))
    chips = [chip] + [lax.ppermute(chip, "expert", [(e, (e + k) % 4) for e in range(4)]) for k in range(1, 4)]
    streams = pack(owner, new_lengths, new_scales, cache_t, sibling, units, capacity)
    facts = lax.dynamic_slice_in_dim(jnp.concatenate(chips[::-1] * 2), (3 - me) * 2, 8, 0)
    branch = choose(facts)[0]

    def take(hot, plan):
        def run(operands):
            streams, facts, *inputs = operands
            owned = exchange(streams, facts, me, hot, plan, capacity, columns, positions, new_scales.shape[1])
            return (*attention(*inputs), *owned)

        return run

    branches = [take(hot, plan) for hot in range(4) for plan in range(len(PLANS))]
    res_context, new_context, owned, owned_scales = by_halves(branches, branch, (streams, facts, *inputs))
    return (res_context, new_context, jnp.transpose(owned, (0, 2, 1)), owned_scales)


def solution(mesh):
    placed = (
        P(("group", "expert", "segment", "attn"), None, None),
        P(("group", "expert", "segment", "attn"), None, None),
        P(("group", "expert", "segment", "attn")),
        P(("group", "expert", "segment", "attn"), None, None),
        P(("group", "expert", "segment", "attn"), None, None),
        P(("group", "expert", "segment", "attn"), None, None),
        P(("group", "expert", "segment", "attn")),
        P(("group", "expert", "segment", "attn"), None, None),
        P(("group", "expert", "segment", "attn")),
    )
    return jax.shard_map(
        on_device,
        mesh=mesh,
        in_specs=placed,
        out_specs=(
            P(("group", "expert", "segment", "attn"), None, None),
            P(("group", "expert", "segment", "attn"), None, None),
            P(("group", "expert", "segment", "attn"), None, None),
            P(("group", "expert", "segment", "attn"), None, None),
        ),
        check_vma=False,
    )
```

```python
import functools
import jax
import jax.numpy as jnp
from jax import lax
from jax.experimental import pallas as pl
from jax.experimental.pallas import tpu as pltpu
from jax.sharding import PartitionSpec as P

LATENT = 512
BLOCK = 128
UNIT_BITS = 6
UNIT = 1 << UNIT_BITS
SPLIT = 6
PLANS = ((12, 7), (13, 8), (14, 10))
SWAPS = ((0, 2), (0, 3), (1, 2), (1, 3))
FACT_BITS = 8
FACT = 1 << FACT_BITS

softmax_scale = 192.0 ** (-0.5)
MIB = 1 << 20
VMEM_LIMIT = 56 * MIB


def attend_kernel(lengths_ref, query_ref, cache_ref, scales_ref, out_ref, factors_ref):
    blocks = scales_ref.shape[1]
    positions = cache_ref.shape[2]
    contract_rows = (((0,), (0,)), ((), ()))
    contract_positions = (((1,), (1,)), ((), ()))
    length = lengths_ref[pl.program_id(0)]

    def block(b):
        return pl.ds(pl.multiple_of(b * BLOCK, BLOCK), BLOCK)

    for b in range(blocks):
        factors_ref[b] = scales_ref[0, b : b + 1, :].astype(jnp.float32)

    def add(b, scores):
        part = lax.dot_general(
            query_ref[0, block(b), :], cache_ref[0, block(b), :], contract_rows, preferred_element_type=jnp.float32
        )
        return scores + part * factors_ref[b]

    scores = lax.dot_general(
        query_ref[0, LATENT:, :], cache_ref[0, LATENT:, :], contract_rows, preferred_element_type=jnp.float32
    )
    scores = lax.fori_loop(0, blocks, add, scores)
    live = lax.broadcasted_iota(jnp.int32, (1, positions), 1) < length
    scores = jnp.where(live, scores * softmax_scale, -jnp.inf)
    exponent = jnp.exp(scores - jnp.max(scores, axis=-1, keepdims=True))
    probabilities = exponent * (1.0 / jnp.sum(exponent, axis=-1, keepdims=True))

    def put(b, _):
        out_ref[0, :, block(b)] = lax.dot_general(
            (probabilities * factors_ref[b]).astype(jnp.bfloat16),
            cache_ref[0, block(b), :],
            contract_positions,
            preferred_element_type=jnp.float32,
        ).astype(jnp.bfloat16)
        return 0

    lax.fori_loop(0, blocks, put, 0)


def attend(query, cache, scales, lengths):
    requests, columns, heads = query.shape
    positions = cache.shape[2]
    return pl.pallas_call(
        attend_kernel,
        grid=(requests,),
        in_specs=[
            pl.BlockSpec(memory_space=pltpu.SMEM),
            pl.BlockSpec((1, columns, heads), lambda i: (i, 0, 0)),
            pl.BlockSpec((1, columns, positions), lambda i: (i, 0, 0)),
            pl.BlockSpec((1, scales.shape[1], positions), lambda i: (i, 0, 0)),
        ],
        out_specs=pl.BlockSpec((1, heads, LATENT), lambda i: (i, 0, 0)),
        out_shape=jax.ShapeDtypeStruct((requests, heads, LATENT), jnp.bfloat16),
        scratch_shapes=[pltpu.VMEM((scales.shape[1], 1, positions), jnp.float32)],
        compiler_params=pltpu.CompilerParams(vmem_limit_bytes=VMEM_LIMIT),
        cost_estimate=pl.CostEstimate(
            flops=4 * requests * heads * positions * columns,
            bytes_accessed=2 * requests * (heads * (columns + LATENT) + positions * columns),
            transcendentals=requests * heads * positions,
        ),
    )(lengths, query, cache, scales)


def stream_gap(rows, positions, units):
    window = units * 2 * UNIT
    shape = (window, 2 * positions) if rows == "window" else (2 * positions, window)
    first, second = lax.broadcasted_iota(jnp.int32, shape, 0), lax.broadcasted_iota(jnp.int32, shape, 1)
    lane, own = (first, second) if rows == "window" else (second, first)
    within = lane % (2 * UNIT)
    place = lane // (2 * UNIT) * UNIT + within % UNIT
    meet = within // UNIT == own // positions
    side = (1, 2 * positions) if rows == "window" else (2 * positions, 1)
    position = lax.broadcasted_iota(jnp.int32, side, 1 if rows == "window" else 0) % positions
    return jnp.where(meet, place - own % positions, -512).astype(jnp.bfloat16), position


def moving(gap, position, shift, length):
    wanted = jnp.where(position < length, shift, 512).astype(jnp.bfloat16)
    return jnp.where(gap == wanted, jnp.ones((), jnp.bfloat16), jnp.zeros((), jnp.bfloat16))


def targets_of(way):
    if way == 0:
        return [e ^ 1 for e in range(4)]
    a, b = SWAPS[way - 1]
    return [b if e == a else a if e == b else e for e in range(4)]


def staying(e):
    return [way for way in range(5) if targets_of(way)[e] == e]


def pick(index, values):
    value = jnp.int32(values[0])
    for at in range(1, len(values)):
        value = jnp.where(index == at, values[at], value)
    return value


def pack_kernel(owner_ref, lengths_ref, scales_ref, cache_ref, after_ref, *refs):
    outs, (held, acc, slots, ends, ranks, in_sem, out_sem) = refs[:5], refs[5:]
    experts = 4
    requests, columns, positions = cache_ref.shape
    blocks = scales_ref.shape[1]
    half = columns // 2
    tail = slots.shape[1]
    window = positions // UNIT + 1
    me = lax.axis_index("expert")
    parts = in_sem.shape[0]
    share = requests // parts

    def rows_of(unit):
        return pl.ds(pl.multiple_of(tail + unit * half, 16), half)

    def fetch(part):
        here = pl.ds(part * share, share)
        return pltpu.make_async_copy(cache_ref.at[here], held.at[here], in_sem.at[part])

    for part in range(parts):
        fetch(part).start()
    gap, position = stream_gap("request", positions, window)
    for k in range(experts):
        ends[k] = 0
        ranks[k] = 0
        acc[k, rows_of(0), :] = jnp.zeros((half, 2 * UNIT), jnp.bfloat16)
    slots[...] = jnp.zeros(slots.shape, jnp.float32)
    live = lax.broadcasted_iota(jnp.int32, (blocks, positions), 1)

    def place(i, _):
        k = owner_ref[i]
        length = lengths_ref[i]
        start, rank = ends[k], ranks[k]
        ends[k] = start + length
        ranks[k] = rank + 1
        slots[k, pl.ds(rank * blocks, blocks), :] = jnp.where(live < length, scales_ref[i].astype(jnp.float32), 0.0)
        unit, shift = start >> UNIT_BITS, start & (UNIT - 1)
        move = moving(gap, position, shift, length)
        both = jnp.concatenate([held[i, :half, :], held[i, half:, :]], axis=1)
        moved = jnp.dot(both, move, preferred_element_type=jnp.float32).astype(jnp.bfloat16)
        acc[k, rows_of(unit), :] += moved[:, : 2 * UNIT]
        for j in range(1, window):
            acc[k, rows_of(unit + j), :] = moved[:, 2 * UNIT * j : 2 * UNIT * (j + 1)]
        return 0

    for part in range(parts):
        fetch(part).wait()
        lax.fori_loop(part * share, (part + 1) * share, place, 0, unroll=2)
    acc[:, :tail, :] = slots[...].astype(jnp.bfloat16)
    copies = []
    for way, out in enumerate(outs):
        k = pick(me, targets_of(way))
        skipped = pick(me, [SPLIT * half if way == staying(e)[1] else 0 for e in range(experts)])
        for part in range(2):
            rows = out.shape[0] // 2
            here = pl.ds(pl.multiple_of(part * rows + skipped, 16), rows)
            copy = pltpu.make_async_copy(acc.at[k, here], out.at[pl.ds(part * rows, rows)], out_sem.at[way, part])
            copies.append(copy)
    for each in copies:
        each.start()
    for each in copies:
        each.wait()


def pack(owner, lengths, scales, cache, after, units, capacity):
    requests, columns, positions = cache.shape
    half = columns // 2
    window = positions // UNIT + 1
    tail = capacity * scales.shape[1]
    smem = pl.BlockSpec(memory_space=pltpu.SMEM)
    vmem = pl.BlockSpec(memory_space=pltpu.VMEM)
    hbm = pl.BlockSpec(memory_space=pl.ANY)
    lanes = 2 * UNIT
    return pl.pallas_call(
        pack_kernel,
        in_specs=[smem, smem, vmem, hbm, hbm],
        out_specs=[hbm] * 5,
        out_shape=[jax.ShapeDtypeStruct((tail + units * half, lanes), jnp.bfloat16)] * 5,
        scratch_shapes=[
            pltpu.VMEM(cache.shape, jnp.bfloat16),
            pltpu.VMEM((4, tail + (units + SPLIT) * half, lanes), jnp.bfloat16),
            pltpu.VMEM((4, tail, positions), jnp.float32),
            pltpu.SMEM((4,), jnp.int32),
            pltpu.SMEM((4,), jnp.int32),
            pltpu.SemaphoreType.DMA((4,)),
            pltpu.SemaphoreType.DMA((5, 2)),
        ],
        compiler_params=pltpu.CompilerParams(vmem_limit_bytes=VMEM_LIMIT),
        cost_estimate=pl.CostEstimate(flops=2 * requests * half * 256 * 384, bytes_accessed=8 * MIB, transcendentals=0),
    )(owner, lengths, scales, cache, after)


def unpack_kernel(facts_ref, g0, g1, g2, g3, g4, out_ref, scales_ref, *scratch):
    held, stage, tails, slots, starts, counts, sems, out_sem = scratch
    got = (g0, g1, g2, g3, g4)
    experts = 4
    requests = facts_ref.shape[1]
    capacity = out_ref.shape[0] // experts
    columns, positions = out_ref.shape[1], out_ref.shape[2]
    blocks = scales_ref.shape[1]
    half = columns // 2
    tail = tails.shape[1]
    window = positions // UNIT + 1
    me = lax.axis_index("expert")

    def rows_of(unit):
        return pl.ds(pl.multiple_of(unit * half, 16), half)

    def units_of(unit):
        return pl.ds(pl.multiple_of(tail + unit * half, 16), half)

    def source_of(k):
        return (me - k) & (experts - 1)

    def scan(k, _):
        def note(i, carry):
            rank, end = carry
            mine = facts_ref[k, i] >> FACT_BITS == me
            length = facts_ref[k, i] & (FACT - 1)

            @pl.when(mine)
            def _():
                starts[k, rank] = end
                counts[k, rank] = length

            return (jnp.where(mine, rank + 1, rank), jnp.where(mine, end + length, end))

        rank, end = lax.fori_loop(0, requests, note, (0, 0))
        starts[k, capacity] = rank
        counts[k, capacity] = (end + UNIT - 1) >> UNIT_BITS
        return 0

    lax.fori_loop(0, experts, scan, 0)

    def fetch_stream(k, _):
        used = counts[k, capacity]
        for way in range(5):
            came = pick(source_of(k), targets_of(way)) == me
            later = jnp.logical_and(k == 0, pick(me, [int(way == staying(e)[1]) for e in range(experts)]) == 1)
            low = jnp.where(later, SPLIT, 0)
            high = jnp.where(jnp.logical_and(k == 0, jnp.logical_not(later)), jnp.minimum(used, SPLIT), used)

            @pl.when(came)
            def _():
                @pl.when(jnp.logical_not(later))
                def _():
                    pltpu.make_async_copy(got[way].at[pl.ds(0, tail)], tails.at[k], sems.at[experts]).start()

                def fetch(u, _):
                    there = held.at[k, rows_of(u)]
                    pltpu.make_async_copy(got[way].at[units_of(u - low)], there, sems.at[k]).start()
                    return 0

                lax.fori_loop(low, high, fetch, 0)

        return 0

    lax.fori_loop(0, experts, fetch_stream, 0)
    gap, position = stream_gap("window", positions, window)

    def write(k):
        there = out_ref.at[pl.ds(source_of(k) * capacity, capacity)]
        return pltpu.make_async_copy(stage.at[k], there, out_sem.at[k])

    def put_stream(k, _):
        used, ranks = counts[k, capacity], starts[k, capacity]

        def arrive(u, _):
            pltpu.make_async_copy(g0.at[units_of(0)], held.at[k, rows_of(0)], sems.at[k]).wait()
            return 0

        lax.fori_loop(0, used, arrive, 0)
        for j in range(window):
            held[k, rows_of(used + j), :] = jnp.zeros((half, 2 * UNIT), jnp.bfloat16)

        def put(pair, _):
            for rank in (2 * pair, 2 * pair + 1):
                filled = rank < ranks
                start, length = jnp.where(filled, starts[k, rank], 0), jnp.where(filled, counts[k, rank], 0)
                unit, shift = start >> UNIT_BITS, start & (UNIT - 1)
                move = moving(gap, position, shift, length)
                seen = jnp.concatenate([held[k, rows_of(unit + j), :] for j in range(window)], axis=1)
                moved = jnp.dot(seen, move, preferred_element_type=jnp.float32).astype(jnp.bfloat16)
                stage[k, rank, :half, :] = moved[:, :positions]
                stage[k, rank, half:, :] = moved[:, positions:]
            return 0

        def clear(pair, _):
            stage[k, pl.ds(2 * pair, 2)] = jnp.zeros((2, columns, positions), jnp.bfloat16)
            return 0

        pairs = (ranks + 1) >> 1
        lax.fori_loop(0, pairs, put, 0)
        lax.fori_loop(pairs, capacity // 2, clear, 0)
        write(k).start()
        return 0

    lax.fori_loop(0, experts, put_stream, 0)
    for k in range(experts):
        pltpu.make_async_copy(g0.at[pl.ds(0, tail)], tails.at[k], sems.at[experts]).wait()
    slots[...] = tails[...].astype(jnp.float32)

    def put_scales(k, _):
        for rank in range(capacity):
            scales_ref[source_of(k) * capacity + rank] = slots[k, rank * blocks : (rank + 1) * blocks, :].astype(
                jnp.bfloat16
            )
        return 0

    lax.fori_loop(0, experts, put_scales, 0)
    for k in range(experts):
        write(k).wait()


def unpack(facts, got, units, capacity, columns, positions, blocks):
    half = columns // 2
    window = positions // UNIT + 1
    smem = pl.BlockSpec(memory_space=pltpu.SMEM)
    vmem = pl.BlockSpec(memory_space=pltpu.VMEM)
    hbm = pl.BlockSpec(memory_space=pl.ANY)
    return pl.pallas_call(
        unpack_kernel,
        in_specs=[smem] + [hbm] * 5,
        out_specs=[hbm, vmem],
        out_shape=[
            jax.ShapeDtypeStruct((4 * capacity, columns, positions), jnp.bfloat16),
            jax.ShapeDtypeStruct((4 * capacity, blocks, positions), jnp.bfloat16),
        ],
        scratch_shapes=[
            pltpu.VMEM((4, (units + window) * half, 2 * UNIT), jnp.bfloat16),
            pltpu.VMEM((4, capacity, columns, positions), jnp.bfloat16),
            pltpu.VMEM((4, capacity * blocks, positions), jnp.bfloat16),
            pltpu.VMEM((4, capacity * blocks, positions), jnp.float32),
            pltpu.SMEM((4, capacity + 1), jnp.int32),
            pltpu.SMEM((4, capacity + 1), jnp.int32),
            pltpu.SemaphoreType.DMA((5,)),
            pltpu.SemaphoreType.DMA((4,)),
        ],
        compiler_params=pltpu.CompilerParams(vmem_limit_bytes=24 * MIB),
        cost_estimate=pl.CostEstimate(flops=2 * 32 * half * 256 * 384, bytes_accessed=10 * MIB, transcendentals=0),
    )(facts, *got)


def choose_kernel(c0, c1, c2, c3, out_ref, facts_ref, loads_ref):
    experts = 4
    requests = c0.shape[1]
    me, other = lax.axis_index("expert"), 1 - lax.axis_index("segment")
    for k, chip in enumerate((c0, c1, c2, c3)):
        most = [jnp.int32(0)] * experts
        for section in range(2):

            def add(i, sums):
                fact = chip[section, i]
                owner, length = fact >> FACT_BITS, fact & (FACT - 1)
                part = length << ((owner >> 1) << 4)
                odd = (owner & 1) == 1
                return (sums[0] + jnp.where(odd, 0, part), sums[1] + jnp.where(odd, part, 0))

            even, odd = lax.fori_loop(0, requests, add, (jnp.int32(0), jnp.int32(0)), unroll=8)
            for o, sums in enumerate((even, odd, even >> 16, odd >> 16)):
                most[o] = jnp.maximum(most[o], ((sums & 0xFFFF) + UNIT - 1) >> UNIT_BITS)
        for o in range(experts):
            loads_ref[((me - k) & (experts - 1)) * experts + o] = most[o]

        def keep(i, _):
            facts_ref[k, i] = chip[other, i]
            return 0

        lax.fori_loop(0, requests, keep, 0, unroll=8)
    load = [[loads_ref[source * experts + o] for o in range(experts)] for source in range(experts)]
    hot, highest = jnp.int32(0), jnp.int32(-1)
    for o in range(experts):
        worst = functools.reduce(jnp.maximum, [load[source][o] for source in range(experts) if source != o])
        hot = jnp.where(worst > highest, o, hot)
        highest = jnp.maximum(worst, highest)
    paired = functools.reduce(jnp.maximum, [load[e][e ^ 1] for e in range(experts)])
    stays = functools.reduce(jnp.maximum, [load[e][e] for e in range(experts)])
    most, second = paired, stays - SPLIT
    for a, b in SWAPS:
        both = jnp.maximum(load[a][b], load[b][a])
        with_hot = jnp.logical_or(hot == a, hot == b)
        most = jnp.where(with_hot, jnp.maximum(most, both), most)
        second = jnp.where(with_hot, second, jnp.maximum(second, both))
    plan, fits = jnp.int32(len(PLANS) - 1), jnp.bool_(False)
    for p in range(len(PLANS) - 1, -1, -1):
        here = jnp.logical_and(most <= PLANS[p][0], second <= PLANS[p][1])
        plan, fits = jnp.where(here, p, plan), jnp.logical_or(fits, here)
    out_ref[0] = jnp.where(fits, hot * len(PLANS) + plan, experts * len(PLANS))


def choose(chips):
    smem = pl.BlockSpec(memory_space=pltpu.SMEM)
    return pl.pallas_call(
        choose_kernel,
        in_specs=[smem] * 4,
        out_specs=[smem] * 2,
        out_shape=[jax.ShapeDtypeStruct((1,), jnp.int32), jax.ShapeDtypeStruct((4, chips[0].shape[1]), jnp.int32)],
        scratch_shapes=[pltpu.SMEM((16,), jnp.int32)],
    )(*chips)


def crossed(targets):
    return [(source * 2 + s, target * 2 + 1 - s) for source, target in enumerate(targets) for s in range(2)]


def by_halves(branches, index, operands):
    def run(low, high, operands):
        if high - low == 1:
            return branches[low](operands)
        middle = (low + high) // 2
        return lax.cond(
            index < middle, functools.partial(run, low, middle), functools.partial(run, middle, high), operands
        )

    return run(0, len(branches), operands)


def sizes_of(branch, units):
    if branch == 4 * len(PLANS):
        return [units] * 5
    hot, plan = divmod(branch, len(PLANS))
    most, second = PLANS[plan]
    return [most] + [most if hot in swap else second for swap in SWAPS]


def slot_layout(owner, experts, capacity):
    requests = owner.shape[0]
    indices = jnp.arange(requests, dtype=jnp.int32)
    earlier = indices[None, :] < indices[:, None]
    same_owner = owner[:, None] == owner[None, :]
    arrival_rank = jnp.sum(jnp.logical_and(same_owner, earlier), axis=1)
    target = owner * capacity + arrival_rank
    routing = target[None, :] == jnp.arange(experts * capacity, dtype=jnp.int32)[:, None]
    filled = jnp.any(routing, axis=1)
    source = jnp.sum(jnp.where(routing, indices[None, :], 0), axis=1)
    return (filled, source)


def pick_slots(values, filled, source):
    zero_value = jnp.zeros((), values.dtype)
    return jnp.where(filled[:, None, None], jnp.take(values, source, axis=0), zero_value)


def on_device(
    res_cache,
    res_scales,
    res_lengths,
    res_query,
    new_cache,
    new_scales,
    new_lengths,
    new_query,
    owner,
):
    experts = lax.axis_size("expert")
    sections = lax.axis_size("segment")
    requests, positions, columns = new_cache.shape
    capacity = max(2, 2 * requests // experts)
    swap = [(0, 1), (1, 0)]
    cache_t = jnp.transpose(new_cache, (0, 2, 1))
    res_inputs = (jnp.transpose(res_query, (0, 2, 1)), jnp.transpose(res_cache, (0, 2, 1)), res_scales, res_lengths)
    inputs = (res_inputs, (jnp.transpose(new_query, (0, 2, 1)), cache_t, new_scales, new_lengths))

    def attention(res_inputs, new_inputs):
        return attend(*res_inputs), attend(*new_inputs)

    if experts != 4 or sections != 2 or positions % UNIT or columns % 32:
        live_rows = jnp.arange(positions)[None, :] < new_lengths[:, None]
        zero_value = jnp.zeros((), jnp.bfloat16)
        filled, source = slot_layout(owner, experts, capacity)
        send_cache = pick_slots(jnp.where(live_rows[:, :, None], new_cache, zero_value), filled, source)
        send_scales = pick_slots(jnp.where(live_rows[:, None, :], new_scales, zero_value), filled, source)
        got_cache = lax.all_to_all(send_cache, "expert", split_axis=0, concat_axis=0, tiled=True)
        got_scales = lax.all_to_all(send_scales, "expert", split_axis=0, concat_axis=0, tiled=True)
        owned_cache, owned_scales = lax.ppermute((got_cache, got_scales), "segment", swap)
        return (*attention(*inputs), owned_cache, owned_scales)

    section = lax.axis_index("segment")
    units, half = capacity * positions // UNIT, columns // 2
    blocks = new_scales.shape[1]
    facts = owner * FACT + new_lengths
    sibling = lax.ppermute(facts, "segment", swap)
    chip = jnp.where(section == 0, jnp.stack([facts, sibling]), jnp.stack([sibling, facts]))
    chips = [chip] + [lax.ppermute(chip, "expert", [(e, (e + k) % 4) for e in range(4)]) for k in range(1, 4)]
    streams = pack(owner, new_lengths, new_scales, cache_t, sibling, units, capacity)
    branch, facts = choose(chips)

    def take(branch):
        def run(operands):
            streams, facts, *inputs = operands
            got = []
            for way, size in enumerate(sizes_of(branch, units)):
                part = streams[way][: capacity * blocks + size * half]
                got.append(lax.ppermute(part, ("expert", "segment"), crossed(targets_of(way))))
            return (*attention(*inputs), *unpack(facts, got, units, capacity, columns, positions, blocks))

        return run

    branches = [take(branch) for branch in range(4 * len(PLANS) + 1)]
    res_context, new_context, owned, owned_scales = by_halves(branches, branch[0], (streams, facts, *inputs))
    return (res_context, new_context, jnp.transpose(owned, (0, 2, 1)), owned_scales)


def solution(mesh):
    placed = (
        P(("group", "expert", "segment", "attn"), None, None),
        P(("group", "expert", "segment", "attn"), None, None),
        P(("group", "expert", "segment", "attn")),
        P(("group", "expert", "segment", "attn"), None, None),
        P(("group", "expert", "segment", "attn"), None, None),
        P(("group", "expert", "segment", "attn"), None, None),
        P(("group", "expert", "segment", "attn")),
        P(("group", "expert", "segment", "attn"), None, None),
        P(("group", "expert", "segment", "attn")),
    )
    return jax.shard_map(
        on_device,
        mesh=mesh,
        in_specs=placed,
        out_specs=(
            P(("group", "expert", "segment", "attn"), None, None),
            P(("group", "expert", "segment", "attn"), None, None),
            P(("group", "expert", "segment", "attn"), None, None),
            P(("group", "expert", "segment", "attn"), None, None),
        ),
        check_vma=False,
    )
```

```python
import functools
import jax
import jax.numpy as jnp
from jax import lax
from jax.experimental import pallas as pl
from jax.experimental.pallas import tpu as pltpu
from jax.sharding import PartitionSpec as P

LATENT = 512
BLOCK = 128
UNIT_BITS = 6
UNIT = 1 << UNIT_BITS
SPLIT = 6
PLANS = ((12, 7), (13, 8), (14, 10))
SWAPS = ((0, 2), (0, 3), (1, 2), (1, 3))
FACT_BITS = 8
FACT = 1 << FACT_BITS

softmax_scale = 192.0 ** (-0.5)
MIB = 1 << 20


def attend_kernel(lengths_ref, query_ref, cache_ref, scales_ref, out_ref, factors_ref):
    blocks = scales_ref.shape[1]
    positions = cache_ref.shape[2]
    contract_rows = (((0,), (0,)), ((), ()))
    contract_positions = (((1,), (1,)), ((), ()))
    length = lengths_ref[pl.program_id(0)]

    def block(b):
        return pl.ds(pl.multiple_of(b * BLOCK, BLOCK), BLOCK)

    for b in range(blocks):
        factors_ref[b] = scales_ref[0, b : b + 1, :].astype(jnp.float32)

    def add(b, scores):
        part = lax.dot_general(
            query_ref[0, block(b), :], cache_ref[0, block(b), :], contract_rows, preferred_element_type=jnp.float32
        )
        return scores + part * factors_ref[b]

    scores = lax.dot_general(
        query_ref[0, LATENT:, :], cache_ref[0, LATENT:, :], contract_rows, preferred_element_type=jnp.float32
    )
    scores = lax.fori_loop(0, blocks, add, scores)
    live = lax.broadcasted_iota(jnp.int32, (1, positions), 1) < length
    scores = jnp.where(live, scores * softmax_scale, -jnp.inf)
    exponent = jnp.exp(scores - jnp.max(scores, axis=-1, keepdims=True))
    probabilities = exponent * (1.0 / jnp.sum(exponent, axis=-1, keepdims=True))

    def put(b, _):
        out_ref[0, :, block(b)] = lax.dot_general(
            (probabilities * factors_ref[b]).astype(jnp.bfloat16),
            cache_ref[0, block(b), :],
            contract_positions,
            preferred_element_type=jnp.float32,
        ).astype(jnp.bfloat16)
        return 0

    lax.fori_loop(0, blocks, put, 0)


def attend(query, cache, scales, lengths):
    requests, columns, heads = query.shape
    positions = cache.shape[2]
    return pl.pallas_call(
        attend_kernel,
        grid=(requests,),
        in_specs=[
            pl.BlockSpec(memory_space=pltpu.SMEM),
            pl.BlockSpec((1, columns, heads), lambda i: (i, 0, 0)),
            pl.BlockSpec((1, columns, positions), lambda i: (i, 0, 0)),
            pl.BlockSpec((1, scales.shape[1], positions), lambda i: (i, 0, 0)),
        ],
        out_specs=pl.BlockSpec((1, heads, LATENT), lambda i: (i, 0, 0)),
        out_shape=jax.ShapeDtypeStruct((requests, heads, LATENT), jnp.bfloat16),
        scratch_shapes=[pltpu.VMEM((scales.shape[1], 1, positions), jnp.float32)],
        compiler_params=pltpu.CompilerParams(vmem_limit_bytes=16 * MIB),
        cost_estimate=pl.CostEstimate(
            flops=4 * requests * heads * positions * columns,
            bytes_accessed=2 * requests * (heads * (columns + LATENT) + positions * columns),
            transcendentals=requests * heads * positions,
        ),
    )(lengths, query, cache, scales)


def stream_gap(rows, positions, first, units):
    window = units * 2 * UNIT
    shape = (window, 2 * positions) if rows == "window" else (2 * positions, window)
    down, across = lax.broadcasted_iota(jnp.int32, shape, 0), lax.broadcasted_iota(jnp.int32, shape, 1)
    lane, own = (down, across) if rows == "window" else (across, down)
    within = lane % (2 * UNIT)
    place = (lane // (2 * UNIT) + first) * UNIT + within % UNIT
    meet = within // UNIT == own // positions
    side = (1, 2 * positions) if rows == "window" else (2 * positions, 1)
    position = lax.broadcasted_iota(jnp.int32, side, 1 if rows == "window" else 0) % positions
    return jnp.where(meet, place - own % positions, -512).astype(jnp.bfloat16), position


def moving(gap, position, shift, length):
    wanted = jnp.where(position < length, shift, 512).astype(jnp.bfloat16)
    return jnp.where(gap == wanted, jnp.ones((), jnp.bfloat16), jnp.zeros((), jnp.bfloat16))


def targets_of(way):
    if way == 0:
        return [e ^ 1 for e in range(4)]
    a, b = SWAPS[way - 1]
    return [b if e == a else a if e == b else e for e in range(4)]


def staying(e):
    return [way for way in range(5) if targets_of(way)[e] == e]


def pick(index, values):
    value = jnp.int32(values[0])
    for at in range(1, len(values)):
        value = jnp.where(index == at, values[at], value)
    return value


def pack_kernel(owner_ref, lengths_ref, scales_ref, cache_ref, after_ref, *refs):
    outs, (held, acc, slots, ends, ranks, in_sem, out_sem) = refs[:5], refs[5:]
    experts = 4
    requests, columns, positions = cache_ref.shape
    blocks = scales_ref.shape[1]
    half = columns // 2
    tail = slots.shape[1]
    window = positions // UNIT
    me = lax.axis_index("expert")
    parts = in_sem.shape[0]
    share = requests // parts

    def rows_of(unit):
        return pl.ds(pl.multiple_of(tail + unit * half, 16), half)

    def fetch(part):
        here = pl.ds(part * share, share)
        return pltpu.make_async_copy(cache_ref.at[here], held.at[here], in_sem.at[part])

    for part in range(parts):
        fetch(part).start()
    gap, position = stream_gap("request", positions, 0, window)
    gap_behind, _ = stream_gap("request", positions, window, 1)
    for k in range(experts):
        ends[k] = 0
        ranks[k] = 0
        acc[k, rows_of(0), :] = jnp.zeros((half, 2 * UNIT), jnp.bfloat16)
    slots[...] = jnp.zeros(slots.shape, jnp.float32)
    live = lax.broadcasted_iota(jnp.int32, (blocks, positions), 1)

    def place(i, _):
        k = owner_ref[i]
        length = lengths_ref[i]
        start, rank = ends[k], ranks[k]
        ends[k] = start + length
        ranks[k] = rank + 1
        slots[k, pl.ds(rank * blocks, blocks), :] = jnp.where(live < length, scales_ref[i].astype(jnp.float32), 0.0)
        unit, shift = start >> UNIT_BITS, start & (UNIT - 1)
        move = moving(gap, position, shift, length)
        both = jnp.concatenate([held[i, :half, :], held[i, half:, :]], axis=1)
        moved = jnp.dot(both, move, preferred_element_type=jnp.float32).astype(jnp.bfloat16)
        acc[k, rows_of(unit), :] += moved[:, : 2 * UNIT]
        for j in range(1, window):
            acc[k, rows_of(unit + j), :] = moved[:, 2 * UNIT * j : 2 * UNIT * (j + 1)]

        @pl.when(shift + length >= window * UNIT)
        def _():
            move = moving(gap_behind, position, shift, length)
            moved = jnp.dot(both, move, preferred_element_type=jnp.float32)
            acc[k, rows_of(unit + window), :] = moved.astype(jnp.bfloat16)

        return 0

    for part in range(parts):
        fetch(part).wait()
        lax.fori_loop(part * share, (part + 1) * share, place, 0, unroll=2)
    acc[:, :tail, :] = slots[...].astype(jnp.bfloat16)
    copies = []
    for way, out in enumerate(outs):
        k = pick(me, targets_of(way))
        skipped = pick(me, [SPLIT if way == staying(e)[1] else 0 for e in range(experts)])
        near = (out.shape[0] - tail) // half // 2
        further = ends[k] > (near + skipped) * UNIT
        for rows, low, needed in ((tail + near * half, 0, True), (near * half, tail + near * half, further)):
            here = pl.ds(pl.multiple_of(low + skipped * half, 16), rows)
            copy = pltpu.make_async_copy(acc.at[k, here], out.at[pl.ds(low, rows)], out_sem.at[way, int(low > 0)])
            copies.append((copy, needed))
    for act in (lambda copy: copy.start(), lambda copy: copy.wait()):
        for copy, needed in copies:
            if needed is True:
                act(copy)
            else:
                pl.when(needed)(functools.partial(act, copy))


def pack(owner, lengths, scales, cache, after, units, capacity):
    requests, columns, positions = cache.shape
    half = columns // 2
    window = positions // UNIT + 1
    tail = capacity * scales.shape[1]
    smem = pl.BlockSpec(memory_space=pltpu.SMEM)
    vmem = pl.BlockSpec(memory_space=pltpu.VMEM)
    hbm = pl.BlockSpec(memory_space=pl.ANY)
    lanes = 2 * UNIT
    return pl.pallas_call(
        pack_kernel,
        in_specs=[smem, smem, vmem, hbm, hbm],
        out_specs=[hbm] * 5,
        out_shape=[jax.ShapeDtypeStruct((tail + units * half, lanes), jnp.bfloat16)] * 5,
        scratch_shapes=[
            pltpu.VMEM(cache.shape, jnp.bfloat16),
            pltpu.VMEM((4, tail + (units + SPLIT) * half, lanes), jnp.bfloat16),
            pltpu.VMEM((4, tail, positions), jnp.float32),
            pltpu.SMEM((4,), jnp.int32),
            pltpu.SMEM((4,), jnp.int32),
            pltpu.SemaphoreType.DMA((4,)),
            pltpu.SemaphoreType.DMA((5, 2)),
        ],
        compiler_params=pltpu.CompilerParams(vmem_limit_bytes=24 * MIB),
        cost_estimate=pl.CostEstimate(flops=2 * requests * half * 256 * 384, bytes_accessed=8 * MIB, transcendentals=0),
    )(owner, lengths, scales, cache, after)


def unpack_kernel(facts_ref, g0, g1, g2, g3, g4, out_ref, scales_ref, *scratch):
    held, stage, starts, counts, out_sem = scratch
    got = (g0, g1, g2, g3, g4)
    experts = 4
    requests = facts_ref.shape[1]
    capacity = out_ref.shape[0] // experts
    columns, positions = out_ref.shape[1], out_ref.shape[2]
    blocks = scales_ref.shape[1]
    half = columns // 2
    tail = capacity * blocks
    window = positions // UNIT
    me = lax.axis_index("expert")

    def rows_of(unit):
        return pl.ds(pl.multiple_of(unit * half, 16), half)

    def units_of(unit):
        return pl.ds(pl.multiple_of(tail + unit * half, 16), half)

    def source_of(k):
        return (me - k) & (experts - 1)

    def scan(k, _):
        def note(i, carry):
            rank, end = carry
            mine = facts_ref[k, i] >> FACT_BITS == me
            length = facts_ref[k, i] & (FACT - 1)

            @pl.when(mine)
            def _():
                starts[k, rank] = end
                counts[k, rank] = length

            return (jnp.where(mine, rank + 1, rank), jnp.where(mine, end + length, end))

        rank, end = lax.fori_loop(0, requests, note, (0, 0))
        starts[k, capacity] = rank
        counts[k, capacity] = (end + UNIT - 1) >> UNIT_BITS
        return 0

    lax.fori_loop(0, experts, scan, 0)

    def fetch_stream(k, _):
        used = counts[k, capacity]
        for way in range(5):
            came = pick(source_of(k), targets_of(way)) == me
            later = jnp.logical_and(k == 0, pick(me, [int(way == staying(e)[1]) for e in range(experts)]) == 1)
            low = jnp.where(later, SPLIT, 0)
            high = jnp.where(jnp.logical_and(k == 0, jnp.logical_not(later)), jnp.minimum(used, SPLIT), used)

            @pl.when(came)
            def _():
                @pl.when(jnp.logical_not(later))
                def _():
                    scales = got[way][:tail, :].astype(jnp.float32)
                    for rank in range(capacity):
                        here = scales[rank * blocks : (rank + 1) * blocks, :]
                        scales_ref[source_of(k) * capacity + rank] = here.astype(jnp.bfloat16)

                def move_unit(u, _):
                    held[k, rows_of(u), :] = got[way][units_of(u - low), :]
                    return 0

                lax.fori_loop(low, high, move_unit, 0)

        return 0

    lax.fori_loop(0, experts, fetch_stream, 0)
    gap, position = stream_gap("window", positions, 0, window)
    gap_behind, _ = stream_gap("window", positions, window, 1)

    def write(k):
        there = out_ref.at[pl.ds(source_of(k) * capacity, capacity)]
        return pltpu.make_async_copy(stage.at[k], there, out_sem.at[k])

    def put_stream(k, _):
        used, ranks = counts[k, capacity], starts[k, capacity]

        for j in range(window):
            held[k, rows_of(used + j), :] = jnp.zeros((half, 2 * UNIT), jnp.bfloat16)

        def put(pair, _):
            for rank in (2 * pair, 2 * pair + 1):
                filled = rank < ranks
                start, length = jnp.where(filled, starts[k, rank], 0), jnp.where(filled, counts[k, rank], 0)
                unit, shift = start >> UNIT_BITS, start & (UNIT - 1)
                move = moving(gap, position, shift, length)
                seen = jnp.concatenate([held[k, rows_of(unit + j), :] for j in range(window)], axis=1)
                moved = jnp.dot(seen, move, preferred_element_type=jnp.float32).astype(jnp.bfloat16)
                stage[k, rank, :half, :] = moved[:, :positions]
                stage[k, rank, half:, :] = moved[:, positions:]

                @pl.when(shift + length > window * UNIT)
                def _():
                    move = moving(gap_behind, position, shift, length)
                    seen = held[k, rows_of(unit + window), :]
                    moved = jnp.dot(seen, move, preferred_element_type=jnp.float32).astype(jnp.bfloat16)
                    stage[k, rank, :half, :] += moved[:, :positions]
                    stage[k, rank, half:, :] += moved[:, positions:]

            return 0

        def clear(pair, _):
            stage[k, pl.ds(2 * pair, 2)] = jnp.zeros((2, columns, positions), jnp.bfloat16)
            return 0

        pairs = (ranks + 1) >> 1
        lax.fori_loop(0, pairs, put, 0)
        lax.fori_loop(pairs, capacity // 2, clear, 0)
        write(k).start()
        return 0

    lax.fori_loop(0, experts, put_stream, 0)
    for k in range(experts):
        write(k).wait()


def unpack(facts, got, units, capacity, columns, positions, blocks):
    half = columns // 2
    window = positions // UNIT + 1
    smem = pl.BlockSpec(memory_space=pltpu.SMEM)
    vmem = pl.BlockSpec(memory_space=pltpu.VMEM)
    hbm = pl.BlockSpec(memory_space=pl.ANY)
    return pl.pallas_call(
        unpack_kernel,
        in_specs=[smem] + [vmem] * 5,
        out_specs=[hbm, vmem],
        out_shape=[
            jax.ShapeDtypeStruct((4 * capacity, columns, positions), jnp.bfloat16),
            jax.ShapeDtypeStruct((4 * capacity, blocks, positions), jnp.bfloat16),
        ],
        scratch_shapes=[
            pltpu.VMEM((4, (units + window) * half, 2 * UNIT), jnp.bfloat16),
            pltpu.VMEM((4, capacity, columns, positions), jnp.bfloat16),
            pltpu.SMEM((4, capacity + 1), jnp.int32),
            pltpu.SMEM((4, capacity + 1), jnp.int32),
            pltpu.SemaphoreType.DMA((4,)),
        ],
        compiler_params=pltpu.CompilerParams(vmem_limit_bytes=24 * MIB),
        cost_estimate=pl.CostEstimate(flops=2 * 32 * half * 256 * 384, bytes_accessed=10 * MIB, transcendentals=0),
    )(facts, *got)


def choose_kernel(c0, c1, c2, c3, out_ref, facts_ref, chips_ref, loads_ref, sem):
    experts = 4
    requests = c0.shape[1]
    me, other = lax.axis_index("expert"), 1 - lax.axis_index("segment")
    copies = [pltpu.make_async_copy(chip, chips_ref.at[k], sem.at[k]) for k, chip in enumerate((c0, c1, c2, c3))]
    for copy in copies:
        copy.start()
    for copy in copies:
        copy.wait()
    for k in range(experts):
        chip = chips_ref.at[k]
        most = [jnp.int32(0)] * experts
        for section in range(2):

            def add(i, sums):
                fact = chip[section, i]
                owner, length = fact >> FACT_BITS, fact & (FACT - 1)
                part = length << ((owner >> 1) << 4)
                odd = (owner & 1) == 1
                return (sums[0] + jnp.where(odd, 0, part), sums[1] + jnp.where(odd, part, 0))

            even, odd = lax.fori_loop(0, requests, add, (jnp.int32(0), jnp.int32(0)), unroll=8)
            for o, sums in enumerate((even, odd, even >> 16, odd >> 16)):
                most[o] = jnp.maximum(most[o], ((sums & 0xFFFF) + UNIT - 1) >> UNIT_BITS)
        for o in range(experts):
            loads_ref[((me - k) & (experts - 1)) * experts + o] = most[o]

        def keep(i, _):
            facts_ref[k, i] = chip[other, i]
            return 0

        lax.fori_loop(0, requests, keep, 0, unroll=8)
    load = [[loads_ref[source * experts + o] for o in range(experts)] for source in range(experts)]
    hot, highest = jnp.int32(0), jnp.int32(-1)
    for o in range(experts):
        worst = functools.reduce(jnp.maximum, [load[source][o] for source in range(experts) if source != o])
        hot = jnp.where(worst > highest, o, hot)
        highest = jnp.maximum(worst, highest)
    paired = functools.reduce(jnp.maximum, [load[e][e ^ 1] for e in range(experts)])
    stays = functools.reduce(jnp.maximum, [load[e][e] for e in range(experts)])
    most, second = paired, stays - SPLIT
    for a, b in SWAPS:
        both = jnp.maximum(load[a][b], load[b][a])
        with_hot = jnp.logical_or(hot == a, hot == b)
        most = jnp.where(with_hot, jnp.maximum(most, both), most)
        second = jnp.where(with_hot, second, jnp.maximum(second, both))
    plan, fits = jnp.int32(len(PLANS) - 1), jnp.bool_(False)
    for p in range(len(PLANS) - 1, -1, -1):
        here = jnp.logical_and(most <= PLANS[p][0], second <= PLANS[p][1])
        plan, fits = jnp.where(here, p, plan), jnp.logical_or(fits, here)
    out_ref[0] = jnp.where(fits, hot * len(PLANS) + plan, experts * len(PLANS))


def choose(chips):
    smem = pl.BlockSpec(memory_space=pltpu.SMEM)
    return pl.pallas_call(
        choose_kernel,
        in_specs=[pl.BlockSpec(memory_space=pltpu.VMEM)] * 4,
        out_specs=[smem] * 2,
        out_shape=[jax.ShapeDtypeStruct((1,), jnp.int32), jax.ShapeDtypeStruct((4, chips[0].shape[1]), jnp.int32)],
        scratch_shapes=[
            pltpu.SMEM((4,) + chips[0].shape, jnp.int32),
            pltpu.SMEM((16,), jnp.int32),
            pltpu.SemaphoreType.DMA((4,)),
        ],
    )(*chips)


def crossed(targets):
    return [(source * 2 + s, target * 2 + 1 - s) for source, target in enumerate(targets) for s in range(2)]


def by_halves(branches, index, operands):
    def run(low, high, operands):
        if high - low == 1:
            return branches[low](operands)
        middle = (low + high) // 2
        return lax.cond(
            index < middle, functools.partial(run, low, middle), functools.partial(run, middle, high), operands
        )

    return run(0, len(branches), operands)


def sizes_of(branch, units):
    if branch == 4 * len(PLANS):
        return [units] * 5
    hot, plan = divmod(branch, len(PLANS))
    most, second = PLANS[plan]
    return [most] + [most if hot in swap else second for swap in SWAPS]


def slot_layout(owner, experts, capacity):
    requests = owner.shape[0]
    indices = jnp.arange(requests, dtype=jnp.int32)
    earlier = indices[None, :] < indices[:, None]
    same_owner = owner[:, None] == owner[None, :]
    arrival_rank = jnp.sum(jnp.logical_and(same_owner, earlier), axis=1)
    target = owner * capacity + arrival_rank
    routing = target[None, :] == jnp.arange(experts * capacity, dtype=jnp.int32)[:, None]
    filled = jnp.any(routing, axis=1)
    source = jnp.sum(jnp.where(routing, indices[None, :], 0), axis=1)
    return (filled, source)


def pick_slots(values, filled, source):
    zero_value = jnp.zeros((), values.dtype)
    return jnp.where(filled[:, None, None], jnp.take(values, source, axis=0), zero_value)


def on_device(
    res_cache,
    res_scales,
    res_lengths,
    res_query,
    new_cache,
    new_scales,
    new_lengths,
    new_query,
    owner,
):
    experts = lax.axis_size("expert")
    sections = lax.axis_size("segment")
    requests, positions, columns = new_cache.shape
    capacity = max(2, 2 * requests // experts)
    swap = [(0, 1), (1, 0)]
    cache_t = jnp.transpose(new_cache, (0, 2, 1))
    res_inputs = (jnp.transpose(res_query, (0, 2, 1)), jnp.transpose(res_cache, (0, 2, 1)), res_scales, res_lengths)
    inputs = (res_inputs, (jnp.transpose(new_query, (0, 2, 1)), cache_t, new_scales, new_lengths))

    def attention(res_inputs, new_inputs):
        return attend(*res_inputs), attend(*new_inputs)

    if experts != 4 or sections != 2 or positions % UNIT or columns % 32:
        live_rows = jnp.arange(positions)[None, :] < new_lengths[:, None]
        zero_value = jnp.zeros((), jnp.bfloat16)
        filled, source = slot_layout(owner, experts, capacity)
        send_cache = pick_slots(jnp.where(live_rows[:, :, None], new_cache, zero_value), filled, source)
        send_scales = pick_slots(jnp.where(live_rows[:, None, :], new_scales, zero_value), filled, source)
        got_cache = lax.all_to_all(send_cache, "expert", split_axis=0, concat_axis=0, tiled=True)
        got_scales = lax.all_to_all(send_scales, "expert", split_axis=0, concat_axis=0, tiled=True)
        owned_cache, owned_scales = lax.ppermute((got_cache, got_scales), "segment", swap)
        return (*attention(*inputs), owned_cache, owned_scales)

    section = lax.axis_index("segment")
    units, half = capacity * positions // UNIT, columns // 2
    blocks = new_scales.shape[1]
    facts = owner * FACT + new_lengths
    sibling = lax.ppermute(facts, "segment", swap)
    chip = jnp.where(section == 0, jnp.stack([facts, sibling]), jnp.stack([sibling, facts]))
    chips = [chip] + [lax.ppermute(chip, "expert", [(e, (e + k) % 4) for e in range(4)]) for k in range(1, 4)]
    streams = pack(owner, new_lengths, new_scales, cache_t, sibling, units, capacity)
    branch, facts = choose(chips)

    def take(branch):
        def run(operands):
            streams, facts, *inputs = operands
            got = []
            for way, size in enumerate(sizes_of(branch, units)):
                part = streams[way][: capacity * blocks + size * half]
                got.append(lax.ppermute(part, ("expert", "segment"), crossed(targets_of(way))))
            return (*attention(*inputs), *unpack(facts, got, units, capacity, columns, positions, blocks))

        return run

    branches = [take(branch) for branch in range(4 * len(PLANS) + 1)]
    res_context, new_context, owned, owned_scales = by_halves(branches, branch[0], (streams, facts, *inputs))
    return (res_context, new_context, jnp.transpose(owned, (0, 2, 1)), owned_scales)


def solution(mesh):
    placed = (
        P(("group", "expert", "segment", "attn"), None, None),
        P(("group", "expert", "segment", "attn"), None, None),
        P(("group", "expert", "segment", "attn")),
        P(("group", "expert", "segment", "attn"), None, None),
        P(("group", "expert", "segment", "attn"), None, None),
        P(("group", "expert", "segment", "attn"), None, None),
        P(("group", "expert", "segment", "attn")),
        P(("group", "expert", "segment", "attn"), None, None),
        P(("group", "expert", "segment", "attn")),
    )
    return jax.shard_map(
        on_device,
        mesh=mesh,
        in_specs=placed,
        out_specs=(
            P(("group", "expert", "segment", "attn"), None, None),
            P(("group", "expert", "segment", "attn"), None, None),
            P(("group", "expert", "segment", "attn"), None, None),
            P(("group", "expert", "segment", "attn"), None, None),
        ),
        check_vma=False,
    )
```

```python
import functools
import jax
import jax.numpy as jnp
from jax import lax
from jax.experimental import pallas as pl
from jax.experimental.pallas import tpu as pltpu
from jax.sharding import PartitionSpec as P

LATENT = 512
BLOCK = 128
UNIT_BITS = 6
UNIT = 1 << UNIT_BITS
SPLIT = 6
CHUNK = 2
SWAPS = ((0, 2), (0, 3), (1, 2), (1, 3))
FACT_BITS = 8
FACT = 1 << FACT_BITS

softmax_scale = 192.0 ** (-0.5)
MIB = 1 << 20


def attend_kernel(lengths_ref, query_ref, cache_ref, scales_ref, out_ref, factors_ref):
    blocks = scales_ref.shape[1]
    positions = cache_ref.shape[2]
    contract_rows = (((0,), (0,)), ((), ()))
    contract_positions = (((1,), (1,)), ((), ()))
    length = lengths_ref[pl.program_id(0)]

    def block(b):
        return pl.ds(pl.multiple_of(b * BLOCK, BLOCK), BLOCK)

    for b in range(blocks):
        factors_ref[b] = scales_ref[0, b : b + 1, :].astype(jnp.float32)

    def add(b, scores):
        part = lax.dot_general(
            query_ref[0, block(b), :], cache_ref[0, block(b), :], contract_rows, preferred_element_type=jnp.float32
        )
        return scores + part * factors_ref[b]

    scores = lax.dot_general(
        query_ref[0, LATENT:, :], cache_ref[0, LATENT:, :], contract_rows, preferred_element_type=jnp.float32
    )
    scores = lax.fori_loop(0, blocks, add, scores)
    live = lax.broadcasted_iota(jnp.int32, (1, positions), 1) < length
    scores = jnp.where(live, scores * softmax_scale, -jnp.inf)
    exponent = jnp.exp(scores - jnp.max(scores, axis=-1, keepdims=True))
    probabilities = exponent * (1.0 / jnp.sum(exponent, axis=-1, keepdims=True))

    def put(b, _):
        out_ref[0, :, block(b)] = lax.dot_general(
            (probabilities * factors_ref[b]).astype(jnp.bfloat16),
            cache_ref[0, block(b), :],
            contract_positions,
            preferred_element_type=jnp.float32,
        ).astype(jnp.bfloat16)
        return 0

    lax.fori_loop(0, blocks, put, 0)


def attend(query, cache, scales, lengths):
    requests, columns, heads = query.shape
    positions = cache.shape[2]
    return pl.pallas_call(
        attend_kernel,
        grid=(requests,),
        in_specs=[
            pl.BlockSpec(memory_space=pltpu.SMEM),
            pl.BlockSpec((1, columns, heads), lambda i: (i, 0, 0)),
            pl.BlockSpec((1, columns, positions), lambda i: (i, 0, 0)),
            pl.BlockSpec((1, scales.shape[1], positions), lambda i: (i, 0, 0)),
        ],
        out_specs=pl.BlockSpec((1, heads, LATENT), lambda i: (i, 0, 0)),
        out_shape=jax.ShapeDtypeStruct((requests, heads, LATENT), jnp.bfloat16),
        scratch_shapes=[pltpu.VMEM((scales.shape[1], 1, positions), jnp.float32)],
        compiler_params=pltpu.CompilerParams(vmem_limit_bytes=16 * MIB),
        cost_estimate=pl.CostEstimate(
            flops=4 * requests * heads * positions * columns,
            bytes_accessed=2 * requests * (heads * (columns + LATENT) + positions * columns),
            transcendentals=requests * heads * positions,
        ),
    )(lengths, query, cache, scales)


def stream_gap(rows, positions, first, units):
    window = units * 2 * UNIT
    shape = (window, 2 * positions) if rows == "window" else (2 * positions, window)
    down, across = lax.broadcasted_iota(jnp.int32, shape, 0), lax.broadcasted_iota(jnp.int32, shape, 1)
    lane, own = (down, across) if rows == "window" else (across, down)
    within = lane % (2 * UNIT)
    place = (lane // (2 * UNIT) + first) * UNIT + within % UNIT
    meet = within // UNIT == own // positions
    side = (1, 2 * positions) if rows == "window" else (2 * positions, 1)
    position = lax.broadcasted_iota(jnp.int32, side, 1 if rows == "window" else 0) % positions
    return jnp.where(meet, place - own % positions, -512).astype(jnp.bfloat16), position


def moving(gap, position, shift, length):
    wanted = jnp.where(position < length, shift, 512).astype(jnp.bfloat16)
    return jnp.where(gap == wanted, jnp.ones((), jnp.bfloat16), jnp.zeros((), jnp.bfloat16))


def targets_of(way):
    if way == 0:
        return [e ^ 1 for e in range(4)]
    a, b = SWAPS[way - 1]
    return [b if e == a else a if e == b else e for e in range(4)]


def staying(e):
    return [way for way in range(5) if targets_of(way)[e] == e]


def pick(index, values):
    value = jnp.int32(values[0])
    for at in range(1, len(values)):
        value = jnp.where(index == at, values[at], value)
    return value


def pack_kernel(owner_ref, lengths_ref, scales_ref, cache_ref, after_ref, *refs):
    outs, (held, acc, slots, ends, ranks, in_sem, out_sem) = refs[:5], refs[5:]
    experts = 4
    requests, columns, positions = cache_ref.shape
    blocks = scales_ref.shape[1]
    half = columns // 2
    tail = slots.shape[1]
    window = positions // UNIT + 1
    me = lax.axis_index("expert")
    parts = in_sem.shape[0]
    share = requests // parts

    def rows_of(unit):
        return pl.ds(pl.multiple_of(tail + unit * half, 16), half)

    def fetch(part):
        here = pl.ds(part * share, share)
        return pltpu.make_async_copy(cache_ref.at[here], held.at[here], in_sem.at[part])

    for part in range(parts):
        fetch(part).start()
    gap, position = stream_gap("request", positions, 0, window)
    for k in range(experts):
        ends[k] = 0
        ranks[k] = 0
        acc[k, rows_of(0), :] = jnp.zeros((half, 2 * UNIT), jnp.bfloat16)
    slots[...] = jnp.zeros(slots.shape, jnp.float32)
    live = lax.broadcasted_iota(jnp.int32, (blocks, positions), 1)

    def place(i, _):
        k = owner_ref[i]
        length = lengths_ref[i]
        start, rank = ends[k], ranks[k]
        ends[k] = start + length
        ranks[k] = rank + 1
        slots[k, pl.ds(rank * blocks, blocks), :] = jnp.where(live < length, scales_ref[i].astype(jnp.float32), 0.0)
        unit, shift = start >> UNIT_BITS, start & (UNIT - 1)
        move = moving(gap, position, shift, length)
        both = jnp.concatenate([held[i, :half, :], held[i, half:, :]], axis=1)
        moved = jnp.dot(both, move, preferred_element_type=jnp.float32).astype(jnp.bfloat16)
        acc[k, rows_of(unit), :] += moved[:, : 2 * UNIT]
        for j in range(1, window):
            acc[k, rows_of(unit + j), :] = moved[:, 2 * UNIT * j : 2 * UNIT * (j + 1)]
        return 0

    for part in range(parts):
        fetch(part).wait()
        lax.fori_loop(part * share, (part + 1) * share, place, 0, unroll=True)
    acc[:, :tail, :] = slots[...].astype(jnp.bfloat16)
    copies = []
    for way, out in enumerate(outs):
        k = pick(me, targets_of(way))
        skipped = pick(me, [SPLIT if way == staying(e)[1] else 0 for e in range(experts)])
        near = 8
        further = ends[k] > (near + skipped) * UNIT
        for rows, low, needed in ((tail + near * half, 0, True), (out.shape[0] - tail - near * half, tail + near * half, further)):
            here = pl.ds(pl.multiple_of(low + skipped * half, 16), rows)
            copy = pltpu.make_async_copy(acc.at[k, here], out.at[pl.ds(low, rows)], out_sem.at[way, int(low > 0)])
            copies.append((copy, needed))
    for act in (lambda copy: copy.start(), lambda copy: copy.wait()):
        for copy, needed in copies:
            if needed is True:
                act(copy)
            else:
                pl.when(needed)(functools.partial(act, copy))


def pack(owner, lengths, scales, cache, after, units, capacity):
    requests, columns, positions = cache.shape
    half = columns // 2
    window = positions // UNIT + 1
    tail = capacity * scales.shape[1]
    smem = pl.BlockSpec(memory_space=pltpu.SMEM)
    vmem = pl.BlockSpec(memory_space=pltpu.VMEM)
    hbm = pl.BlockSpec(memory_space=pl.ANY)
    lanes = 2 * UNIT
    return pl.pallas_call(
        pack_kernel,
        in_specs=[smem, smem, vmem, hbm, hbm],
        out_specs=[hbm] * 5,
        out_shape=[jax.ShapeDtypeStruct((tail + (units + CHUNK) * half, lanes), jnp.bfloat16)] * 5,
        scratch_shapes=[
            pltpu.VMEM(cache.shape, jnp.bfloat16),
            pltpu.VMEM((4, tail + (units + CHUNK + SPLIT) * half, lanes), jnp.bfloat16),
            pltpu.VMEM((4, tail, positions), jnp.float32),
            pltpu.SMEM((4,), jnp.int32),
            pltpu.SMEM((4,), jnp.int32),
            pltpu.SemaphoreType.DMA((4,)),
            pltpu.SemaphoreType.DMA((5, 2)),
        ],
        compiler_params=pltpu.CompilerParams(vmem_limit_bytes=24 * MIB),
        cost_estimate=pl.CostEstimate(flops=2 * requests * half * 256 * 384, bytes_accessed=8 * MIB, transcendentals=0),
    )(owner, lengths, scales, cache, after)


def unpack_kernel(facts_ref, g0, g1, g2, g3, g4, x0, x1, x2, x3, x4, out_ref, scales_ref, *scratch):
    held, stage, tails, starts, counts, sem, out_sem = scratch
    got, steps = (g0, g1, g2, g3, g4), (x0, x1, x2, x3, x4)
    experts = 4
    requests = facts_ref.shape[1]
    capacity = out_ref.shape[0] // experts
    columns, positions = out_ref.shape[1], out_ref.shape[2]
    blocks = scales_ref.shape[1]
    half = columns // 2
    tail = capacity * blocks
    window = positions // UNIT
    me = lax.axis_index("expert")

    def rows_of(unit):
        return pl.ds(pl.multiple_of(unit * half, 16), half)

    def units_of(unit):
        return pl.ds(pl.multiple_of(tail + unit * half, 16), half)

    def source_of(k):
        return (me - k) & (experts - 1)

    def scan(k, _):
        def note(i, carry):
            rank, end = carry
            mine = facts_ref[k, i] >> FACT_BITS == me
            length = facts_ref[k, i] & (FACT - 1)

            @pl.when(mine)
            def _():
                starts[k, rank] = end
                counts[k, rank] = length

            return (jnp.where(mine, rank + 1, rank), jnp.where(mine, end + length, end))

        rank, end = lax.fori_loop(0, requests, note, (0, 0))
        starts[k, capacity] = rank
        counts[k, capacity] = (end + UNIT - 1) >> UNIT_BITS
        return 0

    lax.fori_loop(0, experts, scan, 0)

    def fetch_stream(k, _):
        used = counts[k, capacity]
        for way in range(5):
            came = pick(source_of(k), targets_of(way)) == me
            later = jnp.logical_and(k == 0, pick(me, [int(way == staying(e)[1]) for e in range(experts)]) == 1)
            low = jnp.where(later, SPLIT, 0)
            high = jnp.where(jnp.logical_and(k == 0, jnp.logical_not(later)), jnp.minimum(used, SPLIT), used)

            @pl.when(came)
            def _():
                base = (got[way].shape[0] - tail) // half

                @pl.when(jnp.logical_not(later))
                def _():
                    tails[k] = got[way][:tail, :].astype(jnp.float32)

                def move_unit(u, _):
                    held[k, rows_of(u), :] = got[way][units_of(u - low), :]
                    return 0

                lax.fori_loop(low, jnp.minimum(high, low + base), move_unit, 0)

                def fetch_unit(u, _):
                    source = steps[way].at[rows_of(u - low - base)]
                    copy = pltpu.make_async_copy(source, held.at[k, rows_of(u)], sem)
                    copy.start()
                    copy.wait()
                    return 0

                lax.fori_loop(low + base, high, fetch_unit, 0)

        return 0

    lax.fori_loop(0, experts, fetch_stream, 0)
    gap, position = stream_gap("window", positions, 0, window)
    gap_behind, _ = stream_gap("window", positions, window, 1)

    def write(k):
        there = out_ref.at[pl.ds(source_of(k) * capacity, capacity)]
        return pltpu.make_async_copy(stage.at[k], there, out_sem.at[k])

    def put_stream(k, _):
        used, ranks = counts[k, capacity], starts[k, capacity]

        for j in range(window):
            held[k, rows_of(used + j), :] = jnp.zeros((half, 2 * UNIT), jnp.bfloat16)

        def put(pair, _):
            behind = []
            for rank in (2 * pair, 2 * pair + 1):
                filled = rank < ranks
                start, length = jnp.where(filled, starts[k, rank], 0), jnp.where(filled, counts[k, rank], 0)
                unit, shift = start >> UNIT_BITS, start & (UNIT - 1)
                move = moving(gap, position, shift, length)
                seen = jnp.concatenate([held[k, rows_of(unit + j), :] for j in range(window)], axis=1)
                moved = jnp.dot(seen, move, preferred_element_type=jnp.float32).astype(jnp.bfloat16)
                stage[k, rank, :half, :] = moved[:, :positions]
                stage[k, rank, half:, :] = moved[:, positions:]
                behind.append((rank, unit, shift, length))
            for rank, unit, shift, length in behind:

                @pl.when(shift + length > window * UNIT)
                def _():
                    move = moving(gap_behind, position, shift, length)
                    seen = held[k, rows_of(unit + window), :]
                    moved = jnp.dot(seen, move, preferred_element_type=jnp.float32).astype(jnp.bfloat16)
                    stage[k, rank, :half, :] += moved[:, :positions]
                    stage[k, rank, half:, :] += moved[:, positions:]

            return 0

        def clear(pair, _):
            stage[k, pl.ds(2 * pair, 2)] = jnp.zeros((2, columns, positions), jnp.bfloat16)
            return 0

        pairs = (ranks + 1) >> 1
        lax.fori_loop(0, pairs, put, 0)
        lax.fori_loop(pairs, capacity // 2, clear, 0)
        write(k).start()
        for rank in range(capacity):
            scales = tails[k, rank * blocks : (rank + 1) * blocks, :]
            scales_ref[source_of(k) * capacity + rank] = scales.astype(jnp.bfloat16)
        return 0

    lax.fori_loop(0, experts, put_stream, 0)
    for k in range(experts):
        write(k).wait()


def unpack(facts, got, steps, units, capacity, columns, positions, blocks):
    half = columns // 2
    window = positions // UNIT + 1
    smem = pl.BlockSpec(memory_space=pltpu.SMEM)
    vmem = pl.BlockSpec(memory_space=pltpu.VMEM)
    hbm = pl.BlockSpec(memory_space=pl.ANY)
    return pl.pallas_call(
        unpack_kernel,
        in_specs=[smem] + [vmem] * 5 + [hbm] * 5,
        out_specs=[hbm, vmem],
        out_shape=[
            jax.ShapeDtypeStruct((4 * capacity, columns, positions), jnp.bfloat16),
            jax.ShapeDtypeStruct((4 * capacity, blocks, positions), jnp.bfloat16),
        ],
        scratch_shapes=[
            pltpu.VMEM((4, (units + window) * half, 2 * UNIT), jnp.bfloat16),
            pltpu.VMEM((4, capacity, columns, positions), jnp.bfloat16),
            pltpu.VMEM((4, capacity * blocks, positions), jnp.float32),
            pltpu.SMEM((4, capacity + 1), jnp.int32),
            pltpu.SMEM((4, capacity + 1), jnp.int32),
            pltpu.SemaphoreType.DMA,
            pltpu.SemaphoreType.DMA((4,)),
        ],
        compiler_params=pltpu.CompilerParams(vmem_limit_bytes=24 * MIB),
        cost_estimate=pl.CostEstimate(flops=2 * 32 * half * 256 * 384, bytes_accessed=10 * MIB, transcendentals=0),
    )(facts, *got, *steps)


def choose_kernel(c0, c1, c2, c3, out_ref, facts_ref, loads_ref):
    experts = 4
    requests = c0.shape[1]
    me, other = lax.axis_index("expert"), 1 - lax.axis_index("segment")
    for k, chip in enumerate((c0, c1, c2, c3)):
        most = [jnp.int32(0)] * experts
        for section in range(2):

            def add(i, sums):
                fact = chip[section, i]
                owner, length = fact >> FACT_BITS, fact & (FACT - 1)
                part = length << ((owner >> 1) << 4)
                odd = (owner & 1) == 1
                return (sums[0] + jnp.where(odd, 0, part), sums[1] + jnp.where(odd, part, 0))

            even, odd = lax.fori_loop(0, requests, add, (jnp.int32(0), jnp.int32(0)), unroll=8)
            for o, sums in enumerate((even, odd, even >> 16, odd >> 16)):
                most[o] = jnp.maximum(most[o], ((sums & 0xFFFF) + UNIT - 1) >> UNIT_BITS)
        for o in range(experts):
            loads_ref[((me - k) & (experts - 1)) * experts + o] = most[o]

        def keep(i, _):
            facts_ref[k, i] = chip[other, i]
            return 0

        lax.fori_loop(0, requests, keep, 0, unroll=8)
    load = [[loads_ref[source * experts + o] for o in range(experts)] for source in range(experts)]
    hot, highest = jnp.int32(0), jnp.int32(-1)
    for o in range(experts):
        worst = functools.reduce(jnp.maximum, [load[source][o] for source in range(experts) if source != o])
        hot = jnp.where(worst > highest, o, hot)
        highest = jnp.maximum(worst, highest)
    out_ref[0] = hot
    for way in range(5):
        need = jnp.int32(0)
        for source, target in enumerate(targets_of(way)):
            if source != target:
                need = jnp.maximum(need, load[source][target])
            elif way == staying(source)[0]:
                need = jnp.maximum(need, jnp.minimum(load[source][source], SPLIT))
            else:
                need = jnp.maximum(need, load[source][source] - SPLIT)
        out_ref[1 + way] = need


def choose(chips):
    smem = pl.BlockSpec(memory_space=pltpu.SMEM)
    return pl.pallas_call(
        choose_kernel,
        in_specs=[smem] * 4,
        out_specs=[smem] * 2,
        out_shape=[jax.ShapeDtypeStruct((6,), jnp.int32), jax.ShapeDtypeStruct((4, chips[0].shape[1]), jnp.int32)],
        scratch_shapes=[pltpu.SMEM((16,), jnp.int32)],
    )(*chips)


def crossed(targets):
    return [(source * 2 + s, target * 2 + 1 - s) for source, target in enumerate(targets) for s in range(2)]


def by_halves(branches, index, operands):
    def run(low, high, operands):
        if high - low == 1:
            return branches[low](operands)
        middle = (low + high) // 2
        return lax.cond(
            index < middle, functools.partial(run, low, middle), functools.partial(run, middle, high), operands
        )

    return run(0, len(branches), operands)


def base_sizes(hot):
    return [14 if hot in (1, 2) else 12] + [10 if hot in swap else 6 for swap in SWAPS]


def blank(shapes):
    hbm = pl.BlockSpec(memory_space=pl.ANY)
    return pl.pallas_call(
        lambda *refs: None,
        out_specs=[hbm] * len(shapes),
        out_shape=[jax.ShapeDtypeStruct(shape, jnp.bfloat16) for shape in shapes],
    )()


def send_steps(stream, way, base, need, room, tail, half):
    rows = CHUNK * half

    def step(carry):
        at, room = carry
        part = lax.dynamic_slice_in_dim(stream, tail + base * half + at * rows, rows)
        part = lax.ppermute(part, ("expert", "segment"), crossed(targets_of(way)))
        return at + 1, lax.dynamic_update_slice_in_dim(room, part, at * rows, 0)

    return lax.while_loop(lambda carry: carry[0] * CHUNK + base < need, step, (jnp.int32(0), room))[1]


def slot_layout(owner, experts, capacity):
    requests = owner.shape[0]
    indices = jnp.arange(requests, dtype=jnp.int32)
    earlier = indices[None, :] < indices[:, None]
    same_owner = owner[:, None] == owner[None, :]
    arrival_rank = jnp.sum(jnp.logical_and(same_owner, earlier), axis=1)
    target = owner * capacity + arrival_rank
    routing = target[None, :] == jnp.arange(experts * capacity, dtype=jnp.int32)[:, None]
    filled = jnp.any(routing, axis=1)
    source = jnp.sum(jnp.where(routing, indices[None, :], 0), axis=1)
    return (filled, source)


def pick_slots(values, filled, source):
    zero_value = jnp.zeros((), values.dtype)
    return jnp.where(filled[:, None, None], jnp.take(values, source, axis=0), zero_value)


def on_device(
    res_cache,
    res_scales,
    res_lengths,
    res_query,
    new_cache,
    new_scales,
    new_lengths,
    new_query,
    owner,
):
    experts = lax.axis_size("expert")
    sections = lax.axis_size("segment")
    requests, positions, columns = new_cache.shape
    capacity = max(2, 2 * requests // experts)
    swap = [(0, 1), (1, 0)]
    cache_t = jnp.transpose(new_cache, (0, 2, 1))
    res_inputs = (jnp.transpose(res_query, (0, 2, 1)), jnp.transpose(res_cache, (0, 2, 1)), res_scales, res_lengths)
    inputs = (res_inputs, (jnp.transpose(new_query, (0, 2, 1)), cache_t, new_scales, new_lengths))

    def attention(res_inputs, new_inputs):
        return attend(*res_inputs), attend(*new_inputs)

    if experts != 4 or sections != 2 or positions % UNIT or columns % 32:
        live_rows = jnp.arange(positions)[None, :] < new_lengths[:, None]
        zero_value = jnp.zeros((), jnp.bfloat16)
        filled, source = slot_layout(owner, experts, capacity)
        send_cache = pick_slots(jnp.where(live_rows[:, :, None], new_cache, zero_value), filled, source)
        send_scales = pick_slots(jnp.where(live_rows[:, None, :], new_scales, zero_value), filled, source)
        got_cache = lax.all_to_all(send_cache, "expert", split_axis=0, concat_axis=0, tiled=True)
        got_scales = lax.all_to_all(send_scales, "expert", split_axis=0, concat_axis=0, tiled=True)
        owned_cache, owned_scales = lax.ppermute((got_cache, got_scales), "segment", swap)
        return (*attention(*inputs), owned_cache, owned_scales)

    section = lax.axis_index("segment")
    units, half = capacity * positions // UNIT, columns // 2
    blocks = new_scales.shape[1]
    facts = owner * FACT + new_lengths
    sibling = lax.ppermute(facts, "segment", swap)
    chip = jnp.where(section == 0, jnp.stack([facts, sibling]), jnp.stack([sibling, facts]))
    chips = [chip] + [lax.ppermute(chip, "expert", [(e, (e + k) % 4) for e in range(4)]) for k in range(1, 4)]
    streams = pack(owner, new_lengths, new_scales, cache_t, sibling, units, capacity)
    needs, facts = choose(chips)
    tail = capacity * blocks

    def take(hot):
        def run(operands):
            streams, needs, facts, *inputs = operands
            sizes = base_sizes(hot)
            got = []
            for way, size in enumerate(sizes):
                part = streams[way][: tail + size * half]
                got.append(lax.ppermute(part, ("expert", "segment"), crossed(targets_of(way))))
            rooms = blank([(-(-(units - size) // CHUNK) * CHUNK * half, 2 * UNIT) for size in sizes])
            steps = [
                send_steps(streams[way], way, size, needs[1 + way], rooms[way], tail, half)
                for way, size in enumerate(sizes)
            ]
            return (*attention(*inputs), *unpack(facts, got, steps, units, capacity, columns, positions, blocks))

        return run

    operands = (streams, needs, facts, *inputs)
    res_context, new_context, owned, owned_scales = by_halves([take(hot) for hot in range(4)], needs[0], operands)
    return (res_context, new_context, jnp.transpose(owned, (0, 2, 1)), owned_scales)


def solution(mesh):
    placed = (
        P(("group", "expert", "segment", "attn"), None, None),
        P(("group", "expert", "segment", "attn"), None, None),
        P(("group", "expert", "segment", "attn")),
        P(("group", "expert", "segment", "attn"), None, None),
        P(("group", "expert", "segment", "attn"), None, None),
        P(("group", "expert", "segment", "attn"), None, None),
        P(("group", "expert", "segment", "attn")),
        P(("group", "expert", "segment", "attn"), None, None),
        P(("group", "expert", "segment", "attn")),
    )
    return jax.shard_map(
        on_device,
        mesh=mesh,
        in_specs=placed,
        out_specs=(
            P(("group", "expert", "segment", "attn"), None, None),
            P(("group", "expert", "segment", "attn"), None, None),
            P(("group", "expert", "segment", "attn"), None, None),
            P(("group", "expert", "segment", "attn"), None, None),
        ),
        check_vma=False,
    )
```

```python
import functools
import jax
import jax.numpy as jnp
from jax import lax
from jax.experimental import pallas as pl
from jax.experimental.pallas import tpu as pltpu
from jax.sharding import PartitionSpec as P

LATENT = 512
BLOCK = 128
UNIT_BITS = 6
UNIT = 1 << UNIT_BITS
SPLIT = 6
LONG, SHORT, PAIRED = 10, 6, 12
CHUNK = 2
SWAPS = ((0, 2), (0, 3), (1, 2), (1, 3))
FACT_BITS = 8
FACT = 1 << FACT_BITS

softmax_scale = 192.0 ** (-0.5)
MIB = 1 << 20


def attend_kernel(lengths_ref, query_ref, cache_ref, scales_ref, out_ref):
    per_step, _, positions = cache_ref.shape
    blocks = LATENT // BLOCK
    contract_rows = (((0,), (0,)), ((), ()))
    contract_positions = (((1,), (1,)), ((), ()))
    for r in range(per_step):
        length = lengths_ref[pl.program_id(0) * per_step + r]
        factors = scales_ref[r].astype(jnp.float32)
        scores = lax.dot_general(
            query_ref[r, LATENT:, :], cache_ref[r, LATENT:, :], contract_rows, preferred_element_type=jnp.float32
        )
        for b in range(blocks):
            part = lax.dot_general(
                query_ref[r, b * BLOCK : (b + 1) * BLOCK, :],
                cache_ref[r, b * BLOCK : (b + 1) * BLOCK, :],
                contract_rows,
                preferred_element_type=jnp.float32,
            )
            scores = scores + part * factors[b : b + 1, :]
        live = lax.broadcasted_iota(jnp.int32, (1, positions), 1) < length
        scores = jnp.where(live, scores * softmax_scale, -jnp.inf)
        exponent = jnp.exp(scores - jnp.max(scores, axis=-1, keepdims=True))
        probabilities = exponent * (1.0 / jnp.sum(exponent, axis=-1, keepdims=True))
        for b in range(blocks):
            weights = (probabilities * factors[b : b + 1, :]).astype(jnp.bfloat16)
            out_ref[r, :, b * BLOCK : (b + 1) * BLOCK] = lax.dot_general(
                weights,
                cache_ref[r, b * BLOCK : (b + 1) * BLOCK, :],
                contract_positions,
                preferred_element_type=jnp.float32,
            ).astype(jnp.bfloat16)


def attend(query, cache, scales, lengths, per_step):
    requests, columns, heads = query.shape
    positions = cache.shape[2]
    return pl.pallas_call(
        attend_kernel,
        grid=(requests // per_step,),
        in_specs=[
            pl.BlockSpec(memory_space=pltpu.SMEM),
            pl.BlockSpec((per_step, columns, heads), lambda i: (i, 0, 0)),
            pl.BlockSpec((per_step, columns, positions), lambda i: (i, 0, 0)),
            pl.BlockSpec((per_step, scales.shape[1], positions), lambda i: (i, 0, 0)),
        ],
        out_specs=pl.BlockSpec((per_step, heads, LATENT), lambda i: (i, 0, 0)),
        out_shape=jax.ShapeDtypeStruct((requests, heads, LATENT), jnp.bfloat16),
        compiler_params=pltpu.CompilerParams(vmem_limit_bytes=16 * MIB),
        cost_estimate=pl.CostEstimate(
            flops=4 * requests * heads * positions * columns,
            bytes_accessed=2 * requests * (heads * (columns + LATENT) + positions * columns),
            transcendentals=requests * heads * positions,
        ),
    )(lengths, query, cache, scales)


def stream_gap(rows, positions, first, units):
    window = units * 2 * UNIT
    shape = (window, 2 * positions) if rows == "window" else (2 * positions, window)
    down, across = lax.broadcasted_iota(jnp.int32, shape, 0), lax.broadcasted_iota(jnp.int32, shape, 1)
    lane, own = (down, across) if rows == "window" else (across, down)
    within = lane % (2 * UNIT)
    place = (lane // (2 * UNIT) + first) * UNIT + within % UNIT
    meet = within // UNIT == own // positions
    side = (1, 2 * positions) if rows == "window" else (2 * positions, 1)
    position = lax.broadcasted_iota(jnp.int32, side, 1 if rows == "window" else 0) % positions
    return jnp.where(meet, place - own % positions, -512).astype(jnp.bfloat16), position


def moving(gap, position, shift, length):
    wanted = jnp.where(position < length, shift, 512).astype(jnp.bfloat16)
    return jnp.where(gap == wanted, jnp.ones((), jnp.bfloat16), jnp.zeros((), jnp.bfloat16))


def targets_of(way):
    if way == 0:
        return [e ^ 1 for e in range(4)]
    a, b = SWAPS[way - 1]
    return [b if e == a else a if e == b else e for e in range(4)]


def staying(e):
    return [way for way in range(5) if targets_of(way)[e] == e]


def pick(index, values):
    value = jnp.int32(values[0])
    for at in range(1, len(values)):
        value = jnp.where(index == at, values[at], value)
    return value


def pack_kernel(owner_ref, lengths_ref, scales_ref, cache_ref, after_ref, *refs):
    outs, (held, acc, slots, ends, ranks, in_sem, out_sem) = refs[:-7], refs[-7:]
    experts = 4
    requests, columns, positions = cache_ref.shape
    blocks = scales_ref.shape[1]
    half = columns // 2
    tail = slots.shape[1]
    window = positions // UNIT + 1
    me = lax.axis_index("expert")
    parts = in_sem.shape[0]
    share = requests // parts

    def rows_of(unit):
        return pl.ds(pl.multiple_of(tail + unit * half, 16), half)

    def fetch(part):
        here = pl.ds(part * share, share)
        return pltpu.make_async_copy(cache_ref.at[here], held.at[here], in_sem.at[part])

    for part in range(parts):
        fetch(part).start()
    gap, position = stream_gap("request", positions, 0, window)
    for k in range(experts):
        ends[k] = 0
        ranks[k] = 0
        acc[k, rows_of(0), :] = jnp.zeros((half, 2 * UNIT), jnp.bfloat16)
    slots[...] = jnp.zeros(slots.shape, jnp.float32)
    live = lax.broadcasted_iota(jnp.int32, (blocks, positions), 1)

    def place(i, _):
        k = owner_ref[i]
        length = lengths_ref[i]
        start, rank = ends[k], ranks[k]
        ends[k] = start + length
        ranks[k] = rank + 1
        slots[k, pl.ds(rank * blocks, blocks), :] = jnp.where(live < length, scales_ref[i].astype(jnp.float32), 0.0)
        unit, shift = start >> UNIT_BITS, start & (UNIT - 1)
        move = moving(gap, position, shift, length)
        both = jnp.concatenate([held[i, :half, :], held[i, half:, :]], axis=1)
        moved = jnp.dot(both, move, preferred_element_type=jnp.float32).astype(jnp.bfloat16)
        acc[k, rows_of(unit), :] += moved[:, : 2 * UNIT]
        for j in range(1, window):
            acc[k, rows_of(unit + j), :] = moved[:, 2 * UNIT * j : 2 * UNIT * (j + 1)]
        return 0

    for part in range(parts):
        fetch(part).wait()
        lax.fori_loop(part * share, (part + 1) * share, place, 0, unroll=True)
    acc[:, :tail, :] = slots[...].astype(jnp.bfloat16)
    copies = []
    for at, (way, low, high) in enumerate(stream_parts(acc.shape[1] // half - SPLIT)):
        k = pick(me, targets_of(way))
        skipped = pick(me, [SPLIT if way == staying(e)[1] else 0 for e in range(experts)])
        here = pl.ds(pl.multiple_of((tail + low * half if low else 0) + skipped * half, 16), outs[at].shape[0])
        needed = True if low == 0 else ends[k] > (low + skipped) * UNIT
        copies.append((pltpu.make_async_copy(acc.at[k, here], outs[at], out_sem.at[at]), needed))
    for act in (lambda copy: copy.start(), lambda copy: copy.wait()):
        for copy, needed in copies:
            if needed is True:
                act(copy)
            else:
                pl.when(needed)(functools.partial(act, copy))


def stream_parts(units):
    parts = [(0, 0, PAIRED), (0, PAIRED, units)]
    for way in range(1, 5):
        parts += [(way, 0, LONG), (way, 0, SHORT), (way, SHORT, units)]
    return parts


def pack(owner, lengths, scales, cache, after, units, capacity):
    requests, columns, positions = cache.shape
    half = columns // 2
    window = positions // UNIT + 1
    tail = capacity * scales.shape[1]
    parts = stream_parts(units + CHUNK)
    smem = pl.BlockSpec(memory_space=pltpu.SMEM)
    vmem = pl.BlockSpec(memory_space=pltpu.VMEM)
    hbm = pl.BlockSpec(memory_space=pl.ANY)
    lanes = 2 * UNIT
    return pl.pallas_call(
        pack_kernel,
        in_specs=[smem, smem, vmem, hbm, hbm],
        out_specs=[hbm] * len(parts),
        out_shape=[
            jax.ShapeDtypeStruct(((0 if low else tail) + (high - low) * half, lanes), jnp.bfloat16)
            for _, low, high in parts
        ],
        scratch_shapes=[
            pltpu.VMEM(cache.shape, jnp.bfloat16),
            pltpu.VMEM((4, tail + (units + CHUNK + SPLIT) * half, lanes), jnp.bfloat16),
            pltpu.VMEM((4, tail, positions), jnp.float32),
            pltpu.SMEM((4,), jnp.int32),
            pltpu.SMEM((4,), jnp.int32),
            pltpu.SemaphoreType.DMA((4,)),
            pltpu.SemaphoreType.DMA((len(parts),)),
        ],
        compiler_params=pltpu.CompilerParams(vmem_limit_bytes=24 * MIB),
        cost_estimate=pl.CostEstimate(flops=2 * requests * half * 256 * 384, bytes_accessed=8 * MIB, transcendentals=0),
    )(owner, lengths, scales, cache, after)


def unpack_kernel(facts_ref, g0, g1, g2, g3, g4, x0, x1, x2, x3, x4, out_ref, scales_ref, *scratch):
    held, stage, tails, starts, counts, sem, out_sem = scratch
    got, steps = (g0, g1, g2, g3, g4), (x0, x1, x2, x3, x4)
    experts = 4
    requests = facts_ref.shape[1]
    capacity = out_ref.shape[0] // experts
    columns, positions = out_ref.shape[1], out_ref.shape[2]
    blocks = scales_ref.shape[1]
    half = columns // 2
    tail = capacity * blocks
    window = positions // UNIT
    me = lax.axis_index("expert")

    def rows_of(unit):
        return pl.ds(pl.multiple_of(unit * half, 16), half)

    def units_of(unit):
        return pl.ds(pl.multiple_of(tail + unit * half, 16), half)

    def source_of(k):
        return (me - k) & (experts - 1)

    def scan(k, _):
        def note(i, carry):
            rank, end = carry
            mine = facts_ref[k, i] >> FACT_BITS == me
            length = facts_ref[k, i] & (FACT - 1)

            @pl.when(mine)
            def _():
                starts[k, rank] = end
                counts[k, rank] = length

            return (jnp.where(mine, rank + 1, rank), jnp.where(mine, end + length, end))

        rank, end = lax.fori_loop(0, requests, note, (0, 0))
        starts[k, capacity] = rank
        counts[k, capacity] = (end + UNIT - 1) >> UNIT_BITS
        return 0

    lax.fori_loop(0, experts, scan, 0)

    def fetch_stream(k, _):
        used = counts[k, capacity]
        for way in range(5):
            came = pick(source_of(k), targets_of(way)) == me
            later = jnp.logical_and(k == 0, pick(me, [int(way == staying(e)[1]) for e in range(experts)]) == 1)
            low = jnp.where(later, SPLIT, 0)
            high = jnp.where(jnp.logical_and(k == 0, jnp.logical_not(later)), jnp.minimum(used, SPLIT), used)

            @pl.when(came)
            def _():
                base = (got[way].shape[0] - tail) // half

                @pl.when(jnp.logical_not(later))
                def _():
                    tails[k] = got[way][:tail, :].astype(jnp.float32)

                def move_unit(u, _):
                    held[k, rows_of(u), :] = got[way][units_of(u - low), :]
                    return 0

                lax.fori_loop(low, jnp.minimum(high, low + base), move_unit, 0)

                def fetch_unit(u, _):
                    source = steps[way].at[rows_of(u - low - base)]
                    copy = pltpu.make_async_copy(source, held.at[k, rows_of(u)], sem)
                    copy.start()
                    copy.wait()
                    return 0

                lax.fori_loop(low + base, high, fetch_unit, 0)

        return 0

    lax.fori_loop(0, experts, fetch_stream, 0)
    gap, position = stream_gap("window", positions, 0, window)
    gap_behind, _ = stream_gap("window", positions, window, 1)

    def write(k):
        there = out_ref.at[pl.ds(source_of(k) * capacity, capacity)]
        return pltpu.make_async_copy(stage.at[k], there, out_sem.at[k])

    def put_stream(k, _):
        used, ranks = counts[k, capacity], starts[k, capacity]

        for j in range(window):
            held[k, rows_of(used + j), :] = jnp.zeros((half, 2 * UNIT), jnp.bfloat16)

        def put(pair, _):
            behind = []
            for rank in (2 * pair, 2 * pair + 1):
                filled = rank < ranks
                start, length = jnp.where(filled, starts[k, rank], 0), jnp.where(filled, counts[k, rank], 0)
                unit, shift = start >> UNIT_BITS, start & (UNIT - 1)
                move = moving(gap, position, shift, length)
                seen = jnp.concatenate([held[k, rows_of(unit + j), :] for j in range(window)], axis=1)
                moved = jnp.dot(seen, move, preferred_element_type=jnp.float32).astype(jnp.bfloat16)
                stage[k, rank, :half, :] = moved[:, :positions]
                stage[k, rank, half:, :] = moved[:, positions:]
                behind.append((rank, unit, shift, length))
            for rank, unit, shift, length in behind:

                @pl.when(shift + length > window * UNIT)
                def _():
                    move = moving(gap_behind, position, shift, length)
                    seen = held[k, rows_of(unit + window), :]
                    moved = jnp.dot(seen, move, preferred_element_type=jnp.float32).astype(jnp.bfloat16)
                    stage[k, rank, :half, :] += moved[:, :positions]
                    stage[k, rank, half:, :] += moved[:, positions:]

            return 0

        def clear(pair, _):
            stage[k, pl.ds(2 * pair, 2)] = jnp.zeros((2, columns, positions), jnp.bfloat16)
            return 0

        pairs = (ranks + 1) >> 1
        lax.fori_loop(0, pairs, put, 0)
        lax.fori_loop(pairs, capacity // 2, clear, 0)
        write(k).start()
        for rank in range(capacity):
            scales = tails[k, rank * blocks : (rank + 1) * blocks, :]
            scales_ref[source_of(k) * capacity + rank] = scales.astype(jnp.bfloat16)
        return 0

    lax.fori_loop(0, experts, put_stream, 0)
    for k in range(experts):
        write(k).wait()


def unpack(facts, got, steps, units, capacity, columns, positions, blocks):
    half = columns // 2
    window = positions // UNIT + 1
    smem = pl.BlockSpec(memory_space=pltpu.SMEM)
    vmem = pl.BlockSpec(memory_space=pltpu.VMEM)
    hbm = pl.BlockSpec(memory_space=pl.ANY)
    return pl.pallas_call(
        unpack_kernel,
        in_specs=[smem] + [vmem] * 5 + [hbm] * 5,
        out_specs=[hbm, vmem],
        out_shape=[
            jax.ShapeDtypeStruct((4 * capacity, columns, positions), jnp.bfloat16),
            jax.ShapeDtypeStruct((4 * capacity, blocks, positions), jnp.bfloat16),
        ],
        scratch_shapes=[
            pltpu.VMEM((4, (units + window) * half, 2 * UNIT), jnp.bfloat16),
            pltpu.VMEM((4, capacity, columns, positions), jnp.bfloat16),
            pltpu.VMEM((4, capacity * blocks, positions), jnp.float32),
            pltpu.SMEM((4, capacity + 1), jnp.int32),
            pltpu.SMEM((4, capacity + 1), jnp.int32),
            pltpu.SemaphoreType.DMA,
            pltpu.SemaphoreType.DMA((4,)),
        ],
        compiler_params=pltpu.CompilerParams(vmem_limit_bytes=24 * MIB),
        cost_estimate=pl.CostEstimate(flops=2 * 32 * half * 256 * 384, bytes_accessed=10 * MIB, transcendentals=0),
    )(facts, *got, *steps)


def choose_kernel(c0, c1, c2, c3, out_ref, facts_ref, loads_ref):
    experts = 4
    requests = c0.shape[1]
    me, other = lax.axis_index("expert"), 1 - lax.axis_index("segment")
    for k, chip in enumerate((c0, c1, c2, c3)):
        most = [jnp.int32(0)] * experts
        for section in range(2):

            def add(i, sums):
                fact = chip[section, i]
                owner, length = fact >> FACT_BITS, fact & (FACT - 1)
                part = length << ((owner >> 1) << 4)
                odd = (owner & 1) == 1
                return (sums[0] + jnp.where(odd, 0, part), sums[1] + jnp.where(odd, part, 0))

            even, odd = lax.fori_loop(0, requests, add, (jnp.int32(0), jnp.int32(0)), unroll=8)
            for o, sums in enumerate((even, odd, even >> 16, odd >> 16)):
                most[o] = jnp.maximum(most[o], ((sums & 0xFFFF) + UNIT - 1) >> UNIT_BITS)
        for o in range(experts):
            loads_ref[((me - k) & (experts - 1)) * experts + o] = most[o]

        def keep(i, _):
            facts_ref[k, i] = chip[other, i]
            return 0

        lax.fori_loop(0, requests, keep, 0, unroll=8)
    load = [[loads_ref[source * experts + o] for o in range(experts)] for source in range(experts)]
    hot, highest = jnp.int32(0), jnp.int32(-1)
    for o in range(experts):
        worst = functools.reduce(jnp.maximum, [load[source][o] for source in range(experts) if source != o])
        hot = jnp.where(worst > highest, o, hot)
        highest = jnp.maximum(worst, highest)
    out_ref[0] = hot
    for way in range(5):
        need = jnp.int32(0)
        for source, target in enumerate(targets_of(way)):
            if source != target:
                need = jnp.maximum(need, load[source][target])
            elif way == staying(source)[0]:
                need = jnp.maximum(need, jnp.minimum(load[source][source], SPLIT))
            else:
                need = jnp.maximum(need, load[source][source] - SPLIT)
        out_ref[1 + way] = need


def choose(chips):
    smem = pl.BlockSpec(memory_space=pltpu.SMEM)
    return pl.pallas_call(
        choose_kernel,
        in_specs=[smem] * 4,
        out_specs=[smem] * 2,
        out_shape=[jax.ShapeDtypeStruct((6,), jnp.int32), jax.ShapeDtypeStruct((4, chips[0].shape[1]), jnp.int32)],
        scratch_shapes=[pltpu.SMEM((16,), jnp.int32)],
    )(*chips)


def crossed(targets):
    return [(source * 2 + s, target * 2 + 1 - s) for source, target in enumerate(targets) for s in range(2)]


def by_halves(branches, index, operands):
    def run(low, high, operands):
        if high - low == 1:
            return branches[low](operands)
        middle = (low + high) // 2
        return lax.cond(
            index < middle, functools.partial(run, low, middle), functools.partial(run, middle, high), operands
        )

    return run(0, len(branches), operands)


def base_sizes(hot):
    return [PAIRED] + [LONG if hot in swap else SHORT for swap in SWAPS]


def blank(shapes):
    hbm = pl.BlockSpec(memory_space=pl.ANY)
    return pl.pallas_call(
        lambda *refs: None,
        out_specs=[hbm] * len(shapes),
        out_shape=[jax.ShapeDtypeStruct(shape, jnp.bfloat16) for shape in shapes],
    )()


def send_steps(stream, way, first, need, room, half):
    rows = CHUNK * half

    def step(carry):
        at, room = carry
        part = lax.dynamic_slice_in_dim(stream, first * half + at * rows, rows)
        part = lax.ppermute(part, ("expert", "segment"), crossed(targets_of(way)))
        return at + 1, lax.dynamic_update_slice_in_dim(room, part, at * rows, 0)

    return lax.while_loop(lambda carry: carry[0] * CHUNK < need, step, (jnp.int32(0), room))[1]


def slot_layout(owner, experts, capacity):
    requests = owner.shape[0]
    indices = jnp.arange(requests, dtype=jnp.int32)
    earlier = indices[None, :] < indices[:, None]
    same_owner = owner[:, None] == owner[None, :]
    arrival_rank = jnp.sum(jnp.logical_and(same_owner, earlier), axis=1)
    target = owner * capacity + arrival_rank
    routing = target[None, :] == jnp.arange(experts * capacity, dtype=jnp.int32)[:, None]
    filled = jnp.any(routing, axis=1)
    source = jnp.sum(jnp.where(routing, indices[None, :], 0), axis=1)
    return (filled, source)


def pick_slots(values, filled, source):
    zero_value = jnp.zeros((), values.dtype)
    return jnp.where(filled[:, None, None], jnp.take(values, source, axis=0), zero_value)


def on_device(
    res_cache,
    res_scales,
    res_lengths,
    res_query,
    new_cache,
    new_scales,
    new_lengths,
    new_query,
    owner,
):
    experts = lax.axis_size("expert")
    sections = lax.axis_size("segment")
    requests, positions, columns = new_cache.shape
    capacity = max(2, 2 * requests // experts)
    swap = [(0, 1), (1, 0)]
    cache_t = jnp.transpose(new_cache, (0, 2, 1))
    res_inputs = (jnp.transpose(res_query, (0, 2, 1)), jnp.transpose(res_cache, (0, 2, 1)), res_scales, res_lengths)
    inputs = (res_inputs, (jnp.transpose(new_query, (0, 2, 1)), cache_t, new_scales, new_lengths))

    def attention(res_inputs, new_inputs):
        return attend(*res_inputs, 2), attend(*new_inputs, 4)

    if experts != 4 or sections != 2 or positions % UNIT or columns % 32:
        live_rows = jnp.arange(positions)[None, :] < new_lengths[:, None]
        zero_value = jnp.zeros((), jnp.bfloat16)
        filled, source = slot_layout(owner, experts, capacity)
        send_cache = pick_slots(jnp.where(live_rows[:, :, None], new_cache, zero_value), filled, source)
        send_scales = pick_slots(jnp.where(live_rows[:, None, :], new_scales, zero_value), filled, source)
        got_cache = lax.all_to_all(send_cache, "expert", split_axis=0, concat_axis=0, tiled=True)
        got_scales = lax.all_to_all(send_scales, "expert", split_axis=0, concat_axis=0, tiled=True)
        owned_cache, owned_scales = lax.ppermute((got_cache, got_scales), "segment", swap)
        return (*attention(*inputs), owned_cache, owned_scales)

    section = lax.axis_index("segment")
    units, half = capacity * positions // UNIT, columns // 2
    blocks = new_scales.shape[1]
    facts = owner * FACT + new_lengths
    sibling = lax.ppermute(facts, "segment", swap)
    chip = jnp.where(section == 0, jnp.stack([facts, sibling]), jnp.stack([sibling, facts]))
    chips = [chip] + [lax.ppermute(chip, "expert", [(e, (e + k) % 4) for e in range(4)]) for k in range(1, 4)]
    streams = pack(owner, new_lengths, new_scales, cache_t, sibling, units, capacity)
    needs, facts = choose(chips)

    def take(hot):
        def run(operands):
            streams, needs, facts, *inputs = operands
            parts = stream_parts(units + CHUNK)
            sizes = base_sizes(hot)
            got = []
            for way, size in enumerate(sizes):
                part = streams[parts.index((way, 0, size))]
                got.append(lax.ppermute(part, ("expert", "segment"), crossed(targets_of(way))))
            rooms = blank([(-(-(units - size) // CHUNK) * CHUNK * half, 2 * UNIT) for size in sizes])
            early = sizes.index(SHORT)
            needs, got[early], *contexts = lax.optimization_barrier((needs, got[early], *attention(*inputs)))
            steps = []
            for way, size in enumerate(sizes):
                low = SHORT if way else PAIRED
                stream = streams[parts.index((way, low, units + CHUNK))]
                steps.append(send_steps(stream, way, size - low, needs[1 + way] - size, rooms[way], half))
            return (*contexts, *unpack(facts, got, steps, units, capacity, columns, positions, blocks))

        return run

    operands = (streams, needs, facts, *inputs)
    res_context, new_context, owned, owned_scales = by_halves([take(hot) for hot in range(4)], needs[0], operands)
    return (res_context, new_context, jnp.transpose(owned, (0, 2, 1)), owned_scales)


def solution(mesh):
    placed = (
        P(("group", "expert", "segment", "attn"), None, None),
        P(("group", "expert", "segment", "attn"), None, None),
        P(("group", "expert", "segment", "attn")),
        P(("group", "expert", "segment", "attn"), None, None),
        P(("group", "expert", "segment", "attn"), None, None),
        P(("group", "expert", "segment", "attn"), None, None),
        P(("group", "expert", "segment", "attn")),
        P(("group", "expert", "segment", "attn"), None, None),
        P(("group", "expert", "segment", "attn")),
    )
    return jax.shard_map(
        on_device,
        mesh=mesh,
        in_specs=placed,
        out_specs=(
            P(("group", "expert", "segment", "attn"), None, None),
            P(("group", "expert", "segment", "attn"), None, None),
            P(("group", "expert", "segment", "attn"), None, None),
            P(("group", "expert", "segment", "attn"), None, None),
        ),
        check_vma=False,
    )
```

```python
import functools
import jax
import jax.numpy as jnp
from jax import lax
from jax.experimental import pallas as pl
from jax.experimental.pallas import tpu as pltpu
from jax.sharding import PartitionSpec as P

LATENT = 512
BLOCK = 128
UNIT_BITS = 6
UNIT = 1 << UNIT_BITS
SPLIT = 6
SEGMENTS = (0, 6, 10)
AT_END = ((14, 11, 11, 6, 8), (14, 12, 12, 7, 7), (13, 11, 14, 10, 6), (13, 14, 13, 8, 8))
IN_MIDDLE = ((12, 13, 11, 6, 7), (12, 11, 13, 7, 7), (14, 12, 11, 10, 10), (14, 14, 14, 8, 8))
SWAPS = ((0, 2), (0, 3), (1, 2), (1, 3))
FACT_BITS = 8
FACT = 1 << FACT_BITS

softmax_scale = 192.0 ** (-0.5)
MIB = 1 << 20


def attend_kernel(lengths_ref, query_ref, cache_ref, scales_ref, out_ref, factors_ref):
    blocks = scales_ref.shape[1]
    positions = cache_ref.shape[2]
    contract_rows = (((0,), (0,)), ((), ()))
    contract_positions = (((1,), (1,)), ((), ()))
    length = lengths_ref[pl.program_id(0)]

    def block(b):
        return pl.ds(pl.multiple_of(b * BLOCK, BLOCK), BLOCK)

    for b in range(blocks):
        factors_ref[b] = scales_ref[0, b : b + 1, :].astype(jnp.float32)

    def add(b, scores):
        part = lax.dot_general(
            query_ref[0, block(b), :], cache_ref[0, block(b), :], contract_rows, preferred_element_type=jnp.float32
        )
        return scores + part * factors_ref[b]

    scores = lax.dot_general(
        query_ref[0, LATENT:, :], cache_ref[0, LATENT:, :], contract_rows, preferred_element_type=jnp.float32
    )
    scores = lax.fori_loop(0, blocks, add, scores)
    live = lax.broadcasted_iota(jnp.int32, (1, positions), 1) < length
    scores = jnp.where(live, scores * softmax_scale, -jnp.inf)
    exponent = jnp.exp(scores - jnp.max(scores, axis=-1, keepdims=True))
    probabilities = exponent * (1.0 / jnp.sum(exponent, axis=-1, keepdims=True))

    def put(b, _):
        out_ref[0, :, block(b)] = lax.dot_general(
            (probabilities * factors_ref[b]).astype(jnp.bfloat16),
            cache_ref[0, block(b), :],
            contract_positions,
            preferred_element_type=jnp.float32,
        ).astype(jnp.bfloat16)
        return 0

    lax.fori_loop(0, blocks, put, 0)


def attend(query, cache, scales, lengths):
    requests, columns, heads = query.shape
    positions = cache.shape[2]
    return pl.pallas_call(
        attend_kernel,
        grid=(requests,),
        in_specs=[
            pl.BlockSpec(memory_space=pltpu.SMEM),
            pl.BlockSpec((1, columns, heads), lambda i: (i, 0, 0)),
            pl.BlockSpec((1, columns, positions), lambda i: (i, 0, 0)),
            pl.BlockSpec((1, scales.shape[1], positions), lambda i: (i, 0, 0)),
        ],
        out_specs=pl.BlockSpec((1, heads, LATENT), lambda i: (i, 0, 0)),
        out_shape=jax.ShapeDtypeStruct((requests, heads, LATENT), jnp.bfloat16),
        scratch_shapes=[pltpu.VMEM((scales.shape[1], 1, positions), jnp.float32)],
        compiler_params=pltpu.CompilerParams(vmem_limit_bytes=16 * MIB),
        cost_estimate=pl.CostEstimate(
            flops=4 * requests * heads * positions * columns,
            bytes_accessed=2 * requests * (heads * (columns + LATENT) + positions * columns),
            transcendentals=requests * heads * positions,
        ),
    )(lengths, query, cache, scales)


def stream_gap(rows, positions, first, units):
    window = units * 2 * UNIT
    shape = (window, 2 * positions) if rows == "window" else (2 * positions, window)
    down, across = lax.broadcasted_iota(jnp.int32, shape, 0), lax.broadcasted_iota(jnp.int32, shape, 1)
    lane, own = (down, across) if rows == "window" else (across, down)
    within = lane % (2 * UNIT)
    place = (lane // (2 * UNIT) + first) * UNIT + within % UNIT
    meet = within // UNIT == own // positions
    side = (1, 2 * positions) if rows == "window" else (2 * positions, 1)
    position = lax.broadcasted_iota(jnp.int32, side, 1 if rows == "window" else 0) % positions
    return jnp.where(meet, place - own % positions, -512).astype(jnp.bfloat16), position


def moving(gap, position, shift, length):
    wanted = jnp.where(position < length, shift, 512).astype(jnp.bfloat16)
    return jnp.where(gap == wanted, jnp.ones((), jnp.bfloat16), jnp.zeros((), jnp.bfloat16))


def targets_of(way):
    if way == 0:
        return [e ^ 1 for e in range(4)]
    a, b = SWAPS[way - 1]
    return [b if e == a else a if e == b else e for e in range(4)]


def staying(e):
    return [way for way in range(5) if targets_of(way)[e] == e]


def pick(index, values):
    value = jnp.int32(values[0])
    for at in range(1, len(values)):
        value = jnp.where(index == at, values[at], value)
    return value


def pack_kernel(owner_ref, lengths_ref, scales_ref, cache_ref, after_ref, *refs):
    outs, (held, acc, slots, ends, ranks, in_sem, out_sem) = refs[:5], refs[5:]
    experts = 4
    requests, columns, positions = cache_ref.shape
    blocks = scales_ref.shape[1]
    half = columns // 2
    tail = slots.shape[1]
    window = positions // UNIT + 1
    me = lax.axis_index("expert")
    parts = in_sem.shape[0]
    share = requests // parts

    def rows_of(unit):
        return pl.ds(pl.multiple_of(tail + unit * half, 16), half)

    def fetch(part):
        here = pl.ds(part * share, share)
        return pltpu.make_async_copy(cache_ref.at[here], held.at[here], in_sem.at[part])

    for part in range(parts):
        fetch(part).start()
    gap, position = stream_gap("request", positions, 0, window)
    for k in range(experts):
        ends[k] = 0
        ranks[k] = 0
        acc[k, rows_of(0), :] = jnp.zeros((half, 2 * UNIT), jnp.bfloat16)
    slots[...] = jnp.zeros(slots.shape, jnp.float32)
    live = lax.broadcasted_iota(jnp.int32, (blocks, positions), 1)

    def place(i, _):
        k = owner_ref[i]
        length = lengths_ref[i]
        start, rank = ends[k], ranks[k]
        ends[k] = start + length
        ranks[k] = rank + 1
        slots[k, pl.ds(rank * blocks, blocks), :] = jnp.where(live < length, scales_ref[i].astype(jnp.float32), 0.0)
        unit, shift = start >> UNIT_BITS, start & (UNIT - 1)
        move = moving(gap, position, shift, length)
        both = jnp.concatenate([held[i, :half, :], held[i, half:, :]], axis=1)
        moved = jnp.dot(both, move, preferred_element_type=jnp.float32).astype(jnp.bfloat16)
        acc[k, rows_of(unit), :] += moved[:, : 2 * UNIT]
        for j in range(1, window):
            acc[k, rows_of(unit + j), :] = moved[:, 2 * UNIT * j : 2 * UNIT * (j + 1)]
        return 0

    for part in range(parts):
        fetch(part).wait()
        lax.fori_loop(part * share, (part + 1) * share, place, 0, unroll=True)
    acc[:, :tail, :] = slots[...].astype(jnp.bfloat16)
    copies = []
    for way, out in enumerate(outs):
        k = pick(me, targets_of(way))
        skipped = pick(me, [SPLIT if way == staying(e)[1] else 0 for e in range(experts)])
        for at, first in enumerate(SEGMENTS):
            low = tail + first * half if first else 0
            high = tail + SEGMENTS[at + 1] * half if at + 1 < len(SEGMENTS) else out.shape[0]
            here = pl.ds(pl.multiple_of(low + skipped * half, 16), high - low)
            copy = pltpu.make_async_copy(acc.at[k, here], out.at[pl.ds(low, high - low)], out_sem.at[way, at])
            copies.append((copy, True if first == 0 else ends[k] > (first + skipped) * UNIT))
    for act in (lambda copy: copy.start(), lambda copy: copy.wait()):
        for copy, needed in copies:
            if needed is True:
                act(copy)
            else:
                pl.when(needed)(functools.partial(act, copy))


def pack(owner, lengths, scales, cache, after, units, capacity):
    requests, columns, positions = cache.shape
    half = columns // 2
    window = positions // UNIT + 1
    tail = capacity * scales.shape[1]
    smem = pl.BlockSpec(memory_space=pltpu.SMEM)
    vmem = pl.BlockSpec(memory_space=pltpu.VMEM)
    hbm = pl.BlockSpec(memory_space=pl.ANY)
    lanes = 2 * UNIT
    return pl.pallas_call(
        pack_kernel,
        in_specs=[smem, smem, vmem, hbm, hbm],
        out_specs=[hbm] * 5,
        out_shape=[jax.ShapeDtypeStruct((tail + units * half, lanes), jnp.bfloat16)] * 5,
        scratch_shapes=[
            pltpu.VMEM(cache.shape, jnp.bfloat16),
            pltpu.VMEM((4, tail + (units + SPLIT) * half, lanes), jnp.bfloat16),
            pltpu.VMEM((4, tail, positions), jnp.float32),
            pltpu.SMEM((4,), jnp.int32),
            pltpu.SMEM((4,), jnp.int32),
            pltpu.SemaphoreType.DMA((4,)),
            pltpu.SemaphoreType.DMA((5, len(SEGMENTS))),
        ],
        compiler_params=pltpu.CompilerParams(vmem_limit_bytes=24 * MIB),
        cost_estimate=pl.CostEstimate(flops=2 * requests * half * 256 * 384, bytes_accessed=8 * MIB, transcendentals=0),
    )(owner, lengths, scales, cache, after)


def unpack_kernel(facts_ref, g0, g1, g2, g3, g4, out_ref, scales_ref, *scratch):
    held, stage, tails, starts, counts, out_sem = scratch
    got = (g0, g1, g2, g3, g4)
    experts = 4
    requests = facts_ref.shape[1]
    capacity = out_ref.shape[0] // experts
    columns, positions = out_ref.shape[1], out_ref.shape[2]
    blocks = scales_ref.shape[1]
    half = columns // 2
    tail = capacity * blocks
    window = positions // UNIT
    me = lax.axis_index("expert")

    def rows_of(unit):
        return pl.ds(pl.multiple_of(unit * half, 16), half)

    def units_of(unit):
        return pl.ds(pl.multiple_of(tail + unit * half, 16), half)

    def source_of(k):
        return (me - k) & (experts - 1)

    def scan(k, _):
        def note(i, carry):
            rank, end = carry
            mine = facts_ref[k, i] >> FACT_BITS == me
            length = facts_ref[k, i] & (FACT - 1)

            @pl.when(mine)
            def _():
                starts[k, rank] = end
                counts[k, rank] = length

            return (jnp.where(mine, rank + 1, rank), jnp.where(mine, end + length, end))

        rank, end = lax.fori_loop(0, requests, note, (0, 0))
        starts[k, capacity] = rank
        counts[k, capacity] = (end + UNIT - 1) >> UNIT_BITS
        return 0

    lax.fori_loop(0, experts, scan, 0)

    def fetch_stream(k, _):
        used = counts[k, capacity]
        for way in range(5):
            came = pick(source_of(k), targets_of(way)) == me
            later = jnp.logical_and(k == 0, pick(me, [int(way == staying(e)[1]) for e in range(experts)]) == 1)
            low = jnp.where(later, SPLIT, 0)
            high = jnp.where(jnp.logical_and(k == 0, jnp.logical_not(later)), jnp.minimum(used, SPLIT), used)

            @pl.when(came)
            def _():
                @pl.when(jnp.logical_not(later))
                def _():
                    tails[k] = got[way][:tail, :].astype(jnp.float32)

                def move_unit(u, _):
                    held[k, rows_of(u), :] = got[way][units_of(u - low), :]
                    return 0

                lax.fori_loop(low, high, move_unit, 0)

        return 0

    lax.fori_loop(0, experts, fetch_stream, 0)
    gap, position = stream_gap("window", positions, 0, window)
    gap_behind, _ = stream_gap("window", positions, window, 1)

    def write(k):
        there = out_ref.at[pl.ds(source_of(k) * capacity, capacity)]
        return pltpu.make_async_copy(stage.at[k], there, out_sem.at[k])

    def put_stream(k, _):
        used, ranks = counts[k, capacity], starts[k, capacity]

        for j in range(window):
            held[k, rows_of(used + j), :] = jnp.zeros((half, 2 * UNIT), jnp.bfloat16)

        def put(pair, _):
            def placed(rank):
                filled = rank < ranks
                start, length = jnp.where(filled, starts[k, rank], 0), jnp.where(filled, counts[k, rank], 0)
                return start >> UNIT_BITS, start & (UNIT - 1), length

            for rank in (2 * pair, 2 * pair + 1):
                unit, shift, length = placed(rank)
                move = moving(gap, position, shift, length)
                seen = jnp.concatenate([held[k, rows_of(unit + j), :] for j in range(window)], axis=1)
                moved = jnp.dot(seen, move, preferred_element_type=jnp.float32).astype(jnp.bfloat16)
                stage[k, rank, :half, :] = moved[:, :positions]
                stage[k, rank, half:, :] = moved[:, positions:]

            def put_behind(rank, _):
                unit, shift, length = placed(rank)

                @pl.when(shift + length > window * UNIT)
                def _():
                    move = moving(gap_behind, position, shift, length)
                    seen = held[k, rows_of(unit + window), :]
                    moved = jnp.dot(seen, move, preferred_element_type=jnp.float32).astype(jnp.bfloat16)
                    stage[k, rank, :half, :] += moved[:, :positions]
                    stage[k, rank, half:, :] += moved[:, positions:]

                return 0

            lax.fori_loop(2 * pair, 2 * pair + 2, put_behind, 0)
            return 0

        def clear(pair, _):
            stage[k, pl.ds(2 * pair, 2)] = jnp.zeros((2, columns, positions), jnp.bfloat16)
            return 0

        pairs = (ranks + 1) >> 1
        lax.fori_loop(0, pairs, put, 0)
        lax.fori_loop(pairs, capacity // 2, clear, 0)
        write(k).start()
        for rank in range(capacity):
            scales = tails[k, rank * blocks : (rank + 1) * blocks, :]
            scales_ref[source_of(k) * capacity + rank] = scales.astype(jnp.bfloat16)
        return 0

    lax.fori_loop(0, experts, put_stream, 0)
    for k in range(experts):
        write(k).wait()


def unpack(facts, got, units, capacity, columns, positions, blocks):
    half = columns // 2
    window = positions // UNIT + 1
    smem = pl.BlockSpec(memory_space=pltpu.SMEM)
    vmem = pl.BlockSpec(memory_space=pltpu.VMEM)
    hbm = pl.BlockSpec(memory_space=pl.ANY)
    return pl.pallas_call(
        unpack_kernel,
        in_specs=[smem] + [vmem] * 5,
        out_specs=[hbm, vmem],
        out_shape=[
            jax.ShapeDtypeStruct((4 * capacity, columns, positions), jnp.bfloat16),
            jax.ShapeDtypeStruct((4 * capacity, blocks, positions), jnp.bfloat16),
        ],
        scratch_shapes=[
            pltpu.VMEM((4, (units + window) * half, 2 * UNIT), jnp.bfloat16),
            pltpu.VMEM((4, capacity, columns, positions), jnp.bfloat16),
            pltpu.VMEM((4, capacity * blocks, positions), jnp.float32),
            pltpu.SMEM((4, capacity + 1), jnp.int32),
            pltpu.SMEM((4, capacity + 1), jnp.int32),
            pltpu.SemaphoreType.DMA((4,)),
        ],
        compiler_params=pltpu.CompilerParams(vmem_limit_bytes=24 * MIB),
        cost_estimate=pl.CostEstimate(flops=2 * 32 * half * 256 * 384, bytes_accessed=10 * MIB, transcendentals=0),
    )(facts, *got)


def size_sets():
    branches = []
    for hot in range(4):
        one, two = (2, 3) if hot < 2 else (1, 0)
        for paired, *sizes in AT_END if hot in (0, 3) else IN_MIDDLE:
            swaps = [{hot, one}, {hot, two}, {hot ^ 1, one}, {hot ^ 1, two}]
            branches.append((hot, [paired] + [sizes[swaps.index(set(swap))] for swap in SWAPS]))
    return branches + [(None, [16] * 5)]


BRANCHES = size_sets()


def choose_kernel(c0, c1, c2, c3, out_ref, facts_ref, chips_ref, loads_ref, sem):
    experts = 4
    requests = c0.shape[1]
    me, other = lax.axis_index("expert"), 1 - lax.axis_index("segment")
    copies = [pltpu.make_async_copy(chip, chips_ref.at[k], sem.at[k]) for k, chip in enumerate((c0, c1, c2, c3))]
    for copy in copies:
        copy.start()
    for copy in copies:
        copy.wait()
    for k in range(experts):
        chip = chips_ref.at[k]
        most = [jnp.int32(0)] * experts
        for section in range(2):

            def add(i, sums):
                fact = chip[section, i]
                owner, length = fact >> FACT_BITS, fact & (FACT - 1)
                part = length << ((owner >> 1) << 4)
                odd = (owner & 1) == 1
                return (sums[0] + jnp.where(odd, 0, part), sums[1] + jnp.where(odd, part, 0))

            even, odd = lax.fori_loop(0, requests, add, (jnp.int32(0), jnp.int32(0)), unroll=8)
            for o, sums in enumerate((even, odd, even >> 16, odd >> 16)):
                most[o] = jnp.maximum(most[o], ((sums & 0xFFFF) + UNIT - 1) >> UNIT_BITS)
        for o in range(experts):
            loads_ref[((me - k) & (experts - 1)) * experts + o] = most[o]

        def keep(i, _):
            facts_ref[k, i] = chip[other, i]
            return 0

        lax.fori_loop(0, requests, keep, 0, unroll=8)
    load = [[loads_ref[source * experts + o] for o in range(experts)] for source in range(experts)]
    hot, highest = jnp.int32(0), jnp.int32(-1)
    for o in range(experts):
        worst = functools.reduce(jnp.maximum, [load[source][o] for source in range(experts) if source != o])
        hot = jnp.where(worst > highest, o, hot)
        highest = jnp.maximum(worst, highest)
    needs = []
    for way in range(5):
        need = jnp.int32(0)
        for source, target in enumerate(targets_of(way)):
            if source != target:
                need = jnp.maximum(need, load[source][target])
            elif way == staying(source)[0]:
                need = jnp.maximum(need, jnp.minimum(load[source][source], SPLIT))
            else:
                need = jnp.maximum(need, load[source][source] - SPLIT)
        needs.append(need)
    branch = jnp.int32(len(BRANCHES) - 1)
    for at in range(len(BRANCHES) - 2, -1, -1):
        h, sizes = BRANCHES[at]
        fits = functools.reduce(jnp.logical_and, [need <= size for need, size in zip(needs, sizes)], hot == h)
        branch = jnp.where(fits, at, branch)
    out_ref[0] = branch


def choose(chips):
    smem = pl.BlockSpec(memory_space=pltpu.SMEM)
    return pl.pallas_call(
        choose_kernel,
        in_specs=[pl.BlockSpec(memory_space=pl.ANY)] * 4,
        out_specs=[smem] * 2,
        out_shape=[jax.ShapeDtypeStruct((1,), jnp.int32), jax.ShapeDtypeStruct((4, chips[0].shape[1]), jnp.int32)],
        scratch_shapes=[
            pltpu.SMEM((4,) + chips[0].shape, jnp.int32),
            pltpu.SMEM((16,), jnp.int32),
            pltpu.SemaphoreType.DMA((4,)),
        ],
    )(*chips)


def crossed(targets):
    return [(source * 2 + s, target * 2 + 1 - s) for source, target in enumerate(targets) for s in range(2)]


def by_halves(branches, index, operands):
    def run(low, high, operands):
        if high - low == 1:
            return branches[low](operands)
        middle = (low + high) // 2
        return lax.cond(
            index < middle, functools.partial(run, low, middle), functools.partial(run, middle, high), operands
        )

    return run(0, len(branches), operands)


def cut_kernel(*refs):
    streams, outs, sem = refs[:5], refs[5:10], refs[10]
    copies = [
        pltpu.make_async_copy(stream.at[pl.ds(0, out.shape[0])], out, sem.at[way])
        for way, (stream, out) in enumerate(zip(streams, outs))
    ]
    for copy in copies:
        copy.start()
    for copy in copies:
        copy.wait()


def cut(streams, rows):
    return pl.pallas_call(
        cut_kernel,
        in_specs=[pl.BlockSpec(memory_space=pl.ANY)] * 5,
        out_specs=[pl.BlockSpec(memory_space=pltpu.VMEM)] * 5,
        out_shape=[jax.ShapeDtypeStruct((row, stream.shape[1]), stream.dtype) for row, stream in zip(rows, streams)],
        scratch_shapes=[pltpu.SemaphoreType.DMA((5,))],
        compiler_params=pltpu.CompilerParams(vmem_limit_bytes=8 * MIB),
    )(*streams)


def slot_layout(owner, experts, capacity):
    requests = owner.shape[0]
    indices = jnp.arange(requests, dtype=jnp.int32)
    earlier = indices[None, :] < indices[:, None]
    same_owner = owner[:, None] == owner[None, :]
    arrival_rank = jnp.sum(jnp.logical_and(same_owner, earlier), axis=1)
    target = owner * capacity + arrival_rank
    routing = target[None, :] == jnp.arange(experts * capacity, dtype=jnp.int32)[:, None]
    filled = jnp.any(routing, axis=1)
    source = jnp.sum(jnp.where(routing, indices[None, :], 0), axis=1)
    return (filled, source)


def pick_slots(values, filled, source):
    zero_value = jnp.zeros((), values.dtype)
    return jnp.where(filled[:, None, None], jnp.take(values, source, axis=0), zero_value)


def on_device(
    res_cache,
    res_scales,
    res_lengths,
    res_query,
    new_cache,
    new_scales,
    new_lengths,
    new_query,
    owner,
):
    experts = lax.axis_size("expert")
    sections = lax.axis_size("segment")
    requests, positions, columns = new_cache.shape
    capacity = max(2, 2 * requests // experts)
    swap = [(0, 1), (1, 0)]
    cache_t = jnp.transpose(new_cache, (0, 2, 1))
    res_inputs = (jnp.transpose(res_query, (0, 2, 1)), jnp.transpose(res_cache, (0, 2, 1)), res_scales, res_lengths)
    inputs = (res_inputs, (jnp.transpose(new_query, (0, 2, 1)), cache_t, new_scales, new_lengths))

    def attention(res_inputs, new_inputs):
        return attend(*res_inputs), attend(*new_inputs)

    if experts != 4 or sections != 2 or capacity * positions != 16 * UNIT or positions != 2 * UNIT or columns % 32:
        live_rows = jnp.arange(positions)[None, :] < new_lengths[:, None]
        zero_value = jnp.zeros((), jnp.bfloat16)
        filled, source = slot_layout(owner, experts, capacity)
        send_cache = pick_slots(jnp.where(live_rows[:, :, None], new_cache, zero_value), filled, source)
        send_scales = pick_slots(jnp.where(live_rows[:, None, :], new_scales, zero_value), filled, source)
        got_cache = lax.all_to_all(send_cache, "expert", split_axis=0, concat_axis=0, tiled=True)
        got_scales = lax.all_to_all(send_scales, "expert", split_axis=0, concat_axis=0, tiled=True)
        owned_cache, owned_scales = lax.ppermute((got_cache, got_scales), "segment", swap)
        return (*attention(*inputs), owned_cache, owned_scales)

    section = lax.axis_index("segment")
    units, half = capacity * positions // UNIT, columns // 2
    blocks = new_scales.shape[1]
    facts = owner * FACT + new_lengths
    sibling = lax.ppermute(facts, "segment", swap)
    chip = jnp.where(section == 0, jnp.stack([facts, sibling]), jnp.stack([sibling, facts]))
    chips = [chip] + [lax.ppermute(chip, "expert", [(e, (e + k) % 4) for e in range(4)]) for k in range(1, 4)]
    streams = pack(owner, new_lengths, new_scales, cache_t, sibling, units, capacity)
    branch, facts = choose(chips)

    def take(sizes):
        def run(operands):
            streams, facts, *inputs = operands
            parts = cut(streams, [capacity * blocks + size * half for size in sizes])
            got = [
                lax.ppermute(part, ("expert", "segment"), crossed(targets_of(way))) for way, part in enumerate(parts)
            ]
            return (*attention(*inputs), *unpack(facts, got, units, capacity, columns, positions, blocks))

        return run

    branches = [take(sizes) for _, sizes in BRANCHES]
    res_context, new_context, owned, owned_scales = by_halves(branches, branch[0], (streams, facts, *inputs))
    return (res_context, new_context, jnp.transpose(owned, (0, 2, 1)), owned_scales)


def solution(mesh):
    placed = (
        P(("group", "expert", "segment", "attn"), None, None),
        P(("group", "expert", "segment", "attn"), None, None),
        P(("group", "expert", "segment", "attn")),
        P(("group", "expert", "segment", "attn"), None, None),
        P(("group", "expert", "segment", "attn"), None, None),
        P(("group", "expert", "segment", "attn"), None, None),
        P(("group", "expert", "segment", "attn")),
        P(("group", "expert", "segment", "attn"), None, None),
        P(("group", "expert", "segment", "attn")),
    )
    return jax.shard_map(
        on_device,
        mesh=mesh,
        in_specs=placed,
        out_specs=(
            P(("group", "expert", "segment", "attn"), None, None),
            P(("group", "expert", "segment", "attn"), None, None),
            P(("group", "expert", "segment", "attn"), None, None),
            P(("group", "expert", "segment", "attn"), None, None),
        ),
        check_vma=False,
    )
```

```python
import functools
import jax
import jax.numpy as jnp
from jax import lax
from jax.experimental import pallas as pl
from jax.experimental.pallas import tpu as pltpu
from jax.sharding import PartitionSpec as P

LATENT = 512
BLOCK = 128
UNIT_BITS = 6
UNIT = 1 << UNIT_BITS
SPLIT = 6
SEGMENTS = (0, 6, 10)
AT_END = ((14, 12, 12, 7, 7), (13, 11, 14, 10, 6), (14, 14, 13, 8, 8))
IN_MIDDLE = ((12, 12, 12, 7, 7), (14, 12, 11, 10, 10), (14, 14, 14, 8, 8))
SWAPS = ((0, 2), (0, 3), (1, 2), (1, 3))
FACT_BITS = 8
FACT = 1 << FACT_BITS

softmax_scale = 192.0 ** (-0.5)
MIB = 1 << 20


def attend_kernel(lengths_ref, query_ref, cache_ref, scales_ref, out_ref, factors_ref):
    blocks = scales_ref.shape[1]
    positions = cache_ref.shape[2]
    contract_rows = (((0,), (0,)), ((), ()))
    contract_positions = (((1,), (1,)), ((), ()))
    length = lengths_ref[pl.program_id(0)]

    def block(b):
        return pl.ds(pl.multiple_of(b * BLOCK, BLOCK), BLOCK)

    for b in range(blocks):
        factors_ref[b] = scales_ref[0, b : b + 1, :].astype(jnp.float32)

    def add(b, scores):
        part = lax.dot_general(
            query_ref[0, block(b), :], cache_ref[0, block(b), :], contract_rows, preferred_element_type=jnp.float32
        )
        return scores + part * factors_ref[b]

    scores = lax.dot_general(
        query_ref[0, LATENT:, :], cache_ref[0, LATENT:, :], contract_rows, preferred_element_type=jnp.float32
    )
    scores = lax.fori_loop(0, blocks, add, scores)
    live = lax.broadcasted_iota(jnp.int32, (1, positions), 1) < length
    scores = jnp.where(live, scores * softmax_scale, -jnp.inf)
    exponent = jnp.exp(scores - jnp.max(scores, axis=-1, keepdims=True))
    probabilities = exponent * (1.0 / jnp.sum(exponent, axis=-1, keepdims=True))

    def put(b, _):
        out_ref[0, :, block(b)] = lax.dot_general(
            (probabilities * factors_ref[b]).astype(jnp.bfloat16),
            cache_ref[0, block(b), :],
            contract_positions,
            preferred_element_type=jnp.float32,
        ).astype(jnp.bfloat16)
        return 0

    lax.fori_loop(0, blocks, put, 0)


def attend(query, cache, scales, lengths):
    requests, columns, heads = query.shape
    positions = cache.shape[2]
    return pl.pallas_call(
        attend_kernel,
        grid=(requests,),
        in_specs=[
            pl.BlockSpec(memory_space=pltpu.SMEM),
            pl.BlockSpec((1, columns, heads), lambda i: (i, 0, 0)),
            pl.BlockSpec((1, columns, positions), lambda i: (i, 0, 0)),
            pl.BlockSpec((1, scales.shape[1], positions), lambda i: (i, 0, 0)),
        ],
        out_specs=pl.BlockSpec((1, heads, LATENT), lambda i: (i, 0, 0)),
        out_shape=jax.ShapeDtypeStruct((requests, heads, LATENT), jnp.bfloat16),
        scratch_shapes=[pltpu.VMEM((scales.shape[1], 1, positions), jnp.float32)],
        compiler_params=pltpu.CompilerParams(vmem_limit_bytes=16 * MIB),
        cost_estimate=pl.CostEstimate(
            flops=4 * requests * heads * positions * columns,
            bytes_accessed=2 * requests * (heads * (columns + LATENT) + positions * columns),
            transcendentals=requests * heads * positions,
        ),
    )(lengths, query, cache, scales)


def stream_gap(rows, positions, first, units):
    window = units * 2 * UNIT
    shape = (window, 2 * positions) if rows == "window" else (2 * positions, window)
    down, across = lax.broadcasted_iota(jnp.int32, shape, 0), lax.broadcasted_iota(jnp.int32, shape, 1)
    lane, own = (down, across) if rows == "window" else (across, down)
    within = lane % (2 * UNIT)
    place = (lane // (2 * UNIT) + first) * UNIT + within % UNIT
    meet = within // UNIT == own // positions
    side = (1, 2 * positions) if rows == "window" else (2 * positions, 1)
    position = lax.broadcasted_iota(jnp.int32, side, 1 if rows == "window" else 0) % positions
    return jnp.where(meet, place - own % positions, -512).astype(jnp.bfloat16), position


def moving(gap, position, shift, length):
    wanted = jnp.where(position < length, shift, 512).astype(jnp.bfloat16)
    return jnp.where(gap == wanted, jnp.ones((), jnp.bfloat16), jnp.zeros((), jnp.bfloat16))


def targets_of(way):
    if way == 0:
        return [e ^ 1 for e in range(4)]
    a, b = SWAPS[way - 1]
    return [b if e == a else a if e == b else e for e in range(4)]


def staying(e):
    return [way for way in range(5) if targets_of(way)[e] == e]


def pick(index, values):
    value = jnp.int32(values[0])
    for at in range(1, len(values)):
        value = jnp.where(index == at, values[at], value)
    return value


def pack_kernel(c0, c1, c2, c3, scales_ref, cache_ref, *refs):
    outs, branch_ref, facts_ref = refs[:5], refs[5], refs[6]
    held, acc, slots, ends, ranks, chips_ref, loads_ref, in_sem, out_sem, chip_sem = refs[7:]
    experts = 4
    requests, columns, positions = cache_ref.shape
    blocks = scales_ref.shape[1]
    half = columns // 2
    tail = slots.shape[1]
    window = positions // UNIT + 1
    me = lax.axis_index("expert")
    parts = in_sem.shape[0]
    share = requests // parts

    def rows_of(unit):
        return pl.ds(pl.multiple_of(tail + unit * half, 16), half)

    def fetch(part):
        here = pl.ds(part * share, share)
        return pltpu.make_async_copy(cache_ref.at[here], held.at[here], in_sem.at[part])

    chips = [pltpu.make_async_copy(chip, chips_ref.at[k], chip_sem.at[k]) for k, chip in enumerate((c0, c1, c2, c3))]
    for chip in chips:
        chip.start()
    for part in range(parts):
        fetch(part).start()
    for chip in chips:
        chip.wait()
    section = lax.axis_index("segment")
    choose(chips_ref, me, 1 - section, loads_ref, branch_ref, facts_ref)
    gap, position = stream_gap("request", positions, 0, window)
    for k in range(experts):
        ends[k] = 0
        ranks[k] = 0
        acc[k, rows_of(0), :] = jnp.zeros((half, 2 * UNIT), jnp.bfloat16)
    slots[...] = jnp.zeros(slots.shape, jnp.float32)
    live = lax.broadcasted_iota(jnp.int32, (blocks, positions), 1)

    def place(i, _):
        fact = chips_ref[0, section, i]
        k, length = fact >> FACT_BITS, fact & (FACT - 1)
        start, rank = ends[k], ranks[k]
        ends[k] = start + length
        ranks[k] = rank + 1
        slots[k, pl.ds(rank * blocks, blocks), :] = jnp.where(live < length, scales_ref[i].astype(jnp.float32), 0.0)
        unit, shift = start >> UNIT_BITS, start & (UNIT - 1)
        move = moving(gap, position, shift, length)
        both = jnp.concatenate([held[i, :half, :], held[i, half:, :]], axis=1)
        moved = jnp.dot(both, move, preferred_element_type=jnp.float32).astype(jnp.bfloat16)
        acc[k, rows_of(unit), :] += moved[:, : 2 * UNIT]
        for j in range(1, window):
            acc[k, rows_of(unit + j), :] = moved[:, 2 * UNIT * j : 2 * UNIT * (j + 1)]
        return 0

    for part in range(parts):
        fetch(part).wait()
        lax.fori_loop(part * share, (part + 1) * share, place, 0, unroll=True)
    acc[:, :tail, :] = slots[...].astype(jnp.bfloat16)
    copies = []
    for way, out in enumerate(outs):
        k = pick(me, targets_of(way))
        skipped = pick(me, [SPLIT if way == staying(e)[1] else 0 for e in range(experts)])
        for at, first in enumerate(SEGMENTS):
            low = tail + first * half if first else 0
            high = tail + SEGMENTS[at + 1] * half if at + 1 < len(SEGMENTS) else out.shape[0]
            here = pl.ds(pl.multiple_of(low + skipped * half, 16), high - low)
            copy = pltpu.make_async_copy(acc.at[k, here], out.at[pl.ds(low, high - low)], out_sem.at[way, at])
            copies.append((copy, True if first == 0 else ends[k] > (first + skipped) * UNIT))
    for act in (lambda copy: copy.start(), lambda copy: copy.wait()):
        for copy, needed in copies:
            if needed is True:
                act(copy)
            else:
                pl.when(needed)(functools.partial(act, copy))


def pack(chips, scales, cache, units, capacity):
    requests, columns, positions = cache.shape
    half = columns // 2
    window = positions // UNIT + 1
    tail = capacity * scales.shape[1]
    smem = pl.BlockSpec(memory_space=pltpu.SMEM)
    vmem = pl.BlockSpec(memory_space=pltpu.VMEM)
    hbm = pl.BlockSpec(memory_space=pl.ANY)
    lanes = 2 * UNIT
    return pl.pallas_call(
        pack_kernel,
        in_specs=[hbm] * 4 + [vmem, hbm],
        out_specs=[hbm] * 5 + [smem] * 2,
        out_shape=[jax.ShapeDtypeStruct((tail + units * half, lanes), jnp.bfloat16)] * 5
        + [jax.ShapeDtypeStruct((1,), jnp.int32), jax.ShapeDtypeStruct((4, requests), jnp.int32)],
        scratch_shapes=[
            pltpu.VMEM(cache.shape, jnp.bfloat16),
            pltpu.VMEM((4, tail + (units + SPLIT) * half, lanes), jnp.bfloat16),
            pltpu.VMEM((4, tail, positions), jnp.float32),
            pltpu.SMEM((4,), jnp.int32),
            pltpu.SMEM((4,), jnp.int32),
            pltpu.SMEM((4,) + chips[0].shape, jnp.int32),
            pltpu.SMEM((16,), jnp.int32),
            pltpu.SemaphoreType.DMA((4,)),
            pltpu.SemaphoreType.DMA((5, len(SEGMENTS))),
            pltpu.SemaphoreType.DMA((4,)),
        ],
        compiler_params=pltpu.CompilerParams(vmem_limit_bytes=24 * MIB),
        cost_estimate=pl.CostEstimate(flops=2 * requests * half * 256 * 384, bytes_accessed=8 * MIB, transcendentals=0),
    )(*chips, scales, cache)


def clear_kernel(facts_ref, out_ref, starts, counts, zeros, sem):
    experts = 4
    requests = facts_ref.shape[1]
    capacity = out_ref.shape[0] // experts
    me = lax.axis_index("expert")
    zeros[...] = jnp.zeros(zeros.shape, zeros.dtype)

    def scan(k, cleared):
        def note(i, carry):
            rank, end = carry
            mine = facts_ref[k, i] >> FACT_BITS == me
            length = facts_ref[k, i] & (FACT - 1)

            @pl.when(mine)
            def _():
                starts[k, rank] = end
                counts[k, rank] = length

            return (jnp.where(mine, rank + 1, rank), jnp.where(mine, end + length, end))

        ranks, end = lax.fori_loop(0, requests, note, (0, 0))
        starts[k, capacity] = ranks
        counts[k, capacity] = (end + UNIT - 1) >> UNIT_BITS

        def clear(rank, _):
            starts[k, rank] = 0
            counts[k, rank] = 0
            slot = ((me - k) & (experts - 1)) * capacity + rank
            pltpu.make_async_copy(zeros, out_ref.at[slot], sem).start()
            return 0

        lax.fori_loop(ranks, capacity, clear, 0)
        return cleared + capacity - ranks

    def done(_, carry):
        pltpu.make_async_copy(zeros, out_ref.at[0], sem).wait()
        return carry

    lax.fori_loop(0, lax.fori_loop(0, experts, scan, 0), done, 0)


def clear(facts, capacity, columns, positions):
    smem = pl.BlockSpec(memory_space=pltpu.SMEM)
    table = jax.ShapeDtypeStruct((4, capacity + 1), jnp.int32)
    return pl.pallas_call(
        clear_kernel,
        in_specs=[smem],
        out_specs=[pl.BlockSpec(memory_space=pl.ANY), smem, smem],
        out_shape=[jax.ShapeDtypeStruct((4 * capacity, columns, positions), jnp.bfloat16), table, table],
        scratch_shapes=[pltpu.VMEM((columns, positions), jnp.bfloat16), pltpu.SemaphoreType.DMA],
        compiler_params=pltpu.CompilerParams(vmem_limit_bytes=8 * MIB),
        cost_estimate=pl.CostEstimate(flops=0, bytes_accessed=3 * MIB, transcendentals=0),
    )(facts)


def unpack_kernel(last, late, group, starts, counts, *refs):
    ways = [way for way in range(5) if last or way not in late]
    got = dict(zip(ways, refs))
    out_ref, scales_ref = refs[len(ways) + 1], refs[len(ways) + 2] if last else None
    held, stage, tails, sem = refs[-4:]
    experts = 4
    capacity = out_ref.shape[0] // experts
    columns, positions = out_ref.shape[1], out_ref.shape[2]
    half = columns // 2
    tail = tails.shape[1]
    blocks = tail // capacity
    window = positions // UNIT
    me = lax.axis_index("expert")

    def rows_of(unit):
        return pl.ds(pl.multiple_of(unit * half, 16), half)

    def units_of(unit):
        return pl.ds(pl.multiple_of(tail + unit * half, 16), half)

    def source_of(k):
        return (me - k) & (experts - 1)

    def came(k, way):
        return pick(source_of(k), targets_of(way)) == me

    gap, position = stream_gap("window", positions, 0, window)
    gap_behind, _ = stream_gap("window", positions, window, 1)

    def write(k, rank):
        return pltpu.make_async_copy(stage.at[k, rank], out_ref.at[source_of(k) * capacity + rank], sem)

    def put_stream(k, written):
        used, ranks = counts[k, capacity], starts[k, capacity]
        is_late = functools.reduce(jnp.logical_or, [came(k, way) for way in late])
        ranks = jnp.where(is_late == last, ranks, 0)
        for way in ways:
            later = jnp.logical_and(k == 0, pick(me, [int(way == staying(e)[1]) for e in range(experts)]) == 1)
            low = jnp.where(later, SPLIT, 0)
            high = jnp.where(jnp.logical_and(k == 0, jnp.logical_not(later)), jnp.minimum(used, SPLIT), used)

            @pl.when(came(k, way))
            def _():
                if last:

                    @pl.when(jnp.logical_not(later))
                    def _():
                        tails[k] = got[way][:tail, :].astype(jnp.float32)

                def move_unit(u, _):
                    held[k, rows_of(u), :] = got[way][units_of(u - low), :]
                    return 0

                lax.fori_loop(low, jnp.where(ranks > 0, high, low), move_unit, 0)

        for j in range(window):
            held[k, rows_of(used + j), :] = jnp.zeros((half, 2 * UNIT), jnp.bfloat16)

        def placed(rank):
            filled = rank < ranks
            start, length = jnp.where(filled, starts[k, rank], 0), jnp.where(filled, counts[k, rank], 0)
            return start >> UNIT_BITS, start & (UNIT - 1), length

        def put(at, _):
            for rank in range(group):
                rank = group * at + rank
                unit, shift, length = placed(rank)
                move = moving(gap, position, shift, length)
                seen = jnp.concatenate([held[k, rows_of(unit + j), :] for j in range(window)], axis=1)
                moved = jnp.dot(seen, move, preferred_element_type=jnp.float32).astype(jnp.bfloat16)
                stage[k, rank, :half, :] = moved[:, :positions]
                stage[k, rank, half:, :] = moved[:, positions:]

            def put_behind(rank, _):
                unit, shift, length = placed(rank)

                @pl.when(shift + length > window * UNIT)
                def _():
                    move = moving(gap_behind, position, shift, length)
                    seen = held[k, rows_of(unit + window), :]
                    moved = jnp.dot(seen, move, preferred_element_type=jnp.float32).astype(jnp.bfloat16)
                    stage[k, rank, :half, :] += moved[:, :positions]
                    stage[k, rank, half:, :] += moved[:, positions:]

                @pl.when(rank < ranks)
                def _():
                    write(k, rank).start()

                return 0

            lax.fori_loop(group * at, group * at + group, put_behind, 0)
            return 0

        lax.fori_loop(0, (ranks + group - 1) // group, put, 0)
        if last:
            for rank in range(capacity):
                scales = tails[k, rank * blocks : (rank + 1) * blocks, :]
                scales_ref[source_of(k) * capacity + rank] = scales.astype(jnp.bfloat16)
        return written + ranks

    def done(_, carry):
        write(0, 0).wait()
        return carry

    lax.fori_loop(0, lax.fori_loop(0, experts, put_stream, 0), done, 0)


def unpack(last, late, starts, counts, got, owned, units, blocks):
    slots, columns, positions = owned.shape
    capacity, half = slots // 4, columns // 2
    window = positions // UNIT + 1
    smem = pl.BlockSpec(memory_space=pltpu.SMEM)
    vmem = pl.BlockSpec(memory_space=pltpu.VMEM)
    hbm = pl.BlockSpec(memory_space=pl.ANY)
    got = [part for way, part in enumerate(got) if last or way not in late]
    outs = [jax.ShapeDtypeStruct(owned.shape, owned.dtype)]
    if last:
        outs.append(jax.ShapeDtypeStruct((slots, blocks, positions), owned.dtype))
    return pl.pallas_call(
        functools.partial(unpack_kernel, last, late, 2 if last else 1),
        in_specs=[smem] * 2 + [vmem] * len(got) + [hbm],
        out_specs=[hbm, vmem][: len(outs)],
        out_shape=outs,
        input_output_aliases={2 + len(got): 0},
        scratch_shapes=[
            pltpu.VMEM((4, (units + window) * half, 2 * UNIT), jnp.bfloat16),
            pltpu.VMEM((4, capacity, columns, positions), jnp.bfloat16),
            pltpu.VMEM((4, capacity * blocks, positions), jnp.float32),
            pltpu.SemaphoreType.DMA,
        ],
        compiler_params=pltpu.CompilerParams(vmem_limit_bytes=24 * MIB),
        cost_estimate=pl.CostEstimate(flops=2 * 16 * half * 256 * 384, bytes_accessed=6 * MIB, transcendentals=0),
    )(starts, counts, *got, owned)


def size_sets():
    branches = []
    for hot in range(4):
        one, two = (2, 3) if hot < 2 else (1, 0)
        for paired, *sizes in AT_END if hot in (0, 3) else IN_MIDDLE:
            swaps = [{hot, one}, {hot, two}, {hot ^ 1, one}, {hot ^ 1, two}]
            branches.append((hot, [paired] + [sizes[swaps.index(set(swap))] for swap in SWAPS]))
    return branches + [(None, [16] * 5)]


BRANCHES = size_sets()


def choose(chips_ref, me, other, loads_ref, out_ref, facts_ref):
    experts = 4
    requests = chips_ref.shape[2]
    for k in range(experts):
        chip = chips_ref.at[k]
        most = [jnp.int32(0)] * experts
        for section in range(2):

            def add(i, sums):
                fact = chip[section, i]
                owner, length = fact >> FACT_BITS, fact & (FACT - 1)
                part = length << ((owner >> 1) << 4)
                odd = (owner & 1) == 1
                return (sums[0] + jnp.where(odd, 0, part), sums[1] + jnp.where(odd, part, 0))

            even, odd = lax.fori_loop(0, requests, add, (jnp.int32(0), jnp.int32(0)), unroll=8)
            for o, sums in enumerate((even, odd, even >> 16, odd >> 16)):
                most[o] = jnp.maximum(most[o], ((sums & 0xFFFF) + UNIT - 1) >> UNIT_BITS)
        for o in range(experts):
            loads_ref[((me - k) & (experts - 1)) * experts + o] = most[o]

        def keep(i, _):
            facts_ref[k, i] = chip[other, i]
            return 0

        lax.fori_loop(0, requests, keep, 0, unroll=8)
    load = [[loads_ref[source * experts + o] for o in range(experts)] for source in range(experts)]
    hot, highest = jnp.int32(0), jnp.int32(-1)
    for o in range(experts):
        worst = functools.reduce(jnp.maximum, [load[source][o] for source in range(experts) if source != o])
        hot = jnp.where(worst > highest, o, hot)
        highest = jnp.maximum(worst, highest)
    needs = []
    for way in range(5):
        need = jnp.int32(0)
        for source, target in enumerate(targets_of(way)):
            if source != target:
                need = jnp.maximum(need, load[source][target])
            elif way == staying(source)[0]:
                need = jnp.maximum(need, jnp.minimum(load[source][source], SPLIT))
            else:
                need = jnp.maximum(need, load[source][source] - SPLIT)
        needs.append(need)
    branch = jnp.int32(len(BRANCHES) - 1)
    for at in range(len(BRANCHES) - 2, -1, -1):
        h, sizes = BRANCHES[at]
        fits = functools.reduce(jnp.logical_and, [need <= size for need, size in zip(needs, sizes)], hot == h)
        branch = jnp.where(fits, at, branch)
    out_ref[0] = branch


def crossed(targets):
    return [(source * 2 + s, target * 2 + 1 - s) for source, target in enumerate(targets) for s in range(2)]


def by_halves(branches, index, operands):
    def run(low, high, operands):
        if high - low == 1:
            return branches[low](operands)
        middle = (low + high) // 2
        return lax.cond(
            index < middle, functools.partial(run, low, middle), functools.partial(run, middle, high), operands
        )

    return run(0, len(branches), operands)


def cut_kernel(*refs):
    streams, outs, sem = refs[:5], refs[5:10], refs[10]
    copies = [
        pltpu.make_async_copy(stream.at[pl.ds(0, out.shape[0])], out, sem.at[way])
        for way, (stream, out) in enumerate(zip(streams, outs))
    ]
    for copy in copies:
        copy.start()
    for copy in copies:
        copy.wait()


def cut(streams, rows):
    return pl.pallas_call(
        cut_kernel,
        in_specs=[pl.BlockSpec(memory_space=pl.ANY)] * 5,
        out_specs=[pl.BlockSpec(memory_space=pltpu.VMEM)] * 5,
        out_shape=[jax.ShapeDtypeStruct((row, stream.shape[1]), stream.dtype) for row, stream in zip(rows, streams)],
        scratch_shapes=[pltpu.SemaphoreType.DMA((5,))],
        compiler_params=pltpu.CompilerParams(vmem_limit_bytes=8 * MIB),
    )(*streams)


def slot_layout(owner, experts, capacity):
    requests = owner.shape[0]
    indices = jnp.arange(requests, dtype=jnp.int32)
    earlier = indices[None, :] < indices[:, None]
    same_owner = owner[:, None] == owner[None, :]
    arrival_rank = jnp.sum(jnp.logical_and(same_owner, earlier), axis=1)
    target = owner * capacity + arrival_rank
    routing = target[None, :] == jnp.arange(experts * capacity, dtype=jnp.int32)[:, None]
    filled = jnp.any(routing, axis=1)
    source = jnp.sum(jnp.where(routing, indices[None, :], 0), axis=1)
    return (filled, source)


def pick_slots(values, filled, source):
    zero_value = jnp.zeros((), values.dtype)
    return jnp.where(filled[:, None, None], jnp.take(values, source, axis=0), zero_value)


def on_device(
    res_cache,
    res_scales,
    res_lengths,
    res_query,
    new_cache,
    new_scales,
    new_lengths,
    new_query,
    owner,
):
    experts = lax.axis_size("expert")
    sections = lax.axis_size("segment")
    requests, positions, columns = new_cache.shape
    capacity = max(2, 2 * requests // experts)
    swap = [(0, 1), (1, 0)]
    cache_t = jnp.transpose(new_cache, (0, 2, 1))
    res_inputs = (jnp.transpose(res_query, (0, 2, 1)), jnp.transpose(res_cache, (0, 2, 1)), res_scales, res_lengths)
    inputs = (res_inputs, (jnp.transpose(new_query, (0, 2, 1)), cache_t, new_scales, new_lengths))

    def attention(res_inputs, new_inputs):
        return attend(*res_inputs), attend(*new_inputs)

    if experts != 4 or sections != 2 or capacity * positions != 16 * UNIT or positions != 2 * UNIT or columns % 32:
        live_rows = jnp.arange(positions)[None, :] < new_lengths[:, None]
        zero_value = jnp.zeros((), jnp.bfloat16)
        filled, source = slot_layout(owner, experts, capacity)
        send_cache = pick_slots(jnp.where(live_rows[:, :, None], new_cache, zero_value), filled, source)
        send_scales = pick_slots(jnp.where(live_rows[:, None, :], new_scales, zero_value), filled, source)
        got_cache = lax.all_to_all(send_cache, "expert", split_axis=0, concat_axis=0, tiled=True)
        got_scales = lax.all_to_all(send_scales, "expert", split_axis=0, concat_axis=0, tiled=True)
        owned_cache, owned_scales = lax.ppermute((got_cache, got_scales), "segment", swap)
        return (*attention(*inputs), owned_cache, owned_scales)

    section = lax.axis_index("segment")
    units, half = capacity * positions // UNIT, columns // 2
    blocks = new_scales.shape[1]
    facts = owner * FACT + new_lengths
    sibling = lax.ppermute(facts, "segment", swap)
    chip = jnp.where(section == 0, jnp.stack([facts, sibling]), jnp.stack([sibling, facts]))
    chips = [chip] + [lax.ppermute(chip, "expert", [(e, (e + k) % 4) for e in range(4)]) for k in range(1, 4)]
    *streams, branch, facts = pack(chips, new_scales, cache_t, units, capacity)

    def take(hot, sizes):
        late = [way for way in range(1, 5) if (hot or 0) in SWAPS[way - 1]]

        def run(operands):
            streams, facts, *inputs = operands
            parts = cut(streams, [capacity * blocks + size * half for size in sizes])
            got = [
                lax.ppermute(part, ("expert", "segment"), crossed(targets_of(way))) for way, part in enumerate(parts)
            ]
            owned, starts, counts = clear(facts, capacity, columns, positions)
            (owned,) = unpack(False, late, starts, counts, got, owned, units, blocks)
            return (*attention(*inputs), *unpack(True, late, starts, counts, got, owned, units, blocks))

        return run

    branches = [take(*branch) for branch in BRANCHES]
    res_context, new_context, owned, owned_scales = by_halves(branches, branch[0], (streams, facts, *inputs))
    return (res_context, new_context, jnp.transpose(owned, (0, 2, 1)), owned_scales)


def solution(mesh):
    placed = (
        P(("group", "expert", "segment", "attn"), None, None),
        P(("group", "expert", "segment", "attn"), None, None),
        P(("group", "expert", "segment", "attn")),
        P(("group", "expert", "segment", "attn"), None, None),
        P(("group", "expert", "segment", "attn"), None, None),
        P(("group", "expert", "segment", "attn"), None, None),
        P(("group", "expert", "segment", "attn")),
        P(("group", "expert", "segment", "attn"), None, None),
        P(("group", "expert", "segment", "attn")),
    )
    return jax.shard_map(
        on_device,
        mesh=mesh,
        in_specs=placed,
        out_specs=(
            P(("group", "expert", "segment", "attn"), None, None),
            P(("group", "expert", "segment", "attn"), None, None),
            P(("group", "expert", "segment", "attn"), None, None),
            P(("group", "expert", "segment", "attn"), None, None),
        ),
        check_vma=False,
    )
```

```python
import functools
import jax
import jax.numpy as jnp
from jax import lax
from jax.experimental import pallas as pl
from jax.experimental.pallas import tpu as pltpu
from jax.sharding import PartitionSpec as P

LATENT = 512
BLOCK = 128
UNIT_BITS = 6
UNIT = 1 << UNIT_BITS
SPLIT = 6
SEGMENTS = (0, 6, 10)
AT_END = ((14, 11, 11, 6, 8), (14, 12, 12, 7, 7), (13, 11, 14, 10, 6), (13, 14, 13, 8, 8))
IN_MIDDLE = ((12, 13, 11, 6, 7), (12, 11, 13, 7, 7), (14, 12, 11, 10, 10), (14, 14, 14, 8, 8))
SWAPS = ((0, 2), (0, 3), (1, 2), (1, 3))
FACT_BITS = 8
FACT = 1 << FACT_BITS

softmax_scale = 192.0 ** (-0.5)
MIB = 1 << 20


def attend_kernel(lengths_ref, query_ref, cache_ref, scales_ref, out_ref, factors_ref):
    blocks = scales_ref.shape[1]
    positions = cache_ref.shape[2]
    contract_rows = (((0,), (0,)), ((), ()))
    contract_positions = (((1,), (1,)), ((), ()))
    length = lengths_ref[pl.program_id(0)]

    def block(b):
        return pl.ds(pl.multiple_of(b * BLOCK, BLOCK), BLOCK)

    for b in range(blocks):
        factors_ref[b] = scales_ref[0, b : b + 1, :].astype(jnp.float32)

    def add(b, scores):
        part = lax.dot_general(
            query_ref[0, block(b), :], cache_ref[0, block(b), :], contract_rows, preferred_element_type=jnp.float32
        )
        return scores + part * factors_ref[b]

    scores = lax.dot_general(
        query_ref[0, LATENT:, :], cache_ref[0, LATENT:, :], contract_rows, preferred_element_type=jnp.float32
    )
    scores = lax.fori_loop(0, blocks, add, scores)
    live = lax.broadcasted_iota(jnp.int32, (1, positions), 1) < length
    scores = jnp.where(live, scores * softmax_scale, -jnp.inf)
    exponent = jnp.exp(scores - jnp.max(scores, axis=-1, keepdims=True))
    probabilities = exponent * (1.0 / jnp.sum(exponent, axis=-1, keepdims=True))

    def put(b, _):
        out_ref[0, :, block(b)] = lax.dot_general(
            (probabilities * factors_ref[b]).astype(jnp.bfloat16),
            cache_ref[0, block(b), :],
            contract_positions,
            preferred_element_type=jnp.float32,
        ).astype(jnp.bfloat16)
        return 0

    lax.fori_loop(0, blocks, put, 0)


def attend(query, cache, scales, lengths):
    requests, columns, heads = query.shape
    positions = cache.shape[2]
    return pl.pallas_call(
        attend_kernel,
        grid=(requests,),
        in_specs=[
            pl.BlockSpec(memory_space=pltpu.SMEM),
            pl.BlockSpec((1, columns, heads), lambda i: (i, 0, 0)),
            pl.BlockSpec((1, columns, positions), lambda i: (i, 0, 0)),
            pl.BlockSpec((1, scales.shape[1], positions), lambda i: (i, 0, 0)),
        ],
        out_specs=pl.BlockSpec((1, heads, LATENT), lambda i: (i, 0, 0)),
        out_shape=jax.ShapeDtypeStruct((requests, heads, LATENT), jnp.bfloat16),
        scratch_shapes=[pltpu.VMEM((scales.shape[1], 1, positions), jnp.float32)],
        compiler_params=pltpu.CompilerParams(vmem_limit_bytes=16 * MIB),
        cost_estimate=pl.CostEstimate(
            flops=4 * requests * heads * positions * columns,
            bytes_accessed=2 * requests * (heads * (columns + LATENT) + positions * columns),
            transcendentals=requests * heads * positions,
        ),
    )(lengths, query, cache, scales)


def stream_gap(rows, positions, first, units):
    window = units * 2 * UNIT
    shape = (window, 2 * positions) if rows == "window" else (2 * positions, window)
    down, across = lax.broadcasted_iota(jnp.int32, shape, 0), lax.broadcasted_iota(jnp.int32, shape, 1)
    lane, own = (down, across) if rows == "window" else (across, down)
    within = lane % (2 * UNIT)
    place = (lane // (2 * UNIT) + first) * UNIT + within % UNIT
    meet = within // UNIT == own // positions
    side = (1, 2 * positions) if rows == "window" else (2 * positions, 1)
    position = lax.broadcasted_iota(jnp.int32, side, 1 if rows == "window" else 0) % positions
    return jnp.where(meet, place - own % positions, -512).astype(jnp.bfloat16), position


def moving(gap, position, shift, length):
    wanted = jnp.where(position < length, shift, 512).astype(jnp.bfloat16)
    return jnp.where(gap == wanted, jnp.ones((), jnp.bfloat16), jnp.zeros((), jnp.bfloat16))


def targets_of(way):
    if way == 0:
        return [e ^ 1 for e in range(4)]
    a, b = SWAPS[way - 1]
    return [b if e == a else a if e == b else e for e in range(4)]


def staying(e):
    return [way for way in range(5) if targets_of(way)[e] == e]


def pick(index, values):
    value = jnp.int32(values[0])
    for at in range(1, len(values)):
        value = jnp.where(index == at, values[at], value)
    return value


def pack_kernel(c0, c1, c2, c3, scales_ref, cache_ref, *refs):
    outs, branch_ref, facts_ref = refs[:5], refs[5], refs[6]
    held, acc, slots, ends, ranks, chips_ref, loads_ref, in_sem, out_sem, chip_sem = refs[7:]
    experts = 4
    requests, columns, positions = cache_ref.shape
    blocks = scales_ref.shape[1]
    half = columns // 2
    tail = slots.shape[1]
    window = positions // UNIT + 1
    me = lax.axis_index("expert")
    parts = in_sem.shape[0]
    share = requests // parts

    def rows_of(unit):
        return pl.ds(pl.multiple_of(tail + unit * half, 16), half)

    def fetch(part):
        here = pl.ds(part * share, share)
        return pltpu.make_async_copy(cache_ref.at[here], held.at[here], in_sem.at[part])

    chips = [pltpu.make_async_copy(chip, chips_ref.at[k], chip_sem.at[k]) for k, chip in enumerate((c0, c1, c2, c3))]
    for chip in chips:
        chip.start()
    for part in range(parts):
        fetch(part).start()
    for chip in chips:
        chip.wait()
    section = lax.axis_index("segment")
    choose(chips_ref, me, 1 - section, loads_ref, branch_ref, facts_ref)
    gap, position = stream_gap("request", positions, 0, window)
    for k in range(experts):
        ends[k] = 0
        ranks[k] = 0
        acc[k, rows_of(0), :] = jnp.zeros((half, 2 * UNIT), jnp.bfloat16)
    slots[...] = jnp.zeros(slots.shape, jnp.float32)
    live = lax.broadcasted_iota(jnp.int32, (blocks, positions), 1)

    def place(i, _):
        fact = chips_ref[0, section, i]
        k, length = fact >> FACT_BITS, fact & (FACT - 1)
        start, rank = ends[k], ranks[k]
        ends[k] = start + length
        ranks[k] = rank + 1
        slots[k, pl.ds(rank * blocks, blocks), :] = jnp.where(live < length, scales_ref[i].astype(jnp.float32), 0.0)
        unit, shift = start >> UNIT_BITS, start & (UNIT - 1)
        move = moving(gap, position, shift, length)
        both = jnp.concatenate([held[i, :half, :], held[i, half:, :]], axis=1)
        moved = jnp.dot(both, move, preferred_element_type=jnp.float32).astype(jnp.bfloat16)
        acc[k, rows_of(unit), :] += moved[:, : 2 * UNIT]
        for j in range(1, window):
            acc[k, rows_of(unit + j), :] = moved[:, 2 * UNIT * j : 2 * UNIT * (j + 1)]
        return 0

    for part in range(parts):
        fetch(part).wait()
        lax.fori_loop(part * share, (part + 1) * share, place, 0, unroll=True)
    acc[:, :tail, :] = slots[...].astype(jnp.bfloat16)
    copies = []
    for way, out in enumerate(outs):
        k = pick(me, targets_of(way))
        skipped = pick(me, [SPLIT if way == staying(e)[1] else 0 for e in range(experts)])
        for at, first in enumerate(SEGMENTS):
            low = tail + first * half if first else 0
            high = tail + SEGMENTS[at + 1] * half if at + 1 < len(SEGMENTS) else out.shape[0]
            here = pl.ds(pl.multiple_of(low + skipped * half, 16), high - low)
            copy = pltpu.make_async_copy(acc.at[k, here], out.at[pl.ds(low, high - low)], out_sem.at[way, at])
            copies.append((copy, True if first == 0 else ends[k] > (first + skipped) * UNIT))
    for act in (lambda copy: copy.start(), lambda copy: copy.wait()):
        for copy, needed in copies:
            if needed is True:
                act(copy)
            else:
                pl.when(needed)(functools.partial(act, copy))


def pack(chips, scales, cache, units, capacity):
    requests, columns, positions = cache.shape
    half = columns // 2
    window = positions // UNIT + 1
    tail = capacity * scales.shape[1]
    smem = pl.BlockSpec(memory_space=pltpu.SMEM)
    vmem = pl.BlockSpec(memory_space=pltpu.VMEM)
    hbm = pl.BlockSpec(memory_space=pl.ANY)
    lanes = 2 * UNIT
    return pl.pallas_call(
        pack_kernel,
        in_specs=[hbm] * 4 + [vmem, hbm],
        out_specs=[hbm] * 5 + [smem] * 2,
        out_shape=[jax.ShapeDtypeStruct((tail + units * half, lanes), jnp.bfloat16)] * 5
        + [jax.ShapeDtypeStruct((1,), jnp.int32), jax.ShapeDtypeStruct((4, requests), jnp.int32)],
        scratch_shapes=[
            pltpu.VMEM(cache.shape, jnp.bfloat16),
            pltpu.VMEM((4, tail + (units + SPLIT) * half, lanes), jnp.bfloat16),
            pltpu.VMEM((4, tail, positions), jnp.float32),
            pltpu.SMEM((4,), jnp.int32),
            pltpu.SMEM((4,), jnp.int32),
            pltpu.SMEM((4,) + chips[0].shape, jnp.int32),
            pltpu.SMEM((16,), jnp.int32),
            pltpu.SemaphoreType.DMA((4,)),
            pltpu.SemaphoreType.DMA((5, len(SEGMENTS))),
            pltpu.SemaphoreType.DMA((4,)),
        ],
        compiler_params=pltpu.CompilerParams(vmem_limit_bytes=24 * MIB),
        cost_estimate=pl.CostEstimate(flops=2 * requests * half * 256 * 384, bytes_accessed=8 * MIB, transcendentals=0),
    )(*chips, scales, cache)


def clear_kernel(facts_ref, out_ref, starts, counts, zeros, sem):
    experts = 4
    requests = facts_ref.shape[1]
    capacity = out_ref.shape[0] // experts
    me = lax.axis_index("expert")
    zeros[...] = jnp.zeros(zeros.shape, zeros.dtype)

    def scan(k, cleared):
        def note(i, carry):
            rank, end = carry
            mine = facts_ref[k, i] >> FACT_BITS == me
            length = facts_ref[k, i] & (FACT - 1)

            @pl.when(mine)
            def _():
                starts[k, rank] = end
                counts[k, rank] = length

            return (jnp.where(mine, rank + 1, rank), jnp.where(mine, end + length, end))

        ranks, end = lax.fori_loop(0, requests, note, (0, 0))
        starts[k, capacity] = ranks
        counts[k, capacity] = (end + UNIT - 1) >> UNIT_BITS

        def clear(rank, _):
            starts[k, rank] = 0
            counts[k, rank] = 0
            slot = ((me - k) & (experts - 1)) * capacity + rank
            pltpu.make_async_copy(zeros, out_ref.at[slot], sem).start()
            return 0

        lax.fori_loop(ranks, capacity, clear, 0)
        return cleared + capacity - ranks

    def done(_, carry):
        pltpu.make_async_copy(zeros, out_ref.at[0], sem).wait()
        return carry

    lax.fori_loop(0, lax.fori_loop(0, experts, scan, 0), done, 0)


def clear(facts, capacity, columns, positions):
    smem = pl.BlockSpec(memory_space=pltpu.SMEM)
    table = jax.ShapeDtypeStruct((4, capacity + 1), jnp.int32)
    return pl.pallas_call(
        clear_kernel,
        in_specs=[smem],
        out_specs=[pl.BlockSpec(memory_space=pl.ANY), smem, smem],
        out_shape=[jax.ShapeDtypeStruct((4 * capacity, columns, positions), jnp.bfloat16), table, table],
        scratch_shapes=[pltpu.VMEM((columns, positions), jnp.bfloat16), pltpu.SemaphoreType.DMA],
        compiler_params=pltpu.CompilerParams(vmem_limit_bytes=8 * MIB),
        cost_estimate=pl.CostEstimate(flops=0, bytes_accessed=3 * MIB, transcendentals=0),
    )(facts)


def unpack_kernel(last, late, starts, counts, *refs):
    ways = [way for way in range(5) if last or way not in late]
    got = dict(zip(ways, refs))
    out_ref, scales_ref = refs[len(ways) + 1], refs[len(ways) + 2] if last else None
    held, stage, tails, sem = refs[-4:]
    experts = 4
    capacity = out_ref.shape[0] // experts
    columns, positions = out_ref.shape[1], out_ref.shape[2]
    half = columns // 2
    tail = tails.shape[1]
    blocks = tail // capacity
    reach = positions // UNIT + 1
    window = reach - 1 if last else reach
    me = lax.axis_index("expert")

    def rows_of(unit):
        return pl.ds(pl.multiple_of(unit * half, 16), half)

    def units_of(unit):
        return pl.ds(pl.multiple_of(tail + unit * half, 16), half)

    def source_of(k):
        return (me - k) & (experts - 1)

    def came(k, way):
        return pick(source_of(k), targets_of(way)) == me

    gap, position = stream_gap("window", positions, 0, window)
    gap_behind, _ = stream_gap("window", positions, window, 1)

    def write(k, rank):
        return pltpu.make_async_copy(stage.at[k, rank], out_ref.at[source_of(k) * capacity + rank], sem)

    def put_stream(k, written):
        used, ranks = counts[k, capacity], starts[k, capacity]
        is_late = functools.reduce(jnp.logical_or, [came(k, way) for way in late])
        ranks = jnp.where(is_late == last, ranks, 0)
        for way in ways:
            later = jnp.logical_and(k == 0, pick(me, [int(way == staying(e)[1]) for e in range(experts)]) == 1)
            low = jnp.where(later, SPLIT, 0)
            high = jnp.where(jnp.logical_and(k == 0, jnp.logical_not(later)), jnp.minimum(used, SPLIT), used)

            @pl.when(came(k, way))
            def _():
                if last:

                    @pl.when(jnp.logical_not(later))
                    def _():
                        tails[k] = got[way][:tail, :].astype(jnp.float32)

                def move_unit(u, _):
                    held[k, rows_of(u), :] = got[way][units_of(u - low), :]
                    return 0

                lax.fori_loop(low, jnp.where(ranks > 0, high, low), move_unit, 0)

        for j in range(reach):
            held[k, rows_of(used + j), :] = jnp.zeros((half, 2 * UNIT), jnp.bfloat16)

        def put_rows(rank, unit, units, move, low, rows, add):
            here = [pl.ds(pl.multiple_of((unit + j) * half + low, 16), rows) for j in range(units)]
            seen = jnp.concatenate([held[k, each, :] for each in here], axis=1)
            moved = jnp.dot(seen, move, preferred_element_type=jnp.float32).astype(jnp.bfloat16)
            for side in range(2):
                there = pl.ds(pl.multiple_of(side * half + low, 16), rows)
                part = moved[:, side * positions : (side + 1) * positions]
                stage[k, rank, there, :] = stage[k, rank, there, :] + part if add else part

        def in_chunks(rank, unit, units, move, add):
            rows = half // 3

            def chunk(at, _):
                put_rows(rank, unit, units, move, at * rows, rows, add)
                return 0

            lax.fori_loop(0, 3, chunk, 0)

        def put(rank, _):
            start, length = starts[k, rank], counts[k, rank]
            unit, shift = start >> UNIT_BITS, start & (UNIT - 1)
            move = moving(gap, position, shift, length)
            if last:
                put_rows(rank, unit, window, move, 0, half, False)

                @pl.when(shift + length > window * UNIT)
                def _():
                    in_chunks(rank, unit + window, 1, moving(gap_behind, position, shift, length), True)

            else:
                in_chunks(rank, unit, window, move, False)
            write(k, rank).start()
            return 0

        lax.fori_loop(0, ranks, put, 0)
        if last:
            for rank in range(capacity):
                scales = tails[k, rank * blocks : (rank + 1) * blocks, :]
                scales_ref[source_of(k) * capacity + rank] = scales.astype(jnp.bfloat16)
        return written + ranks

    def done(_, carry):
        write(0, 0).wait()
        return carry

    lax.fori_loop(0, lax.fori_loop(0, experts, put_stream, 0), done, 0)


def unpack(last, late, starts, counts, got, owned, units, blocks):
    slots, columns, positions = owned.shape
    capacity, half = slots // 4, columns // 2
    window = positions // UNIT + 1
    smem = pl.BlockSpec(memory_space=pltpu.SMEM)
    vmem = pl.BlockSpec(memory_space=pltpu.VMEM)
    hbm = pl.BlockSpec(memory_space=pl.ANY)
    got = [part for way, part in enumerate(got) if last or way not in late]
    outs = [jax.ShapeDtypeStruct(owned.shape, owned.dtype)]
    if last:
        outs.append(jax.ShapeDtypeStruct((slots, blocks, positions), owned.dtype))
    return pl.pallas_call(
        functools.partial(unpack_kernel, last, late),
        in_specs=[smem] * 2 + [vmem] * len(got) + [hbm],
        out_specs=[hbm, vmem][: len(outs)],
        out_shape=outs,
        input_output_aliases={2 + len(got): 0},
        scratch_shapes=[
            pltpu.VMEM((4, (units + window + 1) * half, 2 * UNIT), jnp.bfloat16),
            pltpu.VMEM((4, capacity, columns, positions), jnp.bfloat16),
            pltpu.VMEM((4, capacity * blocks, positions), jnp.float32),
            pltpu.SemaphoreType.DMA,
        ],
        compiler_params=pltpu.CompilerParams(vmem_limit_bytes=24 * MIB),
        cost_estimate=pl.CostEstimate(flops=2 * 16 * half * 256 * 384, bytes_accessed=6 * MIB, transcendentals=0),
    )(starts, counts, *got, owned)


def size_sets():
    branches = []
    for hot in range(4):
        one, two = (2, 3) if hot < 2 else (1, 0)
        for paired, *sizes in AT_END if hot in (0, 3) else IN_MIDDLE:
            swaps = [{hot, one}, {hot, two}, {hot ^ 1, one}, {hot ^ 1, two}]
            branches.append((hot, [paired] + [sizes[swaps.index(set(swap))] for swap in SWAPS]))
    return branches + [(None, [16] * 5)]


BRANCHES = size_sets()


def choose(chips_ref, me, other, loads_ref, out_ref, facts_ref):
    experts = 4
    requests = chips_ref.shape[2]
    for k in range(experts):
        chip = chips_ref.at[k]
        most = [jnp.int32(0)] * experts
        for section in range(2):

            def add(i, sums):
                fact = chip[section, i]
                owner, length = fact >> FACT_BITS, fact & (FACT - 1)
                part = length << ((owner >> 1) << 4)
                odd = (owner & 1) == 1
                return (sums[0] + jnp.where(odd, 0, part), sums[1] + jnp.where(odd, part, 0))

            even, odd = lax.fori_loop(0, requests, add, (jnp.int32(0), jnp.int32(0)), unroll=8)
            for o, sums in enumerate((even, odd, even >> 16, odd >> 16)):
                most[o] = jnp.maximum(most[o], ((sums & 0xFFFF) + UNIT - 1) >> UNIT_BITS)
        for o in range(experts):
            loads_ref[((me - k) & (experts - 1)) * experts + o] = most[o]

        def keep(i, _):
            facts_ref[k, i] = chip[other, i]
            return 0

        lax.fori_loop(0, requests, keep, 0, unroll=8)
    load = [[loads_ref[source * experts + o] for o in range(experts)] for source in range(experts)]
    hot, highest = jnp.int32(0), jnp.int32(-1)
    for o in range(experts):
        worst = functools.reduce(jnp.maximum, [load[source][o] for source in range(experts) if source != o])
        hot = jnp.where(worst > highest, o, hot)
        highest = jnp.maximum(worst, highest)
    needs = []
    for way in range(5):
        need = jnp.int32(0)
        for source, target in enumerate(targets_of(way)):
            if source != target:
                need = jnp.maximum(need, load[source][target])
            elif way == staying(source)[0]:
                need = jnp.maximum(need, jnp.minimum(load[source][source], SPLIT))
            else:
                need = jnp.maximum(need, load[source][source] - SPLIT)
        needs.append(need)
    branch = jnp.int32(len(BRANCHES) - 1)
    for at in range(len(BRANCHES) - 2, -1, -1):
        h, sizes = BRANCHES[at]
        fits = functools.reduce(jnp.logical_and, [need <= size for need, size in zip(needs, sizes)], hot == h)
        branch = jnp.where(fits, at, branch)
    out_ref[0] = branch


def crossed(targets):
    return [(source * 2 + s, target * 2 + 1 - s) for source, target in enumerate(targets) for s in range(2)]


def by_halves(branches, index, operands):
    def run(low, high, operands):
        if high - low == 1:
            return branches[low](operands)
        middle = (low + high) // 2
        return lax.cond(
            index < middle, functools.partial(run, low, middle), functools.partial(run, middle, high), operands
        )

    return run(0, len(branches), operands)


def cut_kernel(tail, half, *refs):
    count = len(refs) // 2
    for stream, out in zip(refs[:count], refs[count:]):
        out[:tail, :] = stream[:tail, :]

        def move_unit(u, _):
            rows = pl.ds(pl.multiple_of(tail + u * half, 16), half)
            out[rows, :] = stream[rows, :]
            return 0

        lax.fori_loop(0, (out.shape[0] - tail) // half, move_unit, 0)


def cut(streams, sizes, tail, half):
    vmem = pl.BlockSpec(memory_space=pltpu.VMEM)
    return pl.pallas_call(
        functools.partial(cut_kernel, tail, half),
        in_specs=[vmem] * len(streams),
        out_specs=[vmem] * len(streams),
        out_shape=[jax.ShapeDtypeStruct((tail + size * half, streams[0].shape[1]), jnp.bfloat16) for size in sizes],
        compiler_params=pltpu.CompilerParams(vmem_limit_bytes=16 * MIB),
    )(*streams)


def slot_layout(owner, experts, capacity):
    requests = owner.shape[0]
    indices = jnp.arange(requests, dtype=jnp.int32)
    earlier = indices[None, :] < indices[:, None]
    same_owner = owner[:, None] == owner[None, :]
    arrival_rank = jnp.sum(jnp.logical_and(same_owner, earlier), axis=1)
    target = owner * capacity + arrival_rank
    routing = target[None, :] == jnp.arange(experts * capacity, dtype=jnp.int32)[:, None]
    filled = jnp.any(routing, axis=1)
    source = jnp.sum(jnp.where(routing, indices[None, :], 0), axis=1)
    return (filled, source)


def pick_slots(values, filled, source):
    zero_value = jnp.zeros((), values.dtype)
    return jnp.where(filled[:, None, None], jnp.take(values, source, axis=0), zero_value)


def on_device(
    res_cache,
    res_scales,
    res_lengths,
    res_query,
    new_cache,
    new_scales,
    new_lengths,
    new_query,
    owner,
):
    experts = lax.axis_size("expert")
    sections = lax.axis_size("segment")
    requests, positions, columns = new_cache.shape
    capacity = max(2, 2 * requests // experts)
    swap = [(0, 1), (1, 0)]
    cache_t = jnp.transpose(new_cache, (0, 2, 1))
    res_inputs = (jnp.transpose(res_query, (0, 2, 1)), jnp.transpose(res_cache, (0, 2, 1)), res_scales, res_lengths)
    inputs = (res_inputs, (jnp.transpose(new_query, (0, 2, 1)), cache_t, new_scales, new_lengths))

    def attention(res_inputs, new_inputs):
        return attend(*res_inputs), attend(*new_inputs)

    if experts != 4 or sections != 2 or capacity * positions != 16 * UNIT or positions != 2 * UNIT or columns % 32:
        live_rows = jnp.arange(positions)[None, :] < new_lengths[:, None]
        zero_value = jnp.zeros((), jnp.bfloat16)
        filled, source = slot_layout(owner, experts, capacity)
        send_cache = pick_slots(jnp.where(live_rows[:, :, None], new_cache, zero_value), filled, source)
        send_scales = pick_slots(jnp.where(live_rows[:, None, :], new_scales, zero_value), filled, source)
        got_cache = lax.all_to_all(send_cache, "expert", split_axis=0, concat_axis=0, tiled=True)
        got_scales = lax.all_to_all(send_scales, "expert", split_axis=0, concat_axis=0, tiled=True)
        owned_cache, owned_scales = lax.ppermute((got_cache, got_scales), "segment", swap)
        return (*attention(*inputs), owned_cache, owned_scales)

    section = lax.axis_index("segment")
    units, half = capacity * positions // UNIT, columns // 2
    blocks = new_scales.shape[1]
    facts = owner * FACT + new_lengths
    sibling = lax.ppermute(facts, "segment", swap)
    chip = jnp.where(section == 0, jnp.stack([facts, sibling]), jnp.stack([sibling, facts]))
    chips = [chip] + [lax.ppermute(chip, "expert", [(e, (e + k) % 4) for e in range(4)]) for k in range(1, 4)]
    *streams, branch, facts = pack(chips, new_scales, cache_t, units, capacity)

    def take(hot, sizes):
        late = [way for way in range(1, 5) if (hot or 0) in SWAPS[way - 1]]

        def run(operands):
            streams, facts, *inputs = operands
            parts = cut(streams, sizes, capacity * blocks, half)
            got = [
                lax.ppermute(part, ("expert", "segment"), crossed(targets_of(way))) for way, part in enumerate(parts)
            ]
            owned, starts, counts = clear(facts, capacity, columns, positions)
            (owned,) = unpack(False, late, starts, counts, got, owned, units, blocks)
            return (*attention(*inputs), *unpack(True, late, starts, counts, got, owned, units, blocks))

        return run

    branches = [take(*branch) for branch in BRANCHES]
    res_context, new_context, owned, owned_scales = by_halves(branches, branch[0], (streams, facts, *inputs))
    return (res_context, new_context, jnp.transpose(owned, (0, 2, 1)), owned_scales)


def solution(mesh):
    placed = (
        P(("group", "expert", "segment", "attn"), None, None),
        P(("group", "expert", "segment", "attn"), None, None),
        P(("group", "expert", "segment", "attn")),
        P(("group", "expert", "segment", "attn"), None, None),
        P(("group", "expert", "segment", "attn"), None, None),
        P(("group", "expert", "segment", "attn"), None, None),
        P(("group", "expert", "segment", "attn")),
        P(("group", "expert", "segment", "attn"), None, None),
        P(("group", "expert", "segment", "attn")),
    )
    return jax.shard_map(
        on_device,
        mesh=mesh,
        in_specs=placed,
        out_specs=(
            P(("group", "expert", "segment", "attn"), None, None),
            P(("group", "expert", "segment", "attn"), None, None),
            P(("group", "expert", "segment", "attn"), None, None),
            P(("group", "expert", "segment", "attn"), None, None),
        ),
        check_vma=False,
    )
```

```python
import functools
import jax
import jax.numpy as jnp
from jax import lax
from jax.experimental import pallas as pl
from jax.experimental.pallas import tpu as pltpu
from jax.sharding import PartitionSpec as P

LATENT = 512
BLOCK = 128
UNIT_BITS = 6
UNIT = 1 << UNIT_BITS
SPLIT = 6
SEGMENTS = (0, 6, 10)
AT_END = ((14, 11, 11, 6, 8), (14, 12, 12, 7, 7), (13, 11, 14, 10, 6), (13, 14, 13, 8, 8))
IN_MIDDLE = ((12, 13, 11, 6, 7), (12, 11, 13, 7, 7), (14, 12, 11, 10, 10), (14, 14, 14, 8, 8))
SWAPS = ((0, 2), (0, 3), (1, 2), (1, 3))
FACT_BITS = 8
FACT = 1 << FACT_BITS

softmax_scale = 192.0 ** (-0.5)
MIB = 1 << 20


def attend_kernel(lengths_ref, query_ref, cache_ref, scales_ref, out_ref, factors_ref):
    blocks = scales_ref.shape[1]
    positions = cache_ref.shape[2]
    contract_rows = (((0,), (0,)), ((), ()))
    contract_positions = (((1,), (1,)), ((), ()))
    length = lengths_ref[pl.program_id(0)]

    def block(b):
        return pl.ds(pl.multiple_of(b * BLOCK, BLOCK), BLOCK)

    for b in range(blocks):
        factors_ref[b] = scales_ref[0, b : b + 1, :].astype(jnp.float32)

    def add(b, scores):
        part = lax.dot_general(
            query_ref[0, block(b), :], cache_ref[0, block(b), :], contract_rows, preferred_element_type=jnp.float32
        )
        return scores + part * factors_ref[b]

    scores = lax.dot_general(
        query_ref[0, LATENT:, :], cache_ref[0, LATENT:, :], contract_rows, preferred_element_type=jnp.float32
    )
    scores = lax.fori_loop(0, blocks, add, scores)
    live = lax.broadcasted_iota(jnp.int32, (1, positions), 1) < length
    scores = jnp.where(live, scores * softmax_scale, -jnp.inf)
    exponent = jnp.exp(scores - jnp.max(scores, axis=-1, keepdims=True))
    probabilities = exponent * (1.0 / jnp.sum(exponent, axis=-1, keepdims=True))

    def put(b, _):
        out_ref[0, :, block(b)] = lax.dot_general(
            (probabilities * factors_ref[b]).astype(jnp.bfloat16),
            cache_ref[0, block(b), :],
            contract_positions,
            preferred_element_type=jnp.float32,
        ).astype(jnp.bfloat16)
        return 0

    lax.fori_loop(0, blocks, put, 0)


def attend(query, cache, scales, lengths):
    requests, columns, heads = query.shape
    positions = cache.shape[2]
    return pl.pallas_call(
        attend_kernel,
        grid=(requests,),
        in_specs=[
            pl.BlockSpec(memory_space=pltpu.SMEM),
            pl.BlockSpec((1, columns, heads), lambda i: (i, 0, 0)),
            pl.BlockSpec((1, columns, positions), lambda i: (i, 0, 0)),
            pl.BlockSpec((1, scales.shape[1], positions), lambda i: (i, 0, 0)),
        ],
        out_specs=pl.BlockSpec((1, heads, LATENT), lambda i: (i, 0, 0)),
        out_shape=jax.ShapeDtypeStruct((requests, heads, LATENT), jnp.bfloat16),
        scratch_shapes=[pltpu.VMEM((scales.shape[1], 1, positions), jnp.float32)],
        compiler_params=pltpu.CompilerParams(vmem_limit_bytes=16 * MIB),
        cost_estimate=pl.CostEstimate(
            flops=4 * requests * heads * positions * columns,
            bytes_accessed=2 * requests * (heads * (columns + LATENT) + positions * columns),
            transcendentals=requests * heads * positions,
        ),
    )(lengths, query, cache, scales)


def lanes_of(rows):
    return lax.broadcasted_iota(jnp.int32, (rows, 2 * UNIT), 1).astype(jnp.bfloat16)


def turned(value, by):
    return pltpu.roll(value, by & (2 * UNIT - 1), 1)


def targets_of(way):
    if way == 0:
        return [e ^ 1 for e in range(4)]
    a, b = SWAPS[way - 1]
    return [b if e == a else a if e == b else e for e in range(4)]


def staying(e):
    return [way for way in range(5) if targets_of(way)[e] == e]


def pick(index, values):
    value = jnp.int32(values[0])
    for at in range(1, len(values)):
        value = jnp.where(index == at, values[at], value)
    return value


def pack_kernel(c0, c1, c2, c3, scales_ref, cache_ref, *refs):
    outs, branch_ref, facts_ref = refs[:5], refs[5], refs[6]
    held, tiles, acc, slots, ends, ranks, chips_ref, loads_ref, in_sem, out_sem, chip_sem = refs[7:]
    experts = 4
    requests, columns, positions = cache_ref.shape
    blocks = scales_ref.shape[1]
    half = columns // 2
    tail = slots.shape[1]
    me = lax.axis_index("expert")
    parts = in_sem.shape[0]
    share = requests // parts

    def rows_of(unit):
        return pl.ds(pl.multiple_of(tail + unit * half, 16), half)

    def fetch(part):
        here = pl.ds(part * share, share)
        return pltpu.make_async_copy(cache_ref.at[here], held.at[here], in_sem.at[part])

    chips = [pltpu.make_async_copy(chip, chips_ref.at[k], chip_sem.at[k]) for k, chip in enumerate((c0, c1, c2, c3))]
    for chip in chips:
        chip.start()
    for part in range(parts):
        fetch(part).start()
    for chip in chips:
        chip.wait()
    section = lax.axis_index("segment")
    choose(chips_ref, me, 1 - section, loads_ref, branch_ref, facts_ref)
    lane = lanes_of(half)
    for k in range(experts):
        ends[k] = 0
        ranks[k] = 0
    slots[...] = jnp.zeros(slots.shape, jnp.float32)
    live = lax.broadcasted_iota(jnp.int32, (blocks, positions), 1)

    def place(i, _):
        fact = chips_ref[0, section, i]
        k, length = fact >> FACT_BITS, fact & (FACT - 1)
        start, rank = ends[k], ranks[k]
        ends[k] = start + length
        ranks[k] = rank + 1
        slots[k, pl.ds(rank * blocks, blocks), :] = jnp.where(live < length, scales_ref[i].astype(jnp.float32), 0.0)
        tile, shift = start >> (UNIT_BITS + 1), start & (2 * UNIT - 1)
        ahead = lane < shift.astype(jnp.bfloat16)
        for side in range(2):
            moved = turned(held[i, side * half : (side + 1) * half, :], shift)
            tiles[k, tile, side] = jnp.where(ahead, tiles[k, tile, side], moved)
            tiles[k, tile + 1, side] = moved
        return 0

    for part in range(parts):
        fetch(part).wait()
        lax.fori_loop(part * share, (part + 1) * share, place, 0, unroll=True)
    acc[:, :tail, :] = slots[...].astype(jnp.bfloat16)
    first = lane < float(UNIT)
    for k in range(experts):

        def split(tile, _):
            upper, lower = tiles[k, tile, 0], tiles[k, tile, 1]
            acc[k, rows_of(2 * tile), :] = jnp.where(first, upper, turned(lower, UNIT))
            acc[k, rows_of(2 * tile + 1), :] = jnp.where(first, turned(upper, UNIT), lower)
            return 0

        lax.fori_loop(0, (ends[k] + positions - 1) >> (UNIT_BITS + 1), split, 0)
    copies = []
    for way, out in enumerate(outs):
        k = pick(me, targets_of(way))
        skipped = pick(me, [SPLIT if way == staying(e)[1] else 0 for e in range(experts)])
        for at, first in enumerate(SEGMENTS):
            low = tail + first * half if first else 0
            high = tail + SEGMENTS[at + 1] * half if at + 1 < len(SEGMENTS) else out.shape[0]
            here = pl.ds(pl.multiple_of(low + skipped * half, 16), high - low)
            copy = pltpu.make_async_copy(acc.at[k, here], out.at[pl.ds(low, high - low)], out_sem.at[way, at])
            copies.append((copy, True if first == 0 else ends[k] > (first + skipped) * UNIT))
    for act in (lambda copy: copy.start(), lambda copy: copy.wait()):
        for copy, needed in copies:
            if needed is True:
                act(copy)
            else:
                pl.when(needed)(functools.partial(act, copy))


def pack(chips, scales, cache, units, capacity):
    requests, columns, positions = cache.shape
    half = columns // 2
    tail = capacity * scales.shape[1]
    smem = pl.BlockSpec(memory_space=pltpu.SMEM)
    vmem = pl.BlockSpec(memory_space=pltpu.VMEM)
    hbm = pl.BlockSpec(memory_space=pl.ANY)
    lanes = 2 * UNIT
    return pl.pallas_call(
        pack_kernel,
        in_specs=[hbm] * 4 + [vmem, hbm],
        out_specs=[hbm] * 5 + [smem] * 2,
        out_shape=[jax.ShapeDtypeStruct((tail + units * half, lanes), jnp.bfloat16)] * 5
        + [jax.ShapeDtypeStruct((1,), jnp.int32), jax.ShapeDtypeStruct((4, requests), jnp.int32)],
        scratch_shapes=[
            pltpu.VMEM(cache.shape, jnp.bfloat16),
            pltpu.VMEM((4, units // 2 + 1, 2, half, lanes), jnp.bfloat16),
            pltpu.VMEM((4, tail + (units + SPLIT) * half, lanes), jnp.bfloat16),
            pltpu.VMEM((4, tail, positions), jnp.float32),
            pltpu.SMEM((4,), jnp.int32),
            pltpu.SMEM((4,), jnp.int32),
            pltpu.SMEM((4,) + chips[0].shape, jnp.int32),
            pltpu.SMEM((16,), jnp.int32),
            pltpu.SemaphoreType.DMA((4,)),
            pltpu.SemaphoreType.DMA((5, len(SEGMENTS))),
            pltpu.SemaphoreType.DMA((4,)),
        ],
        compiler_params=pltpu.CompilerParams(vmem_limit_bytes=28 * MIB),
        cost_estimate=pl.CostEstimate(flops=2 * requests * half * 256, bytes_accessed=8 * MIB, transcendentals=0),
    )(*chips, scales, cache)


def clear_kernel(facts_ref, out_ref, starts, counts, zeros, sem):
    experts = 4
    requests = facts_ref.shape[1]
    capacity = out_ref.shape[0] // experts
    me = lax.axis_index("expert")
    zeros[...] = jnp.zeros(zeros.shape, zeros.dtype)

    def scan(k, cleared):
        def note(i, carry):
            rank, end = carry
            mine = facts_ref[k, i] >> FACT_BITS == me
            length = facts_ref[k, i] & (FACT - 1)

            @pl.when(mine)
            def _():
                starts[k, rank] = end
                counts[k, rank] = length

            return (jnp.where(mine, rank + 1, rank), jnp.where(mine, end + length, end))

        ranks, end = lax.fori_loop(0, requests, note, (0, 0))
        starts[k, capacity] = ranks
        counts[k, capacity] = (end + UNIT - 1) >> UNIT_BITS

        def clear(rank, _):
            starts[k, rank] = 0
            counts[k, rank] = 0
            slot = ((me - k) & (experts - 1)) * capacity + rank
            pltpu.make_async_copy(zeros, out_ref.at[slot], sem).start()
            return 0

        lax.fori_loop(ranks, capacity, clear, 0)
        return cleared + capacity - ranks

    def done(_, carry):
        pltpu.make_async_copy(zeros, out_ref.at[0], sem).wait()
        return carry

    lax.fori_loop(0, lax.fori_loop(0, experts, scan, 0), done, 0)


def clear(facts, capacity, columns, positions):
    smem = pl.BlockSpec(memory_space=pltpu.SMEM)
    table = jax.ShapeDtypeStruct((4, capacity + 1), jnp.int32)
    return pl.pallas_call(
        clear_kernel,
        in_specs=[smem],
        out_specs=[pl.BlockSpec(memory_space=pl.ANY), smem, smem],
        out_shape=[jax.ShapeDtypeStruct((4 * capacity, columns, positions), jnp.bfloat16), table, table],
        scratch_shapes=[pltpu.VMEM((columns, positions), jnp.bfloat16), pltpu.SemaphoreType.DMA],
        compiler_params=pltpu.CompilerParams(vmem_limit_bytes=8 * MIB),
        cost_estimate=pl.CostEstimate(flops=0, bytes_accessed=3 * MIB, transcendentals=0),
    )(facts)


def unpack_kernel(starts, counts, g0, g1, g2, g3, g4, cleared_ref, out_ref, scales_ref, *scratch):
    tiles, stage, tails, sem = scratch
    got = (g0, g1, g2, g3, g4)
    experts = 4
    capacity = out_ref.shape[0] // experts
    columns, positions = out_ref.shape[1], out_ref.shape[2]
    half = columns // 2
    tail = tails.shape[1]
    blocks = tail // capacity
    me = lax.axis_index("expert")
    lane = lanes_of(half)
    first = lane < float(UNIT)

    def units_of(unit):
        return pl.ds(pl.multiple_of(tail + unit * half, 16), half)

    def source_of(k):
        return (me - k) & (experts - 1)

    def write(k, rank):
        return pltpu.make_async_copy(stage.at[k, rank], out_ref.at[source_of(k) * capacity + rank], sem)

    def put_stream(k, written):
        used, ranks = counts[k, capacity], starts[k, capacity]
        for way in range(5):
            came = pick(source_of(k), targets_of(way)) == me
            later = jnp.logical_and(k == 0, pick(me, [int(way == staying(e)[1]) for e in range(experts)]) == 1)
            low = jnp.where(later, SPLIT, 0)
            high = jnp.where(jnp.logical_and(k == 0, jnp.logical_not(later)), jnp.minimum(used, SPLIT), used)
            units = (got[way].shape[0] - tail) // half

            @pl.when(came)
            def _():
                @pl.when(jnp.logical_not(later))
                def _():
                    tails[k] = got[way][:tail, :].astype(jnp.float32)

                def join(tile, _):
                    one = got[way][units_of(2 * tile - low), :]
                    two = got[way][units_of(jnp.minimum(2 * tile - low + 1, units - 1)), :]
                    tiles[k, tile, 0] = jnp.where(first, one, turned(two, UNIT))
                    tiles[k, tile, 1] = jnp.where(first, turned(one, UNIT), two)
                    return 0

                lax.fori_loop(low >> 1, (high + 1) >> 1, join, 0)

        def put(rank, _):
            start, length = starts[k, rank], counts[k, rank]
            tile, shift = start >> (UNIT_BITS + 1), start & (2 * UNIT - 1)
            here = lane < (2 * UNIT - shift).astype(jnp.bfloat16)
            live = lane < length.astype(jnp.bfloat16)
            for side in range(2):
                ahead = turned(tiles[k, tile, side], 2 * UNIT - shift)
                behind = turned(tiles[k, tile + 1, side], 2 * UNIT - shift)
                value = jnp.where(live, jnp.where(here, ahead, behind), jnp.zeros((), jnp.bfloat16))
                stage[k, rank, side * half : (side + 1) * half, :] = value
            write(k, rank).start()
            return 0

        lax.fori_loop(0, ranks, put, 0)
        for rank in range(capacity):
            scales = tails[k, rank * blocks : (rank + 1) * blocks, :]
            scales_ref[source_of(k) * capacity + rank] = scales.astype(jnp.bfloat16)
        return written + ranks

    def done(_, carry):
        write(0, 0).wait()
        return carry

    lax.fori_loop(0, lax.fori_loop(0, experts, put_stream, 0), done, 0)


def unpack(starts, counts, got, cleared, units, blocks):
    slots, columns, positions = cleared.shape
    capacity, half = slots // 4, columns // 2
    smem = pl.BlockSpec(memory_space=pltpu.SMEM)
    vmem = pl.BlockSpec(memory_space=pltpu.VMEM)
    hbm = pl.BlockSpec(memory_space=pl.ANY)
    return pl.pallas_call(
        unpack_kernel,
        in_specs=[smem] * 2 + [vmem] * 5 + [hbm],
        out_specs=[hbm, vmem],
        out_shape=[
            jax.ShapeDtypeStruct(cleared.shape, cleared.dtype),
            jax.ShapeDtypeStruct((slots, blocks, positions), cleared.dtype),
        ],
        input_output_aliases={7: 0},
        scratch_shapes=[
            pltpu.VMEM((4, units // 2 + 1, 2, half, positions), jnp.bfloat16),
            pltpu.VMEM((4, capacity, columns, positions), jnp.bfloat16),
            pltpu.VMEM((4, capacity * blocks, positions), jnp.float32),
            pltpu.SemaphoreType.DMA,
        ],
        compiler_params=pltpu.CompilerParams(vmem_limit_bytes=24 * MIB),
        cost_estimate=pl.CostEstimate(flops=0, bytes_accessed=10 * MIB, transcendentals=0),
    )(starts, counts, *got, cleared)


def size_sets():
    branches = []
    for hot in range(4):
        one, two = (2, 3) if hot < 2 else (1, 0)
        for paired, *sizes in AT_END if hot in (0, 3) else IN_MIDDLE:
            swaps = [{hot, one}, {hot, two}, {hot ^ 1, one}, {hot ^ 1, two}]
            branches.append((hot, [paired] + [sizes[swaps.index(set(swap))] for swap in SWAPS]))
    return branches + [(None, [16] * 5)]


BRANCHES = size_sets()


def choose(chips_ref, me, other, loads_ref, out_ref, facts_ref):
    experts = 4
    requests = chips_ref.shape[2]
    for k in range(experts):
        chip = chips_ref.at[k]
        most = [jnp.int32(0)] * experts
        for section in range(2):

            def add(i, sums):
                fact = chip[section, i]
                owner, length = fact >> FACT_BITS, fact & (FACT - 1)
                part = length << ((owner >> 1) << 4)
                odd = (owner & 1) == 1
                return (sums[0] + jnp.where(odd, 0, part), sums[1] + jnp.where(odd, part, 0))

            even, odd = lax.fori_loop(0, requests, add, (jnp.int32(0), jnp.int32(0)), unroll=8)
            for o, sums in enumerate((even, odd, even >> 16, odd >> 16)):
                most[o] = jnp.maximum(most[o], ((sums & 0xFFFF) + UNIT - 1) >> UNIT_BITS)
        for o in range(experts):
            loads_ref[((me - k) & (experts - 1)) * experts + o] = most[o]

        def keep(i, _):
            facts_ref[k, i] = chip[other, i]
            return 0

        lax.fori_loop(0, requests, keep, 0, unroll=8)
    load = [[loads_ref[source * experts + o] for o in range(experts)] for source in range(experts)]
    hot, highest = jnp.int32(0), jnp.int32(-1)
    for o in range(experts):
        worst = functools.reduce(jnp.maximum, [load[source][o] for source in range(experts) if source != o])
        hot = jnp.where(worst > highest, o, hot)
        highest = jnp.maximum(worst, highest)
    needs = []
    for way in range(5):
        need = jnp.int32(0)
        for source, target in enumerate(targets_of(way)):
            if source != target:
                need = jnp.maximum(need, load[source][target])
            elif way == staying(source)[0]:
                need = jnp.maximum(need, jnp.minimum(load[source][source], SPLIT))
            else:
                need = jnp.maximum(need, load[source][source] - SPLIT)
        needs.append(need)
    branch = jnp.int32(len(BRANCHES) - 1)
    for at in range(len(BRANCHES) - 2, -1, -1):
        h, sizes = BRANCHES[at]
        fits = functools.reduce(jnp.logical_and, [need <= size for need, size in zip(needs, sizes)], hot == h)
        branch = jnp.where(fits, at, branch)
    out_ref[0] = branch


def crossed(targets):
    return [(source * 2 + s, target * 2 + 1 - s) for source, target in enumerate(targets) for s in range(2)]


def by_halves(branches, index, operands):
    def run(low, high, operands):
        if high - low == 1:
            return branches[low](operands)
        middle = (low + high) // 2
        return lax.cond(
            index < middle, functools.partial(run, low, middle), functools.partial(run, middle, high), operands
        )

    return run(0, len(branches), operands)


def slot_layout(owner, experts, capacity):
    requests = owner.shape[0]
    indices = jnp.arange(requests, dtype=jnp.int32)
    earlier = indices[None, :] < indices[:, None]
    same_owner = owner[:, None] == owner[None, :]
    arrival_rank = jnp.sum(jnp.logical_and(same_owner, earlier), axis=1)
    target = owner * capacity + arrival_rank
    routing = target[None, :] == jnp.arange(experts * capacity, dtype=jnp.int32)[:, None]
    filled = jnp.any(routing, axis=1)
    source = jnp.sum(jnp.where(routing, indices[None, :], 0), axis=1)
    return (filled, source)


def pick_slots(values, filled, source):
    zero_value = jnp.zeros((), values.dtype)
    return jnp.where(filled[:, None, None], jnp.take(values, source, axis=0), zero_value)


def on_device(
    res_cache,
    res_scales,
    res_lengths,
    res_query,
    new_cache,
    new_scales,
    new_lengths,
    new_query,
    owner,
):
    experts = lax.axis_size("expert")
    sections = lax.axis_size("segment")
    requests, positions, columns = new_cache.shape
    capacity = max(2, 2 * requests // experts)
    swap = [(0, 1), (1, 0)]
    cache_t = jnp.transpose(new_cache, (0, 2, 1))
    res_inputs = (jnp.transpose(res_query, (0, 2, 1)), jnp.transpose(res_cache, (0, 2, 1)), res_scales, res_lengths)
    inputs = (res_inputs, (jnp.transpose(new_query, (0, 2, 1)), cache_t, new_scales, new_lengths))

    def attention(res_inputs, new_inputs):
        return attend(*res_inputs), attend(*new_inputs)

    if experts != 4 or sections != 2 or capacity * positions != 16 * UNIT or positions != 2 * UNIT or columns % 32:
        live_rows = jnp.arange(positions)[None, :] < new_lengths[:, None]
        zero_value = jnp.zeros((), jnp.bfloat16)
        filled, source = slot_layout(owner, experts, capacity)
        send_cache = pick_slots(jnp.where(live_rows[:, :, None], new_cache, zero_value), filled, source)
        send_scales = pick_slots(jnp.where(live_rows[:, None, :], new_scales, zero_value), filled, source)
        got_cache = lax.all_to_all(send_cache, "expert", split_axis=0, concat_axis=0, tiled=True)
        got_scales = lax.all_to_all(send_scales, "expert", split_axis=0, concat_axis=0, tiled=True)
        owned_cache, owned_scales = lax.ppermute((got_cache, got_scales), "segment", swap)
        return (*attention(*inputs), owned_cache, owned_scales)

    section = lax.axis_index("segment")
    units, half = capacity * positions // UNIT, columns // 2
    blocks = new_scales.shape[1]
    facts = owner * FACT + new_lengths
    sibling = lax.ppermute(facts, "segment", swap)
    chip = jnp.where(section == 0, jnp.stack([facts, sibling]), jnp.stack([sibling, facts]))
    chips = [chip] + [lax.ppermute(chip, "expert", [(e, (e + k) % 4) for e in range(4)]) for k in range(1, 4)]
    *streams, branch, facts = pack(chips, new_scales, cache_t, units, capacity)

    def take(sizes):
        def run(operands):
            streams, facts, *inputs = operands
            got = []
            for way, size in enumerate(sizes):
                part = streams[way][: capacity * blocks + size * half]
                got.append(lax.ppermute(part, ("expert", "segment"), crossed(targets_of(way))))
            cleared, starts, counts = clear(facts, capacity, columns, positions)
            return (*attention(*inputs), *unpack(starts, counts, got, cleared, units, blocks))

        return run

    branches = [take(sizes) for _, sizes in BRANCHES]
    res_context, new_context, owned, owned_scales = by_halves(branches, branch[0], (streams, facts, *inputs))
    return (res_context, new_context, jnp.transpose(owned, (0, 2, 1)), owned_scales)


def solution(mesh):
    placed = (
        P(("group", "expert", "segment", "attn"), None, None),
        P(("group", "expert", "segment", "attn"), None, None),
        P(("group", "expert", "segment", "attn")),
        P(("group", "expert", "segment", "attn"), None, None),
        P(("group", "expert", "segment", "attn"), None, None),
        P(("group", "expert", "segment", "attn"), None, None),
        P(("group", "expert", "segment", "attn")),
        P(("group", "expert", "segment", "attn"), None, None),
        P(("group", "expert", "segment", "attn")),
    )
    return jax.shard_map(
        on_device,
        mesh=mesh,
        in_specs=placed,
        out_specs=(
            P(("group", "expert", "segment", "attn"), None, None),
            P(("group", "expert", "segment", "attn"), None, None),
            P(("group", "expert", "segment", "attn"), None, None),
            P(("group", "expert", "segment", "attn"), None, None),
        ),
        check_vma=False,
    )
```

```python
import functools
import jax
import jax.numpy as jnp
from jax import lax
from jax.experimental import pallas as pl
from jax.experimental.pallas import tpu as pltpu
from jax.sharding import PartitionSpec as P

LATENT = 512
BLOCK = 128
UNIT_BITS = 6
UNIT = 1 << UNIT_BITS
SPLIT = 6
AT_END = ((14, 11, 11, 6, 8), (14, 12, 12, 7, 7), (13, 11, 14, 10, 6), (13, 14, 13, 8, 8))
IN_MIDDLE = ((12, 13, 11, 6, 7), (12, 11, 13, 7, 7), (14, 12, 11, 10, 10), (14, 14, 14, 8, 8))
SWAPS = ((0, 2), (0, 3), (1, 2), (1, 3))
FACT_BITS = 8
FACT = 1 << FACT_BITS

softmax_scale = 192.0 ** (-0.5)
MIB = 1 << 20


def attend_kernel(lengths_ref, query_ref, cache_ref, scales_ref, out_ref, factors_ref):
    blocks = scales_ref.shape[1]
    positions = cache_ref.shape[2]
    contract_rows = (((0,), (0,)), ((), ()))
    contract_positions = (((1,), (1,)), ((), ()))
    length = lengths_ref[pl.program_id(0)]

    def block(b):
        return pl.ds(pl.multiple_of(b * BLOCK, BLOCK), BLOCK)

    for b in range(blocks):
        factors_ref[b] = scales_ref[0, b : b + 1, :].astype(jnp.float32)

    def add(b, scores):
        part = lax.dot_general(
            query_ref[0, block(b), :], cache_ref[0, block(b), :], contract_rows, preferred_element_type=jnp.float32
        )
        return scores + part * factors_ref[b]

    scores = lax.dot_general(
        query_ref[0, LATENT:, :], cache_ref[0, LATENT:, :], contract_rows, preferred_element_type=jnp.float32
    )
    scores = lax.fori_loop(0, blocks, add, scores)
    live = lax.broadcasted_iota(jnp.int32, (1, positions), 1) < length
    scores = jnp.where(live, scores * softmax_scale, -jnp.inf)
    exponent = jnp.exp(scores - jnp.max(scores, axis=-1, keepdims=True))
    probabilities = exponent * (1.0 / jnp.sum(exponent, axis=-1, keepdims=True))

    def put(b, _):
        out_ref[0, :, block(b)] = lax.dot_general(
            (probabilities * factors_ref[b]).astype(jnp.bfloat16),
            cache_ref[0, block(b), :],
            contract_positions,
            preferred_element_type=jnp.float32,
        ).astype(jnp.bfloat16)
        return 0

    lax.fori_loop(0, blocks, put, 0)


def attend(query, cache, scales, lengths):
    requests, columns, heads = query.shape
    positions = cache.shape[2]
    return pl.pallas_call(
        attend_kernel,
        grid=(requests,),
        in_specs=[
            pl.BlockSpec(memory_space=pltpu.SMEM),
            pl.BlockSpec((1, columns, heads), lambda i: (i, 0, 0)),
            pl.BlockSpec((1, columns, positions), lambda i: (i, 0, 0)),
            pl.BlockSpec((1, scales.shape[1], positions), lambda i: (i, 0, 0)),
        ],
        out_specs=pl.BlockSpec((1, heads, LATENT), lambda i: (i, 0, 0)),
        out_shape=jax.ShapeDtypeStruct((requests, heads, LATENT), jnp.bfloat16),
        scratch_shapes=[pltpu.VMEM((scales.shape[1], 1, positions), jnp.float32)],
        compiler_params=pltpu.CompilerParams(vmem_limit_bytes=16 * MIB),
        cost_estimate=pl.CostEstimate(
            flops=4 * requests * heads * positions * columns,
            bytes_accessed=2 * requests * (heads * (columns + LATENT) + positions * columns),
            transcendentals=requests * heads * positions,
        ),
    )(lengths, query, cache, scales)


def lanes_of(rows):
    return lax.broadcasted_iota(jnp.int32, (rows, 2 * UNIT), 1).astype(jnp.bfloat16)


def turned(value, by):
    return pltpu.roll(value, by & (2 * UNIT - 1), 1)


def targets_of(way):
    if way == 0:
        return [e ^ 1 for e in range(4)]
    a, b = SWAPS[way - 1]
    return [b if e == a else a if e == b else e for e in range(4)]


def staying(e):
    return [way for way in range(5) if targets_of(way)[e] == e]


def pick(index, values):
    value = jnp.int32(values[0])
    for at in range(1, len(values)):
        value = jnp.where(index == at, values[at], value)
    return value


def pack_kernel(c0, c1, c2, c3, scales_ref, cache_ref, *refs):
    outs, facts_ref = refs[:5], refs[5]
    held, tiles, slots, ends, ranks, chips_ref, loads_ref, in_sem, chip_sem = refs[6:]
    experts = 4
    requests, columns, positions = cache_ref.shape
    blocks = scales_ref.shape[1]
    half = columns // 2
    tail = slots.shape[1]
    me = lax.axis_index("expert")
    parts = in_sem.shape[0]
    share = requests // parts

    def rows_of(unit):
        return pl.ds(pl.multiple_of(tail + unit * half, 16), half)

    def fetch(part):
        here = pl.ds(part * share, share)
        return pltpu.make_async_copy(cache_ref.at[here], held.at[here], in_sem.at[part])

    chips = [pltpu.make_async_copy(chip, chips_ref.at[k], chip_sem.at[k]) for k, chip in enumerate((c0, c1, c2, c3))]
    for chip in chips:
        chip.start()
    for part in range(parts):
        fetch(part).start()
    for chip in chips:
        chip.wait()
    section = lax.axis_index("segment")
    choose(chips_ref, me, 1 - section, loads_ref, facts_ref)
    lane = lanes_of(half)
    for k in range(experts):
        ends[k] = 0
        ranks[k] = 0
    slots[...] = jnp.zeros(slots.shape, jnp.float32)
    live = lax.broadcasted_iota(jnp.int32, (blocks, positions), 1)

    def place(i, _):
        fact = chips_ref[0, section, i]
        k, length = fact >> FACT_BITS, fact & (FACT - 1)
        start, rank = ends[k], ranks[k]
        ends[k] = start + length
        ranks[k] = rank + 1
        slots[k, pl.ds(rank * blocks, blocks), :] = jnp.where(live < length, scales_ref[i].astype(jnp.float32), 0.0)
        tile, shift = start >> (UNIT_BITS + 1), start & (2 * UNIT - 1)
        ahead = lane < shift.astype(jnp.bfloat16)
        for side in range(2):
            moved = turned(held[i, side * half : (side + 1) * half, :], shift)
            tiles[k, tile, side] = jnp.where(ahead, tiles[k, tile, side], moved)
            tiles[k, tile + 1, side] = moved
        return 0

    for part in range(parts):
        fetch(part).wait()
        lax.fori_loop(part * share, (part + 1) * share, place, 0, unroll=True)
    first = lane < float(UNIT)
    for way, out in enumerate(outs):
        k = pick(me, targets_of(way))
        out[:tail, :] = slots[k].astype(jnp.bfloat16)
        skipped = pick(me, [SPLIT if way == staying(e)[1] else 0 for e in range(experts)])

        def split(tile, _):
            upper, lower = tiles[k, tile, 0], tiles[k, tile, 1]
            out[rows_of(2 * tile - skipped), :] = jnp.where(first, upper, turned(lower, UNIT))
            out[rows_of(2 * tile - skipped + 1), :] = jnp.where(first, turned(upper, UNIT), lower)
            return 0

        lax.fori_loop(skipped >> 1, (ends[k] + positions - 1) >> (UNIT_BITS + 1), split, 0)


def pack(chips, scales, cache, units, capacity):
    requests, columns, positions = cache.shape
    half = columns // 2
    tail = capacity * scales.shape[1]
    smem = pl.BlockSpec(memory_space=pltpu.SMEM)
    vmem = pl.BlockSpec(memory_space=pltpu.VMEM)
    hbm = pl.BlockSpec(memory_space=pl.ANY)
    lanes = 2 * UNIT
    return pl.pallas_call(
        pack_kernel,
        in_specs=[hbm] * 4 + [vmem, hbm],
        out_specs=[vmem] * 5 + [smem],
        out_shape=[jax.ShapeDtypeStruct((tail + units * half, lanes), jnp.bfloat16)] * 5
        + [jax.ShapeDtypeStruct((5, requests), jnp.int32)],
        scratch_shapes=[
            pltpu.VMEM(cache.shape, jnp.bfloat16),
            pltpu.VMEM((4, units // 2 + 1, 2, half, lanes), jnp.bfloat16),
            pltpu.VMEM((4, tail, positions), jnp.float32),
            pltpu.SMEM((4,), jnp.int32),
            pltpu.SMEM((4,), jnp.int32),
            pltpu.SMEM((4,) + chips[0].shape, jnp.int32),
            pltpu.SMEM((16,), jnp.int32),
            pltpu.SemaphoreType.DMA((4,)),
            pltpu.SemaphoreType.DMA((4,)),
        ],
        compiler_params=pltpu.CompilerParams(vmem_limit_bytes=28 * MIB),
        cost_estimate=pl.CostEstimate(flops=2 * requests * half * 256, bytes_accessed=8 * MIB, transcendentals=0),
    )(*chips, scales, cache)


def clear_kernel(facts_ref, out_ref, starts, counts, zeros, sem):
    experts = 4
    requests = facts_ref.shape[1]
    capacity = out_ref.shape[0] // experts
    me = lax.axis_index("expert")
    zeros[...] = jnp.zeros(zeros.shape, zeros.dtype)

    def scan(k, cleared):
        def note(i, carry):
            rank, end = carry
            mine = facts_ref[k, i] >> FACT_BITS == me
            length = facts_ref[k, i] & (FACT - 1)

            @pl.when(mine)
            def _():
                starts[k, rank] = end
                counts[k, rank] = length

            return (jnp.where(mine, rank + 1, rank), jnp.where(mine, end + length, end))

        ranks, end = lax.fori_loop(0, requests, note, (0, 0))
        starts[k, capacity] = ranks
        counts[k, capacity] = (end + UNIT - 1) >> UNIT_BITS

        def clear(rank, _):
            starts[k, rank] = 0
            counts[k, rank] = 0
            slot = ((me - k) & (experts - 1)) * capacity + rank
            pltpu.make_async_copy(zeros, out_ref.at[slot], sem).start()
            return 0

        lax.fori_loop(ranks, capacity, clear, 0)
        return cleared + capacity - ranks

    def done(_, carry):
        pltpu.make_async_copy(zeros, out_ref.at[0], sem).wait()
        return carry

    lax.fori_loop(0, lax.fori_loop(0, experts, scan, 0), done, 0)


def clear(facts, capacity, columns, positions):
    smem = pl.BlockSpec(memory_space=pltpu.SMEM)
    table = jax.ShapeDtypeStruct((4, capacity + 1), jnp.int32)
    return pl.pallas_call(
        clear_kernel,
        in_specs=[smem],
        out_specs=[pl.BlockSpec(memory_space=pl.ANY), smem, smem],
        out_shape=[jax.ShapeDtypeStruct((4 * capacity, columns, positions), jnp.bfloat16), table, table],
        scratch_shapes=[pltpu.VMEM((columns, positions), jnp.bfloat16), pltpu.SemaphoreType.DMA],
        compiler_params=pltpu.CompilerParams(vmem_limit_bytes=8 * MIB),
        cost_estimate=pl.CostEstimate(flops=0, bytes_accessed=3 * MIB, transcendentals=0),
    )(facts)


def unpack_kernel(starts, counts, g0, g1, g2, g3, g4, cleared_ref, out_ref, scales_ref, *scratch):
    tiles, stage, tails, sem = scratch
    got = (g0, g1, g2, g3, g4)
    experts = 4
    capacity = out_ref.shape[0] // experts
    columns, positions = out_ref.shape[1], out_ref.shape[2]
    half = columns // 2
    tail = tails.shape[1]
    blocks = tail // capacity
    me = lax.axis_index("expert")
    lane = lanes_of(half)
    first = lane < float(UNIT)

    def units_of(unit):
        return pl.ds(pl.multiple_of(tail + unit * half, 16), half)

    def source_of(k):
        return (me - k) & (experts - 1)

    def write(k, rank):
        return pltpu.make_async_copy(stage.at[k, rank], out_ref.at[source_of(k) * capacity + rank], sem)

    def put_stream(k, written):
        used, ranks = counts[k, capacity], starts[k, capacity]
        for way in range(5):
            came = pick(source_of(k), targets_of(way)) == me
            later = jnp.logical_and(k == 0, pick(me, [int(way == staying(e)[1]) for e in range(experts)]) == 1)
            low = jnp.where(later, SPLIT, 0)
            high = jnp.where(jnp.logical_and(k == 0, jnp.logical_not(later)), jnp.minimum(used, SPLIT), used)
            units = (got[way].shape[0] - tail) // half

            @pl.when(came)
            def _():
                @pl.when(jnp.logical_not(later))
                def _():
                    tails[k] = got[way][:tail, :].astype(jnp.float32)

                def join(tile, _):
                    one = got[way][units_of(2 * tile - low), :]
                    two = got[way][units_of(jnp.minimum(2 * tile - low + 1, units - 1)), :]
                    tiles[k, tile, 0] = jnp.where(first, one, turned(two, UNIT))
                    tiles[k, tile, 1] = jnp.where(first, turned(one, UNIT), two)
                    return 0

                lax.fori_loop(low >> 1, (high + 1) >> 1, join, 0)

        def put(rank, _):
            start, length = starts[k, rank], counts[k, rank]
            tile, shift = start >> (UNIT_BITS + 1), start & (2 * UNIT - 1)
            here = lane < (2 * UNIT - shift).astype(jnp.bfloat16)
            live = lane < length.astype(jnp.bfloat16)
            for side in range(2):
                ahead = turned(tiles[k, tile, side], 2 * UNIT - shift)
                behind = turned(tiles[k, tile + 1, side], 2 * UNIT - shift)
                value = jnp.where(live, jnp.where(here, ahead, behind), jnp.zeros((), jnp.bfloat16))
                stage[k, rank, side * half : (side + 1) * half, :] = value
            write(k, rank).start()
            return 0

        lax.fori_loop(0, ranks, put, 0)
        for rank in range(capacity):
            scales = tails[k, rank * blocks : (rank + 1) * blocks, :]
            scales_ref[source_of(k) * capacity + rank] = scales.astype(jnp.bfloat16)
        return written + ranks

    def done(_, carry):
        write(0, 0).wait()
        return carry

    lax.fori_loop(0, lax.fori_loop(0, experts, put_stream, 0), done, 0)


def unpack(starts, counts, got, cleared, units, blocks):
    slots, columns, positions = cleared.shape
    capacity, half = slots // 4, columns // 2
    smem = pl.BlockSpec(memory_space=pltpu.SMEM)
    vmem = pl.BlockSpec(memory_space=pltpu.VMEM)
    hbm = pl.BlockSpec(memory_space=pl.ANY)
    return pl.pallas_call(
        unpack_kernel,
        in_specs=[smem] * 2 + [vmem] * 5 + [hbm],
        out_specs=[hbm, vmem],
        out_shape=[
            jax.ShapeDtypeStruct(cleared.shape, cleared.dtype),
            jax.ShapeDtypeStruct((slots, blocks, positions), cleared.dtype),
        ],
        input_output_aliases={7: 0},
        scratch_shapes=[
            pltpu.VMEM((4, units // 2 + 1, 2, half, positions), jnp.bfloat16),
            pltpu.VMEM((4, capacity, columns, positions), jnp.bfloat16),
            pltpu.VMEM((4, capacity * blocks, positions), jnp.float32),
            pltpu.SemaphoreType.DMA,
        ],
        compiler_params=pltpu.CompilerParams(vmem_limit_bytes=24 * MIB),
        cost_estimate=pl.CostEstimate(flops=0, bytes_accessed=10 * MIB, transcendentals=0),
    )(starts, counts, *got, cleared)


def size_sets():
    branches = []
    for hot in range(4):
        one, two = (2, 3) if hot < 2 else (1, 0)
        for paired, *sizes in AT_END if hot in (0, 3) else IN_MIDDLE:
            swaps = [{hot, one}, {hot, two}, {hot ^ 1, one}, {hot ^ 1, two}]
            branches.append((hot, [paired] + [sizes[swaps.index(set(swap))] for swap in SWAPS]))
    return branches + [(None, [16] * 5)]


BRANCHES = size_sets()


def choose(chips_ref, me, other, loads_ref, facts_ref):
    experts = 4
    requests = chips_ref.shape[2]
    for k in range(experts):
        chip = chips_ref.at[k]
        most = [jnp.int32(0)] * experts
        for section in range(2):

            def add(i, sums):
                fact = chip[section, i]
                owner, length = fact >> FACT_BITS, fact & (FACT - 1)
                part = length << ((owner >> 1) << 4)
                odd = (owner & 1) == 1
                return (sums[0] + jnp.where(odd, 0, part), sums[1] + jnp.where(odd, part, 0))

            even, odd = lax.fori_loop(0, requests, add, (jnp.int32(0), jnp.int32(0)), unroll=8)
            for o, sums in enumerate((even, odd, even >> 16, odd >> 16)):
                most[o] = jnp.maximum(most[o], ((sums & 0xFFFF) + UNIT - 1) >> UNIT_BITS)
        for o in range(experts):
            loads_ref[((me - k) & (experts - 1)) * experts + o] = most[o]

        def keep(i, _):
            facts_ref[k, i] = chip[other, i]
            return 0

        lax.fori_loop(0, requests, keep, 0, unroll=8)
    load = [[loads_ref[source * experts + o] for o in range(experts)] for source in range(experts)]
    hot, highest = jnp.int32(0), jnp.int32(-1)
    for o in range(experts):
        worst = functools.reduce(jnp.maximum, [load[source][o] for source in range(experts) if source != o])
        hot = jnp.where(worst > highest, o, hot)
        highest = jnp.maximum(worst, highest)
    needs = []
    for way in range(5):
        need = jnp.int32(0)
        for source, target in enumerate(targets_of(way)):
            if source != target:
                need = jnp.maximum(need, load[source][target])
            elif way == staying(source)[0]:
                need = jnp.maximum(need, jnp.minimum(load[source][source], SPLIT))
            else:
                need = jnp.maximum(need, load[source][source] - SPLIT)
        needs.append(need)
    branch = jnp.int32(len(BRANCHES) - 1)
    for at in range(len(BRANCHES) - 2, -1, -1):
        h, sizes = BRANCHES[at]
        fits = functools.reduce(jnp.logical_and, [need <= size for need, size in zip(needs, sizes)], hot == h)
        branch = jnp.where(fits, at, branch)
    facts_ref[experts, 0] = branch


def crossed(targets):
    return [(source * 2 + s, target * 2 + 1 - s) for source, target in enumerate(targets) for s in range(2)]


def by_halves(branches, operands):
    def run(low, high, operands):
        if high - low == 1:
            return branches[low](operands)
        middle = (low + high) // 2
        left, right = functools.partial(run, low, middle), functools.partial(run, middle, high)
        return lax.cond(jnp.all(operands[1][4:, :1] < middle), left, right, operands)

    return run(0, len(branches), operands)


def slot_layout(owner, experts, capacity):
    requests = owner.shape[0]
    indices = jnp.arange(requests, dtype=jnp.int32)
    earlier = indices[None, :] < indices[:, None]
    same_owner = owner[:, None] == owner[None, :]
    arrival_rank = jnp.sum(jnp.logical_and(same_owner, earlier), axis=1)
    target = owner * capacity + arrival_rank
    routing = target[None, :] == jnp.arange(experts * capacity, dtype=jnp.int32)[:, None]
    filled = jnp.any(routing, axis=1)
    source = jnp.sum(jnp.where(routing, indices[None, :], 0), axis=1)
    return (filled, source)


def pick_slots(values, filled, source):
    zero_value = jnp.zeros((), values.dtype)
    return jnp.where(filled[:, None, None], jnp.take(values, source, axis=0), zero_value)


def on_device(
    res_cache,
    res_scales,
    res_lengths,
    res_query,
    new_cache,
    new_scales,
    new_lengths,
    new_query,
    owner,
):
    experts = lax.axis_size("expert")
    sections = lax.axis_size("segment")
    requests, positions, columns = new_cache.shape
    capacity = max(2, 2 * requests // experts)
    swap = [(0, 1), (1, 0)]
    cache_t = jnp.transpose(new_cache, (0, 2, 1))
    res_inputs = (jnp.transpose(res_query, (0, 2, 1)), jnp.transpose(res_cache, (0, 2, 1)), res_scales, res_lengths)
    inputs = (res_inputs, (jnp.transpose(new_query, (0, 2, 1)), cache_t, new_scales, new_lengths))

    def attention(res_inputs, new_inputs):
        return attend(*res_inputs), attend(*new_inputs)

    if experts != 4 or sections != 2 or capacity * positions != 16 * UNIT or positions != 2 * UNIT or columns % 32:
        live_rows = jnp.arange(positions)[None, :] < new_lengths[:, None]
        zero_value = jnp.zeros((), jnp.bfloat16)
        filled, source = slot_layout(owner, experts, capacity)
        send_cache = pick_slots(jnp.where(live_rows[:, :, None], new_cache, zero_value), filled, source)
        send_scales = pick_slots(jnp.where(live_rows[:, None, :], new_scales, zero_value), filled, source)
        got_cache = lax.all_to_all(send_cache, "expert", split_axis=0, concat_axis=0, tiled=True)
        got_scales = lax.all_to_all(send_scales, "expert", split_axis=0, concat_axis=0, tiled=True)
        owned_cache, owned_scales = lax.ppermute((got_cache, got_scales), "segment", swap)
        return (*attention(*inputs), owned_cache, owned_scales)

    section = lax.axis_index("segment")
    units, half = capacity * positions // UNIT, columns // 2
    blocks = new_scales.shape[1]
    facts = owner * FACT + new_lengths
    sibling = lax.ppermute(facts, "segment", swap)
    chip = jnp.where(section == 0, jnp.stack([facts, sibling]), jnp.stack([sibling, facts]))
    chips = [chip] + [lax.ppermute(chip, "expert", [(e, (e + k) % 4) for e in range(4)]) for k in range(1, 4)]
    *streams, facts = pack(chips, new_scales, cache_t, units, capacity)

    def take(sizes):
        def run(operands):
            streams, facts, *inputs = operands
            got = []
            for way, size in enumerate(sizes):
                part = streams[way][: capacity * blocks + size * half]
                got.append(lax.ppermute(part, ("expert", "segment"), crossed(targets_of(way))))
            cleared, starts, counts = clear(facts, capacity, columns, positions)
            return (*attention(*inputs), *unpack(starts, counts, got, cleared, units, blocks))

        return run

    branches = [take(sizes) for _, sizes in BRANCHES]
    res_context, new_context, owned, owned_scales = by_halves(branches, (streams, facts, *inputs))
    return (res_context, new_context, jnp.transpose(owned, (0, 2, 1)), owned_scales)


def solution(mesh):
    placed = (
        P(("group", "expert", "segment", "attn"), None, None),
        P(("group", "expert", "segment", "attn"), None, None),
        P(("group", "expert", "segment", "attn")),
        P(("group", "expert", "segment", "attn"), None, None),
        P(("group", "expert", "segment", "attn"), None, None),
        P(("group", "expert", "segment", "attn"), None, None),
        P(("group", "expert", "segment", "attn")),
        P(("group", "expert", "segment", "attn"), None, None),
        P(("group", "expert", "segment", "attn")),
    )
    return jax.shard_map(
        on_device,
        mesh=mesh,
        in_specs=placed,
        out_specs=(
            P(("group", "expert", "segment", "attn"), None, None),
            P(("group", "expert", "segment", "attn"), None, None),
            P(("group", "expert", "segment", "attn"), None, None),
            P(("group", "expert", "segment", "attn"), None, None),
        ),
        check_vma=False,
    )
```

```python
import functools
import jax
import jax.numpy as jnp
from jax import lax
from jax.experimental import pallas as pl
from jax.experimental.pallas import tpu as pltpu
from jax.sharding import PartitionSpec as P

LATENT = 512
BLOCK = 128
UNIT_BITS = 6
UNIT = 1 << UNIT_BITS
SPLIT = 6
AT_END = ((14, 11, 11, 6, 8), (14, 12, 12, 7, 7), (13, 11, 14, 10, 6), (13, 14, 13, 8, 8))
IN_MIDDLE = ((12, 13, 11, 6, 7), (12, 11, 13, 7, 7), (14, 12, 11, 10, 10), (14, 14, 14, 8, 8))
SWAPS = ((0, 2), (0, 3), (1, 2), (1, 3))
FACT_BITS = 8
FACT = 1 << FACT_BITS

softmax_scale = 192.0 ** (-0.5)
MIB = 1 << 20


def attend_kernel(lengths_ref, query_ref, cache_ref, scales_ref, out_ref, factors_ref):
    blocks = scales_ref.shape[1]
    positions = cache_ref.shape[2]
    contract_rows = (((0,), (0,)), ((), ()))
    contract_positions = (((1,), (1,)), ((), ()))
    length = lengths_ref[pl.program_id(0)]

    def block(b):
        return pl.ds(pl.multiple_of(b * BLOCK, BLOCK), BLOCK)

    for b in range(blocks):
        factors_ref[b] = scales_ref[0, b : b + 1, :].astype(jnp.float32)

    def add(b, scores):
        part = lax.dot_general(
            query_ref[0, block(b), :], cache_ref[0, block(b), :], contract_rows, preferred_element_type=jnp.float32
        )
        return scores + part * factors_ref[b]

    scores = lax.dot_general(
        query_ref[0, LATENT:, :], cache_ref[0, LATENT:, :], contract_rows, preferred_element_type=jnp.float32
    )
    scores = lax.fori_loop(0, blocks, add, scores)
    live = lax.broadcasted_iota(jnp.int32, (1, positions), 1) < length
    scores = jnp.where(live, scores * softmax_scale, -jnp.inf)
    exponent = jnp.exp(scores - jnp.max(scores, axis=-1, keepdims=True))
    probabilities = exponent * (1.0 / jnp.sum(exponent, axis=-1, keepdims=True))

    def put(b, _):
        out_ref[0, :, block(b)] = lax.dot_general(
            (probabilities * factors_ref[b]).astype(jnp.bfloat16),
            cache_ref[0, block(b), :],
            contract_positions,
            preferred_element_type=jnp.float32,
        ).astype(jnp.bfloat16)
        return 0

    lax.fori_loop(0, blocks, put, 0)


def attend(query, cache, scales, lengths):
    requests, columns, heads = query.shape
    positions = cache.shape[2]
    return pl.pallas_call(
        attend_kernel,
        grid=(requests,),
        in_specs=[
            pl.BlockSpec(memory_space=pltpu.SMEM),
            pl.BlockSpec((1, columns, heads), lambda i: (i, 0, 0)),
            pl.BlockSpec((1, columns, positions), lambda i: (i, 0, 0)),
            pl.BlockSpec((1, scales.shape[1], positions), lambda i: (i, 0, 0)),
        ],
        out_specs=pl.BlockSpec((1, heads, LATENT), lambda i: (i, 0, 0)),
        out_shape=jax.ShapeDtypeStruct((requests, heads, LATENT), jnp.bfloat16),
        scratch_shapes=[pltpu.VMEM((scales.shape[1], 1, positions), jnp.float32)],
        compiler_params=pltpu.CompilerParams(vmem_limit_bytes=16 * MIB),
        cost_estimate=pl.CostEstimate(
            flops=4 * requests * heads * positions * columns,
            bytes_accessed=2 * requests * (heads * (columns + LATENT) + positions * columns),
            transcendentals=requests * heads * positions,
        ),
    )(lengths, query, cache, scales)


def lanes_of(rows):
    return lax.broadcasted_iota(jnp.int32, (rows, 2 * UNIT), 1).astype(jnp.bfloat16)


def turned(value, by):
    return pltpu.roll(value, by & (2 * UNIT - 1), 1)


def targets_of(way):
    if way == 0:
        return [e ^ 1 for e in range(4)]
    a, b = SWAPS[way - 1]
    return [b if e == a else a if e == b else e for e in range(4)]


def staying(e):
    return [way for way in range(5) if targets_of(way)[e] == e]


def pick(index, values):
    value = jnp.int32(values[0])
    for at in range(1, len(values)):
        value = jnp.where(index == at, values[at], value)
    return value


def pack_kernel(c0, c1, c2, c3, scales_ref, cache_ref, *refs):
    outs, facts_ref = refs[:5], refs[5]
    held, tiles, slots, ends, ranks, chips_ref, loads_ref, in_sem, chip_sem = refs[6:]
    experts = 4
    requests, columns, positions = cache_ref.shape
    blocks = scales_ref.shape[1]
    half = columns // 2
    tail = slots.shape[1]
    me = lax.axis_index("expert")
    parts = in_sem.shape[0]
    share = requests // parts

    def rows_of(unit):
        return pl.ds(pl.multiple_of(tail + unit * half, 16), half)

    def fetch(part):
        here = pl.ds(part * share, share)
        return pltpu.make_async_copy(cache_ref.at[here], held.at[here], in_sem.at[part])

    chips = [pltpu.make_async_copy(chip, chips_ref.at[k], chip_sem.at[k]) for k, chip in enumerate((c0, c1, c2, c3))]
    for chip in chips:
        chip.start()
    for part in range(parts):
        fetch(part).start()
    for chip in chips:
        chip.wait()
    section = lax.axis_index("segment")
    choose(chips_ref, me, 1 - section, loads_ref, facts_ref)
    lane = lanes_of(half)
    for k in range(experts):
        ends[k] = 0
        ranks[k] = 0
    slots[...] = jnp.zeros(slots.shape, jnp.float32)
    live = lax.broadcasted_iota(jnp.int32, (blocks, positions), 1)

    def place(i, _):
        fact = chips_ref[0, section, i]
        k, length = fact >> FACT_BITS, fact & (FACT - 1)
        start, rank = ends[k], ranks[k]
        ends[k] = start + length
        ranks[k] = rank + 1
        slots[k, pl.ds(rank * blocks, blocks), :] = jnp.where(live < length, scales_ref[i].astype(jnp.float32), 0.0)
        tile, shift = start >> (UNIT_BITS + 1), start & (2 * UNIT - 1)
        ahead = lane < shift.astype(jnp.bfloat16)
        for side in range(2):
            moved = turned(held[i, side * half : (side + 1) * half, :], shift)
            tiles[k, tile, side] = jnp.where(ahead, tiles[k, tile, side], moved)
            tiles[k, tile + 1, side] = moved
        return 0

    for part in range(parts):
        fetch(part).wait()
        lax.fori_loop(part * share, (part + 1) * share, place, 0, unroll=True)
    first = lane < float(UNIT)
    for way, out in enumerate(outs):
        k = pick(me, targets_of(way))
        out[:tail, :] = slots[k].astype(jnp.bfloat16)
        skipped = pick(me, [SPLIT if way == staying(e)[1] else 0 for e in range(experts)])

        def split(tile, _):
            upper, lower = tiles[k, tile, 0], tiles[k, tile, 1]
            out[rows_of(2 * tile - skipped), :] = jnp.where(first, upper, turned(lower, UNIT))
            out[rows_of(2 * tile - skipped + 1), :] = jnp.where(first, turned(upper, UNIT), lower)
            return 0

        lax.fori_loop(skipped >> 1, (ends[k] + positions - 1) >> (UNIT_BITS + 1), split, 0)


def pack(chips, scales, cache, units, capacity):
    requests, columns, positions = cache.shape
    half = columns // 2
    tail = capacity * scales.shape[1]
    smem = pl.BlockSpec(memory_space=pltpu.SMEM)
    vmem = pl.BlockSpec(memory_space=pltpu.VMEM)
    hbm = pl.BlockSpec(memory_space=pl.ANY)
    lanes = 2 * UNIT
    return pl.pallas_call(
        pack_kernel,
        in_specs=[hbm] * 4 + [vmem, hbm],
        out_specs=[vmem] * 5 + [smem],
        out_shape=[jax.ShapeDtypeStruct((tail + units * half, lanes), jnp.bfloat16)] * 5
        + [jax.ShapeDtypeStruct((1 + 4 * requests,), jnp.int32)],
        scratch_shapes=[
            pltpu.VMEM(cache.shape, jnp.bfloat16),
            pltpu.VMEM((4, units // 2 + 1, 2, half, lanes), jnp.bfloat16),
            pltpu.VMEM((4, tail, positions), jnp.float32),
            pltpu.SMEM((4,), jnp.int32),
            pltpu.SMEM((4,), jnp.int32),
            pltpu.SMEM((4,) + chips[0].shape, jnp.int32),
            pltpu.SMEM((16,), jnp.int32),
            pltpu.SemaphoreType.DMA((4,)),
            pltpu.SemaphoreType.DMA((4,)),
        ],
        compiler_params=pltpu.CompilerParams(vmem_limit_bytes=28 * MIB),
        cost_estimate=pl.CostEstimate(flops=2 * requests * half * 256, bytes_accessed=8 * MIB, transcendentals=0),
    )(*chips, scales, cache)


def clear_kernel(facts_ref, out_ref, starts, counts, zeros, sem):
    experts = 4
    requests = facts_ref.shape[0] // experts
    capacity = out_ref.shape[0] // experts
    me = lax.axis_index("expert")
    zeros[...] = jnp.zeros(zeros.shape, zeros.dtype)

    def scan(k, cleared):
        def note(i, carry):
            rank, end = carry
            fact = facts_ref[1 + k * requests + i]
            mine = fact >> FACT_BITS == me
            length = fact & (FACT - 1)

            @pl.when(mine)
            def _():
                starts[k, rank] = end
                counts[k, rank] = length

            return (jnp.where(mine, rank + 1, rank), jnp.where(mine, end + length, end))

        ranks, end = lax.fori_loop(0, requests, note, (0, 0))
        starts[k, capacity] = ranks
        counts[k, capacity] = (end + UNIT - 1) >> UNIT_BITS

        def clear(rank, _):
            starts[k, rank] = 0
            counts[k, rank] = 0
            slot = ((me - k) & (experts - 1)) * capacity + rank
            pltpu.make_async_copy(zeros, out_ref.at[slot], sem).start()
            return 0

        lax.fori_loop(ranks, capacity, clear, 0)
        return cleared + capacity - ranks

    def done(_, carry):
        pltpu.make_async_copy(zeros, out_ref.at[0], sem).wait()
        return carry

    lax.fori_loop(0, lax.fori_loop(0, experts, scan, 0), done, 0)


def clear(facts, capacity, columns, positions):
    smem = pl.BlockSpec(memory_space=pltpu.SMEM)
    table = jax.ShapeDtypeStruct((4, capacity + 1), jnp.int32)
    return pl.pallas_call(
        clear_kernel,
        in_specs=[smem],
        out_specs=[pl.BlockSpec(memory_space=pl.ANY), smem, smem],
        out_shape=[jax.ShapeDtypeStruct((4 * capacity, columns, positions), jnp.bfloat16), table, table],
        scratch_shapes=[pltpu.VMEM((columns, positions), jnp.bfloat16), pltpu.SemaphoreType.DMA],
        compiler_params=pltpu.CompilerParams(vmem_limit_bytes=8 * MIB),
        cost_estimate=pl.CostEstimate(flops=0, bytes_accessed=3 * MIB, transcendentals=0),
    )(facts)


def unpack_kernel(starts, counts, g0, g1, g2, g3, g4, cleared_ref, out_ref, scales_ref, *scratch):
    tiles, stage, tails, sem = scratch
    got = (g0, g1, g2, g3, g4)
    experts = 4
    capacity = out_ref.shape[0] // experts
    columns, positions = out_ref.shape[1], out_ref.shape[2]
    half = columns // 2
    tail = tails.shape[1]
    blocks = tail // capacity
    me = lax.axis_index("expert")
    lane = lanes_of(half)
    first = lane < float(UNIT)

    def units_of(unit):
        return pl.ds(pl.multiple_of(tail + unit * half, 16), half)

    def source_of(k):
        return (me - k) & (experts - 1)

    def write(k, rank):
        return pltpu.make_async_copy(stage.at[k, rank], out_ref.at[source_of(k) * capacity + rank], sem)

    def put_stream(k, written):
        used, ranks = counts[k, capacity], starts[k, capacity]
        for way in range(5):
            came = pick(source_of(k), targets_of(way)) == me
            later = jnp.logical_and(k == 0, pick(me, [int(way == staying(e)[1]) for e in range(experts)]) == 1)
            low = jnp.where(later, SPLIT, 0)
            high = jnp.where(jnp.logical_and(k == 0, jnp.logical_not(later)), jnp.minimum(used, SPLIT), used)
            units = (got[way].shape[0] - tail) // half

            @pl.when(came)
            def _():
                @pl.when(jnp.logical_not(later))
                def _():
                    tails[k] = got[way][:tail, :].astype(jnp.float32)

                def join(tile, _):
                    one = got[way][units_of(2 * tile - low), :]
                    two = got[way][units_of(jnp.minimum(2 * tile - low + 1, units - 1)), :]
                    tiles[k, tile, 0] = jnp.where(first, one, turned(two, UNIT))
                    tiles[k, tile, 1] = jnp.where(first, turned(one, UNIT), two)
                    return 0

                lax.fori_loop(low >> 1, (high + 1) >> 1, join, 0)

        def put(rank, _):
            start, length = starts[k, rank], counts[k, rank]
            tile, shift = start >> (UNIT_BITS + 1), start & (2 * UNIT - 1)
            here = lane < (2 * UNIT - shift).astype(jnp.bfloat16)
            live = lane < length.astype(jnp.bfloat16)
            for side in range(2):
                ahead = turned(tiles[k, tile, side], 2 * UNIT - shift)
                behind = turned(tiles[k, tile + 1, side], 2 * UNIT - shift)
                value = jnp.where(live, jnp.where(here, ahead, behind), jnp.zeros((), jnp.bfloat16))
                stage[k, rank, side * half : (side + 1) * half, :] = value
            write(k, rank).start()
            return 0

        lax.fori_loop(0, ranks, put, 0)
        for rank in range(capacity):
            scales = tails[k, rank * blocks : (rank + 1) * blocks, :]
            scales_ref[source_of(k) * capacity + rank] = scales.astype(jnp.bfloat16)
        return written + ranks

    def done(_, carry):
        write(0, 0).wait()
        return carry

    lax.fori_loop(0, lax.fori_loop(0, experts, put_stream, 0), done, 0)


def unpack(starts, counts, got, cleared, units, blocks):
    slots, columns, positions = cleared.shape
    capacity, half = slots // 4, columns // 2
    smem = pl.BlockSpec(memory_space=pltpu.SMEM)
    vmem = pl.BlockSpec(memory_space=pltpu.VMEM)
    hbm = pl.BlockSpec(memory_space=pl.ANY)
    return pl.pallas_call(
        unpack_kernel,
        in_specs=[smem] * 2 + [vmem] * 5 + [hbm],
        out_specs=[hbm, vmem],
        out_shape=[
            jax.ShapeDtypeStruct(cleared.shape, cleared.dtype),
            jax.ShapeDtypeStruct((slots, blocks, positions), cleared.dtype),
        ],
        input_output_aliases={7: 0},
        scratch_shapes=[
            pltpu.VMEM((4, units // 2 + 1, 2, half, positions), jnp.bfloat16),
            pltpu.VMEM((4, capacity, columns, positions), jnp.bfloat16),
            pltpu.VMEM((4, capacity * blocks, positions), jnp.float32),
            pltpu.SemaphoreType.DMA,
        ],
        compiler_params=pltpu.CompilerParams(vmem_limit_bytes=24 * MIB),
        cost_estimate=pl.CostEstimate(flops=0, bytes_accessed=10 * MIB, transcendentals=0),
    )(starts, counts, *got, cleared)


def size_sets():
    branches = []
    for hot in range(4):
        one, two = (2, 3) if hot < 2 else (1, 0)
        for paired, *sizes in AT_END if hot in (0, 3) else IN_MIDDLE:
            swaps = [{hot, one}, {hot, two}, {hot ^ 1, one}, {hot ^ 1, two}]
            branches.append((hot, [paired] + [sizes[swaps.index(set(swap))] for swap in SWAPS]))
    return branches + [(None, [16] * 5)]


BRANCHES = size_sets()


def choose(chips_ref, me, other, loads_ref, facts_ref):
    experts = 4
    requests = chips_ref.shape[2]
    for k in range(experts):
        chip = chips_ref.at[k]
        most = [jnp.int32(0)] * experts
        for section in range(2):

            def add(i, sums):
                fact = chip[section, i]
                owner, length = fact >> FACT_BITS, fact & (FACT - 1)
                part = length << ((owner >> 1) << 4)
                odd = (owner & 1) == 1
                return (sums[0] + jnp.where(odd, 0, part), sums[1] + jnp.where(odd, part, 0))

            even, odd = lax.fori_loop(0, requests, add, (jnp.int32(0), jnp.int32(0)), unroll=8)
            for o, sums in enumerate((even, odd, even >> 16, odd >> 16)):
                most[o] = jnp.maximum(most[o], ((sums & 0xFFFF) + UNIT - 1) >> UNIT_BITS)
        for o in range(experts):
            loads_ref[((me - k) & (experts - 1)) * experts + o] = most[o]

        def keep(i, _):
            facts_ref[1 + k * requests + i] = chip[other, i]
            return 0

        lax.fori_loop(0, requests, keep, 0, unroll=8)
    load = [[loads_ref[source * experts + o] for o in range(experts)] for source in range(experts)]
    hot, highest = jnp.int32(0), jnp.int32(-1)
    for o in range(experts):
        worst = functools.reduce(jnp.maximum, [load[source][o] for source in range(experts) if source != o])
        hot = jnp.where(worst > highest, o, hot)
        highest = jnp.maximum(worst, highest)
    needs = []
    for way in range(5):
        need = jnp.int32(0)
        for source, target in enumerate(targets_of(way)):
            if source != target:
                need = jnp.maximum(need, load[source][target])
            elif way == staying(source)[0]:
                need = jnp.maximum(need, jnp.minimum(load[source][source], SPLIT))
            else:
                need = jnp.maximum(need, load[source][source] - SPLIT)
        needs.append(need)
    branch = jnp.int32(len(BRANCHES) - 1)
    for at in range(len(BRANCHES) - 2, -1, -1):
        h, sizes = BRANCHES[at]
        fits = functools.reduce(jnp.logical_and, [need <= size for need, size in zip(needs, sizes)], hot == h)
        branch = jnp.where(fits, at, branch)
    facts_ref[0] = branch


def crossed(targets):
    return [(source * 2 + s, target * 2 + 1 - s) for source, target in enumerate(targets) for s in range(2)]


def by_halves(branches, operands):
    def run(low, high, operands):
        if high - low == 1:
            return branches[low](operands)
        middle = (low + high) // 2
        left, right = functools.partial(run, low, middle), functools.partial(run, middle, high)
        return lax.cond(operands[1][0] < middle, left, right, operands)

    return run(0, len(branches), operands)


def slot_layout(owner, experts, capacity):
    requests = owner.shape[0]
    indices = jnp.arange(requests, dtype=jnp.int32)
    earlier = indices[None, :] < indices[:, None]
    same_owner = owner[:, None] == owner[None, :]
    arrival_rank = jnp.sum(jnp.logical_and(same_owner, earlier), axis=1)
    target = owner * capacity + arrival_rank
    routing = target[None, :] == jnp.arange(experts * capacity, dtype=jnp.int32)[:, None]
    filled = jnp.any(routing, axis=1)
    source = jnp.sum(jnp.where(routing, indices[None, :], 0), axis=1)
    return (filled, source)


def pick_slots(values, filled, source):
    zero_value = jnp.zeros((), values.dtype)
    return jnp.where(filled[:, None, None], jnp.take(values, source, axis=0), zero_value)


def on_device(
    res_cache,
    res_scales,
    res_lengths,
    res_query,
    new_cache,
    new_scales,
    new_lengths,
    new_query,
    owner,
):
    experts = lax.axis_size("expert")
    sections = lax.axis_size("segment")
    requests, positions, columns = new_cache.shape
    capacity = max(2, 2 * requests // experts)
    swap = [(0, 1), (1, 0)]
    cache_t = jnp.transpose(new_cache, (0, 2, 1))
    res_inputs = (jnp.transpose(res_query, (0, 2, 1)), jnp.transpose(res_cache, (0, 2, 1)), res_scales, res_lengths)
    inputs = (res_inputs, (jnp.transpose(new_query, (0, 2, 1)), cache_t, new_scales, new_lengths))

    def attention(res_inputs, new_inputs):
        return attend(*res_inputs), attend(*new_inputs)

    if experts != 4 or sections != 2 or capacity * positions != 16 * UNIT or positions != 2 * UNIT or columns % 32:
        live_rows = jnp.arange(positions)[None, :] < new_lengths[:, None]
        zero_value = jnp.zeros((), jnp.bfloat16)
        filled, source = slot_layout(owner, experts, capacity)
        send_cache = pick_slots(jnp.where(live_rows[:, :, None], new_cache, zero_value), filled, source)
        send_scales = pick_slots(jnp.where(live_rows[:, None, :], new_scales, zero_value), filled, source)
        got_cache = lax.all_to_all(send_cache, "expert", split_axis=0, concat_axis=0, tiled=True)
        got_scales = lax.all_to_all(send_scales, "expert", split_axis=0, concat_axis=0, tiled=True)
        owned_cache, owned_scales = lax.ppermute((got_cache, got_scales), "segment", swap)
        return (*attention(*inputs), owned_cache, owned_scales)

    section = lax.axis_index("segment")
    units, half = capacity * positions // UNIT, columns // 2
    blocks = new_scales.shape[1]
    facts = owner * FACT + new_lengths
    sibling = lax.ppermute(facts, "segment", swap)
    chip = jnp.where(section == 0, jnp.stack([facts, sibling]), jnp.stack([sibling, facts]))
    chips = [chip] + [lax.ppermute(chip, "expert", [(e, (e + k) % 4) for e in range(4)]) for k in range(1, 4)]
    *streams, facts = pack(chips, new_scales, cache_t, units, capacity)

    def take(sizes):
        def run(operands):
            streams, facts, *inputs = operands
            got = []
            for way, size in enumerate(sizes):
                part = streams[way][: capacity * blocks + size * half]
                got.append(lax.ppermute(part, ("expert", "segment"), crossed(targets_of(way))))
            cleared, starts, counts = clear(facts, capacity, columns, positions)
            return (*attention(*inputs), *unpack(starts, counts, got, cleared, units, blocks))

        return run

    branches = [take(sizes) for _, sizes in BRANCHES]
    res_context, new_context, owned, owned_scales = by_halves(branches, (streams, facts, *inputs))
    return (res_context, new_context, jnp.transpose(owned, (0, 2, 1)), owned_scales)


def solution(mesh):
    placed = (
        P(("group", "expert", "segment", "attn"), None, None),
        P(("group", "expert", "segment", "attn"), None, None),
        P(("group", "expert", "segment", "attn")),
        P(("group", "expert", "segment", "attn"), None, None),
        P(("group", "expert", "segment", "attn"), None, None),
        P(("group", "expert", "segment", "attn"), None, None),
        P(("group", "expert", "segment", "attn")),
        P(("group", "expert", "segment", "attn"), None, None),
        P(("group", "expert", "segment", "attn")),
    )
    return jax.shard_map(
        on_device,
        mesh=mesh,
        in_specs=placed,
        out_specs=(
            P(("group", "expert", "segment", "attn"), None, None),
            P(("group", "expert", "segment", "attn"), None, None),
            P(("group", "expert", "segment", "attn"), None, None),
            P(("group", "expert", "segment", "attn"), None, None),
        ),
        check_vma=False,
    )
```

```python
import functools
import jax
import jax.numpy as jnp
from jax import lax
from jax.experimental import pallas as pl
from jax.experimental.pallas import tpu as pltpu
from jax.sharding import PartitionSpec as P

LATENT = 512
BLOCK = 128
UNIT_BITS = 6
UNIT = 1 << UNIT_BITS
SPLIT = 6
AT_END = ((14, 11, 11, 6, 8), (14, 12, 12, 7, 7), (13, 11, 14, 10, 6), (13, 14, 13, 8, 8))
IN_MIDDLE = ((12, 13, 11, 6, 7), (12, 11, 13, 7, 7), (14, 12, 11, 10, 10), (14, 14, 14, 8, 8))
SWAPS = ((0, 2), (0, 3), (1, 2), (1, 3))
FACT_BITS = 8
FACT = 1 << FACT_BITS

softmax_scale = 192.0 ** (-0.5)
MIB = 1 << 20


def attend_kernel(lengths_ref, query_ref, cache_ref, scales_ref, out_ref, factors_ref):
    blocks = scales_ref.shape[1]
    positions = cache_ref.shape[2]
    contract_rows = (((0,), (0,)), ((), ()))
    contract_positions = (((1,), (1,)), ((), ()))
    length = lengths_ref[pl.program_id(0)]

    def block(b):
        return pl.ds(pl.multiple_of(b * BLOCK, BLOCK), BLOCK)

    for b in range(blocks):
        factors_ref[b] = scales_ref[0, b : b + 1, :].astype(jnp.float32)

    def add(b, scores):
        part = lax.dot_general(
            query_ref[0, block(b), :], cache_ref[0, block(b), :], contract_rows, preferred_element_type=jnp.float32
        )
        return scores + part * factors_ref[b]

    scores = lax.dot_general(
        query_ref[0, LATENT:, :], cache_ref[0, LATENT:, :], contract_rows, preferred_element_type=jnp.float32
    )
    scores = lax.fori_loop(0, blocks, add, scores)
    live = lax.broadcasted_iota(jnp.int32, (1, positions), 1) < length
    scores = jnp.where(live, scores * softmax_scale, -jnp.inf)
    exponent = jnp.exp(scores - jnp.max(scores, axis=-1, keepdims=True))
    probabilities = exponent * (1.0 / jnp.sum(exponent, axis=-1, keepdims=True))

    def put(b, _):
        out_ref[0, :, block(b)] = lax.dot_general(
            (probabilities * factors_ref[b]).astype(jnp.bfloat16),
            cache_ref[0, block(b), :],
            contract_positions,
            preferred_element_type=jnp.float32,
        ).astype(jnp.bfloat16)
        return 0

    lax.fori_loop(0, blocks, put, 0)


def attend(query, cache, scales, lengths):
    requests, columns, heads = query.shape
    positions = cache.shape[2]
    return pl.pallas_call(
        attend_kernel,
        grid=(requests,),
        in_specs=[
            pl.BlockSpec(memory_space=pltpu.SMEM),
            pl.BlockSpec((1, columns, heads), lambda i: (i, 0, 0)),
            pl.BlockSpec((1, columns, positions), lambda i: (i, 0, 0)),
            pl.BlockSpec((1, scales.shape[1], positions), lambda i: (i, 0, 0)),
        ],
        out_specs=pl.BlockSpec((1, heads, LATENT), lambda i: (i, 0, 0)),
        out_shape=jax.ShapeDtypeStruct((requests, heads, LATENT), jnp.bfloat16),
        scratch_shapes=[pltpu.VMEM((scales.shape[1], 1, positions), jnp.float32)],
        compiler_params=pltpu.CompilerParams(vmem_limit_bytes=16 * MIB),
        cost_estimate=pl.CostEstimate(
            flops=4 * requests * heads * positions * columns,
            bytes_accessed=2 * requests * (heads * (columns + LATENT) + positions * columns),
            transcendentals=requests * heads * positions,
        ),
    )(lengths, query, cache, scales)


def lanes_of(rows):
    return lax.broadcasted_iota(jnp.int32, (rows, 2 * UNIT), 1).astype(jnp.bfloat16)


def turned(value, by):
    return pltpu.roll(value, by & (2 * UNIT - 1), 1)


def targets_of(way):
    if way == 0:
        return [e ^ 1 for e in range(4)]
    a, b = SWAPS[way - 1]
    return [b if e == a else a if e == b else e for e in range(4)]


def staying(e):
    return [way for way in range(5) if targets_of(way)[e] == e]


def pick(index, values):
    value = jnp.int32(values[0])
    for at in range(1, len(values)):
        value = jnp.where(index == at, values[at], value)
    return value


def pack_kernel(c0, c1, c2, c3, scales_ref, cache_ref, *refs):
    outs, facts_ref = refs[:5], refs[5]
    held, tiles, slots, ends, ranks, chips_ref, loads_ref, in_sem, chip_sem = refs[6:]
    experts = 4
    requests, columns, positions = cache_ref.shape
    blocks = scales_ref.shape[1]
    half = columns // 2
    tail = slots.shape[1]
    me = lax.axis_index("expert")
    parts = in_sem.shape[0]
    share = requests // parts

    def rows_of(unit):
        return pl.ds(pl.multiple_of(tail + unit * half, 16), half)

    def fetch(part):
        here = pl.ds(part * share, share)
        return pltpu.make_async_copy(cache_ref.at[here], held.at[here], in_sem.at[part])

    chips = [pltpu.make_async_copy(chip, chips_ref.at[k], chip_sem.at[k]) for k, chip in enumerate((c0, c1, c2, c3))]
    for chip in chips:
        chip.start()
    for part in range(parts):
        fetch(part).start()
    for chip in chips:
        chip.wait()
    section = lax.axis_index("segment")
    choose(chips_ref, me, 1 - section, loads_ref, facts_ref)
    lane = lanes_of(half)
    for k in range(experts):
        ends[k] = 0
        ranks[k] = 0
    slots[...] = jnp.zeros(slots.shape, jnp.float32)
    live = lax.broadcasted_iota(jnp.int32, (blocks, positions), 1)

    def place(i, _):
        fact = chips_ref[0, section, i]
        k, length = fact >> FACT_BITS, fact & (FACT - 1)
        start, rank = ends[k], ranks[k]
        ends[k] = start + length
        ranks[k] = rank + 1
        slots[k, pl.ds(rank * blocks, blocks), :] = jnp.where(live < length, scales_ref[i].astype(jnp.float32), 0.0)
        tile, shift = start >> (UNIT_BITS + 1), start & (2 * UNIT - 1)
        ahead = lane < shift.astype(jnp.bfloat16)
        for side in range(2):
            moved = turned(held[i, side * half : (side + 1) * half, :], shift)
            tiles[k, tile, side] = jnp.where(ahead, tiles[k, tile, side], moved)
            tiles[k, tile + 1, side] = moved
        return 0

    for part in range(parts):
        fetch(part).wait()
        lax.fori_loop(part * share, (part + 1) * share, place, 0, unroll=True)
    first = lane < float(UNIT)
    for way, out in enumerate(outs):
        k = pick(me, targets_of(way))
        out[:tail, :] = slots[k].astype(jnp.bfloat16)
        skipped = pick(me, [SPLIT if way == staying(e)[1] else 0 for e in range(experts)])

        def split(tile, _):
            upper, lower = tiles[k, tile, 0], tiles[k, tile, 1]
            swapped = turned(jnp.where(first, lower, upper), UNIT)
            out[rows_of(2 * tile - skipped), :] = jnp.where(first, upper, swapped)
            out[rows_of(2 * tile - skipped + 1), :] = jnp.where(first, swapped, lower)
            return 0

        lax.fori_loop(skipped >> 1, (ends[k] + positions - 1) >> (UNIT_BITS + 1), split, 0)


def pack(chips, scales, cache, units, capacity):
    requests, columns, positions = cache.shape
    half = columns // 2
    tail = capacity * scales.shape[1]
    smem = pl.BlockSpec(memory_space=pltpu.SMEM)
    vmem = pl.BlockSpec(memory_space=pltpu.VMEM)
    hbm = pl.BlockSpec(memory_space=pl.ANY)
    lanes = 2 * UNIT
    return pl.pallas_call(
        pack_kernel,
        in_specs=[hbm] * 4 + [vmem, hbm],
        out_specs=[vmem] * 5 + [smem],
        out_shape=[jax.ShapeDtypeStruct((tail + units * half, lanes), jnp.bfloat16)] * 5
        + [jax.ShapeDtypeStruct((1 + 4 * requests,), jnp.int32)],
        scratch_shapes=[
            pltpu.VMEM(cache.shape, jnp.bfloat16),
            pltpu.VMEM((4, units // 2 + 1, 2, half, lanes), jnp.bfloat16),
            pltpu.VMEM((4, tail, positions), jnp.float32),
            pltpu.SMEM((4,), jnp.int32),
            pltpu.SMEM((4,), jnp.int32),
            pltpu.SMEM((4,) + chips[0].shape, jnp.int32),
            pltpu.SMEM((16,), jnp.int32),
            pltpu.SemaphoreType.DMA((4,)),
            pltpu.SemaphoreType.DMA((4,)),
        ],
        compiler_params=pltpu.CompilerParams(vmem_limit_bytes=28 * MIB),
        cost_estimate=pl.CostEstimate(flops=2 * requests * half * 256, bytes_accessed=8 * MIB, transcendentals=0),
    )(*chips, scales, cache)


def clear_kernel(facts_ref, out_ref, starts, counts, zeros, sem):
    experts = 4
    requests = facts_ref.shape[0] // experts
    capacity = out_ref.shape[0] // experts
    me = lax.axis_index("expert")
    zeros[...] = jnp.zeros(zeros.shape, zeros.dtype)

    def scan(k, cleared):
        def note(i, carry):
            rank, end = carry
            fact = facts_ref[1 + k * requests + i]
            mine = fact >> FACT_BITS == me
            length = fact & (FACT - 1)

            @pl.when(mine)
            def _():
                starts[k, rank] = end
                counts[k, rank] = length

            return (jnp.where(mine, rank + 1, rank), jnp.where(mine, end + length, end))

        ranks, end = lax.fori_loop(0, requests, note, (0, 0))
        starts[k, capacity] = ranks
        counts[k, capacity] = (end + UNIT - 1) >> UNIT_BITS

        def clear(rank, _):
            starts[k, rank] = 0
            counts[k, rank] = 0
            slot = ((me - k) & (experts - 1)) * capacity + rank
            pltpu.make_async_copy(zeros, out_ref.at[slot], sem).start()
            return 0

        lax.fori_loop(ranks, capacity, clear, 0)
        return cleared + capacity - ranks

    def done(_, carry):
        pltpu.make_async_copy(zeros, out_ref.at[0], sem).wait()
        return carry

    lax.fori_loop(0, lax.fori_loop(0, experts, scan, 0), done, 0)


def clear(facts, capacity, columns, positions):
    smem = pl.BlockSpec(memory_space=pltpu.SMEM)
    table = jax.ShapeDtypeStruct((4, capacity + 1), jnp.int32)
    return pl.pallas_call(
        clear_kernel,
        in_specs=[smem],
        out_specs=[pl.BlockSpec(memory_space=pl.ANY), smem, smem],
        out_shape=[jax.ShapeDtypeStruct((4 * capacity, columns, positions), jnp.bfloat16), table, table],
        scratch_shapes=[pltpu.VMEM((columns, positions), jnp.bfloat16), pltpu.SemaphoreType.DMA],
        compiler_params=pltpu.CompilerParams(vmem_limit_bytes=8 * MIB),
        cost_estimate=pl.CostEstimate(flops=0, bytes_accessed=3 * MIB, transcendentals=0),
    )(facts)


def unpack_kernel(starts, counts, g0, g1, g2, g3, g4, cleared_ref, out_ref, scales_ref, *scratch):
    tiles, stage, tails, sem = scratch
    got = (g0, g1, g2, g3, g4)
    experts = 4
    capacity = out_ref.shape[0] // experts
    columns, positions = out_ref.shape[1], out_ref.shape[2]
    half = columns // 2
    tail = tails.shape[1]
    blocks = tail // capacity
    me = lax.axis_index("expert")
    lane = lanes_of(half)
    first = lane < float(UNIT)

    def units_of(unit):
        return pl.ds(pl.multiple_of(tail + unit * half, 16), half)

    def source_of(k):
        return (me - k) & (experts - 1)

    def write(k, rank):
        return pltpu.make_async_copy(stage.at[k, rank], out_ref.at[source_of(k) * capacity + rank], sem)

    def put_stream(k, written):
        used, ranks = counts[k, capacity], starts[k, capacity]
        for way in range(5):
            came = pick(source_of(k), targets_of(way)) == me
            later = jnp.logical_and(k == 0, pick(me, [int(way == staying(e)[1]) for e in range(experts)]) == 1)
            low = jnp.where(later, SPLIT, 0)
            high = jnp.where(jnp.logical_and(k == 0, jnp.logical_not(later)), jnp.minimum(used, SPLIT), used)
            units = (got[way].shape[0] - tail) // half

            @pl.when(came)
            def _():
                @pl.when(jnp.logical_not(later))
                def _():
                    tails[k] = got[way][:tail, :].astype(jnp.float32)

                def join(tile, _):
                    one = got[way][units_of(2 * tile - low), :]
                    two = got[way][units_of(jnp.minimum(2 * tile - low + 1, units - 1)), :]
                    swapped = turned(jnp.where(first, two, one), UNIT)
                    tiles[k, tile, 0] = jnp.where(first, one, swapped)
                    tiles[k, tile, 1] = jnp.where(first, swapped, two)
                    return 0

                lax.fori_loop(low >> 1, (high + 1) >> 1, join, 0)

        def put(rank, _):
            start, length = starts[k, rank], counts[k, rank]
            tile, shift = start >> (UNIT_BITS + 1), start & (2 * UNIT - 1)
            behind = lane < shift.astype(jnp.bfloat16)
            live = lane < length.astype(jnp.bfloat16)
            for side in range(2):
                both = jnp.where(behind, tiles[k, tile + 1, side], tiles[k, tile, side])
                value = jnp.where(live, turned(both, 2 * UNIT - shift), jnp.zeros((), jnp.bfloat16))
                stage[k, rank, side * half : (side + 1) * half, :] = value
            write(k, rank).start()
            return 0

        lax.fori_loop(0, ranks, put, 0)
        for rank in range(capacity):
            scales = tails[k, rank * blocks : (rank + 1) * blocks, :]
            scales_ref[source_of(k) * capacity + rank] = scales.astype(jnp.bfloat16)
        return written + ranks

    def done(_, carry):
        write(0, 0).wait()
        return carry

    lax.fori_loop(0, lax.fori_loop(0, experts, put_stream, 0), done, 0)


def unpack(starts, counts, got, cleared, units, blocks):
    slots, columns, positions = cleared.shape
    capacity, half = slots // 4, columns // 2
    smem = pl.BlockSpec(memory_space=pltpu.SMEM)
    vmem = pl.BlockSpec(memory_space=pltpu.VMEM)
    hbm = pl.BlockSpec(memory_space=pl.ANY)
    return pl.pallas_call(
        unpack_kernel,
        in_specs=[smem] * 2 + [vmem] * 5 + [hbm],
        out_specs=[hbm, vmem],
        out_shape=[
            jax.ShapeDtypeStruct(cleared.shape, cleared.dtype),
            jax.ShapeDtypeStruct((slots, blocks, positions), cleared.dtype),
        ],
        input_output_aliases={7: 0},
        scratch_shapes=[
            pltpu.VMEM((4, units // 2 + 1, 2, half, positions), jnp.bfloat16),
            pltpu.VMEM((4, capacity, columns, positions), jnp.bfloat16),
            pltpu.VMEM((4, capacity * blocks, positions), jnp.float32),
            pltpu.SemaphoreType.DMA,
        ],
        compiler_params=pltpu.CompilerParams(vmem_limit_bytes=24 * MIB),
        cost_estimate=pl.CostEstimate(flops=0, bytes_accessed=10 * MIB, transcendentals=0),
    )(starts, counts, *got, cleared)


def size_sets():
    branches = []
    for hot in range(4):
        one, two = (2, 3) if hot < 2 else (1, 0)
        for paired, *sizes in AT_END if hot in (0, 3) else IN_MIDDLE:
            swaps = [{hot, one}, {hot, two}, {hot ^ 1, one}, {hot ^ 1, two}]
            branches.append((hot, [paired] + [sizes[swaps.index(set(swap))] for swap in SWAPS]))
    return branches + [(None, [16] * 5)]


BRANCHES = size_sets()


def choose(chips_ref, me, other, loads_ref, facts_ref):
    experts = 4
    requests = chips_ref.shape[2]
    for k in range(experts):
        chip = chips_ref.at[k]
        most = [jnp.int32(0)] * experts
        for section in range(2):

            def add(i, sums):
                fact = chip[section, i]
                owner, length = fact >> FACT_BITS, fact & (FACT - 1)
                part = length << ((owner >> 1) << 4)
                odd = (owner & 1) == 1
                return (sums[0] + jnp.where(odd, 0, part), sums[1] + jnp.where(odd, part, 0))

            even, odd = lax.fori_loop(0, requests, add, (jnp.int32(0), jnp.int32(0)), unroll=8)
            for o, sums in enumerate((even, odd, even >> 16, odd >> 16)):
                most[o] = jnp.maximum(most[o], ((sums & 0xFFFF) + UNIT - 1) >> UNIT_BITS)
        for o in range(experts):
            loads_ref[((me - k) & (experts - 1)) * experts + o] = most[o]

        def keep(i, _):
            facts_ref[1 + k * requests + i] = chip[other, i]
            return 0

        lax.fori_loop(0, requests, keep, 0, unroll=8)
    load = [[loads_ref[source * experts + o] for o in range(experts)] for source in range(experts)]
    hot, highest = jnp.int32(0), jnp.int32(-1)
    for o in range(experts):
        worst = functools.reduce(jnp.maximum, [load[source][o] for source in range(experts) if source != o])
        hot = jnp.where(worst > highest, o, hot)
        highest = jnp.maximum(worst, highest)
    needs = []
    for way in range(5):
        need = jnp.int32(0)
        for source, target in enumerate(targets_of(way)):
            if source != target:
                need = jnp.maximum(need, load[source][target])
            elif way == staying(source)[0]:
                need = jnp.maximum(need, jnp.minimum(load[source][source], SPLIT))
            else:
                need = jnp.maximum(need, load[source][source] - SPLIT)
        needs.append(need)
    branch = jnp.int32(len(BRANCHES) - 1)
    for at in range(len(BRANCHES) - 2, -1, -1):
        h, sizes = BRANCHES[at]
        fits = functools.reduce(jnp.logical_and, [need <= size for need, size in zip(needs, sizes)], hot == h)
        branch = jnp.where(fits, at, branch)
    facts_ref[0] = branch


def crossed(targets):
    return [(source * 2 + s, target * 2 + 1 - s) for source, target in enumerate(targets) for s in range(2)]


def by_halves(branches, operands):
    def run(low, high, operands):
        if high - low == 1:
            return branches[low](operands)
        middle = (low + high) // 2
        left, right = functools.partial(run, low, middle), functools.partial(run, middle, high)
        return lax.cond(operands[1][0] < middle, left, right, operands)

    return run(0, len(branches), operands)


def slot_layout(owner, experts, capacity):
    requests = owner.shape[0]
    indices = jnp.arange(requests, dtype=jnp.int32)
    earlier = indices[None, :] < indices[:, None]
    same_owner = owner[:, None] == owner[None, :]
    arrival_rank = jnp.sum(jnp.logical_and(same_owner, earlier), axis=1)
    target = owner * capacity + arrival_rank
    routing = target[None, :] == jnp.arange(experts * capacity, dtype=jnp.int32)[:, None]
    filled = jnp.any(routing, axis=1)
    source = jnp.sum(jnp.where(routing, indices[None, :], 0), axis=1)
    return (filled, source)


def pick_slots(values, filled, source):
    zero_value = jnp.zeros((), values.dtype)
    return jnp.where(filled[:, None, None], jnp.take(values, source, axis=0), zero_value)


def on_device(
    res_cache,
    res_scales,
    res_lengths,
    res_query,
    new_cache,
    new_scales,
    new_lengths,
    new_query,
    owner,
):
    experts = lax.axis_size("expert")
    sections = lax.axis_size("segment")
    requests, positions, columns = new_cache.shape
    capacity = max(2, 2 * requests // experts)
    swap = [(0, 1), (1, 0)]
    cache_t = jnp.transpose(new_cache, (0, 2, 1))
    res_inputs = (jnp.transpose(res_query, (0, 2, 1)), jnp.transpose(res_cache, (0, 2, 1)), res_scales, res_lengths)
    inputs = (res_inputs, (jnp.transpose(new_query, (0, 2, 1)), cache_t, new_scales, new_lengths))

    def attention(res_inputs, new_inputs):
        return attend(*res_inputs), attend(*new_inputs)

    if experts != 4 or sections != 2 or capacity * positions != 16 * UNIT or positions != 2 * UNIT or columns % 32:
        live_rows = jnp.arange(positions)[None, :] < new_lengths[:, None]
        zero_value = jnp.zeros((), jnp.bfloat16)
        filled, source = slot_layout(owner, experts, capacity)
        send_cache = pick_slots(jnp.where(live_rows[:, :, None], new_cache, zero_value), filled, source)
        send_scales = pick_slots(jnp.where(live_rows[:, None, :], new_scales, zero_value), filled, source)
        got_cache = lax.all_to_all(send_cache, "expert", split_axis=0, concat_axis=0, tiled=True)
        got_scales = lax.all_to_all(send_scales, "expert", split_axis=0, concat_axis=0, tiled=True)
        owned_cache, owned_scales = lax.ppermute((got_cache, got_scales), "segment", swap)
        return (*attention(*inputs), owned_cache, owned_scales)

    section = lax.axis_index("segment")
    units, half = capacity * positions // UNIT, columns // 2
    blocks = new_scales.shape[1]
    facts = owner * FACT + new_lengths
    sibling = lax.ppermute(facts, "segment", swap)
    chip = jnp.where(section == 0, jnp.stack([facts, sibling]), jnp.stack([sibling, facts]))
    chips = [chip] + [lax.ppermute(chip, "expert", [(e, (e + k) % 4) for e in range(4)]) for k in range(1, 4)]
    *streams, facts = pack(chips, new_scales, cache_t, units, capacity)

    def take(sizes):
        def run(operands):
            streams, facts, *inputs = operands
            got = []
            for way, size in enumerate(sizes):
                part = streams[way][: capacity * blocks + size * half]
                got.append(lax.ppermute(part, ("expert", "segment"), crossed(targets_of(way))))
            cleared, starts, counts = clear(facts, capacity, columns, positions)
            return (*attention(*inputs), *unpack(starts, counts, got, cleared, units, blocks))

        return run

    branches = [take(sizes) for _, sizes in BRANCHES]
    res_context, new_context, owned, owned_scales = by_halves(branches, (streams, facts, *inputs))
    return (res_context, new_context, jnp.transpose(owned, (0, 2, 1)), owned_scales)


def solution(mesh):
    placed = (
        P(("group", "expert", "segment", "attn"), None, None),
        P(("group", "expert", "segment", "attn"), None, None),
        P(("group", "expert", "segment", "attn")),
        P(("group", "expert", "segment", "attn"), None, None),
        P(("group", "expert", "segment", "attn"), None, None),
        P(("group", "expert", "segment", "attn"), None, None),
        P(("group", "expert", "segment", "attn")),
        P(("group", "expert", "segment", "attn"), None, None),
        P(("group", "expert", "segment", "attn")),
    )
    return jax.shard_map(
        on_device,
        mesh=mesh,
        in_specs=placed,
        out_specs=(
            P(("group", "expert", "segment", "attn"), None, None),
            P(("group", "expert", "segment", "attn"), None, None),
            P(("group", "expert", "segment", "attn"), None, None),
            P(("group", "expert", "segment", "attn"), None, None),
        ),
        check_vma=False,
    )
```

```python
import functools
import jax
import jax.numpy as jnp
from jax import lax
from jax.experimental import pallas as pl
from jax.experimental.pallas import tpu as pltpu
from jax.sharding import PartitionSpec as P

LATENT = 512
BLOCK = 128
UNIT_BITS = 6
UNIT = 1 << UNIT_BITS
SPLIT = 6
AT_END = ((13, 12, 12, 7, 6), (15, 11, 11, 8, 7), (14, 13, 12, 6, 8), (15, 11, 14, 10, 6), (16, 14, 13, 8, 10))
IN_MIDDLE = ((13, 13, 11, 6, 7), (14, 11, 13, 7, 6), (13, 12, 11, 9, 9), (14, 14, 15, 8, 8))
SWAPS = ((0, 2), (0, 3), (1, 2), (1, 3))
FACT_BITS = 8
FACT = 1 << FACT_BITS

softmax_scale = 192.0 ** (-0.5)
MIB = 1 << 20


def attend_kernel(lengths_ref, query_ref, cache_ref, scales_ref, out_ref, factors_ref):
    blocks = scales_ref.shape[1]
    positions = cache_ref.shape[2]
    contract_rows = (((0,), (0,)), ((), ()))
    contract_positions = (((1,), (1,)), ((), ()))
    length = lengths_ref[pl.program_id(0)]

    def block(b):
        return pl.ds(pl.multiple_of(b * BLOCK, BLOCK), BLOCK)

    for b in range(blocks):
        factors_ref[b] = scales_ref[0, b : b + 1, :].astype(jnp.float32)

    def add(b, scores):
        part = lax.dot_general(
            query_ref[0, block(b), :], cache_ref[0, block(b), :], contract_rows, preferred_element_type=jnp.float32
        )
        return scores + part * factors_ref[b]

    scores = lax.dot_general(
        query_ref[0, LATENT:, :], cache_ref[0, LATENT:, :], contract_rows, preferred_element_type=jnp.float32
    )
    scores = lax.fori_loop(0, blocks, add, scores)
    live = lax.broadcasted_iota(jnp.int32, (1, positions), 1) < length
    scores = jnp.where(live, scores * softmax_scale, -jnp.inf)
    exponent = jnp.exp(scores - jnp.max(scores, axis=-1, keepdims=True))
    probabilities = exponent * (1.0 / jnp.sum(exponent, axis=-1, keepdims=True))

    def put(b, _):
        out_ref[0, :, block(b)] = lax.dot_general(
            (probabilities * factors_ref[b]).astype(jnp.bfloat16),
            cache_ref[0, block(b), :],
            contract_positions,
            preferred_element_type=jnp.float32,
        ).astype(jnp.bfloat16)
        return 0

    lax.fori_loop(0, blocks, put, 0)


def attend(query, cache, scales, lengths):
    requests, columns, heads = query.shape
    positions = cache.shape[2]
    return pl.pallas_call(
        attend_kernel,
        grid=(requests,),
        in_specs=[
            pl.BlockSpec(memory_space=pltpu.SMEM),
            pl.BlockSpec((1, columns, heads), lambda i: (i, 0, 0)),
            pl.BlockSpec((1, columns, positions), lambda i: (i, 0, 0)),
            pl.BlockSpec((1, scales.shape[1], positions), lambda i: (i, 0, 0)),
        ],
        out_specs=pl.BlockSpec((1, heads, LATENT), lambda i: (i, 0, 0)),
        out_shape=jax.ShapeDtypeStruct((requests, heads, LATENT), jnp.bfloat16),
        scratch_shapes=[pltpu.VMEM((scales.shape[1], 1, positions), jnp.float32)],
        compiler_params=pltpu.CompilerParams(vmem_limit_bytes=16 * MIB),
        cost_estimate=pl.CostEstimate(
            flops=4 * requests * heads * positions * columns,
            bytes_accessed=2 * requests * (heads * (columns + LATENT) + positions * columns),
            transcendentals=requests * heads * positions,
        ),
    )(lengths, query, cache, scales)


def lanes_of(rows):
    return lax.broadcasted_iota(jnp.int32, (rows, 2 * UNIT), 1).astype(jnp.bfloat16)


def turned(value, by):
    return pltpu.roll(value, by & (2 * UNIT - 1), 1)


def targets_of(way):
    if way == 0:
        return [e ^ 1 for e in range(4)]
    a, b = SWAPS[way - 1]
    return [b if e == a else a if e == b else e for e in range(4)]


def staying(e):
    return [way for way in range(5) if targets_of(way)[e] == e]


def pick(index, values):
    value = jnp.int32(values[0])
    for at in range(1, len(values)):
        value = jnp.where(index == at, values[at], value)
    return value


def pack_kernel(c0, c1, c2, c3, scales_ref, cache_ref, *refs):
    outs, facts_ref = refs[:5], refs[5]
    held, tiles, slots, ends, ranks, chips_ref, loads_ref, in_sem, chip_sem = refs[6:]
    experts = 4
    requests, columns, positions = cache_ref.shape
    blocks = scales_ref.shape[1]
    half = columns // 2
    tail = slots.shape[1]
    me = lax.axis_index("expert")
    parts = in_sem.shape[0]
    share = requests // parts

    def rows_of(unit):
        return pl.ds(pl.multiple_of(tail + unit * half, 16), half)

    def fetch(part):
        here = pl.ds(part * share, share)
        return pltpu.make_async_copy(cache_ref.at[here], held.at[here], in_sem.at[part])

    chips = [pltpu.make_async_copy(chip, chips_ref.at[k], chip_sem.at[k]) for k, chip in enumerate((c0, c1, c2, c3))]
    for chip in chips:
        chip.start()
    for part in range(parts):
        fetch(part).start()
    for chip in chips:
        chip.wait()
    section = lax.axis_index("segment")
    choose(chips_ref, me, 1 - section, loads_ref, facts_ref)
    lane = lanes_of(half)
    for k in range(experts):
        ends[k] = 0
        ranks[k] = 0
    slots[...] = jnp.zeros(slots.shape, jnp.float32)
    live = lax.broadcasted_iota(jnp.int32, (blocks, positions), 1)

    def place(i, _):
        fact = chips_ref[0, section, i]
        k, length = fact >> FACT_BITS, fact & (FACT - 1)
        start, rank = ends[k], ranks[k]
        ends[k] = start + length
        ranks[k] = rank + 1
        slots[k, pl.ds(rank * blocks, blocks), :] = jnp.where(live < length, scales_ref[i].astype(jnp.float32), 0.0)
        tile, shift = start >> (UNIT_BITS + 1), start & (2 * UNIT - 1)
        ahead = lane < shift.astype(jnp.bfloat16)
        for side in range(2):
            moved = turned(held[i, side * half : (side + 1) * half, :], shift)
            tiles[k, tile, side] = jnp.where(ahead, tiles[k, tile, side], moved)
            tiles[k, tile + 1, side] = moved
        return 0

    for part in range(parts):
        fetch(part).wait()
        lax.fori_loop(part * share, (part + 1) * share, place, 0, unroll=True)
    first = lane < float(UNIT)
    for way, out in enumerate(outs):
        k = pick(me, targets_of(way))
        out[:tail, :] = slots[k].astype(jnp.bfloat16)
        skipped = pick(me, [SPLIT if way == staying(e)[1] else 0 for e in range(experts)])

        def split(tile, _):
            upper, lower = tiles[k, tile, 0], tiles[k, tile, 1]
            swapped = turned(jnp.where(first, lower, upper), UNIT)
            out[rows_of(2 * tile - skipped), :] = jnp.where(first, upper, swapped)
            out[rows_of(2 * tile - skipped + 1), :] = jnp.where(first, swapped, lower)
            return 0

        lax.fori_loop(skipped >> 1, (ends[k] + positions - 1) >> (UNIT_BITS + 1), split, 0)


def pack(chips, scales, cache, units, capacity):
    requests, columns, positions = cache.shape
    half = columns // 2
    tail = capacity * scales.shape[1]
    smem = pl.BlockSpec(memory_space=pltpu.SMEM)
    vmem = pl.BlockSpec(memory_space=pltpu.VMEM)
    hbm = pl.BlockSpec(memory_space=pl.ANY)
    lanes = 2 * UNIT
    return pl.pallas_call(
        pack_kernel,
        in_specs=[hbm] * 4 + [vmem, hbm],
        out_specs=[vmem] * 5 + [smem],
        out_shape=[jax.ShapeDtypeStruct((tail + units * half, lanes), jnp.bfloat16)] * 5
        + [jax.ShapeDtypeStruct((1 + 4 * requests,), jnp.int32)],
        scratch_shapes=[
            pltpu.VMEM(cache.shape, jnp.bfloat16),
            pltpu.VMEM((4, units // 2 + 1, 2, half, lanes), jnp.bfloat16),
            pltpu.VMEM((4, tail, positions), jnp.float32),
            pltpu.SMEM((4,), jnp.int32),
            pltpu.SMEM((4,), jnp.int32),
            pltpu.SMEM((4,) + chips[0].shape, jnp.int32),
            pltpu.SMEM((16,), jnp.int32),
            pltpu.SemaphoreType.DMA((4,)),
            pltpu.SemaphoreType.DMA((4,)),
        ],
        compiler_params=pltpu.CompilerParams(vmem_limit_bytes=28 * MIB),
        cost_estimate=pl.CostEstimate(flops=2 * requests * half * 256, bytes_accessed=8 * MIB, transcendentals=0),
    )(*chips, scales, cache)


def clear_kernel(facts_ref, out_ref, starts, counts, zeros, sem):
    experts = 4
    requests = facts_ref.shape[0] // experts
    capacity = out_ref.shape[0] // experts
    me = lax.axis_index("expert")
    zeros[...] = jnp.zeros(zeros.shape, zeros.dtype)

    def scan(k, cleared):
        def note(i, carry):
            rank, end = carry
            fact = facts_ref[1 + k * requests + i]
            mine = fact >> FACT_BITS == me
            length = fact & (FACT - 1)

            @pl.when(mine)
            def _():
                starts[k, rank] = end
                counts[k, rank] = length

            return (jnp.where(mine, rank + 1, rank), jnp.where(mine, end + length, end))

        ranks, end = lax.fori_loop(0, requests, note, (0, 0))
        starts[k, capacity] = ranks
        counts[k, capacity] = (end + UNIT - 1) >> UNIT_BITS

        def clear(rank, _):
            starts[k, rank] = 0
            counts[k, rank] = 0
            slot = ((me - k) & (experts - 1)) * capacity + rank
            pltpu.make_async_copy(zeros, out_ref.at[slot], sem).start()
            return 0

        lax.fori_loop(ranks, capacity, clear, 0)
        return cleared + capacity - ranks

    def done(_, carry):
        pltpu.make_async_copy(zeros, out_ref.at[0], sem).wait()
        return carry

    lax.fori_loop(0, lax.fori_loop(0, experts, scan, 0), done, 0)


def clear(facts, capacity, columns, positions):
    smem = pl.BlockSpec(memory_space=pltpu.SMEM)
    table = jax.ShapeDtypeStruct((4, capacity + 1), jnp.int32)
    return pl.pallas_call(
        clear_kernel,
        in_specs=[smem],
        out_specs=[pl.BlockSpec(memory_space=pl.ANY), smem, smem],
        out_shape=[jax.ShapeDtypeStruct((4 * capacity, columns, positions), jnp.bfloat16), table, table],
        scratch_shapes=[pltpu.VMEM((columns, positions), jnp.bfloat16), pltpu.SemaphoreType.DMA],
        compiler_params=pltpu.CompilerParams(vmem_limit_bytes=8 * MIB),
        cost_estimate=pl.CostEstimate(flops=0, bytes_accessed=3 * MIB, transcendentals=0),
    )(facts)


def unpack_kernel(starts, counts, g0, g1, g2, g3, g4, cleared_ref, out_ref, scales_ref, *scratch):
    tiles, stage, tails, sem = scratch
    got = (g0, g1, g2, g3, g4)
    experts = 4
    capacity = out_ref.shape[0] // experts
    columns, positions = out_ref.shape[1], out_ref.shape[2]
    half = columns // 2
    tail = tails.shape[1]
    blocks = tail // capacity
    me = lax.axis_index("expert")
    lane = lanes_of(half)
    first = lane < float(UNIT)

    def units_of(unit):
        return pl.ds(pl.multiple_of(tail + unit * half, 16), half)

    def source_of(k):
        return (me - k) & (experts - 1)

    def write(k, rank):
        return pltpu.make_async_copy(stage.at[k, rank], out_ref.at[source_of(k) * capacity + rank], sem)

    def put_stream(k, written):
        used, ranks = counts[k, capacity], starts[k, capacity]
        for way in range(5):
            came = pick(source_of(k), targets_of(way)) == me
            later = jnp.logical_and(k == 0, pick(me, [int(way == staying(e)[1]) for e in range(experts)]) == 1)
            low = jnp.where(later, SPLIT, 0)
            high = jnp.where(jnp.logical_and(k == 0, jnp.logical_not(later)), jnp.minimum(used, SPLIT), used)
            units = (got[way].shape[0] - tail) // half

            @pl.when(came)
            def _():
                @pl.when(jnp.logical_not(later))
                def _():
                    tails[k] = got[way][:tail, :].astype(jnp.float32)

                def join(tile, _):
                    one = got[way][units_of(2 * tile - low), :]
                    two = got[way][units_of(jnp.minimum(2 * tile - low + 1, units - 1)), :]
                    swapped = turned(jnp.where(first, two, one), UNIT)
                    tiles[k, tile, 0] = jnp.where(first, one, swapped)
                    tiles[k, tile, 1] = jnp.where(first, swapped, two)
                    return 0

                lax.fori_loop(low >> 1, (high + 1) >> 1, join, 0)

        def put(rank, _):
            start, length = starts[k, rank], counts[k, rank]
            tile, shift = start >> (UNIT_BITS + 1), start & (2 * UNIT - 1)
            behind = lane < shift.astype(jnp.bfloat16)
            live = lane < length.astype(jnp.bfloat16)
            for side in range(2):
                both = jnp.where(behind, tiles[k, tile + 1, side], tiles[k, tile, side])
                value = jnp.where(live, turned(both, 2 * UNIT - shift), jnp.zeros((), jnp.bfloat16))
                stage[k, rank, side * half : (side + 1) * half, :] = value
            write(k, rank).start()
            return 0

        lax.fori_loop(0, ranks, put, 0)
        for rank in range(capacity):
            scales = tails[k, rank * blocks : (rank + 1) * blocks, :]
            scales_ref[source_of(k) * capacity + rank] = scales.astype(jnp.bfloat16)
        return written + ranks

    def done(_, carry):
        write(0, 0).wait()
        return carry

    lax.fori_loop(0, lax.fori_loop(0, experts, put_stream, 0), done, 0)


def unpack(starts, counts, got, cleared, units, blocks):
    slots, columns, positions = cleared.shape
    capacity, half = slots // 4, columns // 2
    smem = pl.BlockSpec(memory_space=pltpu.SMEM)
    vmem = pl.BlockSpec(memory_space=pltpu.VMEM)
    hbm = pl.BlockSpec(memory_space=pl.ANY)
    return pl.pallas_call(
        unpack_kernel,
        in_specs=[smem] * 2 + [vmem] * 5 + [hbm],
        out_specs=[hbm, vmem],
        out_shape=[
            jax.ShapeDtypeStruct(cleared.shape, cleared.dtype),
            jax.ShapeDtypeStruct((slots, blocks, positions), cleared.dtype),
        ],
        input_output_aliases={7: 0},
        scratch_shapes=[
            pltpu.VMEM((4, units // 2 + 1, 2, half, positions), jnp.bfloat16),
            pltpu.VMEM((4, capacity, columns, positions), jnp.bfloat16),
            pltpu.VMEM((4, capacity * blocks, positions), jnp.float32),
            pltpu.SemaphoreType.DMA,
        ],
        compiler_params=pltpu.CompilerParams(vmem_limit_bytes=24 * MIB),
        cost_estimate=pl.CostEstimate(flops=0, bytes_accessed=10 * MIB, transcendentals=0),
    )(starts, counts, *got, cleared)


def size_sets():
    branches = []
    for hot in range(4):
        one, two = (2, 3) if hot < 2 else (1, 0)
        for paired, *sizes in AT_END if hot in (0, 3) else IN_MIDDLE:
            swaps = [{hot, one}, {hot, two}, {hot ^ 1, one}, {hot ^ 1, two}]
            branches.append((hot, [paired] + [sizes[swaps.index(set(swap))] for swap in SWAPS]))
    return branches + [(None, [16] * 5)]


BRANCHES = size_sets()


def choose(chips_ref, me, other, loads_ref, facts_ref):
    experts = 4
    requests = chips_ref.shape[2]
    for k in range(experts):
        chip = chips_ref.at[k]
        most = [jnp.int32(0)] * experts
        for section in range(2):

            def add(i, sums):
                fact = chip[section, i]
                owner, length = fact >> FACT_BITS, fact & (FACT - 1)
                part = length << ((owner >> 1) << 4)
                odd = (owner & 1) == 1
                return (sums[0] + jnp.where(odd, 0, part), sums[1] + jnp.where(odd, part, 0))

            even, odd = lax.fori_loop(0, requests, add, (jnp.int32(0), jnp.int32(0)), unroll=8)
            for o, sums in enumerate((even, odd, even >> 16, odd >> 16)):
                most[o] = jnp.maximum(most[o], ((sums & 0xFFFF) + UNIT - 1) >> UNIT_BITS)
        for o in range(experts):
            loads_ref[((me - k) & (experts - 1)) * experts + o] = most[o]

        def keep(i, _):
            facts_ref[1 + k * requests + i] = chip[other, i]
            return 0

        lax.fori_loop(0, requests, keep, 0, unroll=8)
    load = [[loads_ref[source * experts + o] for o in range(experts)] for source in range(experts)]
    hot, highest = jnp.int32(0), jnp.int32(-1)
    for o in range(experts):
        worst = functools.reduce(jnp.maximum, [load[source][o] for source in range(experts) if source != o])
        hot = jnp.where(worst > highest, o, hot)
        highest = jnp.maximum(worst, highest)
    needs = []
    for way in range(5):
        need = jnp.int32(0)
        for source, target in enumerate(targets_of(way)):
            if source != target:
                need = jnp.maximum(need, load[source][target])
            elif way == staying(source)[0]:
                need = jnp.maximum(need, jnp.minimum(load[source][source], SPLIT))
            else:
                need = jnp.maximum(need, load[source][source] - SPLIT)
        needs.append(need)
    branch = jnp.int32(len(BRANCHES) - 1)
    for at in range(len(BRANCHES) - 2, -1, -1):
        h, sizes = BRANCHES[at]
        fits = functools.reduce(jnp.logical_and, [need <= size for need, size in zip(needs, sizes)], hot == h)
        branch = jnp.where(fits, at, branch)
    facts_ref[0] = branch


def crossed(targets):
    return [(source * 2 + s, target * 2 + 1 - s) for source, target in enumerate(targets) for s in range(2)]


def by_halves(branches, operands):
    def run(low, high, operands):
        if high - low == 1:
            return branches[low](operands)
        middle = (low + high) // 2
        left, right = functools.partial(run, low, middle), functools.partial(run, middle, high)
        return lax.cond(operands[1][0] < middle, left, right, operands)

    return run(0, len(branches), operands)


def slot_layout(owner, experts, capacity):
    requests = owner.shape[0]
    indices = jnp.arange(requests, dtype=jnp.int32)
    earlier = indices[None, :] < indices[:, None]
    same_owner = owner[:, None] == owner[None, :]
    arrival_rank = jnp.sum(jnp.logical_and(same_owner, earlier), axis=1)
    target = owner * capacity + arrival_rank
    routing = target[None, :] == jnp.arange(experts * capacity, dtype=jnp.int32)[:, None]
    filled = jnp.any(routing, axis=1)
    source = jnp.sum(jnp.where(routing, indices[None, :], 0), axis=1)
    return (filled, source)


def pick_slots(values, filled, source):
    zero_value = jnp.zeros((), values.dtype)
    return jnp.where(filled[:, None, None], jnp.take(values, source, axis=0), zero_value)


def on_device(
    res_cache,
    res_scales,
    res_lengths,
    res_query,
    new_cache,
    new_scales,
    new_lengths,
    new_query,
    owner,
):
    experts = lax.axis_size("expert")
    sections = lax.axis_size("segment")
    requests, positions, columns = new_cache.shape
    capacity = max(2, 2 * requests // experts)
    swap = [(0, 1), (1, 0)]
    cache_t = jnp.transpose(new_cache, (0, 2, 1))
    res_inputs = (jnp.transpose(res_query, (0, 2, 1)), jnp.transpose(res_cache, (0, 2, 1)), res_scales, res_lengths)
    inputs = (res_inputs, (jnp.transpose(new_query, (0, 2, 1)), cache_t, new_scales, new_lengths))

    def attention(res_inputs, new_inputs):
        return attend(*res_inputs), attend(*new_inputs)

    if experts != 4 or sections != 2 or capacity * positions != 16 * UNIT or positions != 2 * UNIT or columns % 32:
        live_rows = jnp.arange(positions)[None, :] < new_lengths[:, None]
        zero_value = jnp.zeros((), jnp.bfloat16)
        filled, source = slot_layout(owner, experts, capacity)
        send_cache = pick_slots(jnp.where(live_rows[:, :, None], new_cache, zero_value), filled, source)
        send_scales = pick_slots(jnp.where(live_rows[:, None, :], new_scales, zero_value), filled, source)
        got_cache = lax.all_to_all(send_cache, "expert", split_axis=0, concat_axis=0, tiled=True)
        got_scales = lax.all_to_all(send_scales, "expert", split_axis=0, concat_axis=0, tiled=True)
        owned_cache, owned_scales = lax.ppermute((got_cache, got_scales), "segment", swap)
        return (*attention(*inputs), owned_cache, owned_scales)

    section = lax.axis_index("segment")
    units, half = capacity * positions // UNIT, columns // 2
    blocks = new_scales.shape[1]
    facts = owner * FACT + new_lengths
    sibling = lax.ppermute(facts, "segment", swap)
    chip = jnp.where(section == 0, jnp.stack([facts, sibling]), jnp.stack([sibling, facts]))
    chips = [chip] + [lax.ppermute(chip, "expert", [(e, (e + k) % 4) for e in range(4)]) for k in range(1, 4)]
    *streams, facts = pack(chips, new_scales, cache_t, units, capacity)

    def take(sizes):
        def run(operands):
            streams, facts, *inputs = operands
            got = []
            for way, size in enumerate(sizes):
                part = streams[way][: capacity * blocks + size * half]
                got.append(lax.ppermute(part, ("expert", "segment"), crossed(targets_of(way))))
            cleared, starts, counts = clear(facts, capacity, columns, positions)
            return (*attention(*inputs), *unpack(starts, counts, got, cleared, units, blocks))

        return run

    branches = [take(sizes) for _, sizes in BRANCHES]
    res_context, new_context, owned, owned_scales = by_halves(branches, (streams, facts, *inputs))
    return (res_context, new_context, jnp.transpose(owned, (0, 2, 1)), owned_scales)


def solution(mesh):
    placed = (
        P(("group", "expert", "segment", "attn"), None, None),
        P(("group", "expert", "segment", "attn"), None, None),
        P(("group", "expert", "segment", "attn")),
        P(("group", "expert", "segment", "attn"), None, None),
        P(("group", "expert", "segment", "attn"), None, None),
        P(("group", "expert", "segment", "attn"), None, None),
        P(("group", "expert", "segment", "attn")),
        P(("group", "expert", "segment", "attn"), None, None),
        P(("group", "expert", "segment", "attn")),
    )
    return jax.shard_map(
        on_device,
        mesh=mesh,
        in_specs=placed,
        out_specs=(
            P(("group", "expert", "segment", "attn"), None, None),
            P(("group", "expert", "segment", "attn"), None, None),
            P(("group", "expert", "segment", "attn"), None, None),
            P(("group", "expert", "segment", "attn"), None, None),
        ),
        check_vma=False,
    )
```
